32 devices in a mesh: dp: 8 (over z, x), fsdp: 4 (over y, core).
Axes of the slice: x: 2, y: 2, z: 4, core: 2. Of those that a mesh axis runs over, the one named last changes fastest.
Arguments:
- pixels: bfloat16 [64, 256, 13, 64], P(('dp', 'fsdp')), may hold values from -6 to 6
- sensor: int32 [64], P(('dp', 'fsdp')), may hold values from 0 to 3
- band_wave: int32 [64, 13], P(('dp', 'fsdp')), may hold values from 0 to 31
- visible: int32 [64, 256], P(('dp', 'fsdp')), may hold values from 0 to 1023, as said below
- block_order: int32 [1024], replicated, may hold values from 0 to 1023, each once
- pre_gain: bfloat16 [768], P(('dp', 'fsdp')), may hold values from 0.5 to 1.5
- pre_shift: bfloat16 [768], P(('dp', 'fsdp')), may hold values from -1.1953125 to 1.1953125
- qkv_weight: bfloat16 [768, 2304], P(('dp', 'fsdp')), may hold values from -0.21875 to 0.21875
- out_weight: bfloat16 [768, 768], P(('dp', 'fsdp')), may hold values from -0.625 to 0.625
- mid_gain: bfloat16 [768], P(('dp', 'fsdp')), may hold values from 0.5 to 1.5
- mid_shift: bfloat16 [768], P(('dp', 'fsdp')), may hold values from -1.1953125 to 1.1953125
- up_weight: bfloat16 [768, 3072], P(('dp', 'fsdp')), may hold values from -0.21875 to 0.21875
- up_bias: bfloat16 [3072], P(('dp', 'fsdp')), may hold values from -1.1953125 to 1.1953125
- down_weight: bfloat16 [3072, 768], P(('dp', 'fsdp')), may hold values from -0.109375 to 0.109375
- down_bias: bfloat16 [768], P(('dp', 'fsdp')), may hold values from -1.1953125 to 1.1953125
- dec_weight: bfloat16 [768, 512], P(('dp', 'fsdp')), may hold values from -0.21875 to 0.21875
- dec_bias: bfloat16 [512], P(('dp', 'fsdp')), may hold values from -1.1953125 to 1.1953125
- mask_token: bfloat16 [512], P(('dp', 'fsdp')), may hold values from -6 to 6
- gen_tokens: bfloat16 [129, 128], P(None, ('dp', 'fsdp')), may hold values from -6 to 6
- gen_qkv: bfloat16 [128, 384], P(('dp', 'fsdp')), may hold values from -0.5 to 0.5
- gen_out: bfloat16 [128, 128], P(('dp', 'fsdp')), may hold values from -1 to 1
- gen_out_bias: bfloat16 [128], P(('dp', 'fsdp')), may hold values from -1.1953125 to 1.1953125
- gen_gain1: bfloat16 [128], P(('dp', 'fsdp')), may hold values from 0.5 to 1.5
- gen_shift1: bfloat16 [128], P(('dp', 'fsdp')), may hold values from -1.1953125 to 1.1953125
- gen_up: bfloat16 [128, 2048], P(('dp', 'fsdp')), may hold values from -0.5 to 0.5
- gen_up_bias: bfloat16 [2048], P(('dp', 'fsdp')), may hold values from -1.1953125 to 1.1953125
- gen_down: bfloat16 [2048, 128], P(('dp', 'fsdp')), may hold values from -0.125 to 0.125
- gen_down_bias: bfloat16 [128], P(('dp', 'fsdp')), may hold values from -1.1953125 to 1.1953125
- gen_gain2: bfloat16 [128], P(('dp', 'fsdp')), may hold values from 0.5 to 1.5
- gen_shift2: bfloat16 [128], P(('dp', 'fsdp')), may hold values from -1.1953125 to 1.1953125
- kernel_weight: bfloat16 [128, 49152], P(None, ('dp', 'fsdp')), may hold values from -0.0234375 to 0.0234375
- kernel_bias: bfloat16 [49152], P(('dp', 'fsdp')), may hold values from -0.119628906 to 0.119628906
- bias_weight: bfloat16 [128, 768], P(('dp', 'fsdp')), may hold values from -0.5 to 0.5
- cotangent: bfloat16 [64, 1024, 512], P(None, ('dp', 'fsdp')), may hold values from -6 to 6
Outputs:
- decoder_in: bfloat16 [64, 1024, 512], P(None, ('dp', 'fsdp'))
- grad_pixels: float32 [64, 256, 13, 64], P(('dp', 'fsdp'))
- grad_pre_gain: float32 [768], P(('dp', 'fsdp'))
- grad_pre_shift: float32 [768], P(('dp', 'fsdp'))
- grad_qkv_weight: float32 [768, 2304], P(('dp', 'fsdp'))
- grad_out_weight: float32 [768, 768], P(('dp', 'fsdp'))
- grad_mid_gain: float32 [768], P(('dp', 'fsdp'))
- grad_mid_shift: float32 [768], P(('dp', 'fsdp'))
- grad_up_weight: float32 [768, 3072], P(('dp', 'fsdp'))
- grad_up_bias: float32 [3072], P(('dp', 'fsdp'))
- grad_down_weight: float32 [3072, 768], P(('dp', 'fsdp'))
- grad_down_bias: float32 [768], P(('dp', 'fsdp'))
- grad_dec_weight: float32 [768, 512], P(('dp', 'fsdp'))
- grad_dec_bias: float32 [512], P(('dp', 'fsdp'))
- grad_mask_token: float32 [512], P(('dp', 'fsdp'))
- grad_gen_tokens: float32 [129, 128], P(None, ('dp', 'fsdp'))
- grad_gen_qkv: float32 [128, 384], P(('dp', 'fsdp'))
- grad_gen_out: float32 [128, 128], P(('dp', 'fsdp'))
- grad_gen_out_bias: float32 [128], P(('dp', 'fsdp'))
- grad_gen_gain1: float32 [128], P(('dp', 'fsdp'))
- grad_gen_shift1: float32 [128], P(('dp', 'fsdp'))
- grad_gen_up: float32 [128, 2048], P(('dp', 'fsdp'))
- grad_gen_up_bias: float32 [2048], P(('dp', 'fsdp'))
- grad_gen_down: float32 [2048, 128], P(('dp', 'fsdp'))
- grad_gen_down_bias: float32 [128], P(('dp', 'fsdp'))
- grad_gen_gain2: float32 [128], P(('dp', 'fsdp'))
- grad_gen_shift2: float32 [128], P(('dp', 'fsdp'))
- grad_kernel_weight: float32 [128, 49152], P(None, ('dp', 'fsdp'))
- grad_kernel_bias: float32 [49152], P(('dp', 'fsdp'))
- grad_bias_weight: float32 [128, 768], P(('dp', 'fsdp'))
The draws below stay inside these ranges and needn't reach their ends.
Inputs may be any that keep to these rules, and one draw needn't show every extreme that they name: Each row of visible holds 256 different patch indices.
All inputs are finite; a program needn't handle non-finite values.
Results may differ from the reference program's by a relative error of at most 0.014.
Values may be sent and summed in bfloat16 or wider, within the bound.
A program may use at most 256 MiB of HBM per device.

```python
import math
import jax
import jax.numpy as jnp
from jax import lax

D = 768
HEADS = 12
FF = 3072
DEC = 512
WD = 128
GHEADS = 4
GFF = 2048
LAT = 128
PIX = 64
BANDS = 13
NWAVE = 32
GRID = 32
VIS = 256
CHIP_DEV = 2
PATCH = 1024
GTOK = 129
CHIPS = 64


def draw_visible(key, part):
    key = jax.random.fold_in(key, 7)
    row_keys = jax.random.split(key, CHIPS)

    def pick_row(row_key):
        return jax.random.permutation(row_key, PATCH)[:VIS]
    chosen = jax.vmap(pick_row)(row_keys)
    return chosen.astype(jnp.int32)


def with_ends(values, rng, low, high):
    spot = [jax.random.randint(jax.random.fold_in(rng, axis), (), 0, length) for axis, length in enumerate(values.shape)]
    widest = values.shape.index(max(values.shape))
    neighbour = spot[:widest] + [(spot[widest] + 1) % values.shape[widest]] + spot[widest + 1:]
    return values.at[tuple(spot)].set(low).at[tuple(neighbour)].set(high)


def levels(rng, shape, cuts, smallest, top_value):
    level = 1.0
    for axis_at, blocks in cuts:
        draws = jax.random.uniform(jax.random.fold_in(jax.random.fold_in(rng, 6), axis_at), (blocks,), jnp.float32, smallest / len(cuts), top_value / len(cuts))
        level = level * jnp.repeat(jnp.exp(draws), shape[axis_at] // blocks).reshape((-1,) + (1,) * (len(shape) - 1 - axis_at))
    return level


def normal_values(rng, dims, deviation, reach, shards=(), held_as=jnp.bfloat16):
    values = deviation * jax.random.normal(rng, dims, jnp.float32)
    if shards:
        values = values * levels(rng, dims, shards, -0.22, 0.18)
    return jnp.clip(values, -reach, reach).astype(held_as)


def setup_inputs(seed: int = 0) -> dict:
    key_of = jax.random.split(jax.random.key(seed), 35)
    return {
        "pixels": normal_values(key_of[0], (CHIPS, VIS, BANDS, PIX), 1.0, 6.0, ((0, 32),)),
        "sensor": with_ends(jax.random.randint(key_of[1], (CHIPS,), 0, 4), jax.random.fold_in(key_of[1], 1), 0, 3).astype(jnp.int32),
        "band_wave": with_ends(jax.random.randint(key_of[2], (CHIPS, BANDS), 0, NWAVE), jax.random.fold_in(key_of[2], 1), 0, NWAVE - 1).astype(jnp.int32),
        "visible": draw_visible(jax.random.fold_in(key_of[34], 71), 0),
        "block_order": jax.random.permutation(key_of[4], PATCH).astype(jnp.int32),
        "pre_gain": jnp.clip(1.0 + 0.1 * jax.random.normal(key_of[5], (D,), jnp.float32), 0.5, 1.5).astype(jnp.bfloat16),
        "pre_shift": normal_values(key_of[6], (D,), 0.2, 1.1953125, ((0, 32),)),
        "qkv_weight": normal_values(key_of[7], (D, 3 * D), D ** -0.5, 0.21875, ((0, 32),)),
        "out_weight": normal_values(key_of[8], (D, D), (D // 8) ** -0.5, 0.625, ((0, 32),)),
        "mid_gain": jnp.clip(1.0 + 0.1 * jax.random.normal(key_of[9], (D,), jnp.float32), 0.5, 1.5).astype(jnp.bfloat16),
        "mid_shift": normal_values(key_of[10], (D,), 0.2, 1.1953125, ((0, 32),)),
        "up_weight": normal_values(key_of[11], (D, FF), D ** -0.5, 0.21875, ((0, 32),)),
        "up_bias": normal_values(key_of[12], (FF,), 0.2, 1.1953125, ((0, 32),)),
        "down_weight": normal_values(key_of[13], (FF, D), FF ** -0.5, 0.109375, ((0, 32),)),
        "down_bias": normal_values(key_of[14], (D,), 0.2, 1.1953125, ((0, 32),)),
        "dec_weight": normal_values(key_of[15], (D, DEC), D ** -0.5, 0.21875, ((0, 32),)),
        "dec_bias": normal_values(key_of[16], (DEC,), 0.2, 1.1953125, ((0, 32),)),
        "mask_token": normal_values(key_of[17], (DEC,), 1.0, 6.0, ((0, 32),)),
        "gen_tokens": normal_values(key_of[18], (GTOK, WD), 1.0, 6.0, ((1, 32),)),
        "gen_qkv": normal_values(key_of[19], (WD, 3 * WD), WD ** -0.5, 0.5, ((0, 32),)),
        "gen_out": normal_values(key_of[20], (WD, WD), (WD // 4) ** -0.5, 1.0, ((0, 32),)),
        "gen_out_bias": normal_values(key_of[21], (WD,), 0.2, 1.1953125, ((0, 32),)),
        "gen_gain1": jnp.clip(1.0 + 0.1 * jax.random.normal(key_of[22], (WD,), jnp.float32), 0.5, 1.5).astype(jnp.bfloat16),
        "gen_shift1": normal_values(key_of[23], (WD,), 0.2, 1.1953125, ((0, 32),)),
        "gen_up": normal_values(key_of[24], (WD, GFF), WD ** -0.5, 0.5, ((0, 32),)),
        "gen_up_bias": normal_values(key_of[25], (GFF,), 0.2, 1.1953125, ((0, 32),)),
        "gen_down": normal_values(key_of[26], (GFF, WD), GFF ** -0.5, 0.125, ((0, 32),)),
        "gen_down_bias": normal_values(key_of[27], (WD,), 0.2, 1.1953125, ((0, 32),)),
        "gen_gain2": jnp.clip(1.0 + 0.1 * jax.random.normal(key_of[28], (WD,), jnp.float32), 0.5, 1.5).astype(jnp.bfloat16),
        "gen_shift2": normal_values(key_of[29], (WD,), 0.2, 1.1953125, ((0, 32),)),
        "kernel_weight": normal_values(key_of[30], (WD, PIX * D), (WD * PIX * 8) ** -0.5, 0.0234375, ((1, 32),)),
        "kernel_bias": normal_values(key_of[31], (PIX * D,), 0.02, 0.119628906, ((0, 32),)),
        "bias_weight": normal_values(key_of[32], (WD, D), WD ** -0.5, 0.5, ((0, 32),)),
        "cotangent": normal_values(key_of[33], (CHIPS, PATCH, DEC), 1.0, 6.0, ((1, 32),)),
    }


@jax.custom_vjp
def low(v):
    return lax.optimization_barrier(v.astype(jnp.bfloat16)).astype(jnp.float32)

@jax.custom_vjp
def low_back(v):
    return v

def low_keep(v):
    return (low(v), None)

def low_pass(kept, grad):
    return (grad,)

def back_keep(v):
    return (v, None)

def back_low(kept, grad):
    return (low(grad),)
low.defvjp(low_keep, low_pass)
low_back.defvjp(back_keep, back_low)
EPS = 1e-05
BAND_DROP = (0, 6, 9, 7)
HIGH = lax.Precision.HIGHEST

def sincos(values, count):
    freq = jnp.exp(jnp.arange(count, dtype=jnp.float32) * (-math.log(10000.0) / count))
    angle = values[..., None] * freq
    return jnp.concatenate([jnp.sin(angle), jnp.cos(angle)], axis=-1)

def norm_rows(rows, gain, shift):
    mean = lax.optimization_barrier(jnp.mean(rows, axis=-1, keepdims=True))
    centred = rows - mean
    spread = lax.optimization_barrier(jnp.mean(centred * centred, axis=-1, keepdims=True))
    return centred * lax.rsqrt(spread + EPS) * gain + shift

def band_valid(sensor, bands):
    drops = jnp.array(BAND_DROP, jnp.int32)
    picked = jnp.where(sensor[:, None] == jnp.arange(4, dtype=jnp.int32)[None, :], drops[None, :], 0)
    count = bands - lax.optimization_barrier(jnp.sum(picked, axis=1))
    return (jnp.arange(bands, dtype=jnp.int32)[None, :] < count[:, None]).astype(jnp.float32)

def place_code(visible, width):
    row = (visible // GRID).astype(jnp.float32)
    col = (visible % GRID).astype(jnp.float32)
    return jnp.concatenate([sincos(row, width // 4), sincos(col, width // 4)], axis=-1)

def gen_core(wave_code, tokens, gen_qkv, gen_out, gen_out_bias, gen_gain1, gen_shift1, gen_up, gen_up_bias, gen_down, gen_down_bias, gen_gain2, gen_shift2):
    sequence = jnp.concatenate([tokens[:LAT], wave_code, tokens[LAT:]], axis=0)
    length = sequence.shape[0]
    width = sequence.shape[1]
    head_dim = width // GHEADS
    joint = jnp.dot(sequence, gen_qkv, precision=HIGH).reshape(length, 3, GHEADS, head_dim)
    scores = jnp.einsum('qhe,khe->hqk', joint[:, 0], joint[:, 1], precision=HIGH) / math.sqrt(head_dim)
    probs = jax.nn.softmax(scores, axis=-1)
    context = jnp.einsum('hqk,khe->qhe', probs, joint[:, 2], precision=HIGH).reshape(length, width)
    mixed = norm_rows(sequence + jnp.dot(context, gen_out, precision=HIGH) + gen_out_bias, gen_gain1, gen_shift1)
    hidden = jax.nn.gelu(jnp.dot(mixed, gen_up, precision=HIGH) + gen_up_bias, approximate=False)
    final = norm_rows(mixed + jnp.dot(hidden, gen_down, precision=HIGH) + gen_down_bias, gen_gain2, gen_shift2)
    feature = final[LAT:LAT + NWAVE] + sequence[LAT:LAT + NWAVE]
    return (feature, final[length - 1])

def generator(tokens, gen_qkv, gen_out, gen_out_bias, gen_gain1, gen_shift1, gen_up, gen_up_bias, gen_down, gen_down_bias, gen_gain2, gen_shift2, kernel_weight, kernel_bias, bias_weight):
    wave_code = low(sincos(jnp.arange(NWAVE, dtype=jnp.float32), WD // 2))
    feature, source = gen_core(wave_code, tokens, gen_qkv, gen_out, gen_out_bias, gen_gain1, gen_shift1, gen_up, gen_up_bias, gen_down, gen_down_bias, gen_gain2, gen_shift2)
    kernels = low_back(low(jnp.dot(low(feature), kernel_weight, precision=HIGH) + kernel_bias))
    conv_bias = jnp.dot(low(source), bias_weight, precision=HIGH)
    return (kernels, conv_bias)

def group_forward(pixels, valid, onehot, place, visible, block_order, kernels, conv_bias, pre_gain, pre_shift, qkv_weight, out_weight, mid_gain, mid_shift, up_weight, up_bias, down_weight, down_bias, dec_weight, dec_bias, mask_token):
    chips = pixels.shape[0]
    seen = pixels.shape[1]
    width = qkv_weight.shape[0]
    head_dim = width // HEADS
    band_kernels = jnp.einsum('cbw,wk->cbk', onehot, kernels, precision=HIGH)
    band_kernels = band_kernels.reshape(chips, BANDS, PIX, width)
    masked = pixels * valid[:, None, :, None]
    embedded = low_back(jnp.einsum('cvbp,cbpd->cvd', masked, band_kernels, precision=HIGH))
    start = embedded + conv_bias + place
    normed = low(norm_rows(start, pre_gain, pre_shift))
    joint = jnp.einsum('cvd,de->cve', normed, qkv_weight, precision=HIGH).reshape(chips, seen, 3, HEADS, head_dim)
    queries = low_back(low(joint[:, :, 0]))
    keys = low_back(low(joint[:, :, 1]))
    values = low_back(low(joint[:, :, 2]))
    scores = low_back(jnp.einsum('cqhe,ckhe->chqk', queries, keys, precision=HIGH) / math.sqrt(head_dim))
    probs = low(jax.nn.softmax(scores, axis=-1))
    context = jnp.einsum('chqk,ckhe->cqhe', probs, values, precision=HIGH).reshape(chips, seen, width)
    context = low_back(low(context))
    attended = low_back(jnp.einsum('cvd,de->cve', context, out_weight, precision=HIGH))
    middle = start + attended
    normed2 = low(norm_rows(middle, mid_gain, mid_shift))
    upper = low_back(jnp.einsum('cvd,df->cvf', normed2, up_weight, precision=HIGH) + up_bias)
    activ = low(jax.nn.gelu(upper, approximate=False))
    branch = low_back(jnp.einsum('cvf,fd->cvd', activ, down_weight, precision=HIGH) + down_bias)
    ending = middle + branch
    decoded = low(jnp.einsum('cvd,de->cve', low(ending), dec_weight, precision=HIGH) + dec_bias)
    canvas = jnp.broadcast_to(mask_token, (chips, PATCH, mask_token.shape[0]))
    canvas = canvas.at[jnp.arange(chips)[:, None], visible].set(decoded)
    return jnp.take(canvas, block_order, axis=1)

def reference(pixels, sensor, band_wave, visible, block_order, pre_gain, pre_shift, qkv_weight, out_weight, mid_gain, mid_shift, up_weight, up_bias, down_weight, down_bias, dec_weight, dec_bias, mask_token, gen_tokens, gen_qkv, gen_out, gen_out_bias, gen_gain1, gen_shift1, gen_up, gen_up_bias, gen_down, gen_down_bias, gen_gain2, gen_shift2, kernel_weight, kernel_bias, bias_weight, cotangent):
    layer = (pre_gain, pre_shift, qkv_weight, out_weight, mid_gain, mid_shift, up_weight, up_bias, down_weight, down_bias, dec_weight, dec_bias, mask_token)
    layer = tuple((item.astype(jnp.float32) for item in layer))
    gen = (gen_tokens, gen_qkv, gen_out, gen_out_bias, gen_gain1, gen_shift1, gen_up, gen_up_bias, gen_down, gen_down_bias, gen_gain2, gen_shift2, kernel_weight, kernel_bias, bias_weight)
    gen = tuple((item.astype(jnp.float32) for item in gen))
    (kernels, conv_bias), gen_pull = jax.vjp(generator, *gen)
    groups = CHIPS // CHIP_DEV

    def one_group(totals, index):
        first = index * CHIP_DEV
        pix_group = lax.dynamic_slice_in_dim(pixels, first, CHIP_DEV, 0).astype(jnp.float32)
        sensor_group = lax.dynamic_slice_in_dim(sensor, first, CHIP_DEV, 0)
        wave_group = lax.dynamic_slice_in_dim(band_wave, first, CHIP_DEV, 0)
        seen_group = lax.dynamic_slice_in_dim(visible, first, CHIP_DEV, 0)
        cot_group = lax.dynamic_slice_in_dim(cotangent, first, CHIP_DEV, 0).astype(jnp.float32)
        valid = band_valid(sensor_group, BANDS)
        onehot = (wave_group[:, :, None] == jnp.arange(NWAVE, dtype=jnp.int32)[None, None, :]).astype(jnp.float32)
        place = place_code(seen_group, D)

        def forward(pix_in, kern, cbias, *params):
            return group_forward(pix_in, valid, onehot, place, seen_group, block_order, kern, cbias, *params)
        result, pull = jax.vjp(forward, pix_group, kernels, conv_bias, *layer)
        grads = pull(cot_group)
        totals = tuple((total + grad for total, grad in zip(totals, grads[1:])))
        return (totals, (result.astype(jnp.bfloat16), grads[0]))
    zeros = (jnp.zeros_like(kernels), jnp.zeros_like(conv_bias)) + tuple((jnp.zeros_like(item) for item in layer))
    totals, outputs = lax.scan(one_group, zeros, jnp.arange(groups, dtype=jnp.int32))
    decoder_in = outputs[0].reshape(CHIPS, PATCH, DEC)
    grad_pixels = outputs[1].reshape(CHIPS, VIS, BANDS, PIX)
    gen_grads = gen_pull((totals[0], totals[1]))
    return (decoder_in, grad_pixels, totals[2], totals[3], totals[4], totals[5], totals[6], totals[7], totals[8], totals[9], totals[10], totals[11], totals[12], totals[13], totals[14], gen_grads[0], gen_grads[1], gen_grads[2], gen_grads[3], gen_grads[4], gen_grads[5], gen_grads[6], gen_grads[7], gen_grads[8], gen_grads[9], gen_grads[10], gen_grads[11], gen_grads[12], gen_grads[13], gen_grads[14])
```

```python
from functools import partial
import math

import jax
import jax.numpy as jnp
from jax import lax
from jax.experimental import pallas as pl
from jax.experimental.pallas import tpu as pltpu
from jax.sharding import PartitionSpec as P

HEADS = 12
WD = 128
GHEADS = 4
LAT = 128
NWAVE = 32
GRID = 32
PATCH = 1024


EPS = 1e-05
AXES = ("dp", "fsdp")
BAND_DROP = (0, 6, 9, 7)
HIGH = lax.Precision.HIGHEST


def sincos(values, count):
    freq = jnp.exp(jnp.arange(count, dtype=jnp.float32) * (-math.log(10000.0) / count))
    angle = values[..., None] * freq
    return jnp.concatenate([jnp.sin(angle), jnp.cos(angle)], axis=-1)


def norm_rows(rows, gain, shift):
    mean = jnp.mean(rows, axis=-1, keepdims=True)
    centred = rows - mean
    spread = jnp.mean(centred * centred, axis=-1, keepdims=True)
    return centred * lax.rsqrt(spread + EPS) * gain + shift


def exact_gelu(values):
    return jax.nn.gelu(values, approximate=False)


def band_valid(sensor, bands):
    drops = jnp.array(BAND_DROP, jnp.int32)
    picked = jnp.where(
        sensor[:, None] == jnp.arange(4, dtype=jnp.int32)[None, :], drops[None, :], 0
    )
    count = bands - jnp.sum(picked, axis=1)
    return (jnp.arange(bands, dtype=jnp.int32)[None, :] < count[:, None]).astype(jnp.float32)


def place_code(visible, width):
    row = (visible // GRID).astype(jnp.float32)
    col = (visible % GRID).astype(jnp.float32)
    return jnp.concatenate([sincos(row, width // 4), sincos(col, width // 4)], axis=-1)


def gen_core(
    wave_code,
    tokens,
    gen_qkv,
    gen_out,
    gen_out_bias,
    gen_gain1,
    gen_shift1,
    gen_up,
    gen_up_bias,
    gen_down,
    gen_down_bias,
    gen_gain2,
    gen_shift2,
):
    sequence = jnp.concatenate([tokens[:LAT], wave_code, tokens[LAT:]], axis=0)
    length = sequence.shape[0]
    width = sequence.shape[1]
    head_dim = width // GHEADS
    joint = jnp.dot(sequence, gen_qkv, precision=HIGH).reshape(length, 3, GHEADS, head_dim)
    scores = jnp.einsum("qhe,khe->hqk", joint[:, 0], joint[:, 1], precision=HIGH) / math.sqrt(
        head_dim
    )
    probs = jax.nn.softmax(scores, axis=-1)
    context = jnp.einsum("hqk,khe->qhe", probs, joint[:, 2], precision=HIGH).reshape(length, width)
    mixed = norm_rows(
        sequence + jnp.dot(context, gen_out, precision=HIGH) + gen_out_bias, gen_gain1, gen_shift1
    )
    hidden = jax.nn.gelu(jnp.dot(mixed, gen_up, precision=HIGH) + gen_up_bias, approximate=False)
    final = norm_rows(
        mixed + jnp.dot(hidden, gen_down, precision=HIGH) + gen_down_bias, gen_gain2, gen_shift2
    )
    feature = final[LAT : LAT + NWAVE] + sequence[LAT : LAT + NWAVE]
    return (feature, final[length - 1])


def own_part(full, dim):
    count = lax.axis_size("dp") * lax.axis_size("fsdp")
    index = lax.axis_index("dp") * lax.axis_size("fsdp") + lax.axis_index("fsdp")
    piece = full.shape[dim] // count
    return lax.dynamic_slice_in_dim(full, index * piece, piece, dim)


def tdot(left, right):
    return lax.dot_general(
        left, right, (((0,), (0,)), ((), ())), preferred_element_type=jnp.float32
    )


def ndot(left, right):
    return lax.dot_general(
        left, right, (((1,), (1,)), ((), ())), preferred_element_type=jnp.float32
    )


MESH_ID = pl.DeviceIdType.MESH
ANY = pl.BlockSpec(memory_space=pl.ANY)
VMEM = pl.BlockSpec(memory_space=pltpu.VMEM)


class Net:
    def __init__(self, planes):
        dp, fs = lax.axis_index("dp"), lax.axis_index("fsdp")
        self.planes = planes
        self.z, self.x = lax.div(dp, 2), lax.rem(dp, 2)
        self.y, self.c = lax.div(fs, 2), lax.rem(fs, 2)
        self.sib = self.at(self.z, self.x, self.y, 1 - self.c)
        self.nx = self.at(self.z, 1 - self.x, self.y, self.c)
        self.ny = self.at(self.z, self.x, 1 - self.y, self.c)

    def at(self, z, x, y, c):
        return (z * 2 + x, y * 2 + c)

    def plane(self, k):
        return lax.rem(self.z + k, self.planes)

    def zpeer(self, k):
        return self.at(self.plane(k), self.x, self.y, self.c)

    def chip(self, k, dx=0, dy=0):
        x = 1 - self.x if dx else self.x
        y = 1 - self.y if dy else self.y
        return self.plane(k) * 4 + x * 2 + y

    def greet(self):
        barrier = pltpu.get_barrier_semaphore()
        partners = [self.sib, self.nx, self.ny]
        partners += [self.zpeer(k) for k in range(1, self.planes)]
        for partner in partners:
            pl.semaphore_signal(barrier, inc=1, device_id=partner, device_id_type=MESH_ID)
        pl.semaphore_wait(barrier, len(partners))


class Wires:
    def __init__(self, send, recv):
        self.send, self.recv, self.used, self.started = send, recv, 0, []

    def push(self, src, dst, device):
        index = self.used
        self.used += 1
        copy = pltpu.make_async_remote_copy(
            src_ref=src,
            dst_ref=dst,
            send_sem=self.send.at[index],
            recv_sem=self.recv.at[index],
            device_id=device,
            device_id_type=MESH_ID,
        )
        copy.start()
        self.started.append(copy)
        return copy

    def drain(self):
        for copy in self.started:
            copy.wait_send()


class Gather:
    def __init__(self, net, wires, own, piece):
        self.net, self.wires, self.own, self.piece = net, wires, own, piece
        self.z_in, self.first, self.second, self.twins = {}, {}, {}, []

    def near(self, h):
        return self.net.ny if h else self.net.nx

    def far(self, h):
        return self.net.nx if h else self.net.ny

    def share(self, chip, h, src=None):
        spot = self.piece(chip, h)
        self.twins.append(self.wires.push(spot if src is None else src, spot, self.net.sib))

    def begin(self):
        for k in range(1, self.net.planes):
            for h in range(2):
                spot = self.piece(self.net.chip(0), h)
                self.z_in[k, h] = self.wires.push(self.own(h), spot, self.net.zpeer(k))
        self.spread(0)

    def spread(self, k):
        back = (self.net.planes - k) % self.net.planes
        for h in range(2):
            if k:
                self.z_in[k, h].wait_recv()
            spot = self.piece(self.net.chip(back), h)
            src = self.own(h) if k == 0 else spot
            self.first[k, h] = self.wires.push(src, spot, self.near(h))
            self.second[k, h, 0] = self.wires.push(src, spot, self.far(h))
            self.share(self.net.chip(back), h, src)

    def relay(self, k):
        back = (self.net.planes - k) % self.net.planes
        for h in range(2):
            self.first[k, h].wait_recv()
            chip = self.net.chip(back, dx=h == 0, dy=h == 1)
            spot = self.piece(chip, h)
            self.second[k, h, 1] = self.wires.push(spot, spot, self.far(h))
            self.share(chip, h)

    def close(self, k):
        back = (self.net.planes - k) % self.net.planes
        for h in range(2):
            for hop in range(2):
                self.second[k, h, hop].wait_recv()
                chip = self.net.chip(back, dx=hop == 1 or h == 1, dy=hop == 1 or h == 0)
                self.share(chip, h)

    def finish(self):
        for copy in self.twins:
            copy.wait_recv()


def gather_copies(planes):
    return 2 * (planes - 1) + 4 * planes + 2 * planes + 8 * planes


def run_gathers(gathers, planes):
    for item in gathers:
        item.begin()
    for k in range(planes):
        for item in gathers:
            if k:
                item.spread(k)
            item.relay(k)
    for k in range(planes):
        for item in gathers:
            item.close(k)
    for item in gathers:
        item.finish()


def small_gather_kernel(planes, src, out, send, recv, local):
    net = Net(planes)
    net.greet()
    wires = Wires(send, recv)
    half = src.shape[0] // 2
    own = lambda h: src.at[pl.ds(h * half, half)]
    piece = lambda chip, h: out.at[chip * 2 + net.c, pl.ds(h * half, half)]
    here = pltpu.make_async_copy(src, out.at[net.chip(0) * 2 + net.c], local)
    here.start()
    run_gathers([Gather(net, wires, own, piece)], planes)
    here.wait()
    wires.drain()


def small_gather(packed, planes, devices):
    copies = gather_copies(planes)
    return pl.pallas_call(
        partial(small_gather_kernel, planes),
        out_shape=jax.ShapeDtypeStruct((devices,) + packed.shape, packed.dtype),
        in_specs=[VMEM],
        out_specs=VMEM,
        scratch_shapes=[
            pltpu.SemaphoreType.DMA((copies,)),
            pltpu.SemaphoreType.DMA((copies,)),
            pltpu.SemaphoreType.DMA,
        ],
        compiler_params=pltpu.CompilerParams(collective_id=0, has_side_effects=True),
    )(packed)


def weight_gather_kernel(
    planes, wide, down, table, wide_out, down_out, table_out, fresh, joined, send, recv, local
):
    net = Net(planes)
    net.greet()
    wires = Wires(send, recv)
    rows = wide.shape[0]
    cols = wide.shape[1] // 2
    quarter = cols // 2
    mine = pl.ds(pl.multiple_of(net.c * cols, 128), cols)
    theirs = pl.ds(pl.multiple_of((1 - net.c) * cols, 128), cols)
    pair = wires.push(wide.at[:, theirs], fresh, net.sib)
    t_rows, t_cols = table.shape
    t_half = t_cols // 2
    t_own = lambda h: table.at[:, pl.ds(h * t_half, t_half)]
    t_piece = lambda chip, h: table_out.at[
        :, pl.ds(pl.multiple_of((chip * 2 + net.c) * t_cols + h * t_half, 128), t_half)
    ]
    d_rows = down.shape[0]
    d_half = d_rows // 2
    d_own = lambda h: down.at[pl.ds(h * d_half, d_half)]
    d_piece = lambda chip, h: down_out.at[
        pl.ds(pl.multiple_of((chip * 2 + net.c) * d_rows + h * d_half, 16), d_half)
    ]
    w_own = lambda h: joined.at[:, pl.ds(h * quarter, quarter)]
    w_piece = lambda chip, h: wide_out.at[
        pl.ds(pl.multiple_of(chip * 2 * rows, 16), 2 * rows),
        pl.ds(pl.multiple_of((net.c * 2 + h) * quarter, 128), quarter),
    ]
    t_gather = Gather(net, wires, t_own, t_piece)
    d_gather = Gather(net, wires, d_own, d_piece)
    w_gather = Gather(net, wires, w_own, w_piece)
    here = []
    for own, piece in ((t_own, t_piece), (d_own, d_piece)):
        for h in range(2):
            here.append(pltpu.make_async_copy(own(h), piece(net.chip(0), h), local.at[len(here)]))
            here[-1].start()
    t_gather.begin()
    d_gather.begin()
    pair.wait_recv()
    own32 = wide[:, mine].astype(jnp.float32)
    sib32 = fresh[...].astype(jnp.float32)
    first = net.c == 0
    joined[...] = jnp.concatenate(
        [jnp.where(first, own32, sib32), jnp.where(first, sib32, own32)], axis=0
    ).astype(joined.dtype)
    for h in range(2):
        here.append(pltpu.make_async_copy(w_own(h), w_piece(net.chip(0), h), local.at[len(here)]))
        here[-1].start()
    w_gather.begin()
    gathers = [t_gather, d_gather, w_gather]
    for k in range(planes):
        for item in gathers:
            if k:
                item.spread(k)
            item.relay(k)
    for k in range(planes):
        for item in gathers:
            item.close(k)
    for item in gathers:
        item.finish()
    for copy in here:
        copy.wait()
    wires.drain()


def weight_gather(wide, down, table, planes, devices):
    copies = 3 * gather_copies(planes) + 1
    rows, cols = wide.shape
    low = wide.dtype
    return pl.pallas_call(
        partial(weight_gather_kernel, planes),
        out_shape=(
            jax.ShapeDtypeStruct((rows * devices, cols), low),
            jax.ShapeDtypeStruct((down.shape[0] * devices, down.shape[1]), low),
            jax.ShapeDtypeStruct((table.shape[0], table.shape[1] * devices), low),
        ),
        in_specs=[VMEM] * 3,
        out_specs=[ANY] * 3,
        scratch_shapes=[
            pltpu.VMEM((rows, cols // 2), low),
            pltpu.VMEM((2 * rows, cols // 2), low),
            pltpu.SemaphoreType.DMA((copies,)),
            pltpu.SemaphoreType.DMA((copies,)),
            pltpu.SemaphoreType.DMA((6,)),
        ],
        compiler_params=pltpu.CompilerParams(
            collective_id=1, has_side_effects=True, vmem_limit_bytes=40 * 2**20
        ),
    )(wide, down, table)


class Reduce:
    def __init__(self, net, wires, part, held, near_in, far_in, z_in):
        self.net, self.wires, self.part, self.held = net, wires, part, held
        self.near_in, self.far_in, self.z_in = near_in, far_in, z_in
        self.pairs, self.near, self.far, self.along = {}, {}, {}, {}

    def add(self, spot, other):
        size = 16 if spot.shape[0] % 16 == 0 else 8

        def some(i, _):
            at = pl.ds(pl.multiple_of(i * size, size), size)
            total = spot[at].astype(jnp.float32) + other[at].astype(jnp.float32)
            spot[at] = total.astype(spot.dtype)
            return 0

        lax.fori_loop(0, spot.shape[0] // size, some, 0)

    def begin(self, k):
        for dx in range(2):
            for dy in range(2):
                for h in range(2):
                    chip = self.net.chip(k, dx, dy)
                    self.pairs[k, dx, dy, h] = self.wires.push(
                        self.part(chip, 1 - self.net.c, h), self.held.at[chip, h], self.net.sib
                    )

    def stage0(self, k):
        for dx, dy in ((1, 1), (0, 1), (1, 0), (0, 0)):
            for h in range(2):
                self.pairs[k, dx, dy, h].wait_recv()
                chip = self.net.chip(k, dx, dy)
                self.add(self.held.at[chip, h], self.part(chip, self.net.c, h))
                if (dy if h == 0 else dx) == 1:
                    other = dx if h == 0 else dy
                    self.near[k, h, other] = self.wires.push(
                        self.held.at[chip, h],
                        self.near_in.at[k, h, other],
                        self.net.ny if h == 0 else self.net.nx,
                    )

    def stage1(self, k):
        for h in range(2):
            for other in (1, 0):
                self.near[k, h, other].wait_recv()
                chip = self.net.chip(k, other, 0) if h == 0 else self.net.chip(k, 0, other)
                self.add(self.held.at[chip, h], self.near_in.at[k, h, other])
                if other:
                    self.far[k, h] = self.wires.push(
                        self.held.at[chip, h],
                        self.far_in.at[k, h],
                        self.net.nx if h == 0 else self.net.ny,
                    )

    def stage2(self, k):
        for h in range(2):
            self.far[k, h].wait_recv()
            spot = self.held.at[self.net.chip(k), h]
            self.add(spot, self.far_in.at[k, h])
            if k:
                self.along[k, h] = self.wires.push(spot, self.z_in.at[k - 1, h], self.net.zpeer(k))

    def total(self, h):
        value = self.held[self.net.chip(0), h].astype(jnp.float32)
        for k in range(1, self.net.planes):
            self.along[k, h].wait_recv()
            value = value + self.z_in[k - 1, h].astype(jnp.float32)
        return value


def reduce_copies(planes):
    return 8 * planes + 4 * planes + 2 * planes + 2 * (planes - 1)


def reduce_scratch(planes, rows, cols, dtype):
    return [
        pltpu.VMEM((planes * 4, 2, rows, cols), dtype),
        pltpu.VMEM((planes, 2, 2, rows, cols), dtype),
        pltpu.VMEM((planes, 2, rows, cols), dtype),
        pltpu.VMEM((planes - 1, 2, rows, cols), dtype),
    ]


def grad_reduce_kernel(planes, steps, *refs):
    wide, down, table, vec, conv, weight = refs[:6]
    wide_out, down_out, table_out, vec_out, all_out = refs[6:11]
    scratch = refs[11:27]
    final, hand, box, send, recv = refs[27:]
    net = Net(planes)
    net.greet()
    wires = Wires(send, recv)
    w_rows, w_cols = final.shape[1:]
    d_rows = down_out.shape[0] // 2
    t_cols = table_out.shape[1] // 2
    w_part = lambda chip, c, h: wide.at[
        pl.ds(pl.multiple_of(chip * w_rows, 16), w_rows),
        pl.ds(pl.multiple_of((c * 2 + h) * w_cols, 128), w_cols),
    ]
    d_part = lambda chip, c, h: down.at[
        pl.ds(pl.multiple_of(((chip * 2 + c) * 2 + h) * d_rows, 16), d_rows)
    ]
    t_part = lambda chip, c, h: table.at[
        :, pl.ds(pl.multiple_of(((chip * 2 + c) * 2 + h) * t_cols, 128), t_cols)
    ]
    v_part = lambda chip, c, h: vec.at[chip, c, h]
    items = [
        Reduce(net, wires, part, *scratch[i * 4 : i * 4 + 4])
        for i, part in enumerate((t_part, v_part, w_part, d_part))
    ]
    order = list(range(1, planes)) + [0]
    units = [(item, k) for item in items for k in order]
    for item, k in units:
        item.begin(k)
    for t in range(len(units) + 2):
        if t < len(units):
            units[t][0].stage0(units[t][1])
        if 0 <= t - 1 < len(units):
            units[t - 1][0].stage1(units[t - 1][1])
        if 0 <= t - 2 < len(units):
            units[t - 2][0].stage2(units[t - 2][1])
    tables, vecs, wides, downs = items
    for h in range(2):
        table_out[:, pl.ds(h * t_cols, t_cols)] = tables.total(h).astype(table_out.dtype)
    box[0, pl.ds(0, table.shape[0])] = lax.dot_general(
        table_out[...], weight[...], (((1,), (1,)), ((), ())), preferred_element_type=jnp.float32
    )
    box[0, pl.ds(table.shape[0], conv.shape[0])] = conv[...]
    peers = [net.sib, net.nx, net.ny]
    for bit in range(steps):
        step = 1 << bit
        up = lax.rem(lax.div(net.z, step), 2) == 0
        peers.append(net.at(jnp.where(up, net.z + step, net.z - step), net.x, net.y, net.c))
    for i, peer in enumerate(peers):
        hop = wires.push(box.at[2 * i], box.at[2 * i + 1], peer)
        hop.wait_recv()
        box[2 * i + 2] = box[2 * i] + box[2 * i + 1]
    all_out[...] = box[2 * len(peers)]
    for h in range(2):
        vec_out[h] = vecs.total(h)
    for h in range(2):
        final[h] = wides.total(h)
    half = w_rows // 2
    mine = pl.ds(pl.multiple_of(net.c * half, 8), half)
    theirs = pl.ds(pl.multiple_of((1 - net.c) * half, 8), half)
    swaps = [
        wires.push(final.at[h, theirs], hand.at[h], net.sib) for h in range(2)
    ]
    for h in range(2):
        down_out[pl.ds(h * d_rows, d_rows)] = downs.total(h)
    for h in range(2):
        own = pl.ds(pl.multiple_of((net.c * 2 + h) * w_cols, 128), w_cols)
        wide_out[:, own] = final[h, mine]
    for h in range(2):
        swaps[h].wait_recv()
        other = pl.ds(pl.multiple_of(((1 - net.c) * 2 + h) * w_cols, 128), w_cols)
        wide_out[:, other] = hand[h]
    wires.drain()


def grad_reduce(wide, down, table, vec, conv, weight, planes):
    devices = planes * 8
    low = wide.dtype
    steps = (planes - 1).bit_length()
    w_rows, w_cols = wide.shape[0] // (devices // 2), wide.shape[1] // 4
    d_rows = down.shape[0] // devices // 2
    t_cols = table.shape[1] // devices // 2
    copies = 4 * reduce_copies(planes) + 2 + 3 + steps
    box = (table.shape[0] + conv.shape[0], conv.shape[1])
    return pl.pallas_call(
        partial(grad_reduce_kernel, planes, steps),
        out_shape=(
            jax.ShapeDtypeStruct((w_rows // 2, wide.shape[1]), jnp.float32),
            jax.ShapeDtypeStruct((2 * d_rows, down.shape[1]), jnp.float32),
            jax.ShapeDtypeStruct((table.shape[0], 2 * t_cols), low),
            jax.ShapeDtypeStruct(vec.shape[2:], jnp.float32),
            jax.ShapeDtypeStruct(box, jnp.float32),
        ),
        in_specs=[VMEM] * 6,
        out_specs=[VMEM] * 5,
        scratch_shapes=reduce_scratch(planes, table.shape[0], t_cols, low)
        + reduce_scratch(planes, *vec.shape[3:], jnp.float32)
        + reduce_scratch(planes, w_rows, w_cols, low)
        + reduce_scratch(planes, d_rows, down.shape[1], low)
        + [
            pltpu.VMEM((2, w_rows, w_cols), jnp.float32),
            pltpu.VMEM((2, w_rows // 2, w_cols), jnp.float32),
            pltpu.VMEM((2 * (3 + steps) + 1,) + box, jnp.float32),
            pltpu.SemaphoreType.DMA((copies,)),
            pltpu.SemaphoreType.DMA((copies,)),
        ],
        compiler_params=pltpu.CompilerParams(
            collective_id=2, has_side_effects=True, vmem_limit_bytes=62 * 2**20
        ),
    )(wide, down, table, vec, conv, weight)


def on_device_plain(
    pixels,
    sensor,
    band_wave,
    visible,
    block_order,
    pre_gain,
    pre_shift,
    qkv_weight,
    out_weight,
    mid_gain,
    mid_shift,
    up_weight,
    up_bias,
    down_weight,
    down_bias,
    dec_weight,
    dec_bias,
    mask_token,
    gen_tokens,
    gen_qkv,
    gen_out,
    gen_out_bias,
    gen_gain1,
    gen_shift1,
    gen_up,
    gen_up_bias,
    gen_down,
    gen_down_bias,
    gen_gain2,
    gen_shift2,
    kernel_weight,
    kernel_bias,
    bias_weight,
    cotangent,
):
    fetched = (
        lax.all_gather(pre_gain, AXES, axis=0, tiled=True),
        lax.all_gather(pre_shift, AXES, axis=0, tiled=True),
        lax.all_gather(qkv_weight, AXES, axis=0, tiled=True),
        lax.all_gather(out_weight, AXES, axis=0, tiled=True),
        lax.all_gather(mid_gain, AXES, axis=0, tiled=True),
        lax.all_gather(mid_shift, AXES, axis=0, tiled=True),
        lax.all_gather(up_weight, AXES, axis=0, tiled=True),
        lax.all_gather(up_bias, AXES, axis=0, tiled=True),
        lax.all_gather(down_weight, AXES, axis=0, tiled=True),
        lax.all_gather(down_bias, AXES, axis=0, tiled=True),
        lax.all_gather(dec_weight, AXES, axis=0, tiled=True),
        lax.all_gather(dec_bias, AXES, axis=0, tiled=True),
        lax.all_gather(mask_token, AXES, axis=0, tiled=True),
        lax.all_gather(gen_tokens, AXES, axis=1, tiled=True),
        lax.all_gather(gen_qkv, AXES, axis=0, tiled=True),
        lax.all_gather(gen_out, AXES, axis=0, tiled=True),
        lax.all_gather(gen_out_bias, AXES, axis=0, tiled=True),
        lax.all_gather(gen_gain1, AXES, axis=0, tiled=True),
        lax.all_gather(gen_shift1, AXES, axis=0, tiled=True),
        lax.all_gather(gen_up, AXES, axis=0, tiled=True),
        lax.all_gather(gen_up_bias, AXES, axis=0, tiled=True),
        lax.all_gather(gen_down, AXES, axis=0, tiled=True),
        lax.all_gather(gen_down_bias, AXES, axis=0, tiled=True),
        lax.all_gather(gen_gain2, AXES, axis=0, tiled=True),
        lax.all_gather(gen_shift2, AXES, axis=0, tiled=True),
        lax.all_gather(kernel_weight, AXES, axis=1, tiled=True),
        lax.all_gather(kernel_bias, AXES, axis=0, tiled=True),
        lax.all_gather(bias_weight, AXES, axis=0, tiled=True),
    )
    full_kernel = fetched[25]
    full_kernel_bias = fetched[26]
    full_bias_weight = fetched[27]
    (
        full_pre_gain,
        full_pre_shift,
        full_qkv,
        full_out,
        full_mid_gain,
        full_mid_shift,
        full_up,
        full_up_bias,
        full_down,
        full_down_bias,
        full_dec,
        full_dec_bias,
        full_mask,
    ) = fetched[:13]
    core32 = tuple((item.astype(jnp.float32) for item in fetched[13:25]))
    chips, seen, bands, pix = pixels.shape
    width = full_qkv.shape[0]
    head_dim = width // HEADS
    scale = 1.0 / math.sqrt(head_dim)
    dec_width = full_dec.shape[1]
    rows = chips * seen
    wave_code = lax.optimization_barrier(
        sincos(jnp.arange(NWAVE, dtype=jnp.float32), WD // 2).astype(jnp.bfloat16)
    ).astype(jnp.float32)
    (feature, source), core_back = jax.vjp(partial(gen_core, wave_code), *core32)
    feature_low = feature.astype(jnp.bfloat16)
    source_low = source.astype(jnp.bfloat16)
    conv_bias = jnp.dot(source_low[None, :], full_bias_weight, preferred_element_type=jnp.float32)[
        0
    ]
    kernels = (
        jnp.dot(feature_low, full_kernel, preferred_element_type=jnp.float32)
        + full_kernel_bias.astype(jnp.float32)[None, :]
    ).astype(jnp.bfloat16)
    valid = band_valid(sensor, bands)
    onehot = (band_wave[:, :, None] == jnp.arange(NWAVE, dtype=jnp.int32)[None, None, :]).astype(
        jnp.float32
    )
    place = place_code(visible, width)
    band_kernels = jnp.einsum(
        "cbw,wk->cbk", onehot.astype(jnp.bfloat16), kernels, preferred_element_type=jnp.float32
    ).astype(jnp.bfloat16)
    band_kernels = band_kernels.reshape(chips, bands, pix, width)
    masked = pixels * valid.astype(jnp.bfloat16)[:, None, :, None]
    embedded = jnp.einsum(
        "cvbp,cbpd->cvd", masked, band_kernels, preferred_element_type=jnp.float32
    )
    start = (embedded + conv_bias + place).reshape(rows, width)
    pre_gain32 = full_pre_gain.astype(jnp.float32)
    pre_shift32 = full_pre_shift.astype(jnp.float32)
    normed = norm_rows(start, pre_gain32, pre_shift32).astype(jnp.bfloat16)
    joint = jnp.dot(normed, full_qkv, preferred_element_type=jnp.float32).astype(jnp.bfloat16)
    joint = joint.reshape(chips, seen, 3, HEADS, head_dim)
    queries = joint[:, :, 0]
    keys = joint[:, :, 1]
    values = joint[:, :, 2]
    scores = (
        jnp.einsum("cqhe,ckhe->chqk", queries, keys, preferred_element_type=jnp.float32) * scale
    )
    peak = jnp.max(scores, axis=-1, keepdims=True)
    expd = jnp.exp(scores - peak)
    total = jnp.sum(expd, axis=-1, keepdims=True)
    probs = (expd / total).astype(jnp.bfloat16)
    log_total = peak + jnp.log(total)
    context = jnp.einsum("chqk,ckhe->cqhe", probs, values, preferred_element_type=jnp.float32)
    context = context.astype(jnp.bfloat16).reshape(rows, width)
    attended = jnp.dot(context, full_out, preferred_element_type=jnp.float32)
    middle = start + attended
    mid_gain32 = full_mid_gain.astype(jnp.float32)
    mid_shift32 = full_mid_shift.astype(jnp.float32)
    normed2 = norm_rows(middle, mid_gain32, mid_shift32).astype(jnp.bfloat16)
    upper = jnp.dot(normed2, full_up, preferred_element_type=jnp.float32) + full_up_bias.astype(
        jnp.float32
    )
    activ = exact_gelu(upper).astype(jnp.bfloat16)
    branch = jnp.dot(activ, full_down, preferred_element_type=jnp.float32) + full_down_bias.astype(
        jnp.float32
    )
    ending = (middle + branch).astype(jnp.bfloat16)
    decoded = jnp.dot(ending, full_dec, preferred_element_type=jnp.float32) + full_dec_bias.astype(
        jnp.float32
    )
    decoded = decoded.astype(jnp.bfloat16).reshape(chips, seen, dec_width)
    chip_ids = jnp.arange(chips, dtype=jnp.int32)[:, None]
    canvas = jnp.broadcast_to(full_mask, (chips, PATCH, dec_width))
    canvas = canvas.at[chip_ids, visible].set(decoded)
    ordered = jnp.take(canvas, block_order, axis=1)
    decoder_in = lax.all_to_all(ordered, AXES, split_axis=1, concat_axis=0, tiled=True)
    returned = lax.all_to_all(cotangent, AXES, split_axis=0, concat_axis=1, tiled=True)
    (
        full_pre_gain,
        full_pre_shift,
        full_qkv,
        full_out,
        full_mid_gain,
        full_mid_shift,
        full_up,
        full_up_bias,
        full_down,
        full_down_bias,
        full_dec,
        full_dec_bias,
        full_mask,
    ) = (
        lax.all_gather(pre_gain, AXES, axis=0, tiled=True),
        lax.all_gather(pre_shift, AXES, axis=0, tiled=True),
        lax.all_gather(qkv_weight, AXES, axis=0, tiled=True),
        lax.all_gather(out_weight, AXES, axis=0, tiled=True),
        lax.all_gather(mid_gain, AXES, axis=0, tiled=True),
        lax.all_gather(mid_shift, AXES, axis=0, tiled=True),
        lax.all_gather(up_weight, AXES, axis=0, tiled=True),
        lax.all_gather(up_bias, AXES, axis=0, tiled=True),
        lax.all_gather(down_weight, AXES, axis=0, tiled=True),
        lax.all_gather(down_bias, AXES, axis=0, tiled=True),
        lax.all_gather(dec_weight, AXES, axis=0, tiled=True),
        lax.all_gather(dec_bias, AXES, axis=0, tiled=True),
        lax.all_gather(mask_token, AXES, axis=0, tiled=True),
    )
    restored = jnp.zeros_like(returned).at[:, block_order].set(returned)
    seen_grad = jnp.take_along_axis(restored, visible[:, :, None], axis=1)
    grad_mask = jnp.sum(restored.astype(jnp.float32), axis=(0, 1)) - jnp.sum(
        seen_grad.astype(jnp.float32), axis=(0, 1)
    )
    grad_rows = seen_grad.reshape(rows, dec_width)
    grad_dec_weight = tdot(ending, grad_rows)
    grad_dec_bias = jnp.sum(grad_rows.astype(jnp.float32), axis=0)
    grad_ending = ndot(grad_rows, full_dec)
    grad_branch = grad_ending.astype(jnp.bfloat16)
    grad_down_bias = jnp.sum(grad_branch.astype(jnp.float32), axis=0)
    grad_down_weight = tdot(activ, grad_branch)
    grad_activ = ndot(grad_branch, full_down)
    gelu_out, gelu_back = jax.vjp(exact_gelu, upper)
    grad_upper = gelu_back(grad_activ)[0].astype(jnp.bfloat16)
    grad_up_bias = jnp.sum(grad_upper.astype(jnp.float32), axis=0)
    grad_up_weight = tdot(normed2, grad_upper)
    grad_normed2 = ndot(grad_upper, full_up)
    norm_out, norm_back = jax.vjp(norm_rows, middle, mid_gain32, mid_shift32)
    through_mid, grad_mid_gain, grad_mid_shift = norm_back(grad_normed2)
    grad_middle = grad_ending + through_mid
    grad_attended = grad_middle.astype(jnp.bfloat16)
    grad_out_weight = tdot(context, grad_attended)
    grad_context = (
        ndot(grad_attended, full_out).astype(jnp.bfloat16).reshape(chips, seen, HEADS, head_dim)
    )
    again_scores = (
        jnp.einsum("cqhe,ckhe->chqk", queries, keys, preferred_element_type=jnp.float32) * scale
    )
    probs_full = jnp.exp(again_scores - log_total)
    probs_low = probs_full.astype(jnp.bfloat16)
    grad_values = jnp.einsum(
        "chqk,cqhe->ckhe", probs_low, grad_context, preferred_element_type=jnp.float32
    ).astype(jnp.bfloat16)
    grad_probs = jnp.einsum(
        "cqhe,ckhe->chqk", grad_context, values, preferred_element_type=jnp.float32
    )
    row_dot = jnp.sum(probs_full * grad_probs, axis=-1, keepdims=True)
    grad_scores = (probs_full * (grad_probs - row_dot)).astype(jnp.bfloat16)
    grad_queries = (
        jnp.einsum("chqk,ckhe->cqhe", grad_scores, keys, preferred_element_type=jnp.float32) * scale
    ).astype(jnp.bfloat16)
    grad_keys = (
        jnp.einsum("chqk,cqhe->ckhe", grad_scores, queries, preferred_element_type=jnp.float32)
        * scale
    ).astype(jnp.bfloat16)
    grad_joint = jnp.stack([grad_queries, grad_keys, grad_values], axis=2).reshape(rows, 3 * width)
    grad_qkv_weight = tdot(normed, grad_joint)
    grad_normed = ndot(grad_joint, full_qkv)
    first_out, first_back = jax.vjp(norm_rows, start, pre_gain32, pre_shift32)
    through_pre, grad_pre_gain, grad_pre_shift = first_back(grad_normed)
    grad_start = grad_middle + through_pre
    grad_conv_part = jnp.sum(grad_start, axis=0)
    grad_embedded = grad_start.astype(jnp.bfloat16).reshape(chips, seen, width)
    grad_band = jnp.einsum(
        "cvbp,cvd->cbpd", masked, grad_embedded, preferred_element_type=jnp.float32
    )
    grad_band = grad_band.reshape(chips, bands, pix * width)
    grad_pixels = jnp.einsum(
        "cvd,cbpd->cvbp", grad_embedded, band_kernels, preferred_element_type=jnp.float32
    )
    grad_pixels = grad_pixels * valid[:, None, :, None]
    grad_kernels_part = jnp.einsum("cbw,cbk->wk", onehot, grad_band, precision=HIGH)
    kernel_sum, grad_conv = lax.psum((grad_kernels_part, grad_conv_part), AXES)
    kernel_low = kernel_sum.astype(jnp.bfloat16)
    own_low = own_part(kernel_low, 1)
    grad_kernel_weight = tdot(feature_low, own_low)
    grad_kernel_bias = jnp.sum(own_low.astype(jnp.float32), axis=0)
    grad_feature = ndot(kernel_low, full_kernel)
    grad_bias_weight = own_part(source_low.astype(jnp.float32)[:, None] * grad_conv[None, :], 0)
    grad_source = jnp.dot(full_bias_weight.astype(jnp.float32), grad_conv, precision=HIGH)
    core_grads = core_back((grad_feature, grad_source))
    summed = (
        lax.psum_scatter(grad_pre_gain, AXES, scatter_dimension=0, tiled=True),
        lax.psum_scatter(grad_pre_shift, AXES, scatter_dimension=0, tiled=True),
        lax.psum_scatter(grad_qkv_weight, AXES, scatter_dimension=0, tiled=True),
        lax.psum_scatter(grad_out_weight, AXES, scatter_dimension=0, tiled=True),
        lax.psum_scatter(grad_mid_gain, AXES, scatter_dimension=0, tiled=True),
        lax.psum_scatter(grad_mid_shift, AXES, scatter_dimension=0, tiled=True),
        lax.psum_scatter(grad_up_weight, AXES, scatter_dimension=0, tiled=True),
        lax.psum_scatter(grad_up_bias, AXES, scatter_dimension=0, tiled=True),
        lax.psum_scatter(grad_down_weight, AXES, scatter_dimension=0, tiled=True),
        lax.psum_scatter(grad_down_bias, AXES, scatter_dimension=0, tiled=True),
        lax.psum_scatter(grad_dec_weight, AXES, scatter_dimension=0, tiled=True),
        lax.psum_scatter(grad_dec_bias, AXES, scatter_dimension=0, tiled=True),
        lax.psum_scatter(grad_mask, AXES, scatter_dimension=0, tiled=True),
    )
    return (
        decoder_in,
        grad_pixels,
        summed[0],
        summed[1],
        summed[2],
        summed[3],
        summed[4],
        summed[5],
        summed[6],
        summed[7],
        summed[8],
        summed[9],
        summed[10],
        summed[11],
        summed[12],
        own_part(core_grads[0], 1),
        own_part(core_grads[1], 0),
        own_part(core_grads[2], 0),
        own_part(core_grads[3], 0),
        own_part(core_grads[4], 0),
        own_part(core_grads[5], 0),
        own_part(core_grads[6], 0),
        own_part(core_grads[7], 0),
        own_part(core_grads[8], 0),
        own_part(core_grads[9], 0),
        own_part(core_grads[10], 0),
        own_part(core_grads[11], 0),
        grad_kernel_weight,
        grad_kernel_bias,
        grad_bias_weight,
    )


def on_device(
    pixels,
    sensor,
    band_wave,
    visible,
    block_order,
    pre_gain,
    pre_shift,
    qkv_weight,
    out_weight,
    mid_gain,
    mid_shift,
    up_weight,
    up_bias,
    down_weight,
    down_bias,
    dec_weight,
    dec_bias,
    mask_token,
    gen_tokens,
    gen_qkv,
    gen_out,
    gen_out_bias,
    gen_gain1,
    gen_shift1,
    gen_up,
    gen_up_bias,
    gen_down,
    gen_down_bias,
    gen_gain2,
    gen_shift2,
    kernel_weight,
    kernel_bias,
    bias_weight,
    cotangent,
):
    arguments = (
        pixels,
        sensor,
        band_wave,
        visible,
        block_order,
        pre_gain,
        pre_shift,
        qkv_weight,
        out_weight,
        mid_gain,
        mid_shift,
        up_weight,
        up_bias,
        down_weight,
        down_bias,
        dec_weight,
        dec_bias,
        mask_token,
        gen_tokens,
        gen_qkv,
        gen_out,
        gen_out_bias,
        gen_gain1,
        gen_shift1,
        gen_up,
        gen_up_bias,
        gen_down,
        gen_down_bias,
        gen_gain2,
        gen_shift2,
        kernel_weight,
        kernel_bias,
        bias_weight,
        cotangent,
    )
    planes = lax.axis_size("dp") // 2
    devices = planes * 8
    if lax.axis_size("fsdp") != 4 or planes & (planes - 1) or pre_gain.shape[0] % 8:
        return on_device_plain(*arguments)
    low = jnp.bfloat16
    smalls = (
        gen_up, gen_down, bias_weight, gen_qkv, gen_out, up_bias, gen_up_bias,
        pre_gain, pre_shift, mid_gain, mid_shift, down_bias, dec_bias, mask_token,
        gen_out_bias, gen_gain1, gen_shift1, gen_down_bias, gen_gain2, gen_shift2, gen_tokens,
    )
    flat = jnp.concatenate([item.reshape(-1) for item in smalls])
    lines = -(-flat.shape[0] // (128 * 32)) * 32
    flat = jnp.pad(flat, (0, lines * 128 - flat.shape[0])).reshape(lines, 128)
    spread = small_gather(flat, planes, devices).reshape(devices, lines * 128)
    fulls = []
    start_at = 0
    for item in smalls[:-1]:
        piece = spread[:, start_at : start_at + item.size]
        start_at += item.size
        fulls.append(piece.reshape((devices * item.shape[0],) + item.shape[1:]))
    piece = spread[:, start_at : start_at + gen_tokens.size]
    piece = piece.reshape(devices, gen_tokens.shape[0], gen_tokens.shape[1])
    full_tokens = jnp.swapaxes(piece, 0, 1).reshape(gen_tokens.shape[0], -1)
    (
        full_gen_up, full_gen_down, full_bias_weight, full_gen_qkv, full_gen_out, full_up_bias,
        full_gen_up_bias, full_pre_gain, full_pre_shift, full_mid_gain, full_mid_shift,
        full_down_bias, full_dec_bias, full_mask, full_gen_out_bias, full_gain1, full_shift1,
        full_gen_down_bias, full_gain2, full_shift2,
    ) = fulls
    core32 = tuple(
        item.astype(jnp.float32)
        for item in (
            full_tokens, full_gen_qkv, full_gen_out, full_gen_out_bias, full_gain1, full_shift1,
            full_gen_up, full_gen_up_bias, full_gen_down, full_gen_down_bias, full_gain2,
            full_shift2,
        )
    )
    chips, seen, bands, pix = pixels.shape
    width = qkv_weight.shape[0] * devices
    hidden_width = up_weight.shape[1]
    head_dim = width // HEADS
    scale = 1.0 / math.sqrt(head_dim)
    dec_width = dec_weight.shape[1]
    rows = chips * seen
    wave_code = lax.optimization_barrier(
        sincos(jnp.arange(NWAVE, dtype=jnp.float32), WD // 2).astype(jnp.bfloat16)
    ).astype(jnp.float32)
    (feature, source), core_back = jax.vjp(partial(gen_core, wave_code), *core32)
    feature_low = feature.astype(jnp.bfloat16)
    source_low = source.astype(jnp.bfloat16)
    conv_bias = jnp.dot(source_low[None, :], full_bias_weight, preferred_element_type=jnp.float32)[
        0
    ]
    own_table = (
        jnp.dot(feature_low, kernel_weight, preferred_element_type=jnp.float32)
        + kernel_bias.astype(jnp.float32)[None, :]
    ).astype(low)
    wide = jnp.concatenate([qkv_weight, up_weight, out_weight, dec_weight], axis=1)
    full_wide, full_down, kernels = weight_gather(wide, down_weight, own_table, planes, devices)
    full_down, cotangent = lax.optimization_barrier((full_down, cotangent))
    cuts = (0, 3 * width, 3 * width + hidden_width, 4 * width + hidden_width)
    full_qkv = full_wide[:, : cuts[1]]
    full_up = full_wide[:, cuts[1] : cuts[2]]
    full_out = full_wide[:, cuts[2] : cuts[3]]
    full_dec = full_wide[:, cuts[3] :]
    valid = band_valid(sensor, bands)
    onehot = (band_wave[:, :, None] == jnp.arange(NWAVE, dtype=jnp.int32)[None, None, :]).astype(
        jnp.float32
    )
    place = place_code(visible, width)
    band_kernels = jnp.einsum(
        "cbw,wk->cbk", onehot.astype(jnp.bfloat16), kernels, preferred_element_type=jnp.float32
    ).astype(jnp.bfloat16)
    band_kernels = band_kernels.reshape(chips, bands, pix, width)
    masked = pixels * valid.astype(jnp.bfloat16)[:, None, :, None]
    embedded = jnp.einsum(
        "cvbp,cbpd->cvd", masked, band_kernels, preferred_element_type=jnp.float32
    )
    start = (embedded + conv_bias + place).reshape(rows, width)
    pre_gain32 = full_pre_gain.astype(jnp.float32)
    pre_shift32 = full_pre_shift.astype(jnp.float32)
    normed = norm_rows(start, pre_gain32, pre_shift32).astype(jnp.bfloat16)
    joint = jnp.dot(normed, full_qkv, preferred_element_type=jnp.float32).astype(jnp.bfloat16)
    joint = joint.reshape(chips, seen, 3, HEADS, head_dim)
    queries = joint[:, :, 0]
    keys = joint[:, :, 1]
    values = joint[:, :, 2]
    scores = (
        jnp.einsum("cqhe,ckhe->chqk", queries, keys, preferred_element_type=jnp.float32) * scale
    )
    peak = jnp.max(scores, axis=-1, keepdims=True)
    expd = jnp.exp(scores - peak)
    total = jnp.sum(expd, axis=-1, keepdims=True)
    probs = (expd / total).astype(jnp.bfloat16)
    log_total = peak + jnp.log(total)
    context = jnp.einsum("chqk,ckhe->cqhe", probs, values, preferred_element_type=jnp.float32)
    context = context.astype(jnp.bfloat16).reshape(rows, width)
    attended = jnp.dot(context, full_out, preferred_element_type=jnp.float32)
    middle = start + attended
    mid_gain32 = full_mid_gain.astype(jnp.float32)
    mid_shift32 = full_mid_shift.astype(jnp.float32)
    normed2 = norm_rows(middle, mid_gain32, mid_shift32).astype(jnp.bfloat16)
    upper = jnp.dot(normed2, full_up, preferred_element_type=jnp.float32) + full_up_bias.astype(
        jnp.float32
    )
    activ = exact_gelu(upper).astype(jnp.bfloat16)
    branch = jnp.dot(activ, full_down, preferred_element_type=jnp.float32) + full_down_bias.astype(
        jnp.float32
    )
    ending = (middle + branch).astype(jnp.bfloat16)
    decoded = jnp.dot(ending, full_dec, preferred_element_type=jnp.float32) + full_dec_bias.astype(
        jnp.float32
    )
    decoded = decoded.astype(jnp.bfloat16).reshape(chips, seen, dec_width)
    chosen = block_order[None, :, None] == visible[:, None, :]
    choose = chosen.astype(low)
    ordered = jnp.where(
        jnp.any(chosen, axis=2)[:, :, None],
        jnp.einsum("cjv,cve->cje", choose, decoded, preferred_element_type=jnp.float32).astype(low),
        full_mask,
    )
    decoder_in = lax.all_to_all(ordered, AXES, split_axis=1, concat_axis=0, tiled=True)
    returned = lax.all_to_all(cotangent, AXES, split_axis=0, concat_axis=1, tiled=True)
    seen_grad = jnp.einsum(
        "cjv,cje->cve", choose, returned, preferred_element_type=jnp.float32
    ).astype(low)
    unseen = 1.0 - jnp.any(chosen, axis=2).astype(jnp.float32)
    grad_mask = jnp.einsum(
        "cj,cje->e", unseen.astype(low), returned, preferred_element_type=jnp.float32
    )
    grad_rows = seen_grad.reshape(rows, dec_width)
    grad_dec_weight = tdot(ending, grad_rows).astype(low)
    grad_dec_bias = jnp.sum(grad_rows.astype(jnp.float32), axis=0)
    grad_ending = ndot(grad_rows, full_dec)
    grad_branch = grad_ending.astype(jnp.bfloat16)
    grad_down_bias = jnp.sum(grad_branch.astype(jnp.float32), axis=0)
    grad_down_weight = tdot(activ, grad_branch).astype(low)
    grad_activ = ndot(grad_branch, full_down)
    gelu_out, gelu_back = jax.vjp(exact_gelu, upper)
    grad_upper = gelu_back(grad_activ)[0].astype(jnp.bfloat16)
    grad_up_bias = jnp.sum(grad_upper.astype(jnp.float32), axis=0)
    grad_up_weight = tdot(normed2, grad_upper).astype(low)
    grad_normed2 = ndot(grad_upper, full_up)
    norm_out, norm_back = jax.vjp(norm_rows, middle, mid_gain32, mid_shift32)
    through_mid, grad_mid_gain, grad_mid_shift = norm_back(grad_normed2)
    grad_middle = grad_ending + through_mid
    grad_attended = grad_middle.astype(jnp.bfloat16)
    grad_out_weight = tdot(context, grad_attended).astype(low)
    grad_context = (
        ndot(grad_attended, full_out).astype(jnp.bfloat16).reshape(chips, seen, HEADS, head_dim)
    )
    again_scores = (
        jnp.einsum("cqhe,ckhe->chqk", queries, keys, preferred_element_type=jnp.float32) * scale
    )
    probs_full = jnp.exp(again_scores - log_total)
    probs_low = probs_full.astype(jnp.bfloat16)
    grad_values = jnp.einsum(
        "chqk,cqhe->ckhe", probs_low, grad_context, preferred_element_type=jnp.float32
    ).astype(jnp.bfloat16)
    grad_probs = jnp.einsum(
        "cqhe,ckhe->chqk", grad_context, values, preferred_element_type=jnp.float32
    )
    row_dot = jnp.sum(probs_full * grad_probs, axis=-1, keepdims=True)
    grad_scores = (probs_full * (grad_probs - row_dot)).astype(jnp.bfloat16)
    grad_queries = (
        jnp.einsum("chqk,ckhe->cqhe", grad_scores, keys, preferred_element_type=jnp.float32) * scale
    ).astype(jnp.bfloat16)
    grad_keys = (
        jnp.einsum("chqk,cqhe->ckhe", grad_scores, queries, preferred_element_type=jnp.float32)
        * scale
    ).astype(jnp.bfloat16)
    grad_joint = jnp.stack([grad_queries, grad_keys, grad_values], axis=2).reshape(rows, 3 * width)
    grad_qkv_weight = tdot(normed, grad_joint).astype(low)
    grad_normed = ndot(grad_joint, full_qkv)
    first_out, first_back = jax.vjp(norm_rows, start, pre_gain32, pre_shift32)
    through_pre, grad_pre_gain, grad_pre_shift = first_back(grad_normed)
    grad_start = grad_middle + through_pre
    grad_conv_part = jnp.sum(grad_start, axis=0)
    grad_embedded = grad_start.astype(jnp.bfloat16).reshape(chips, seen, width)
    grad_band = jnp.einsum(
        "cvbp,cvd->cbpd", masked, grad_embedded, preferred_element_type=jnp.float32
    )
    grad_band = grad_band.reshape(chips, bands, pix * width)
    grad_pixels = jnp.einsum(
        "cvd,cbpd->cvbp", grad_embedded, band_kernels, preferred_element_type=jnp.float32
    )
    grad_pixels = grad_pixels * valid[:, None, :, None]
    grad_kernels_part = jnp.einsum("cbw,cbk->wk", onehot, grad_band, precision=HIGH)
    grad_wide = jnp.concatenate(
        [grad_qkv_weight, grad_up_weight, grad_out_weight, grad_dec_weight], axis=1
    )
    vectors = (
        grad_pre_gain, grad_pre_shift, grad_mid_gain, grad_mid_shift, grad_down_bias,
        grad_up_bias, grad_dec_bias, grad_mask,
    )
    vec = jnp.concatenate([item.reshape(devices, -1) for item in vectors], axis=1)
    vec_size = vec.shape[1]
    vec = jnp.pad(vec, ((0, 0), (0, 2048 - vec_size))).reshape(devices // 2, 2, 2, 8, 128)
    sum_wide, sum_down, own_low, sum_vec, sum_all = grad_reduce(
        grad_wide,
        grad_down_weight,
        grad_kernels_part.astype(low),
        vec,
        grad_conv_part.reshape(-1, 128),
        kernel_weight,
        planes,
    )
    grad_feature = sum_all[:NWAVE]
    grad_conv = sum_all[NWAVE:].reshape(-1)
    grad_kernel_weight = tdot(feature_low, own_low)
    grad_kernel_bias = jnp.sum(own_low.astype(jnp.float32), axis=0)
    grad_bias_weight = own_part(source_low.astype(jnp.float32)[:, None] * grad_conv[None, :], 0)
    grad_source = jnp.dot(full_bias_weight.astype(jnp.float32), grad_conv, precision=HIGH)
    core_grads = core_back((grad_feature, grad_source))
    sum_vec = sum_vec.reshape(-1)
    vec_out = []
    at = 0
    for item in vectors:
        vec_out.append(sum_vec[at : at + item.shape[0] // devices])
        at += item.shape[0] // devices
    summed = (
        vec_out[0],
        vec_out[1],
        sum_wide[:, : cuts[1]],
        sum_wide[:, cuts[2] : cuts[3]],
        vec_out[2],
        vec_out[3],
        sum_wide[:, cuts[1] : cuts[2]],
        vec_out[5],
        sum_down,
        vec_out[4],
        sum_wide[:, cuts[3] :],
        vec_out[6],
        vec_out[7],
    )
    return (
        decoder_in,
        grad_pixels,
        summed[0],
        summed[1],
        summed[2],
        summed[3],
        summed[4],
        summed[5],
        summed[6],
        summed[7],
        summed[8],
        summed[9],
        summed[10],
        summed[11],
        summed[12],
        own_part(core_grads[0], 1),
        own_part(core_grads[1], 0),
        own_part(core_grads[2], 0),
        own_part(core_grads[3], 0),
        own_part(core_grads[4], 0),
        own_part(core_grads[5], 0),
        own_part(core_grads[6], 0),
        own_part(core_grads[7], 0),
        own_part(core_grads[8], 0),
        own_part(core_grads[9], 0),
        own_part(core_grads[10], 0),
        own_part(core_grads[11], 0),
        grad_kernel_weight,
        grad_kernel_bias,
        grad_bias_weight,
    )


def solution(mesh):
    in_specs = (
        P(AXES, None, None, None),
        P(AXES),
        P(AXES, None),
        P(AXES, None),
        P(),
        P(AXES),
        P(AXES),
        P(AXES, None),
        P(AXES, None),
        P(AXES),
        P(AXES),
        P(AXES, None),
        P(AXES),
        P(AXES, None),
        P(AXES),
        P(AXES, None),
        P(AXES),
        P(AXES),
        P(None, AXES),
        P(AXES, None),
        P(AXES, None),
        P(AXES),
        P(AXES),
        P(AXES),
        P(AXES, None),
        P(AXES),
        P(AXES, None),
        P(AXES),
        P(AXES),
        P(AXES),
        P(None, AXES),
        P(AXES),
        P(AXES, None),
        P(None, AXES, None),
    )
    out_specs = (
        P(None, AXES, None),
        P(AXES, None, None, None),
        P(AXES),
        P(AXES),
        P(AXES, None),
        P(AXES, None),
        P(AXES),
        P(AXES),
        P(AXES, None),
        P(AXES),
        P(AXES, None),
        P(AXES),
        P(AXES, None),
        P(AXES),
        P(AXES),
        P(None, AXES),
        P(AXES, None),
        P(AXES, None),
        P(AXES),
        P(AXES),
        P(AXES),
        P(AXES, None),
        P(AXES),
        P(AXES, None),
        P(AXES),
        P(AXES),
        P(AXES),
        P(None, AXES),
        P(AXES),
        P(AXES, None),
    )
    return jax.shard_map(
        on_device, mesh=mesh, in_specs=in_specs, out_specs=out_specs, check_vma=False
    )
```

```python
from functools import partial
import math

import jax
import jax.numpy as jnp
from jax import lax
from jax.experimental import pallas as pl
from jax.experimental.pallas import tpu as pltpu
from jax.sharding import PartitionSpec as P

HEADS = 12
WD = 128
GHEADS = 4
LAT = 128
NWAVE = 32
GRID = 32
PATCH = 1024


EPS = 1e-05
AXES = ("dp", "fsdp")
BAND_DROP = (0, 6, 9, 7)
HIGH = lax.Precision.HIGHEST


def sincos(values, count):
    freq = jnp.exp(jnp.arange(count, dtype=jnp.float32) * (-math.log(10000.0) / count))
    angle = values[..., None] * freq
    return jnp.concatenate([jnp.sin(angle), jnp.cos(angle)], axis=-1)


def norm_rows(rows, gain, shift):
    mean = jnp.mean(rows, axis=-1, keepdims=True)
    centred = rows - mean
    spread = jnp.mean(centred * centred, axis=-1, keepdims=True)
    return centred * lax.rsqrt(spread + EPS) * gain + shift


def exact_gelu(values):
    return jax.nn.gelu(values, approximate=False)


def band_valid(sensor, bands):
    drops = jnp.array(BAND_DROP, jnp.int32)
    picked = jnp.where(
        sensor[:, None] == jnp.arange(4, dtype=jnp.int32)[None, :], drops[None, :], 0
    )
    count = bands - jnp.sum(picked, axis=1)
    return (jnp.arange(bands, dtype=jnp.int32)[None, :] < count[:, None]).astype(jnp.float32)


def place_code(visible, width):
    row = (visible // GRID).astype(jnp.float32)
    col = (visible % GRID).astype(jnp.float32)
    return jnp.concatenate([sincos(row, width // 4), sincos(col, width // 4)], axis=-1)


def gen_core(
    wave_code,
    tokens,
    gen_qkv,
    gen_out,
    gen_out_bias,
    gen_gain1,
    gen_shift1,
    gen_up,
    gen_up_bias,
    gen_down,
    gen_down_bias,
    gen_gain2,
    gen_shift2,
):
    sequence = jnp.concatenate([tokens[:LAT], wave_code, tokens[LAT:]], axis=0)
    length = sequence.shape[0]
    width = sequence.shape[1]
    head_dim = width // GHEADS
    joint = jnp.dot(sequence, gen_qkv, precision=HIGH).reshape(length, 3, GHEADS, head_dim)
    scores = jnp.einsum("qhe,khe->hqk", joint[:, 0], joint[:, 1], precision=HIGH) / math.sqrt(
        head_dim
    )
    probs = jax.nn.softmax(scores, axis=-1)
    context = jnp.einsum("hqk,khe->qhe", probs, joint[:, 2], precision=HIGH).reshape(length, width)
    mixed = norm_rows(
        sequence + jnp.dot(context, gen_out, precision=HIGH) + gen_out_bias, gen_gain1, gen_shift1
    )
    hidden = jax.nn.gelu(jnp.dot(mixed, gen_up, precision=HIGH) + gen_up_bias, approximate=False)
    final = norm_rows(
        mixed + jnp.dot(hidden, gen_down, precision=HIGH) + gen_down_bias, gen_gain2, gen_shift2
    )
    feature = final[LAT : LAT + NWAVE] + sequence[LAT : LAT + NWAVE]
    return (feature, final[length - 1])


def own_part(full, dim):
    count = lax.axis_size("dp") * lax.axis_size("fsdp")
    index = lax.axis_index("dp") * lax.axis_size("fsdp") + lax.axis_index("fsdp")
    piece = full.shape[dim] // count
    return lax.dynamic_slice_in_dim(full, index * piece, piece, dim)


def tdot(left, right):
    return lax.dot_general(
        left, right, (((0,), (0,)), ((), ())), preferred_element_type=jnp.float32
    )


def ndot(left, right):
    return lax.dot_general(
        left, right, (((1,), (1,)), ((), ())), preferred_element_type=jnp.float32
    )


MESH_ID = pl.DeviceIdType.MESH
ANY = pl.BlockSpec(memory_space=pl.ANY)
VMEM = pl.BlockSpec(memory_space=pltpu.VMEM)


class Net:
    def __init__(self, planes):
        dp, fs = lax.axis_index("dp"), lax.axis_index("fsdp")
        self.planes = planes
        self.z, self.x = lax.div(dp, 2), lax.rem(dp, 2)
        self.y, self.c = lax.div(fs, 2), lax.rem(fs, 2)
        self.sib = self.at(self.z, self.x, self.y, 1 - self.c)
        self.nx = self.at(self.z, 1 - self.x, self.y, self.c)
        self.ny = self.at(self.z, self.x, 1 - self.y, self.c)

    def at(self, z, x, y, c):
        return (z * 2 + x, y * 2 + c)

    def plane(self, k):
        return lax.rem(self.z + k, self.planes)

    def zpeer(self, k):
        return self.at(self.plane(k), self.x, self.y, self.c)

    def chip(self, k, dx=0, dy=0):
        x = 1 - self.x if dx else self.x
        y = 1 - self.y if dy else self.y
        return self.plane(k) * 4 + x * 2 + y

    def greet(self):
        barrier = pltpu.get_barrier_semaphore()
        partners = [self.sib, self.nx, self.ny]
        partners += [self.zpeer(k) for k in range(1, self.planes)]
        for partner in partners:
            pl.semaphore_signal(barrier, inc=1, device_id=partner, device_id_type=MESH_ID)
        pl.semaphore_wait(barrier, len(partners))


class Wires:
    def __init__(self, send, recv):
        self.send, self.recv, self.used, self.started = send, recv, 0, []

    def push(self, src, dst, device):
        index = self.used
        self.used += 1
        copy = pltpu.make_async_remote_copy(
            src_ref=src,
            dst_ref=dst,
            send_sem=self.send.at[index],
            recv_sem=self.recv.at[index],
            device_id=device,
            device_id_type=MESH_ID,
        )
        copy.start()
        self.started.append(copy)
        return copy

    def drain(self):
        for copy in self.started:
            copy.wait_send()


class Gather:
    def __init__(self, net, wires, own, piece):
        self.net, self.wires, self.own, self.piece = net, wires, own, piece
        self.z_in, self.first, self.second, self.twins = {}, {}, {}, []

    def near(self, h):
        return self.net.ny if h else self.net.nx

    def far(self, h):
        return self.net.nx if h else self.net.ny

    def share(self, chip, h, src=None):
        spot = self.piece(chip, h)
        self.twins.append(self.wires.push(spot if src is None else src, spot, self.net.sib))

    def begin(self):
        for k in range(1, self.net.planes):
            for h in range(2):
                spot = self.piece(self.net.chip(0), h)
                self.z_in[k, h] = self.wires.push(self.own(h), spot, self.net.zpeer(k))
        self.spread(0)

    def spread(self, k):
        back = (self.net.planes - k) % self.net.planes
        for h in range(2):
            if k:
                self.z_in[k, h].wait_recv()
            spot = self.piece(self.net.chip(back), h)
            src = self.own(h) if k == 0 else spot
            self.first[k, h] = self.wires.push(src, spot, self.near(h))
            self.second[k, h, 0] = self.wires.push(src, spot, self.far(h))
            self.share(self.net.chip(back), h, src)

    def relay(self, k):
        back = (self.net.planes - k) % self.net.planes
        for h in range(2):
            self.first[k, h].wait_recv()
            chip = self.net.chip(back, dx=h == 0, dy=h == 1)
            spot = self.piece(chip, h)
            self.second[k, h, 1] = self.wires.push(spot, spot, self.far(h))
            self.share(chip, h)

    def close(self, k):
        back = (self.net.planes - k) % self.net.planes
        for h in range(2):
            for hop in range(2):
                self.second[k, h, hop].wait_recv()
                chip = self.net.chip(back, dx=hop == 1 or h == 1, dy=hop == 1 or h == 0)
                self.share(chip, h)

    def finish(self):
        for copy in self.twins:
            copy.wait_recv()


def gather_copies(planes):
    return 2 * (planes - 1) + 4 * planes + 2 * planes + 8 * planes


def run_gathers(gathers, planes):
    for item in gathers:
        item.begin()
    for k in range(planes):
        for item in gathers:
            if k:
                item.spread(k)
            item.relay(k)
    for k in range(planes):
        for item in gathers:
            item.close(k)
    for item in gathers:
        item.finish()


def small_gather_kernel(planes, src, out, send, recv, local):
    net = Net(planes)
    net.greet()
    wires = Wires(send, recv)
    half = src.shape[0] // 2
    own = lambda h: src.at[pl.ds(h * half, half)]
    piece = lambda chip, h: out.at[chip * 2 + net.c, pl.ds(h * half, half)]
    here = pltpu.make_async_copy(src, out.at[net.chip(0) * 2 + net.c], local)
    here.start()
    run_gathers([Gather(net, wires, own, piece)], planes)
    here.wait()
    wires.drain()


def small_gather(packed, planes, devices):
    copies = gather_copies(planes)
    return pl.pallas_call(
        partial(small_gather_kernel, planes),
        out_shape=jax.ShapeDtypeStruct((devices,) + packed.shape, packed.dtype),
        in_specs=[VMEM],
        out_specs=VMEM,
        scratch_shapes=[
            pltpu.SemaphoreType.DMA((copies,)),
            pltpu.SemaphoreType.DMA((copies,)),
            pltpu.SemaphoreType.DMA,
        ],
        compiler_params=pltpu.CompilerParams(collective_id=0, has_side_effects=True),
    )(packed)


def weight_gather_kernel(
    planes, wide, down, table, wide_out, down_out, table_out, fresh, joined, send, recv, local
):
    net = Net(planes)
    net.greet()
    wires = Wires(send, recv)
    rows = wide.shape[0]
    cols = wide.shape[1] // 2
    quarter = cols // 2
    mine = pl.ds(pl.multiple_of(net.c * cols, 128), cols)
    theirs = pl.ds(pl.multiple_of((1 - net.c) * cols, 128), cols)
    pair = wires.push(wide.at[:, theirs], fresh, net.sib)
    t_rows, t_cols = table.shape
    t_half = t_cols // 2
    t_own = lambda h: table.at[:, pl.ds(h * t_half, t_half)]
    t_piece = lambda chip, h: table_out.at[
        :, pl.ds(pl.multiple_of((chip * 2 + net.c) * t_cols + h * t_half, 128), t_half)
    ]
    d_rows = down.shape[0]
    d_half = d_rows // 2
    d_own = lambda h: down.at[pl.ds(h * d_half, d_half)]
    d_piece = lambda chip, h: down_out.at[
        pl.ds(pl.multiple_of((chip * 2 + net.c) * d_rows + h * d_half, 16), d_half)
    ]
    w_own = lambda h: joined.at[:, pl.ds(h * quarter, quarter)]
    w_piece = lambda chip, h: wide_out.at[
        pl.ds(pl.multiple_of(chip * 2 * rows, 16), 2 * rows),
        pl.ds(pl.multiple_of((net.c * 2 + h) * quarter, 128), quarter),
    ]
    t_gather = Gather(net, wires, t_own, t_piece)
    d_gather = Gather(net, wires, d_own, d_piece)
    w_gather = Gather(net, wires, w_own, w_piece)
    here = []
    for own, piece in ((t_own, t_piece), (d_own, d_piece)):
        for h in range(2):
            here.append(pltpu.make_async_copy(own(h), piece(net.chip(0), h), local.at[len(here)]))
            here[-1].start()
    t_gather.begin()
    d_gather.begin()
    pair.wait_recv()
    own32 = wide[:, mine].astype(jnp.float32)
    sib32 = fresh[...].astype(jnp.float32)
    first = net.c == 0
    joined[...] = jnp.concatenate(
        [jnp.where(first, own32, sib32), jnp.where(first, sib32, own32)], axis=0
    ).astype(joined.dtype)
    for h in range(2):
        here.append(pltpu.make_async_copy(w_own(h), w_piece(net.chip(0), h), local.at[len(here)]))
        here[-1].start()
    w_gather.begin()
    gathers = [t_gather, d_gather, w_gather]
    for k in range(planes):
        for item in gathers:
            if k:
                item.spread(k)
            item.relay(k)
    for k in range(planes):
        for item in gathers:
            item.close(k)
    for item in gathers:
        item.finish()
    for copy in here:
        copy.wait()
    wires.drain()


def weight_gather(wide, down, table, planes, devices):
    copies = 3 * gather_copies(planes) + 1
    rows, cols = wide.shape
    low = wide.dtype
    return pl.pallas_call(
        partial(weight_gather_kernel, planes),
        out_shape=(
            jax.ShapeDtypeStruct((rows * devices, cols), low),
            jax.ShapeDtypeStruct((down.shape[0] * devices, down.shape[1]), low),
            jax.ShapeDtypeStruct((table.shape[0], table.shape[1] * devices), low),
        ),
        in_specs=[VMEM] * 3,
        out_specs=[ANY] * 3,
        scratch_shapes=[
            pltpu.VMEM((rows, cols // 2), low),
            pltpu.VMEM((2 * rows, cols // 2), low),
            pltpu.SemaphoreType.DMA((copies,)),
            pltpu.SemaphoreType.DMA((copies,)),
            pltpu.SemaphoreType.DMA((6,)),
        ],
        compiler_params=pltpu.CompilerParams(
            collective_id=1, has_side_effects=True, vmem_limit_bytes=40 * 2**20
        ),
    )(wide, down, table)


class Reduce:
    def __init__(self, net, wires, part, held, near_in, far_in, z_in):
        self.net, self.wires, self.part, self.held = net, wires, part, held
        self.near_in, self.far_in, self.z_in = near_in, far_in, z_in
        self.pairs, self.near, self.far, self.along = {}, {}, {}, {}

    def add(self, spot, other):
        size = 16 if spot.shape[0] % 16 == 0 else 8

        def some(i, _):
            at = pl.ds(pl.multiple_of(i * size, size), size)
            total = spot[at].astype(jnp.float32) + other[at].astype(jnp.float32)
            spot[at] = total.astype(spot.dtype)
            return 0

        lax.fori_loop(0, spot.shape[0] // size, some, 0)

    def begin(self, k):
        for dx in range(2):
            for dy in range(2):
                for h in range(2):
                    chip = self.net.chip(k, dx, dy)
                    self.pairs[k, dx, dy, h] = self.wires.push(
                        self.part(chip, 1 - self.net.c, h), self.held.at[chip, h], self.net.sib
                    )

    def stage0(self, k):
        for dx, dy in ((1, 1), (0, 1), (1, 0), (0, 0)):
            for h in range(2):
                self.pairs[k, dx, dy, h].wait_recv()
                chip = self.net.chip(k, dx, dy)
                self.add(self.held.at[chip, h], self.part(chip, self.net.c, h))
                if (dy if h == 0 else dx) == 1:
                    other = dx if h == 0 else dy
                    self.near[k, h, other] = self.wires.push(
                        self.held.at[chip, h],
                        self.near_in.at[k, h, other],
                        self.net.ny if h == 0 else self.net.nx,
                    )

    def stage1(self, k):
        for h in range(2):
            for other in (1, 0):
                self.near[k, h, other].wait_recv()
                chip = self.net.chip(k, other, 0) if h == 0 else self.net.chip(k, 0, other)
                self.add(self.held.at[chip, h], self.near_in.at[k, h, other])
                if other:
                    self.far[k, h] = self.wires.push(
                        self.held.at[chip, h],
                        self.far_in.at[k, h],
                        self.net.nx if h == 0 else self.net.ny,
                    )

    def stage2(self, k):
        for h in range(2):
            self.far[k, h].wait_recv()
            spot = self.held.at[self.net.chip(k), h]
            self.add(spot, self.far_in.at[k, h])
            if k:
                self.along[k, h] = self.wires.push(spot, self.z_in.at[k - 1, h], self.net.zpeer(k))

    def total(self, h):
        value = self.held[self.net.chip(0), h].astype(jnp.float32)
        for k in range(1, self.net.planes):
            self.along[k, h].wait_recv()
            value = value + self.z_in[k - 1, h].astype(jnp.float32)
        return value


def reduce_copies(planes):
    return 8 * planes + 4 * planes + 2 * planes + 2 * (planes - 1)


def reduce_scratch(planes, rows, cols, dtype):
    return [
        pltpu.VMEM((planes * 4, 2, rows, cols), dtype),
        pltpu.VMEM((planes, 2, 2, rows, cols), dtype),
        pltpu.VMEM((planes, 2, rows, cols), dtype),
        pltpu.VMEM((planes - 1, 2, rows, cols), dtype),
    ]


def dot_nn(left, right):
    return jnp.dot(left, right, preferred_element_type=jnp.float32)


class Pump:
    def __init__(self):
        self.units, self.at = [], 0

    def put(self, item, order):
        for k in order:
            item.begin(k)
        self.units += [(item, k) for k in order]

    def step(self, count=1):
        for _ in range(count):
            for stage in range(3):
                at = self.at - stage
                if 0 <= at < len(self.units):
                    item, k = self.units[at]
                    (item.stage0, item.stage1, item.stage2)[stage](k)
            self.at += 1

    def until(self, item):
        last = max(i for i, unit in enumerate(self.units) if unit[0] is item)
        while self.at <= last + 2:
            self.step()


def tile_rows(i, size):
    return pl.ds(pl.multiple_of(i * size, size), size)


def norm_back(grad, rows, gain):
    mean = jnp.mean(rows, axis=-1, keepdims=True)
    centred = rows - mean
    spread = jnp.mean(centred * centred, axis=-1, keepdims=True)
    inverse = lax.rsqrt(spread + EPS)
    unit = centred * inverse
    scaled = grad * gain
    inner = scaled - jnp.mean(scaled, axis=-1, keepdims=True)
    inner = inner - unit * jnp.mean(scaled * unit, axis=-1, keepdims=True)
    return inverse * inner, grad * unit


def owner_lanes(vector, devices, lane):
    size = vector.shape[1]
    part = size // devices
    shape = (devices, size)
    column = lax.broadcasted_iota(jnp.int32, shape, 1)
    row = lax.broadcasted_iota(jnp.int32, shape, 0)
    spread = jnp.where(lax.div(column, part) == row, jnp.broadcast_to(vector, shape), 0.0)
    shape = (size, 128)
    column = lax.broadcasted_iota(jnp.int32, shape, 1)
    row = lax.broadcasted_iota(jnp.int32, shape, 0)
    pick = (lax.rem(row, part) + lane == column).astype(jnp.float32)
    return jnp.dot(spread, pick, precision=HIGH, preferred_element_type=jnp.float32)


FT = 256
BLOCK = 128


def backward_kernel(planes, steps, sizes, *refs):
    (rows, width, hidden, dec_width, chips, patches) = sizes
    devices = planes * 8
    seen = rows // chips
    (
        returned, visible, order, ending, wide, down, activ, slope, normed2, middle, context,
        joint, probs, normed, start, slots, gains, weight, feature,
    ) = refs[:19]
    (dec_out, up_out, oq_out, down_out, kw_out, kb_out, all_out, vec_out, embed_out) = refs[19:28]
    scratch = refs[28:52]
    (
        big, left, w_dec, w_down, w_up, t_activ, t_slope, resid, w_sq, t_joint, t_probs,
        g_dec, g_up, g_down, g_oq, g_table, run, back, g_low, g_joint, v_sums, own_low,
        f_dec, f_up, f_oq, hand_dec, hand_up, hand_oq, box, send, recv, tile_sem, load_sem,
    ) = refs[52:]
    loads = {}

    def load(name, src, dst):
        copy = pltpu.make_async_copy(src, dst, load_sem.at[len(loads)])
        copy.start()
        loads[name] = copy

    up_at, out_at, dec_at = 3 * width, 3 * width + hidden, 4 * width + hidden
    load("returned", returned, big)
    load("dec", wide.at[:, pl.ds(dec_at, dec_width)], w_dec)
    load("ending", ending, left.at[0])

    def tile_copies(t):
        slot = lax.rem(t, 2)
        at = tile_rows(t, FT)
        return (
            pltpu.make_async_copy(down.at[at], w_down.at[slot], tile_sem.at[slot, 0]),
            pltpu.make_async_copy(
                wide.at[:, pl.ds(pl.multiple_of(up_at + t * FT, 128), FT)],
                w_up.at[slot],
                tile_sem.at[slot, 1],
            ),
            pltpu.make_async_copy(activ.at[:, at], t_activ.at[slot], tile_sem.at[slot, 2]),
            pltpu.make_async_copy(slope.at[:, at], t_slope.at[slot], tile_sem.at[slot, 3]),
        )

    for copy in tile_copies(0):
        copy.start()
    load("normed2", normed2, left.at[1])
    load("middle", middle, resid)
    load("out", wide.at[:, pl.ds(out_at, width)], w_sq.at[0])
    load("query", wide.at[:, pl.ds(0, width)], w_sq.at[1])
    load("joint", joint, t_joint)

    net = Net(planes)
    net.greet()
    wires = Wires(send, recv)
    pump = Pump()
    shard = width // (devices // 2)
    w_rows = lambda chip: pl.ds(pl.multiple_of(chip * shard, 16), shard)

    def quarter(ref, size):
        return lambda chip, c, h: ref.at[
            w_rows(chip), pl.ds(pl.multiple_of((c * 2 + h) * size, 128), size)
        ]

    def stripe(ref, size):
        return lambda chip, c, h: ref.at[
            pl.ds(pl.multiple_of(((chip * 2 + c) * 2 + h) * size, 16), size)
        ]

    q_dec, q_up = dec_width // 4, hidden // 8
    d_rows = hidden // devices // 2
    t_rows = g_table.shape[0] // devices // 2
    parts = (
        quarter(g_dec, q_dec),
        quarter(g_up.at[0], q_up),
        quarter(g_up.at[1], q_up),
        stripe(g_down, d_rows),
        stripe(g_table, t_rows),
        lambda chip, c, h: g_oq.at[c * 2 + h, w_rows(chip)],
    )
    dec, up0, up1, downs, tables, oq = [
        Reduce(net, wires, part, *scratch[i * 4 : i * 4 + 4]) for i, part in enumerate(parts)
    ]
    away = list(range(1, planes)) + [0]

    loads["returned"].wait()
    unseen = jnp.ones((8, patches), jnp.float32)
    grad_mask = jnp.zeros((8, dec_width), jnp.float32)
    for chip in range(chips):
        seen_at = pl.ds(chip * seen, seen)
        chosen = visible[seen_at] == order[...]
        got = big[pl.ds(chip * patches, patches)]
        picked = dot_nn(chosen.astype(jnp.bfloat16), got)
        g_joint[seen_at, pl.ds(0, dec_width)] = picked.astype(jnp.bfloat16)
        count = jnp.sum(chosen.astype(jnp.float32), axis=0, keepdims=True)
        left_out = jnp.broadcast_to(1.0 - count, (8, patches)).astype(jnp.bfloat16)
        grad_mask = grad_mask + dot_nn(left_out, got)
    load("slots", slots, big)
    grad_rows = g_joint[:, pl.ds(0, dec_width)]
    grad_dec_bias = jnp.sum(grad_rows.astype(jnp.float32), axis=0, keepdims=True)
    loads["ending"].wait()
    g_dec[...] = tdot(left[0], grad_rows).astype(jnp.bfloat16)
    pump.put(dec, away)
    loads["dec"].wait()
    run[...] = ndot(grad_rows, w_dec[...])
    g_low[...] = run[...].astype(jnp.bfloat16)
    load("context", context, left.at[0])
    back[...] = jnp.zeros_like(back)
    v_sums[pl.ds(0, 1), pl.ds(0, width)] = jnp.sum(
        g_low[...].astype(jnp.float32), axis=0, keepdims=True
    )
    loads["normed2"].wait()
    tiles = hidden // FT

    def feed(t, _):
        slot = lax.rem(t, 2)

        @pl.when(t + 1 < tiles)
        def _():
            for copy in tile_copies(t + 1):
                copy.start()

        for copy in tile_copies(t):
            copy.wait()
        grad = ndot(g_low[...], w_down[slot])
        grad_upper = (grad * t_slope[slot].astype(jnp.float32)).astype(jnp.bfloat16)
        at = tile_rows(t, FT)
        v_sums[pl.ds(1, 1), at] = jnp.sum(
            grad_upper.astype(jnp.float32), axis=0, keepdims=True
        )
        g_down[at, :] = tdot(t_activ[slot], g_low[...]).astype(jnp.bfloat16)
        g_up[lax.div(t, tiles // 2), :, tile_rows(lax.rem(t, tiles // 2), FT)] = tdot(
            left[1], grad_upper
        ).astype(jnp.bfloat16)
        back[...] += ndot(grad_upper, w_up[slot])
        return 0

    lax.fori_loop(0, tiles // 4, feed, 0)
    pump.step(2)
    lax.fori_loop(tiles // 4, tiles // 2, feed, 0)
    pump.put(up0, away)
    pump.step(2)
    lax.fori_loop(tiles // 2, 3 * tiles // 4, feed, 0)
    pump.step(2)
    lax.fori_loop(3 * tiles // 4, tiles, feed, 0)
    pump.put(up1, away)
    pump.put(downs, away)
    load("normed", normed, left.at[1])
    loads["middle"].wait()

    def through_norm(gain_row, sums_at):
        gain = gains[pl.ds(gain_row, 1), :]

        def block(i, sums):
            at = tile_rows(i, BLOCK)
            grad = back[at, :]
            inner, terms = norm_back(grad, resid[at, :], gain)
            run[at, :] += inner
            return (
                sums[0] + jnp.sum(terms, axis=0, keepdims=True),
                sums[1] + jnp.sum(grad, axis=0, keepdims=True),
            )

        zero = jnp.zeros((1, width), jnp.float32)
        sums = lax.fori_loop(0, rows // BLOCK, block, (zero, zero))
        v_sums[pl.ds(sums_at, 1), pl.ds(0, width)] = sums[0]
        v_sums[pl.ds(sums_at + 1, 1), pl.ds(0, width)] = sums[1]

    through_norm(0, 2)
    pump.step(2)
    load("start", start, resid)
    g_low[...] = run[...].astype(jnp.bfloat16)
    loads["context"].wait()
    loads["out"].wait()
    g_oq[0] = tdot(left[0], g_low[...]).astype(jnp.bfloat16)
    grad_context = ndot(g_low[...], w_sq[0]).astype(jnp.bfloat16)
    g_low[...] = grad_context
    load("key", wide.at[:, pl.ds(width, width)], w_sq.at[0])
    pump.step(2)

    loads["joint"].wait()
    pairs = width // 128
    head = width // HEADS
    scale = 1.0 / math.sqrt(head)
    odd = lax.broadcasted_iota(jnp.int32, (1, 128), 1) >= head

    def probs_copy(n):
        slot = lax.rem(n, 2)
        return pltpu.make_async_copy(
            probs.at[pl.ds(2 * n, 2)], t_probs.at[slot], tile_sem.at[slot, 0]
        )

    probs_copy(0).start()

    def attend(n, _):
        slot = lax.rem(n, 2)

        @pl.when(n + 1 < chips * pairs)
        def _():
            probs_copy(n + 1).start()

        probs_copy(n).wait()
        chip = lax.div(n, pairs)
        pair = lax.rem(n, pairs)
        at = tile_rows(chip, seen)
        lanes = [
            pl.ds(pl.multiple_of(pair * 128 + i * width, 128), 128) for i in range(3)
        ]
        query, key, value = [t_joint[at, lane] for lane in lanes]
        grad = g_low[at, lanes[0]]
        zero = jnp.zeros_like(grad)
        totals = [None, None, None]
        for h in range(2):
            mine = odd if h else jnp.logical_not(odd)
            grad_h = jnp.where(mine, grad, zero)
            query_h = jnp.where(mine, query, zero)
            key_h = jnp.where(mine, key, zero)
            prob = t_probs[slot, h]
            prob32 = prob.astype(jnp.float32)
            grad_prob = ndot(grad_h, value)
            row_dot = jnp.sum(prob32 * grad_prob, axis=-1, keepdims=True)
            grad_score = (prob32 * (grad_prob - row_dot)).astype(jnp.bfloat16)
            terms = (dot_nn(grad_score, key_h), tdot(grad_score, query_h), tdot(prob, grad_h))
            totals = [new if old is None else old + new for old, new in zip(totals, terms)]
        g_joint[at, lanes[0]] = (totals[0] * scale).astype(jnp.bfloat16)
        g_joint[at, lanes[1]] = (totals[1] * scale).astype(jnp.bfloat16)
        g_joint[at, lanes[2]] = totals[2].astype(jnp.bfloat16)
        return 0

    for chip in range(chips):
        lax.fori_loop(chip * pairs, (chip + 1) * pairs, attend, 0)
        pump.step(2)

    loads["normed"].wait()
    def joint_part(i, _):
        lane = pl.ds(pl.multiple_of(i * width, 128), width)
        g_oq[i + 1] = tdot(left[1], g_joint[:, lane]).astype(jnp.bfloat16)
        return 0

    lax.fori_loop(0, 3, joint_part, 0)
    value = pltpu.make_async_copy(
        wide.at[:, pl.ds(2 * width, width)], w_sq.at[1], load_sem.at[len(loads)]
    )
    back[...] = jnp.zeros_like(back)

    def joint_back(i, _):
        for j, copy in enumerate((loads["query"], loads["key"], value)):

            @pl.when(i == j)
            def _():
                copy.wait()

        lane = pl.ds(pl.multiple_of(i * width, 128), width)
        back[...] += ndot(g_joint[:, lane], w_sq[lax.rem(i + 1, 2)])

        @pl.when(i == 0)
        def _():
            value.start()

        return 0

    lax.fori_loop(0, 3, joint_back, 0)
    pump.step(1)
    loads["start"].wait()
    through_norm(1, 4)
    g_low[...] = run[...].astype(jnp.bfloat16)
    conv = jnp.sum(run[...], axis=0, keepdims=True)
    embed = pltpu.make_async_copy(g_low, embed_out, tile_sem.at[0, 1])
    embed.start()
    loads["slots"].wait()
    span = 512

    def table_block(i, _):
        at = tile_rows(i, span)
        g_table[at, :] = dot_nn(big[at, :], g_low[...]).astype(jnp.bfloat16)
        return 0

    lax.fori_loop(0, g_table.shape[0] // span, table_block, 0)
    pump.put(tables, away)
    pump.put(oq, away)

    waves = t_rows
    lines = width // 128
    for i in range(lines):
        box[0, pl.ds(waves + i, 1), :] = conv[:, i * 128 : (i + 1) * 128]
    box[0, pl.ds(waves + lines, 8 - lines % 8), :] = jnp.zeros((8 - lines % 8, 128), jnp.float32)
    vec_at = waves + lines + 8 - lines % 8
    first = owner_lanes(v_sums[pl.ds(4, 1), pl.ds(0, width)], devices, 0)
    part = width // devices
    for i, row in enumerate((5, 2, 3, 0)):
        first = first + owner_lanes(
            v_sums[pl.ds(row, 1), pl.ds(0, width)], devices, (i + 1) * part
        )
    box[0, pl.ds(vec_at, devices), :] = first
    second = owner_lanes(v_sums[pl.ds(1, 1), :], devices, 0)
    at = hidden // devices
    second = second + owner_lanes(grad_dec_bias, devices, at)
    second = second + owner_lanes(grad_mask[:1], devices, at + dec_width // devices)
    box[0, pl.ds(vec_at + devices, devices), :] = second

    pump.until(tables)
    held = tables.held
    partial_sum = jnp.zeros((waves, 128), jnp.float32)
    for h in range(2):
        own = tables.total(h).astype(jnp.bfloat16)
        own_low[h] = own
        cols = pl.ds(h * width, width)
        kw_out[:, cols] = tdot(feature[...], own)
        kb_out[:, cols] = jnp.sum(own.astype(jnp.float32), axis=0, keepdims=True)
        partial_sum = partial_sum + ndot(own, weight[:, cols])
    box[0, pl.ds(0, waves), :] = partial_sum
    peers = [net.sib, net.nx, net.ny]
    for bit in range(steps):
        step = 1 << bit
        up = lax.rem(lax.div(net.z, step), 2) == 0
        peers.append(net.at(jnp.where(up, net.z + step, net.z - step), net.x, net.y, net.c))
    for i, peer in enumerate(peers):
        hop = wires.push(box.at[2 * i], box.at[2 * i + 1], peer)
        pump.step(1)
        hop.wait_recv()
        box[2 * i + 2] = box[2 * i] + box[2 * i + 1]
    end = box.at[2 * len(peers)]
    all_out[...] = end[pl.ds(0, vec_at), :]
    me = net.chip(0) * 2 + net.c
    mine = lax.broadcasted_iota(jnp.int32, (devices, 128), 0) == me
    for i in range(2):
        rows_i = end[pl.ds(vec_at + i * devices, devices), :]
        vec_out[pl.ds(i, 1), :] = jnp.sum(jnp.where(mine, rows_i, 0.0), axis=0, keepdims=True)
    pump.until(oq)
    half = shard // 2
    own_rows = pl.ds(pl.multiple_of(net.c * half, 8), half)
    their_rows = pl.ds(pl.multiple_of((1 - net.c) * half, 8), half)
    jobs = (
        (dec, f_dec, hand_dec, dec_out, 0, q_dec),
        (up0, f_up.at[0], hand_up.at[0], up_out, 0, q_up),
        (up1, f_up.at[1], hand_up.at[1], up_out, hidden // 2, q_up),
        (oq, f_oq, hand_oq, oq_out, 0, width),
    )
    swaps = []
    for item, final, hand, out, base, size in jobs:
        for h in range(2):
            final[h] = item.total(h)
            swaps.append(wires.push(final.at[h, their_rows], hand.at[h], net.sib))
    for h in range(2):
        down_out[pl.ds(h * d_rows, d_rows)] = downs.total(h)
    for item, final, hand, out, base, size in jobs:
        for h in range(2):
            own = pl.ds(pl.multiple_of(base + (net.c * 2 + h) * size, 128), size)
            other = pl.ds(pl.multiple_of(base + ((1 - net.c) * 2 + h) * size, 128), size)
            out[:, own] = final[h, own_rows]
            swaps.pop(0).wait_recv()
            out[:, other] = hand[h]
    embed.wait()
    wires.drain()


def backward(planes, sizes, *args):
    (rows, width, hidden, dec_width, chips, patches) = sizes
    devices = planes * 8
    steps = (planes - 1).bit_length()
    low, full = jnp.bfloat16, jnp.float32
    shard = width // (devices // 2)
    q_dec, q_up = dec_width // 4, hidden // 8
    d_rows = hidden // devices // 2
    slots = args[15].shape[0]
    t_rows = slots // devices // 2
    lines = width // 128
    vec_at = t_rows + lines + 8 - lines % 8
    copies = 6 * reduce_copies(planes) + 3 + steps + 8
    scratch = []
    for shape in (
        (shard, q_dec), (shard, q_up), (shard, q_up), (d_rows, width), (t_rows, width),
        (shard, width),
    ):
        scratch += reduce_scratch(planes, *shape, low)
    scratch += [
        pltpu.VMEM((chips * patches, dec_width), low),
        pltpu.VMEM((2, rows, width), low),
        pltpu.VMEM((width, dec_width), low),
        pltpu.VMEM((2, FT, width), low),
        pltpu.VMEM((2, width, FT), low),
        pltpu.VMEM((2, rows, FT), low),
        pltpu.VMEM((2, rows, FT), low),
        pltpu.VMEM((rows, width), full),
        pltpu.VMEM((2, width, width), low),
        pltpu.VMEM((rows, 3 * width), low),
        pltpu.VMEM((2, 2, rows // chips, rows // chips), low),
        pltpu.VMEM((width, dec_width), low),
        pltpu.VMEM((2, width, hidden // 2), low),
        pltpu.VMEM((hidden, width), low),
        pltpu.VMEM((4, width, width), low),
        pltpu.VMEM((slots, width), low),
        pltpu.VMEM((rows, width), full),
        pltpu.VMEM((rows, width), full),
        pltpu.VMEM((rows, width), low),
        pltpu.VMEM((rows, 3 * width), low),
        pltpu.VMEM((8, hidden), full),
        pltpu.VMEM((2, t_rows, width), low),
        pltpu.VMEM((2, shard, q_dec), full),
        pltpu.VMEM((2, 2, shard, q_up), full),
        pltpu.VMEM((2, shard, width), full),
        pltpu.VMEM((2, shard // 2, q_dec), full),
        pltpu.VMEM((2, 2, shard // 2, q_up), full),
        pltpu.VMEM((2, shard // 2, width), full),
        pltpu.VMEM((2 * (3 + steps) + 1, vec_at + 2 * devices, 128), full),
        pltpu.SemaphoreType.DMA((copies,)),
        pltpu.SemaphoreType.DMA((copies,)),
        pltpu.SemaphoreType.DMA((2, 4)),
        pltpu.SemaphoreType.DMA((16,)),
    ]
    shapes = (
        ((width // devices, dec_width), full),
        ((width // devices, hidden), full),
        ((width // devices, 4 * width), full),
        ((hidden // devices, width), full),
        ((args[18].shape[1], 2 * width), full),
        ((1, 2 * width), full),
        ((vec_at, 128), full),
        ((2, 128), full),
        ((rows, width), low),
    )
    spots = [ANY, VMEM, VMEM] + [ANY] * 13 + [VMEM] * 3
    return pl.pallas_call(
        partial(backward_kernel, planes, steps, sizes),
        out_shape=tuple(jax.ShapeDtypeStruct(shape, dtype) for shape, dtype in shapes),
        in_specs=spots,
        out_specs=[VMEM] * 8 + [ANY],
        scratch_shapes=scratch,
        compiler_params=pltpu.CompilerParams(
            collective_id=2, has_side_effects=True, vmem_limit_bytes=63 * 2**20
        ),
    )(*args)


def on_device_plain(
    pixels,
    sensor,
    band_wave,
    visible,
    block_order,
    pre_gain,
    pre_shift,
    qkv_weight,
    out_weight,
    mid_gain,
    mid_shift,
    up_weight,
    up_bias,
    down_weight,
    down_bias,
    dec_weight,
    dec_bias,
    mask_token,
    gen_tokens,
    gen_qkv,
    gen_out,
    gen_out_bias,
    gen_gain1,
    gen_shift1,
    gen_up,
    gen_up_bias,
    gen_down,
    gen_down_bias,
    gen_gain2,
    gen_shift2,
    kernel_weight,
    kernel_bias,
    bias_weight,
    cotangent,
):
    fetched = (
        lax.all_gather(pre_gain, AXES, axis=0, tiled=True),
        lax.all_gather(pre_shift, AXES, axis=0, tiled=True),
        lax.all_gather(qkv_weight, AXES, axis=0, tiled=True),
        lax.all_gather(out_weight, AXES, axis=0, tiled=True),
        lax.all_gather(mid_gain, AXES, axis=0, tiled=True),
        lax.all_gather(mid_shift, AXES, axis=0, tiled=True),
        lax.all_gather(up_weight, AXES, axis=0, tiled=True),
        lax.all_gather(up_bias, AXES, axis=0, tiled=True),
        lax.all_gather(down_weight, AXES, axis=0, tiled=True),
        lax.all_gather(down_bias, AXES, axis=0, tiled=True),
        lax.all_gather(dec_weight, AXES, axis=0, tiled=True),
        lax.all_gather(dec_bias, AXES, axis=0, tiled=True),
        lax.all_gather(mask_token, AXES, axis=0, tiled=True),
        lax.all_gather(gen_tokens, AXES, axis=1, tiled=True),
        lax.all_gather(gen_qkv, AXES, axis=0, tiled=True),
        lax.all_gather(gen_out, AXES, axis=0, tiled=True),
        lax.all_gather(gen_out_bias, AXES, axis=0, tiled=True),
        lax.all_gather(gen_gain1, AXES, axis=0, tiled=True),
        lax.all_gather(gen_shift1, AXES, axis=0, tiled=True),
        lax.all_gather(gen_up, AXES, axis=0, tiled=True),
        lax.all_gather(gen_up_bias, AXES, axis=0, tiled=True),
        lax.all_gather(gen_down, AXES, axis=0, tiled=True),
        lax.all_gather(gen_down_bias, AXES, axis=0, tiled=True),
        lax.all_gather(gen_gain2, AXES, axis=0, tiled=True),
        lax.all_gather(gen_shift2, AXES, axis=0, tiled=True),
        lax.all_gather(kernel_weight, AXES, axis=1, tiled=True),
        lax.all_gather(kernel_bias, AXES, axis=0, tiled=True),
        lax.all_gather(bias_weight, AXES, axis=0, tiled=True),
    )
    full_kernel = fetched[25]
    full_kernel_bias = fetched[26]
    full_bias_weight = fetched[27]
    (
        full_pre_gain,
        full_pre_shift,
        full_qkv,
        full_out,
        full_mid_gain,
        full_mid_shift,
        full_up,
        full_up_bias,
        full_down,
        full_down_bias,
        full_dec,
        full_dec_bias,
        full_mask,
    ) = fetched[:13]
    core32 = tuple((item.astype(jnp.float32) for item in fetched[13:25]))
    chips, seen, bands, pix = pixels.shape
    width = full_qkv.shape[0]
    head_dim = width // HEADS
    scale = 1.0 / math.sqrt(head_dim)
    dec_width = full_dec.shape[1]
    rows = chips * seen
    wave_code = lax.optimization_barrier(
        sincos(jnp.arange(NWAVE, dtype=jnp.float32), WD // 2).astype(jnp.bfloat16)
    ).astype(jnp.float32)
    (feature, source), core_back = jax.vjp(partial(gen_core, wave_code), *core32)
    feature_low = feature.astype(jnp.bfloat16)
    source_low = source.astype(jnp.bfloat16)
    conv_bias = jnp.dot(source_low[None, :], full_bias_weight, preferred_element_type=jnp.float32)[
        0
    ]
    kernels = (
        jnp.dot(feature_low, full_kernel, preferred_element_type=jnp.float32)
        + full_kernel_bias.astype(jnp.float32)[None, :]
    ).astype(jnp.bfloat16)
    valid = band_valid(sensor, bands)
    onehot = (band_wave[:, :, None] == jnp.arange(NWAVE, dtype=jnp.int32)[None, None, :]).astype(
        jnp.float32
    )
    place = place_code(visible, width)
    band_kernels = jnp.einsum(
        "cbw,wk->cbk", onehot.astype(jnp.bfloat16), kernels, preferred_element_type=jnp.float32
    ).astype(jnp.bfloat16)
    band_kernels = band_kernels.reshape(chips, bands, pix, width)
    masked = pixels * valid.astype(jnp.bfloat16)[:, None, :, None]
    embedded = jnp.einsum(
        "cvbp,cbpd->cvd", masked, band_kernels, preferred_element_type=jnp.float32
    )
    start = (embedded + conv_bias + place).reshape(rows, width)
    pre_gain32 = full_pre_gain.astype(jnp.float32)
    pre_shift32 = full_pre_shift.astype(jnp.float32)
    normed = norm_rows(start, pre_gain32, pre_shift32).astype(jnp.bfloat16)
    joint = jnp.dot(normed, full_qkv, preferred_element_type=jnp.float32).astype(jnp.bfloat16)
    joint = joint.reshape(chips, seen, 3, HEADS, head_dim)
    queries = joint[:, :, 0]
    keys = joint[:, :, 1]
    values = joint[:, :, 2]
    scores = (
        jnp.einsum("cqhe,ckhe->chqk", queries, keys, preferred_element_type=jnp.float32) * scale
    )
    peak = jnp.max(scores, axis=-1, keepdims=True)
    expd = jnp.exp(scores - peak)
    total = jnp.sum(expd, axis=-1, keepdims=True)
    probs = (expd / total).astype(jnp.bfloat16)
    log_total = peak + jnp.log(total)
    context = jnp.einsum("chqk,ckhe->cqhe", probs, values, preferred_element_type=jnp.float32)
    context = context.astype(jnp.bfloat16).reshape(rows, width)
    attended = jnp.dot(context, full_out, preferred_element_type=jnp.float32)
    middle = start + attended
    mid_gain32 = full_mid_gain.astype(jnp.float32)
    mid_shift32 = full_mid_shift.astype(jnp.float32)
    normed2 = norm_rows(middle, mid_gain32, mid_shift32).astype(jnp.bfloat16)
    upper = jnp.dot(normed2, full_up, preferred_element_type=jnp.float32) + full_up_bias.astype(
        jnp.float32
    )
    activ = exact_gelu(upper).astype(jnp.bfloat16)
    branch = jnp.dot(activ, full_down, preferred_element_type=jnp.float32) + full_down_bias.astype(
        jnp.float32
    )
    ending = (middle + branch).astype(jnp.bfloat16)
    decoded = jnp.dot(ending, full_dec, preferred_element_type=jnp.float32) + full_dec_bias.astype(
        jnp.float32
    )
    decoded = decoded.astype(jnp.bfloat16).reshape(chips, seen, dec_width)
    chip_ids = jnp.arange(chips, dtype=jnp.int32)[:, None]
    canvas = jnp.broadcast_to(full_mask, (chips, PATCH, dec_width))
    canvas = canvas.at[chip_ids, visible].set(decoded)
    ordered = jnp.take(canvas, block_order, axis=1)
    decoder_in = lax.all_to_all(ordered, AXES, split_axis=1, concat_axis=0, tiled=True)
    returned = lax.all_to_all(cotangent, AXES, split_axis=0, concat_axis=1, tiled=True)
    (
        full_pre_gain,
        full_pre_shift,
        full_qkv,
        full_out,
        full_mid_gain,
        full_mid_shift,
        full_up,
        full_up_bias,
        full_down,
        full_down_bias,
        full_dec,
        full_dec_bias,
        full_mask,
    ) = (
        lax.all_gather(pre_gain, AXES, axis=0, tiled=True),
        lax.all_gather(pre_shift, AXES, axis=0, tiled=True),
        lax.all_gather(qkv_weight, AXES, axis=0, tiled=True),
        lax.all_gather(out_weight, AXES, axis=0, tiled=True),
        lax.all_gather(mid_gain, AXES, axis=0, tiled=True),
        lax.all_gather(mid_shift, AXES, axis=0, tiled=True),
        lax.all_gather(up_weight, AXES, axis=0, tiled=True),
        lax.all_gather(up_bias, AXES, axis=0, tiled=True),
        lax.all_gather(down_weight, AXES, axis=0, tiled=True),
        lax.all_gather(down_bias, AXES, axis=0, tiled=True),
        lax.all_gather(dec_weight, AXES, axis=0, tiled=True),
        lax.all_gather(dec_bias, AXES, axis=0, tiled=True),
        lax.all_gather(mask_token, AXES, axis=0, tiled=True),
    )
    restored = jnp.zeros_like(returned).at[:, block_order].set(returned)
    seen_grad = jnp.take_along_axis(restored, visible[:, :, None], axis=1)
    grad_mask = jnp.sum(restored.astype(jnp.float32), axis=(0, 1)) - jnp.sum(
        seen_grad.astype(jnp.float32), axis=(0, 1)
    )
    grad_rows = seen_grad.reshape(rows, dec_width)
    grad_dec_weight = tdot(ending, grad_rows)
    grad_dec_bias = jnp.sum(grad_rows.astype(jnp.float32), axis=0)
    grad_ending = ndot(grad_rows, full_dec)
    grad_branch = grad_ending.astype(jnp.bfloat16)
    grad_down_bias = jnp.sum(grad_branch.astype(jnp.float32), axis=0)
    grad_down_weight = tdot(activ, grad_branch)
    grad_activ = ndot(grad_branch, full_down)
    gelu_out, gelu_back = jax.vjp(exact_gelu, upper)
    grad_upper = gelu_back(grad_activ)[0].astype(jnp.bfloat16)
    grad_up_bias = jnp.sum(grad_upper.astype(jnp.float32), axis=0)
    grad_up_weight = tdot(normed2, grad_upper)
    grad_normed2 = ndot(grad_upper, full_up)
    norm_out, norm_back = jax.vjp(norm_rows, middle, mid_gain32, mid_shift32)
    through_mid, grad_mid_gain, grad_mid_shift = norm_back(grad_normed2)
    grad_middle = grad_ending + through_mid
    grad_attended = grad_middle.astype(jnp.bfloat16)
    grad_out_weight = tdot(context, grad_attended)
    grad_context = (
        ndot(grad_attended, full_out).astype(jnp.bfloat16).reshape(chips, seen, HEADS, head_dim)
    )
    again_scores = (
        jnp.einsum("cqhe,ckhe->chqk", queries, keys, preferred_element_type=jnp.float32) * scale
    )
    probs_full = jnp.exp(again_scores - log_total)
    probs_low = probs_full.astype(jnp.bfloat16)
    grad_values = jnp.einsum(
        "chqk,cqhe->ckhe", probs_low, grad_context, preferred_element_type=jnp.float32
    ).astype(jnp.bfloat16)
    grad_probs = jnp.einsum(
        "cqhe,ckhe->chqk", grad_context, values, preferred_element_type=jnp.float32
    )
    row_dot = jnp.sum(probs_full * grad_probs, axis=-1, keepdims=True)
    grad_scores = (probs_full * (grad_probs - row_dot)).astype(jnp.bfloat16)
    grad_queries = (
        jnp.einsum("chqk,ckhe->cqhe", grad_scores, keys, preferred_element_type=jnp.float32) * scale
    ).astype(jnp.bfloat16)
    grad_keys = (
        jnp.einsum("chqk,cqhe->ckhe", grad_scores, queries, preferred_element_type=jnp.float32)
        * scale
    ).astype(jnp.bfloat16)
    grad_joint = jnp.stack([grad_queries, grad_keys, grad_values], axis=2).reshape(rows, 3 * width)
    grad_qkv_weight = tdot(normed, grad_joint)
    grad_normed = ndot(grad_joint, full_qkv)
    first_out, first_back = jax.vjp(norm_rows, start, pre_gain32, pre_shift32)
    through_pre, grad_pre_gain, grad_pre_shift = first_back(grad_normed)
    grad_start = grad_middle + through_pre
    grad_conv_part = jnp.sum(grad_start, axis=0)
    grad_embedded = grad_start.astype(jnp.bfloat16).reshape(chips, seen, width)
    grad_band = jnp.einsum(
        "cvbp,cvd->cbpd", masked, grad_embedded, preferred_element_type=jnp.float32
    )
    grad_band = grad_band.reshape(chips, bands, pix * width)
    grad_pixels = jnp.einsum(
        "cvd,cbpd->cvbp", grad_embedded, band_kernels, preferred_element_type=jnp.float32
    )
    grad_pixels = grad_pixels * valid[:, None, :, None]
    grad_kernels_part = jnp.einsum("cbw,cbk->wk", onehot, grad_band, precision=HIGH)
    kernel_sum, grad_conv = lax.psum((grad_kernels_part, grad_conv_part), AXES)
    kernel_low = kernel_sum.astype(jnp.bfloat16)
    own_low = own_part(kernel_low, 1)
    grad_kernel_weight = tdot(feature_low, own_low)
    grad_kernel_bias = jnp.sum(own_low.astype(jnp.float32), axis=0)
    grad_feature = ndot(kernel_low, full_kernel)
    grad_bias_weight = own_part(source_low.astype(jnp.float32)[:, None] * grad_conv[None, :], 0)
    grad_source = jnp.dot(full_bias_weight.astype(jnp.float32), grad_conv, precision=HIGH)
    core_grads = core_back((grad_feature, grad_source))
    summed = (
        lax.psum_scatter(grad_pre_gain, AXES, scatter_dimension=0, tiled=True),
        lax.psum_scatter(grad_pre_shift, AXES, scatter_dimension=0, tiled=True),
        lax.psum_scatter(grad_qkv_weight, AXES, scatter_dimension=0, tiled=True),
        lax.psum_scatter(grad_out_weight, AXES, scatter_dimension=0, tiled=True),
        lax.psum_scatter(grad_mid_gain, AXES, scatter_dimension=0, tiled=True),
        lax.psum_scatter(grad_mid_shift, AXES, scatter_dimension=0, tiled=True),
        lax.psum_scatter(grad_up_weight, AXES, scatter_dimension=0, tiled=True),
        lax.psum_scatter(grad_up_bias, AXES, scatter_dimension=0, tiled=True),
        lax.psum_scatter(grad_down_weight, AXES, scatter_dimension=0, tiled=True),
        lax.psum_scatter(grad_down_bias, AXES, scatter_dimension=0, tiled=True),
        lax.psum_scatter(grad_dec_weight, AXES, scatter_dimension=0, tiled=True),
        lax.psum_scatter(grad_dec_bias, AXES, scatter_dimension=0, tiled=True),
        lax.psum_scatter(grad_mask, AXES, scatter_dimension=0, tiled=True),
    )
    return (
        decoder_in,
        grad_pixels,
        summed[0],
        summed[1],
        summed[2],
        summed[3],
        summed[4],
        summed[5],
        summed[6],
        summed[7],
        summed[8],
        summed[9],
        summed[10],
        summed[11],
        summed[12],
        own_part(core_grads[0], 1),
        own_part(core_grads[1], 0),
        own_part(core_grads[2], 0),
        own_part(core_grads[3], 0),
        own_part(core_grads[4], 0),
        own_part(core_grads[5], 0),
        own_part(core_grads[6], 0),
        own_part(core_grads[7], 0),
        own_part(core_grads[8], 0),
        own_part(core_grads[9], 0),
        own_part(core_grads[10], 0),
        own_part(core_grads[11], 0),
        grad_kernel_weight,
        grad_kernel_bias,
        grad_bias_weight,
    )


def on_device(
    pixels,
    sensor,
    band_wave,
    visible,
    block_order,
    pre_gain,
    pre_shift,
    qkv_weight,
    out_weight,
    mid_gain,
    mid_shift,
    up_weight,
    up_bias,
    down_weight,
    down_bias,
    dec_weight,
    dec_bias,
    mask_token,
    gen_tokens,
    gen_qkv,
    gen_out,
    gen_out_bias,
    gen_gain1,
    gen_shift1,
    gen_up,
    gen_up_bias,
    gen_down,
    gen_down_bias,
    gen_gain2,
    gen_shift2,
    kernel_weight,
    kernel_bias,
    bias_weight,
    cotangent,
):
    arguments = (
        pixels,
        sensor,
        band_wave,
        visible,
        block_order,
        pre_gain,
        pre_shift,
        qkv_weight,
        out_weight,
        mid_gain,
        mid_shift,
        up_weight,
        up_bias,
        down_weight,
        down_bias,
        dec_weight,
        dec_bias,
        mask_token,
        gen_tokens,
        gen_qkv,
        gen_out,
        gen_out_bias,
        gen_gain1,
        gen_shift1,
        gen_up,
        gen_up_bias,
        gen_down,
        gen_down_bias,
        gen_gain2,
        gen_shift2,
        kernel_weight,
        kernel_bias,
        bias_weight,
        cotangent,
    )
    planes = lax.axis_size("dp") // 2
    devices = planes * 8
    if lax.axis_size("fsdp") != 4 or planes & (planes - 1) or pre_gain.shape[0] % 8:
        return on_device_plain(*arguments)
    low = jnp.bfloat16
    smalls = (
        gen_up, gen_down, bias_weight, gen_qkv, gen_out, up_bias, gen_up_bias,
        pre_gain, pre_shift, mid_gain, mid_shift, down_bias, dec_bias, mask_token,
        gen_out_bias, gen_gain1, gen_shift1, gen_down_bias, gen_gain2, gen_shift2, gen_tokens,
    )
    flat = jnp.concatenate([item.reshape(-1) for item in smalls])
    lines = -(-flat.shape[0] // (128 * 32)) * 32
    flat = jnp.pad(flat, (0, lines * 128 - flat.shape[0])).reshape(lines, 128)
    spread = small_gather(flat, planes, devices).reshape(devices, lines * 128)
    fulls = []
    start_at = 0
    for item in smalls[:-1]:
        piece = spread[:, start_at : start_at + item.size]
        start_at += item.size
        fulls.append(piece.reshape((devices * item.shape[0],) + item.shape[1:]))
    piece = spread[:, start_at : start_at + gen_tokens.size]
    piece = piece.reshape(devices, gen_tokens.shape[0], gen_tokens.shape[1])
    full_tokens = jnp.swapaxes(piece, 0, 1).reshape(gen_tokens.shape[0], -1)
    (
        full_gen_up, full_gen_down, full_bias_weight, full_gen_qkv, full_gen_out, full_up_bias,
        full_gen_up_bias, full_pre_gain, full_pre_shift, full_mid_gain, full_mid_shift,
        full_down_bias, full_dec_bias, full_mask, full_gen_out_bias, full_gain1, full_shift1,
        full_gen_down_bias, full_gain2, full_shift2,
    ) = fulls
    core32 = tuple(
        item.astype(jnp.float32)
        for item in (
            full_tokens, full_gen_qkv, full_gen_out, full_gen_out_bias, full_gain1, full_shift1,
            full_gen_up, full_gen_up_bias, full_gen_down, full_gen_down_bias, full_gain2,
            full_shift2,
        )
    )
    chips, seen, bands, pix = pixels.shape
    width = qkv_weight.shape[0] * devices
    hidden_width = up_weight.shape[1]
    head_dim = width // HEADS
    scale = 1.0 / math.sqrt(head_dim)
    dec_width = dec_weight.shape[1]
    rows = chips * seen
    wave_code = lax.optimization_barrier(
        sincos(jnp.arange(NWAVE, dtype=jnp.float32), WD // 2).astype(jnp.bfloat16)
    ).astype(jnp.float32)
    (feature, source), core_back = jax.vjp(partial(gen_core, wave_code), *core32)
    feature_low = feature.astype(jnp.bfloat16)
    source_low = source.astype(jnp.bfloat16)
    conv_bias = jnp.dot(source_low[None, :], full_bias_weight, preferred_element_type=jnp.float32)[
        0
    ]
    own_table = (
        jnp.dot(feature_low, kernel_weight, preferred_element_type=jnp.float32)
        + kernel_bias.astype(jnp.float32)[None, :]
    ).astype(low)
    wide = jnp.concatenate([qkv_weight, up_weight, out_weight, dec_weight], axis=1)
    full_wide, full_down, kernels = weight_gather(wide, down_weight, own_table, planes, devices)
    full_down, cotangent = lax.optimization_barrier((full_down, cotangent))
    cuts = (0, 3 * width, 3 * width + hidden_width, 4 * width + hidden_width)
    full_qkv = full_wide[:, : cuts[1]]
    full_up = full_wide[:, cuts[1] : cuts[2]]
    full_out = full_wide[:, cuts[2] : cuts[3]]
    full_dec = full_wide[:, cuts[3] :]
    valid = band_valid(sensor, bands)
    onehot = (band_wave[:, :, None] == jnp.arange(NWAVE, dtype=jnp.int32)[None, None, :]).astype(
        jnp.float32
    )
    place = place_code(visible, width)
    band_kernels = jnp.einsum(
        "cbw,wk->cbk", onehot.astype(jnp.bfloat16), kernels, preferred_element_type=jnp.float32
    ).astype(jnp.bfloat16)
    band_kernels = band_kernels.reshape(chips, bands, pix, width)
    masked = pixels * valid.astype(jnp.bfloat16)[:, None, :, None]
    embedded = jnp.einsum(
        "cvbp,cbpd->cvd", masked, band_kernels, preferred_element_type=jnp.float32
    )
    start = (embedded + conv_bias + place).reshape(rows, width)
    pre_gain32 = full_pre_gain.astype(jnp.float32)
    pre_shift32 = full_pre_shift.astype(jnp.float32)
    normed = norm_rows(start, pre_gain32, pre_shift32).astype(jnp.bfloat16)
    joint = jnp.dot(normed, full_qkv, preferred_element_type=jnp.float32).astype(jnp.bfloat16)
    joint = joint.reshape(chips, seen, 3, HEADS, head_dim)
    queries = joint[:, :, 0]
    keys = joint[:, :, 1]
    values = joint[:, :, 2]
    scores = (
        jnp.einsum("cqhe,ckhe->chqk", queries, keys, preferred_element_type=jnp.float32) * scale
    )
    peak = jnp.max(scores, axis=-1, keepdims=True)
    expd = jnp.exp(scores - peak)
    total = jnp.sum(expd, axis=-1, keepdims=True)
    probs = (expd / total).astype(jnp.bfloat16)
    log_total = peak + jnp.log(total)
    context = jnp.einsum("chqk,ckhe->cqhe", probs, values, preferred_element_type=jnp.float32)
    context = context.astype(jnp.bfloat16).reshape(rows, width)
    attended = jnp.dot(context, full_out, preferred_element_type=jnp.float32)
    middle = start + attended
    mid_gain32 = full_mid_gain.astype(jnp.float32)
    mid_shift32 = full_mid_shift.astype(jnp.float32)
    normed2 = norm_rows(middle, mid_gain32, mid_shift32).astype(jnp.bfloat16)
    upper = jnp.dot(normed2, full_up, preferred_element_type=jnp.float32) + full_up_bias.astype(
        jnp.float32
    )
    bell = 0.5 * (1.0 + lax.erf(upper * math.sqrt(0.5)))
    activ = (upper * bell).astype(jnp.bfloat16)
    slope = bell + upper * jnp.exp(-0.5 * upper * upper) * (1.0 / math.sqrt(2.0 * math.pi))
    slope = slope.astype(low)
    branch = jnp.dot(activ, full_down, preferred_element_type=jnp.float32) + full_down_bias.astype(
        jnp.float32
    )
    ending = (middle + branch).astype(jnp.bfloat16)
    decoded = jnp.dot(ending, full_dec, preferred_element_type=jnp.float32) + full_dec_bias.astype(
        jnp.float32
    )
    decoded = decoded.astype(jnp.bfloat16).reshape(chips, seen, dec_width)
    chosen = block_order[None, :, None] == visible[:, None, :]
    choose = chosen.astype(low)
    ordered = jnp.where(
        jnp.any(chosen, axis=2)[:, :, None],
        jnp.einsum("cjv,cve->cje", choose, decoded, preferred_element_type=jnp.float32).astype(low),
        full_mask,
    )
    decoder_in = lax.all_to_all(ordered, AXES, split_axis=1, concat_axis=0, tiled=True)
    returned = lax.all_to_all(cotangent, AXES, split_axis=0, concat_axis=1, tiled=True)
    slots = jnp.einsum(
        "cvbp,cbw->pwcv", masked, onehot.astype(low), preferred_element_type=jnp.float32
    )
    slots = slots.astype(low).reshape(pix * NWAVE, rows)
    sizes = (rows, width, hidden_width, dec_width, chips, PATCH)
    (
        sum_dec, sum_up, sum_oq, sum_down, grad_kernel_weight, grad_kernel_bias, sum_all,
        sum_vec, grad_embedded,
    ) = backward(
        planes,
        sizes,
        returned.reshape(chips * PATCH, dec_width),
        visible.reshape(rows, 1),
        block_order.reshape(1, PATCH),
        ending,
        full_wide,
        full_down,
        activ,
        slope,
        normed2,
        middle,
        context,
        joint.reshape(rows, 3 * width),
        probs.reshape(chips * HEADS, seen, seen),
        normed,
        start,
        slots,
        jnp.stack([mid_gain32, pre_gain32]),
        kernel_weight,
        feature_low,
    )
    grad_embedded = grad_embedded.reshape(chips, seen, width)
    grad_pixels = jnp.einsum(
        "cvd,cbpd->cvbp", grad_embedded, band_kernels, preferred_element_type=jnp.float32
    )
    grad_pixels = grad_pixels * valid[:, None, :, None]
    grad_feature = sum_all[:NWAVE]
    grad_conv = sum_all[NWAVE : NWAVE + width // 128].reshape(-1)
    grad_bias_weight = own_part(source_low.astype(jnp.float32)[:, None] * grad_conv[None, :], 0)
    grad_source = jnp.dot(full_bias_weight.astype(jnp.float32), grad_conv, precision=HIGH)
    core_grads = core_back((grad_feature, grad_source))
    part = width // devices
    ends = (hidden_width // devices, (hidden_width + dec_width) // devices)
    summed = (
        sum_vec[0, :part],
        sum_vec[0, part : 2 * part],
        sum_oq[:, width:],
        sum_oq[:, :width],
        sum_vec[0, 2 * part : 3 * part],
        sum_vec[0, 3 * part : 4 * part],
        sum_up,
        sum_vec[1, : ends[0]],
        sum_down,
        sum_vec[0, 4 * part : 5 * part],
        sum_dec,
        sum_vec[1, ends[0] : ends[1]],
        sum_vec[1, ends[1] : ends[1] + dec_width // devices],
    )
    return (
        decoder_in,
        grad_pixels,
        summed[0],
        summed[1],
        summed[2],
        summed[3],
        summed[4],
        summed[5],
        summed[6],
        summed[7],
        summed[8],
        summed[9],
        summed[10],
        summed[11],
        summed[12],
        own_part(core_grads[0], 1),
        own_part(core_grads[1], 0),
        own_part(core_grads[2], 0),
        own_part(core_grads[3], 0),
        own_part(core_grads[4], 0),
        own_part(core_grads[5], 0),
        own_part(core_grads[6], 0),
        own_part(core_grads[7], 0),
        own_part(core_grads[8], 0),
        own_part(core_grads[9], 0),
        own_part(core_grads[10], 0),
        own_part(core_grads[11], 0),
        grad_kernel_weight,
        grad_kernel_bias.reshape(-1),
        grad_bias_weight,
    )


def solution(mesh):
    in_specs = (
        P(AXES, None, None, None),
        P(AXES),
        P(AXES, None),
        P(AXES, None),
        P(),
        P(AXES),
        P(AXES),
        P(AXES, None),
        P(AXES, None),
        P(AXES),
        P(AXES),
        P(AXES, None),
        P(AXES),
        P(AXES, None),
        P(AXES),
        P(AXES, None),
        P(AXES),
        P(AXES),
        P(None, AXES),
        P(AXES, None),
        P(AXES, None),
        P(AXES),
        P(AXES),
        P(AXES),
        P(AXES, None),
        P(AXES),
        P(AXES, None),
        P(AXES),
        P(AXES),
        P(AXES),
        P(None, AXES),
        P(AXES),
        P(AXES, None),
        P(None, AXES, None),
    )
    out_specs = (
        P(None, AXES, None),
        P(AXES, None, None, None),
        P(AXES),
        P(AXES),
        P(AXES, None),
        P(AXES, None),
        P(AXES),
        P(AXES),
        P(AXES, None),
        P(AXES),
        P(AXES, None),
        P(AXES),
        P(AXES, None),
        P(AXES),
        P(AXES),
        P(None, AXES),
        P(AXES, None),
        P(AXES, None),
        P(AXES),
        P(AXES),
        P(AXES),
        P(AXES, None),
        P(AXES),
        P(AXES, None),
        P(AXES),
        P(AXES),
        P(AXES),
        P(None, AXES),
        P(AXES),
        P(AXES, None),
    )
    return jax.shard_map(
        on_device, mesh=mesh, in_specs=in_specs, out_specs=out_specs, check_vma=False
    )
```

```python
from functools import partial
import math

import jax
import jax.numpy as jnp
from jax import lax
from jax.experimental import pallas as pl
from jax.experimental.pallas import tpu as pltpu
from jax.sharding import PartitionSpec as P

HEADS = 12
WD = 128
GHEADS = 4
LAT = 128
NWAVE = 32
GRID = 32
PATCH = 1024


EPS = 1e-05
AXES = ("dp", "fsdp")
BAND_DROP = (0, 6, 9, 7)
HIGH = lax.Precision.HIGHEST


def sincos(values, count):
    freq = jnp.exp(jnp.arange(count, dtype=jnp.float32) * (-math.log(10000.0) / count))
    angle = values[..., None] * freq
    return jnp.concatenate([jnp.sin(angle), jnp.cos(angle)], axis=-1)


def norm_rows(rows, gain, shift):
    mean = jnp.mean(rows, axis=-1, keepdims=True)
    centred = rows - mean
    spread = jnp.mean(centred * centred, axis=-1, keepdims=True)
    return centred * lax.rsqrt(spread + EPS) * gain + shift


def exact_gelu(values):
    return jax.nn.gelu(values, approximate=False)


def band_valid(sensor, bands):
    drops = jnp.array(BAND_DROP, jnp.int32)
    picked = jnp.where(
        sensor[:, None] == jnp.arange(4, dtype=jnp.int32)[None, :], drops[None, :], 0
    )
    count = bands - jnp.sum(picked, axis=1)
    return (jnp.arange(bands, dtype=jnp.int32)[None, :] < count[:, None]).astype(jnp.float32)


def place_code(visible, width):
    row = (visible // GRID).astype(jnp.float32)
    col = (visible % GRID).astype(jnp.float32)
    return jnp.concatenate([sincos(row, width // 4), sincos(col, width // 4)], axis=-1)


def gen_core(
    wave_code,
    tokens,
    gen_qkv,
    gen_out,
    gen_out_bias,
    gen_gain1,
    gen_shift1,
    gen_up,
    gen_up_bias,
    gen_down,
    gen_down_bias,
    gen_gain2,
    gen_shift2,
):
    sequence = jnp.concatenate([tokens[:LAT], wave_code, tokens[LAT:]], axis=0)
    length = sequence.shape[0]
    width = sequence.shape[1]
    head_dim = width // GHEADS
    joint = jnp.dot(sequence, gen_qkv, precision=HIGH).reshape(length, 3, GHEADS, head_dim)
    scores = jnp.einsum("qhe,khe->hqk", joint[:, 0], joint[:, 1], precision=HIGH) / math.sqrt(
        head_dim
    )
    probs = jax.nn.softmax(scores, axis=-1)
    context = jnp.einsum("hqk,khe->qhe", probs, joint[:, 2], precision=HIGH).reshape(length, width)
    mixed = norm_rows(
        sequence + jnp.dot(context, gen_out, precision=HIGH) + gen_out_bias, gen_gain1, gen_shift1
    )
    hidden = jax.nn.gelu(jnp.dot(mixed, gen_up, precision=HIGH) + gen_up_bias, approximate=False)
    final = norm_rows(
        mixed + jnp.dot(hidden, gen_down, precision=HIGH) + gen_down_bias, gen_gain2, gen_shift2
    )
    feature = final[LAT : LAT + NWAVE] + sequence[LAT : LAT + NWAVE]
    return (feature, final[length - 1])


def own_part(full, dim):
    count = lax.axis_size("dp") * lax.axis_size("fsdp")
    index = lax.axis_index("dp") * lax.axis_size("fsdp") + lax.axis_index("fsdp")
    piece = full.shape[dim] // count
    return lax.dynamic_slice_in_dim(full, index * piece, piece, dim)


def tdot(left, right):
    return lax.dot_general(
        left, right, (((0,), (0,)), ((), ())), preferred_element_type=jnp.float32
    )


def ndot(left, right):
    return lax.dot_general(
        left, right, (((1,), (1,)), ((), ())), preferred_element_type=jnp.float32
    )


MESH_ID = pl.DeviceIdType.MESH
ANY = pl.BlockSpec(memory_space=pl.ANY)
VMEM = pl.BlockSpec(memory_space=pltpu.VMEM)


class Net:
    def __init__(self, planes):
        dp, fs = lax.axis_index("dp"), lax.axis_index("fsdp")
        self.planes = planes
        self.z, self.x = lax.div(dp, 2), lax.rem(dp, 2)
        self.y, self.c = lax.div(fs, 2), lax.rem(fs, 2)
        self.sib = self.at(self.z, self.x, self.y, 1 - self.c)
        self.nx = self.at(self.z, 1 - self.x, self.y, self.c)
        self.ny = self.at(self.z, self.x, 1 - self.y, self.c)

    def at(self, z, x, y, c):
        return (z * 2 + x, y * 2 + c)

    def plane(self, k):
        return lax.rem(self.z + k, self.planes)

    def zpeer(self, k):
        return self.at(self.plane(k), self.x, self.y, self.c)

    def chip(self, k, dx=0, dy=0):
        x = 1 - self.x if dx else self.x
        y = 1 - self.y if dy else self.y
        return self.plane(k) * 4 + x * 2 + y

    def greet(self):
        barrier = pltpu.get_barrier_semaphore()
        partners = [self.sib, self.nx, self.ny]
        partners += [self.zpeer(k) for k in range(1, self.planes)]
        for partner in partners:
            pl.semaphore_signal(barrier, inc=1, device_id=partner, device_id_type=MESH_ID)
        pl.semaphore_wait(barrier, len(partners))


class Wires:
    def __init__(self, send, recv):
        self.send, self.recv, self.used, self.started = send, recv, 0, []

    def push(self, src, dst, device):
        index = self.used
        self.used += 1
        copy = pltpu.make_async_remote_copy(
            src_ref=src,
            dst_ref=dst,
            send_sem=self.send.at[index],
            recv_sem=self.recv.at[index],
            device_id=device,
            device_id_type=MESH_ID,
        )
        copy.start()
        self.started.append(copy)
        return copy

    def drain(self):
        for copy in self.started:
            copy.wait_send()


class Gather:
    def __init__(self, net, wires, own, piece):
        self.net, self.wires, self.own, self.piece = net, wires, own, piece
        self.z_in, self.first, self.second, self.twins = {}, {}, {}, []

    def near(self, h):
        return self.net.ny if h else self.net.nx

    def far(self, h):
        return self.net.nx if h else self.net.ny

    def share(self, chip, h, src=None):
        spot = self.piece(chip, h)
        self.twins.append(self.wires.push(spot if src is None else src, spot, self.net.sib))

    def begin_z(self):
        for k in range(1, self.net.planes):
            for h in range(2):
                spot = self.piece(self.net.chip(0), h)
                self.z_in[k, h] = self.wires.push(self.own(h), spot, self.net.zpeer(k))

    def spread(self, k):
        back = (self.net.planes - k) % self.net.planes
        for h in range(2):
            if k:
                self.z_in[k, h].wait_recv()
            spot = self.piece(self.net.chip(back), h)
            src = self.own(h) if k == 0 else spot
            self.first[k, h] = self.wires.push(src, spot, self.near(h))
            self.second[k, h, 0] = self.wires.push(src, spot, self.far(h))
            self.share(self.net.chip(back), h, src)

    def relay(self, k):
        back = (self.net.planes - k) % self.net.planes
        for h in range(2):
            self.first[k, h].wait_recv()
            chip = self.net.chip(back, dx=h == 0, dy=h == 1)
            spot = self.piece(chip, h)
            self.second[k, h, 1] = self.wires.push(spot, spot, self.far(h))
            self.share(chip, h)

    def close(self, k):
        back = (self.net.planes - k) % self.net.planes
        for h in range(2):
            for hop in range(2):
                self.second[k, h, hop].wait_recv()
                chip = self.net.chip(back, dx=hop == 1 or h == 1, dy=hop == 1 or h == 0)
                self.share(chip, h)

    def finish(self):
        for copy in self.twins:
            copy.wait_recv()


def gather_copies(planes):
    return 2 * (planes - 1) + 4 * planes + 2 * planes + 8 * planes


class Reduce:
    def __init__(self, net, wires, part, held, near_in, far_in, z_in):
        self.net, self.wires, self.part, self.held = net, wires, part, held
        self.near_in, self.far_in, self.z_in = near_in, far_in, z_in
        self.pairs, self.near, self.far, self.along = {}, {}, {}, {}

    def add(self, spot, other):
        size = 16 if spot.shape[0] % 16 == 0 else 8

        def some(i, _):
            at = pl.ds(pl.multiple_of(i * size, size), size)
            total = spot[at].astype(jnp.float32) + other[at].astype(jnp.float32)
            spot[at] = total.astype(spot.dtype)
            return 0

        lax.fori_loop(0, spot.shape[0] // size, some, 0)

    def begin(self, k):
        for dx in range(2):
            for dy in range(2):
                for h in range(2):
                    chip = self.net.chip(k, dx, dy)
                    self.pairs[k, dx, dy, h] = self.wires.push(
                        self.part(chip, 1 - self.net.c, h), self.held.at[chip, h], self.net.sib
                    )

    def stage0(self, k):
        for dx, dy in ((1, 1), (0, 1), (1, 0), (0, 0)):
            for h in range(2):
                self.pairs[k, dx, dy, h].wait_recv()
                chip = self.net.chip(k, dx, dy)
                self.add(self.held.at[chip, h], self.part(chip, self.net.c, h))
                if (dy if h == 0 else dx) == 1:
                    other = dx if h == 0 else dy
                    self.near[k, h, other] = self.wires.push(
                        self.held.at[chip, h],
                        self.near_in.at[k, h, other],
                        self.net.ny if h == 0 else self.net.nx,
                    )

    def stage1(self, k):
        for h in range(2):
            for other in (1, 0):
                self.near[k, h, other].wait_recv()
                chip = self.net.chip(k, other, 0) if h == 0 else self.net.chip(k, 0, other)
                self.add(self.held.at[chip, h], self.near_in.at[k, h, other])
                if other:
                    self.far[k, h] = self.wires.push(
                        self.held.at[chip, h],
                        self.far_in.at[k, h],
                        self.net.nx if h == 0 else self.net.ny,
                    )

    def stage2(self, k):
        for h in range(2):
            self.far[k, h].wait_recv()
            spot = self.held.at[self.net.chip(k), h]
            self.add(spot, self.far_in.at[k, h])
            if k:
                self.along[k, h] = self.wires.push(spot, self.z_in.at[k - 1, h], self.net.zpeer(k))

    def total(self, h):
        value = self.held[self.net.chip(0), h].astype(jnp.float32)
        for k in range(1, self.net.planes):
            self.along[k, h].wait_recv()
            value = value + self.z_in[k - 1, h].astype(jnp.float32)
        return value


def reduce_copies(planes):
    return 8 * planes + 4 * planes + 2 * planes + 2 * (planes - 1)


def reduce_scratch(planes, rows, cols, dtype):
    return [
        pltpu.VMEM((planes * 4, 2, rows, cols), dtype),
        pltpu.VMEM((planes, 2, 2, rows, cols), dtype),
        pltpu.VMEM((planes, 2, rows, cols), dtype),
        pltpu.VMEM((planes - 1, 2, rows, cols), dtype),
    ]


def dot_nn(left, right):
    return jnp.dot(left, right, preferred_element_type=jnp.float32)


class Pump:
    def __init__(self):
        self.units, self.at = [], 0

    def put(self, item, order):
        for k in order:
            item.begin(k)
        self.units += [(item, k) for k in order]

    def step(self, count=1):
        for _ in range(count):
            for stage in range(3):
                at = self.at - stage
                if 0 <= at < len(self.units):
                    item, k = self.units[at]
                    (item.stage0, item.stage1, item.stage2)[stage](k)
            self.at += 1

    def until(self, item):
        last = max(i for i, unit in enumerate(self.units) if unit[0] is item)
        while self.at <= last + 2:
            self.step()


def tile_rows(i, size):
    return pl.ds(pl.multiple_of(i * size, size), size)


def norm_back(grad, rows, gain):
    mean = jnp.mean(rows, axis=-1, keepdims=True)
    centred = rows - mean
    spread = jnp.mean(centred * centred, axis=-1, keepdims=True)
    inverse = lax.rsqrt(spread + EPS)
    unit = centred * inverse
    scaled = grad * gain
    inner = scaled - jnp.mean(scaled, axis=-1, keepdims=True)
    inner = inner - unit * jnp.mean(scaled * unit, axis=-1, keepdims=True)
    return inverse * inner, grad * unit


def lay_lines(box, at, value):
    for i in range(value.shape[1] // 128):
        box[0, pl.ds(at + i, 1), :] = value[:, i * 128 : (i + 1) * 128]
    return at + value.shape[1] // 128


def box_lines(waves, width, hidden, dec_width):
    used = waves + (6 * width + hidden + 2 * dec_width) // 128
    return used + (-used) % 8


FT = 256
BLOCK = 128


def backward_kernel(planes, steps, sizes, *refs):
    (rows, width, hidden, dec_width, chips, patches) = sizes
    devices = planes * 8
    seen = rows // chips
    (
        returned, visible, order, ending, wide, down, activ, slope, normed2, middle, context,
        joint, probs, normed, start, slots, gains, weight, feature, source, gen_rows, gen_down,
        gen_vec, wave_code,
    ) = refs[:24]
    (
        dec_out, up_out, oq_out, down_out, kw_out, kb_out, all_out, gen_wide, gen_tall, gen_seq,
        gen_lines, bias_out, embed_out,
    ) = refs[24:37]
    scratch = refs[37:59]
    (
        big, left, w_down, w_up, t_activ, t_slope, resid, w_sq, t_joint, t_probs,
        g_dec, g_up, g_down, g_oq, g_table, run, back, g_low, g_joint, v_sums,
        f_dec, f_up, f_oq, hand_dec, hand_up, hand_oq, box, send, recv, tile_sem, load_sem,
    ) = refs[59:]
    loads = {}

    def load(name, src, dst):
        copy = pltpu.make_async_copy(src, dst, load_sem.at[len(loads)])
        copy.start()
        loads[name] = copy

    up_at, out_at, dec_at = 3 * width, 3 * width + hidden, 4 * width + hidden
    load("returned", returned, big)
    w_dec = w_sq.at[0, :, pl.ds(0, dec_width)]
    load("dec", wide.at[:, pl.ds(dec_at, dec_width)], w_dec)
    load("ending", ending, left.at[0])

    def tile_copies(t):
        slot = lax.rem(t, 2)
        at = tile_rows(t, FT)
        return (
            pltpu.make_async_copy(down.at[at], w_down.at[slot], tile_sem.at[slot, 0]),
            pltpu.make_async_copy(
                wide.at[:, pl.ds(pl.multiple_of(up_at + t * FT, 128), FT)],
                w_up.at[slot],
                tile_sem.at[slot, 1],
            ),
            pltpu.make_async_copy(activ.at[:, at], t_activ.at[slot], tile_sem.at[slot, 2]),
            pltpu.make_async_copy(slope.at[:, at], t_slope.at[slot], tile_sem.at[slot, 3]),
        )

    for copy in tile_copies(0):
        copy.start()
    load("normed2", normed2, left.at[1])
    load("middle", middle, resid)
    load("query", wide.at[:, pl.ds(0, width)], w_sq.at[1])

    net = Net(planes)
    net.greet()
    wires = Wires(send, recv)
    pump = Pump()
    shard = width // (devices // 2)
    w_rows = lambda chip: pl.ds(pl.multiple_of(chip * shard, 16), shard)

    def quarter(ref, size):
        return lambda chip, c, h: ref.at[
            w_rows(chip), pl.ds(pl.multiple_of((c * 2 + h) * size, 128), size)
        ]

    def stripe(ref, size):
        return lambda chip, c, h: ref.at[
            pl.ds(pl.multiple_of(((chip * 2 + c) * 2 + h) * size, 16), size)
        ]

    q_dec, q_up = dec_width // 4, hidden // 8
    d_rows = hidden // devices // 2
    t_rows = g_table.shape[0] // devices // 2
    parts = (
        quarter(g_dec, q_dec),
        quarter(g_up.at[0], q_up),
        quarter(g_up.at[1], q_up),
        stripe(g_down, d_rows),
        stripe(g_table, t_rows),
        lambda chip, c, h: g_oq.at[c * 2 + h, w_rows(chip)],
    )
    lands = [scratch[i * 4 : i * 4 + 4] for i in range(5)]
    lands.append((scratch[20], lands[3][1], lands[3][2], scratch[21]))
    dec, up0, up1, downs, tables, oq = [
        Reduce(net, wires, part, *land) for part, land in zip(parts, lands)
    ]
    away = list(range(1, planes)) + [0]

    loads["returned"].wait()

    def pick(i, count):
        at = tile_rows(i, BLOCK)
        chosen = (visible[at] == order[...]).astype(jnp.float32)
        picked = dot_nn(chosen.astype(jnp.bfloat16), big[...])
        g_joint[at, pl.ds(0, dec_width)] = picked.astype(jnp.bfloat16)
        return count + jnp.sum(chosen, axis=0, keepdims=True)

    count = lax.fori_loop(
        0, rows // BLOCK, pick, jnp.zeros((1, chips * patches), jnp.float32)
    )
    left_out = jnp.broadcast_to(1.0 - count, (8, chips * patches)).astype(jnp.bfloat16)
    v_sums[pl.ds(7, 1), pl.ds(dec_width, dec_width)] = dot_nn(left_out, big[...])[:1]
    load("slots", slots, big)
    grad_rows = g_joint[:, pl.ds(0, dec_width)]
    v_sums[pl.ds(7, 1), pl.ds(0, dec_width)] = jnp.sum(
        grad_rows.astype(jnp.float32), axis=0, keepdims=True
    )
    loads["ending"].wait()

    def dec_part(i, _):
        at = tile_rows(i, FT)
        g_dec[at, :] = tdot(left[0, :, at], grad_rows).astype(jnp.bfloat16)
        return 0

    lax.fori_loop(0, width // FT, dec_part, 0)
    pump.put(dec, away)
    loads["dec"].wait()

    def end_part(i, _):
        at = tile_rows(i, FT)
        run[at, :] = ndot(g_joint[at, pl.ds(0, dec_width)], w_dec[...])
        g_low[at, :] = run[at, :].astype(jnp.bfloat16)
        return 0

    lax.fori_loop(0, rows // FT, end_part, 0)
    load("out", wide.at[:, pl.ds(out_at, width)], w_sq.at[0])
    load("context", context, left.at[0])
    back[...] = jnp.zeros_like(back)
    v_sums[pl.ds(0, 1), pl.ds(0, width)] = jnp.sum(
        g_low[...].astype(jnp.float32), axis=0, keepdims=True
    )
    loads["normed2"].wait()
    tiles = hidden // FT

    def feed(t, _):
        slot = lax.rem(t, 2)

        @pl.when(t + 1 < tiles)
        def _():
            for copy in tile_copies(t + 1):
                copy.start()

        for copy in tile_copies(t):
            copy.wait()
        grad = ndot(g_low[...], w_down[slot])
        grad_upper = (grad * t_slope[slot].astype(jnp.float32)).astype(jnp.bfloat16)
        at = tile_rows(t, FT)
        v_sums[pl.ds(1, 1), at] = jnp.sum(
            grad_upper.astype(jnp.float32), axis=0, keepdims=True
        )
        g_down[at, :] = tdot(t_activ[slot], g_low[...]).astype(jnp.bfloat16)
        g_up[lax.div(t, tiles // 2), :, tile_rows(lax.rem(t, tiles // 2), FT)] = tdot(
            left[1], grad_upper
        ).astype(jnp.bfloat16)
        for i in range(rows // FT):
            part = pl.ds(i * FT, FT)
            back[part, :] += ndot(grad_upper[i * FT : (i + 1) * FT], w_up[slot])
        return 0

    lax.fori_loop(0, tiles // 4, feed, 0)
    pump.step(2)
    lax.fori_loop(tiles // 4, tiles // 2, feed, 0)
    pump.put(up0, away)
    pump.step(2)
    lax.fori_loop(tiles // 2, 3 * tiles // 4, feed, 0)
    pump.step(2)
    lax.fori_loop(3 * tiles // 4, tiles, feed, 0)
    pump.put(up1, away)
    pump.put(downs, away)
    load("normed", normed, left.at[1])
    loads["middle"].wait()

    def through_norm(gain_row, sums_at):
        gain = gains[pl.ds(gain_row, 1), pl.ds(0, width)]

        def block(i, sums):
            at = tile_rows(i, BLOCK)
            grad = back[at, :]
            inner, terms = norm_back(grad, resid[at, :], gain)
            run[at, :] += inner
            return (
                sums[0] + jnp.sum(terms, axis=0, keepdims=True),
                sums[1] + jnp.sum(grad, axis=0, keepdims=True),
            )

        zero = jnp.zeros((1, width), jnp.float32)
        sums = lax.fori_loop(0, rows // BLOCK, block, (zero, zero))
        v_sums[pl.ds(sums_at, 1), pl.ds(0, width)] = sums[0]
        v_sums[pl.ds(sums_at + 1, 1), pl.ds(0, width)] = sums[1]

    through_norm(2, 2)
    pump.step(2)
    load("start", start, resid)
    g_low[...] = run[...].astype(jnp.bfloat16)
    loads["context"].wait()
    loads["out"].wait()

    def out_part(i, _):
        at = tile_rows(i, FT)
        g_oq[0, at, :] = tdot(left[0, :, at], g_low[...]).astype(jnp.bfloat16)
        return 0

    lax.fori_loop(0, width // FT, out_part, 0)

    def context_part(i, _):
        at = tile_rows(i, FT)
        g_low[at, :] = ndot(g_low[at, :], w_sq[0]).astype(jnp.bfloat16)
        return 0

    lax.fori_loop(0, rows // FT, context_part, 0)
    load("key", wide.at[:, pl.ds(width, width)], w_sq.at[0])
    pump.step(2)

    pairs = width // 128
    head = width // HEADS
    scale = 1.0 / math.sqrt(head)
    odd = lax.broadcasted_iota(jnp.int32, (1, 128), 1) >= head

    def pair_copies(n):
        slot = lax.rem(n, 2)
        at = tile_rows(lax.div(n, pairs), seen)
        copies = [
            pltpu.make_async_copy(probs.at[pl.ds(2 * n, 2)], t_probs.at[slot], tile_sem.at[slot, 0])
        ]
        for i in range(3):
            lane = pl.ds(pl.multiple_of(lax.rem(n, pairs) * 128 + i * width, 128), 128)
            copies.append(
                pltpu.make_async_copy(
                    joint.at[at, lane], t_joint.at[slot, i], tile_sem.at[slot, i + 1]
                )
            )
        return copies

    for copy in pair_copies(0):
        copy.start()

    def attend(n, _):
        slot = lax.rem(n, 2)

        @pl.when(n + 1 < chips * pairs)
        def _():
            for copy in pair_copies(n + 1):
                copy.start()

        for copy in pair_copies(n):
            copy.wait()
        chip = lax.div(n, pairs)
        pair = lax.rem(n, pairs)
        at = tile_rows(chip, seen)
        lanes = [
            pl.ds(pl.multiple_of(pair * 128 + i * width, 128), 128) for i in range(3)
        ]
        query, key, value = [t_joint[slot, i] for i in range(3)]
        grad = g_low[at, lanes[0]]
        zero = jnp.zeros_like(grad)
        totals = [None, None, None]
        for h in range(2):
            mine = odd if h else jnp.logical_not(odd)
            grad_h = jnp.where(mine, grad, zero)
            query_h = jnp.where(mine, query, zero)
            key_h = jnp.where(mine, key, zero)
            prob = t_probs[slot, h]
            prob32 = prob.astype(jnp.float32)
            grad_prob = ndot(grad_h, value)
            row_dot = jnp.sum(prob32 * grad_prob, axis=-1, keepdims=True)
            grad_score = (prob32 * (grad_prob - row_dot)).astype(jnp.bfloat16)
            terms = (dot_nn(grad_score, key_h), tdot(grad_score, query_h), tdot(prob, grad_h))
            totals = [new if old is None else old + new for old, new in zip(totals, terms)]
        g_joint[at, lanes[0]] = (totals[0] * scale).astype(jnp.bfloat16)
        g_joint[at, lanes[1]] = (totals[1] * scale).astype(jnp.bfloat16)
        g_joint[at, lanes[2]] = totals[2].astype(jnp.bfloat16)
        return 0

    for chip in range(chips):
        lax.fori_loop(chip * pairs, (chip + 1) * pairs, attend, 0)
        pump.step(2)

    loads["normed"].wait()
    def joint_part(i, _):
        which, at = lax.div(i, width // FT), tile_rows(lax.rem(i, width // FT), FT)
        lane = pl.ds(pl.multiple_of(which * width, 128), width)
        g_oq[which + 1, at, :] = tdot(left[1, :, at], g_joint[:, lane]).astype(jnp.bfloat16)
        return 0

    lax.fori_loop(0, 3 * width // FT, joint_part, 0)
    value = pltpu.make_async_copy(
        wide.at[:, pl.ds(2 * width, width)], w_sq.at[1], load_sem.at[len(loads)]
    )
    back[...] = jnp.zeros_like(back)

    def joint_back(i, _):
        for j, copy in enumerate((loads["query"], loads["key"], value)):

            @pl.when(i == j)
            def _():
                copy.wait()

        lane = pl.ds(pl.multiple_of(i * width, 128), width)

        def some(j, _):
            at = tile_rows(j, FT)
            back[at, :] += ndot(g_joint[at, lane], w_sq[lax.rem(i + 1, 2)])
            return 0

        lax.fori_loop(0, rows // FT, some, 0)

        @pl.when(i == 0)
        def _():
            value.start()

        return 0

    lax.fori_loop(0, 3, joint_back, 0)
    pump.step(1)
    loads["start"].wait()
    through_norm(0, 4)
    g_low[...] = run[...].astype(jnp.bfloat16)
    conv = jnp.sum(run[...], axis=0, keepdims=True)
    embed = pltpu.make_async_copy(g_low, embed_out, tile_sem.at[0, 1])
    embed.start()
    loads["slots"].wait()
    span = 512

    def table_block(i, _):
        at = tile_rows(i, span)
        g_table[at, :] = dot_nn(big[at, :], g_low[...]).astype(jnp.bfloat16)
        return 0

    lax.fori_loop(0, g_table.shape[0] // span, table_block, 0)
    pump.put(tables, away)
    pump.put(oq, away)

    waves = t_rows
    lines = width // 128
    box[0, pl.ds(waves, box.shape[1] - waves), :] = jnp.zeros(
        (box.shape[1] - waves, 128), jnp.float32
    )
    at = lay_lines(box, waves, conv)
    for line in (4, 5, 2, 3, 0):
        at = lay_lines(box, at, v_sums[pl.ds(line, 1), pl.ds(0, width)])
    at = lay_lines(box, at, v_sums[pl.ds(1, 1), :])
    lay_lines(box, at, v_sums[pl.ds(7, 1), pl.ds(0, 2 * dec_width)])

    pump.until(tables)
    held = tables.held
    partial_sum = jnp.zeros((waves, 128), jnp.float32)
    for h in range(2):
        own = tables.total(h).astype(jnp.bfloat16)
        cols = pl.ds(h * width, width)
        kw_out[:, cols] = tdot(feature[...], own)
        kb_out[:, cols] = jnp.sum(own.astype(jnp.float32), axis=0, keepdims=True)
        partial_sum = partial_sum + ndot(own, weight[:, cols])
    box[0, pl.ds(0, waves), :] = partial_sum
    peers = [net.sib, net.nx, net.ny]
    for bit in range(steps):
        step = 1 << bit
        up = lax.rem(lax.div(net.z, step), 2) == 0
        peers.append(net.at(jnp.where(up, net.z + step, net.z - step), net.x, net.y, net.c))
    for i, peer in enumerate(peers):
        hop = wires.push(box.at[2 * i], box.at[2 * i + 1], peer)
        pump.step(1)
        hop.wait_recv()
        box[2 * i + 2] = box[2 * i] + box[2 * i + 1]
    end = box.at[2 * len(peers)]
    all_out[...] = end[...]
    me = net.chip(0) * 2 + net.c
    conv = jnp.concatenate(
        [end[pl.ds(waves + i, 1), :] for i in range(lines)], axis=1
    )
    gen_width = gen_rows.shape[0]
    up_size = gen_down.shape[0]
    bias_at = gen_rows.shape[1] - gen_width - width
    grad_source = lax.dot_general(
        jnp.broadcast_to(conv, (8, width)),
        gen_rows[:, pl.ds(bias_at, width)].astype(jnp.float32),
        (((1,), (1,)), ((), ())),
        precision=HIGH,
        preferred_element_type=jnp.float32,
    )
    top = lax.broadcasted_iota(jnp.int32, (8, gen_width), 0)
    grad_source = jnp.where(top == 0, grad_source, 0.0)
    pump.step(1)
    small = gen_width // devices
    lane = lax.broadcasted_iota(jnp.int32, (8, gen_width), 1)
    pick = ((lane == me * small + top) & (top < small)).astype(jnp.float32)
    exact = partial(
        lax.dot_general, precision=HIGH, preferred_element_type=jnp.float32
    )
    rows_of = lambda value: exact(pick, value, (((1,), (0,)), ((), ())))
    lanes_of = lambda value: exact(value, pick, (((1,), (1,)), ((), ())))
    chunk = up_size // 4

    def put_up(i, value):
        gen_wide[:, pl.ds(pl.multiple_of(i * chunk, chunk), chunk)] = rows_of(value)

    def put_down(i, value):
        back[:, pl.ds(pl.multiple_of(i * gen_width, gen_width), gen_width)] = value

    g_seq, g_qkv, g_out, thin = gen_back(
        gen_rows, gen_down, gen_vec, wave_code[...], LAT + NWAVE + 1, end[pl.ds(0, waves), :],
        grad_source, v_sums, put_up, put_down,
    )
    pump.step(2)
    gen_wide[:, pl.ds(up_size, 3 * gen_width)] = rows_of(g_qkv)
    gen_wide[:, pl.ds(up_size + 3 * gen_width, gen_width)] = rows_of(g_out)
    tall = up_size // devices
    per = devices // 4
    gen_tall[...] = back[
        tile_rows(lax.rem(me, per), tall),
        pl.ds(pl.multiple_of(lax.div(me, per) * gen_width, 128), gen_width),
    ]
    gen_seq[...] = lanes_of(g_seq)
    for i, value in enumerate(thin):
        gen_lines[pl.ds(i, 1), pl.ds(0, gen_width)] = value
    gen_lines[pl.ds(6, 1), :] = v_sums[pl.ds(6, 1), pl.ds(0, up_size)]
    own_source = jnp.sum(
        pick * source[pl.ds(0, 1), :].astype(jnp.float32), axis=1, keepdims=True
    )
    bias_out[...] = own_source * conv
    pump.until(oq)
    half = shard // 2
    own_rows = pl.ds(pl.multiple_of(net.c * half, 8), half)
    their_rows = pl.ds(pl.multiple_of((1 - net.c) * half, 8), half)
    jobs = (
        (dec, f_dec, hand_dec, dec_out, 0, q_dec),
        (up0, f_up.at[0], hand_up.at[0], up_out, 0, q_up),
        (up1, f_up.at[1], hand_up.at[1], up_out, hidden // 2, q_up),
        (oq, f_oq, hand_oq, oq_out, 0, width),
    )
    swaps = []
    for item, final, hand, out, base, size in jobs:
        for h in range(2):
            final[h] = item.total(h)
            swaps.append(wires.push(final.at[h, their_rows], hand.at[h], net.sib))
    for h in range(2):
        down_out[pl.ds(h * d_rows, d_rows)] = downs.total(h)
    for item, final, hand, out, base, size in jobs:
        for h in range(2):
            own = pl.ds(pl.multiple_of(base + (net.c * 2 + h) * size, 128), size)
            other = pl.ds(pl.multiple_of(base + ((1 - net.c) * 2 + h) * size, 128), size)
            out[:, own] = final[h, own_rows]
            swaps.pop(0).wait_recv()
            out[:, other] = hand[h]
    embed.wait()
    wires.drain()


def backward(planes, sizes, *args):
    (rows, width, hidden, dec_width, chips, patches) = sizes
    devices = planes * 8
    steps = (planes - 1).bit_length()
    low, full = jnp.bfloat16, jnp.float32
    shard = width // (devices // 2)
    q_dec, q_up = dec_width // 4, hidden // 8
    d_rows = hidden // devices // 2
    slots = args[15].shape[0]
    t_rows = slots // devices // 2
    box_rows = box_lines(t_rows, width, hidden, dec_width)
    up_size, gen_width = args[21].shape
    copies = 6 * reduce_copies(planes) + 3 + steps + 8
    scratch = []
    for shape in (
        (shard, q_dec), (shard, q_up), (shard, q_up), (d_rows, width), (t_rows, width),
    ):
        scratch += reduce_scratch(planes, *shape, low)
    assert d_rows == shard
    last = reduce_scratch(planes, shard, width, low)
    scratch += [last[0], last[3]]
    scratch += [
        pltpu.VMEM((chips * patches, dec_width), low),
        pltpu.VMEM((2, rows, width), low),
        pltpu.VMEM((2, FT, width), low),
        pltpu.VMEM((2, width, FT), low),
        pltpu.VMEM((2, rows, FT), low),
        pltpu.VMEM((2, rows, FT), low),
        pltpu.VMEM((rows, width), full),
        pltpu.VMEM((2, width, width), low),
        pltpu.VMEM((2, 3, rows // chips, 128), low),
        pltpu.VMEM((2, 2, rows // chips, rows // chips), low),
        pltpu.VMEM((width, dec_width), low),
        pltpu.VMEM((2, width, hidden // 2), low),
        pltpu.VMEM((hidden, width), low),
        pltpu.VMEM((4, width, width), low),
        pltpu.VMEM((slots, width), low),
        pltpu.VMEM((rows, width), full),
        pltpu.VMEM((rows, width), full),
        pltpu.VMEM((rows, width), low),
        pltpu.VMEM((rows, 3 * width), low),
        pltpu.VMEM((8, hidden), full),
        pltpu.VMEM((2, shard, q_dec), full),
        pltpu.VMEM((2, 2, shard, q_up), full),
        pltpu.VMEM((2, shard, width), full),
        pltpu.VMEM((2, shard // 2, q_dec), full),
        pltpu.VMEM((2, 2, shard // 2, q_up), full),
        pltpu.VMEM((2, shard // 2, width), full),
        pltpu.VMEM((2 * (3 + steps) + 1, box_rows, 128), full),
        pltpu.SemaphoreType.DMA((copies,)),
        pltpu.SemaphoreType.DMA((copies,)),
        pltpu.SemaphoreType.DMA((2, 4)),
        pltpu.SemaphoreType.DMA((16,)),
    ]
    shapes = (
        ((width // devices, dec_width), full),
        ((width // devices, hidden), full),
        ((width // devices, 4 * width), full),
        ((hidden // devices, width), full),
        ((args[18].shape[1], 2 * width), full),
        ((1, 2 * width), full),
        ((box_rows, 128), full),
        ((8, up_size + 4 * gen_width), full),
        ((up_size // devices, gen_width), full),
        ((args[23].shape[0] + gen_width + 8, 8), full),
        ((8, up_size), full),
        ((8, width), full),
        ((rows, width), low),
    )
    spots = [ANY, VMEM, VMEM] + [ANY] * 13 + [VMEM] * 8
    return pl.pallas_call(
        partial(backward_kernel, planes, steps, sizes),
        out_shape=tuple(jax.ShapeDtypeStruct(shape, dtype) for shape, dtype in shapes),
        in_specs=spots,
        out_specs=[VMEM] * 12 + [ANY],
        scratch_shapes=scratch,
        compiler_params=pltpu.CompilerParams(
            collective_id=2, has_side_effects=True, vmem_limit_bytes=125 * 2**19
        ),
    )(*args)


CHUNK = 896


def gen_layer(
    seq, qkv, out, out_bias, gain1, shift1, up, up_bias, down, down_bias, gain2, shift2, length
):
    width = seq.shape[1]
    size = width // GHEADS

    def times(left, right):
        return jnp.dot(left, right, precision=HIGH, preferred_element_type=jnp.float32)

    joint = times(seq, qkv)
    query, key, value = [joint[:, i * width : (i + 1) * width] for i in range(3)]
    lane = lax.broadcasted_iota(jnp.int32, (1, width), 1)
    spot = lax.broadcasted_iota(jnp.int32, (1, seq.shape[0]), 1)
    context = jnp.zeros_like(seq)
    for h in range(GHEADS):
        mine = (lax.div(lane, size) == h).astype(jnp.float32)
        scores = lax.dot_general(
            query * mine,
            key,
            (((1,), (1,)), ((), ())),
            precision=HIGH,
            preferred_element_type=jnp.float32,
        ) * (1.0 / math.sqrt(size))
        scores = jnp.where(spot < length, scores, -1e30)
        peak = lax.stop_gradient(jnp.max(scores, axis=-1, keepdims=True))
        raised = jnp.exp(scores - peak)
        probs = raised / jnp.sum(raised, axis=-1, keepdims=True)
        context = context + times(probs, value * mine)
    mixed = norm_rows(seq + times(context, out) + out_bias, gain1, shift1)
    inner = times(mixed, up) + up_bias
    hidden = 0.5 * inner * (1.0 + lax.erf(inner * math.sqrt(0.5)))
    return norm_rows(mixed + times(hidden, down) + down_bias, gain2, shift2)


def gen_seq_of(gen_rows, wave_code, up_size):
    width = gen_rows.shape[0]
    full = jnp.float32
    tokens = gen_rows[:, pl.ds(up_size + 4 * width, width)].astype(full).T
    last = gen_rows[:, pl.ds(gen_rows.shape[1] - width, width)].astype(full).T
    return jnp.concatenate([tokens, wave_code, last[:8]], axis=0)


def gen_parts(gen_rows, gen_down, gen_vec, wave_code, up_size):
    width = gen_rows.shape[0]
    full = jnp.float32
    at = up_size
    up = gen_rows[:, pl.ds(0, up_size)].astype(full)
    qkv = gen_rows[:, pl.ds(at, 3 * width)].astype(full)
    out = gen_rows[:, pl.ds(at + 3 * width, width)].astype(full)
    seq = gen_seq_of(gen_rows, wave_code, up_size)
    vec = [gen_vec[pl.ds(i, 1), pl.ds(0, width)] for i in range(6)]
    up_bias = gen_vec[pl.ds(6, 1), :]
    down = gen_down[...].astype(full)
    return (seq, qkv, out, vec[0], vec[1], vec[2], up, up_bias, down, vec[3], vec[4], vec[5])


def join_lanes(parts, size):
    owners = parts.shape[0]
    shape = (128, owners * size)
    lane = lax.broadcasted_iota(jnp.int32, shape, 0)
    column = lax.broadcasted_iota(jnp.int32, shape, 1)
    spread = dot_nn(parts, (lax.rem(column, size) == lane).astype(parts.dtype))
    shape = (owners, owners * size)
    row = lax.broadcasted_iota(jnp.int32, shape, 0)
    column = lax.broadcasted_iota(jnp.int32, shape, 1)
    return jnp.sum(
        jnp.where(lax.div(column, size) == row, spread, 0.0), axis=0, keepdims=True
    )


def prepare_kernel(planes, sizes, *refs):
    (rows, width, hidden, dec_width, chips, up_size) = sizes
    devices = planes * 8
    (
        s_rows, s_tail, qkv, up, out, dec, down, weight, weight_bias, pixels, waves, visible,
        places, wave_code,
    ) = refs[:14]
    (
        wide_out, down_out, table_out, slots_out, start, gen_rows, gen_down, gen_vec, vecs,
        feature_out, source_out,
    ) = refs[14:25]
    (
        g_rows, g_tail, table, slots, wide, fresh, joined, send, recv, local,
    ) = refs[25:]
    net = Net(planes)
    net.greet()
    wires = Wires(send, recv)
    me = net.chip(0) * 2 + net.c
    low = jnp.bfloat16
    copies = []

    def keep(src, dst):
        copy = pltpu.make_async_copy(src, dst, local.at[len(copies)])
        copy.start()
        copies.append(copy)

    r_size, r_cols = s_rows.shape
    r_cut = (r_cols // 256) * 128 + 128
    r_span = lambda h: pl.ds(r_cut * h, r_cols - r_cut if h else r_cut)
    t_size = s_tail.shape[0]
    t_cut = (t_size // 32) * 16 + 16
    t_span = lambda h: pl.ds(t_cut * h, t_size - t_cut if h else t_cut)
    smalls = [
        Gather(
            net,
            wires,
            lambda h: s_rows.at[:, r_span(h)],
            lambda chip, h: g_rows.at[tile_rows(chip * 2 + net.c, r_size), r_span(h)],
        ),
        Gather(
            net,
            wires,
            lambda h: s_tail.at[t_span(h)],
            lambda chip, h: g_tail.at[chip * 2 + net.c, t_span(h)],
        ),
    ]
    for item in smalls:
        item.begin_z()
        item.spread(0)
    keep(s_rows, g_rows.at[tile_rows(me, r_size)])
    keep(s_tail, g_tail.at[me])

    at = 0
    for item in (qkv, up, out, dec):
        wide[:, pl.ds(at, item.shape[1])] = item[...]
        at += item.shape[1]
    w_cols = at // 2
    quarter = w_cols // 2
    shard = wide.shape[0]
    mine = pl.ds(pl.multiple_of(net.c * w_cols, 128), w_cols)
    theirs = pl.ds(pl.multiple_of((1 - net.c) * w_cols, 128), w_cols)
    pair = wires.push(wide.at[:, theirs], fresh, net.sib)
    d_rows = down.shape[0]
    d_half = d_rows // 2
    d_own = lambda h: down.at[pl.ds(h * d_half, d_half)]
    d_piece = lambda chip, h: down_out.at[
        pl.ds(pl.multiple_of((chip * 2 + net.c) * d_rows + h * d_half, 16), d_half)
    ]
    w_own = lambda h: joined.at[:, pl.ds(h * quarter, quarter)]
    w_piece = lambda chip, h: wide_out.at[
        pl.ds(pl.multiple_of(chip * 2 * shard, 16), 2 * shard),
        pl.ds(pl.multiple_of((net.c * 2 + h) * quarter, 128), quarter),
    ]
    t_lines = table.shape[0] // devices // 2
    t_piece = lambda chip, h: table.at[tile_rows((chip * 2 + net.c) * 2 + h, t_lines)]
    t_own = lambda h: table.at[tile_rows(me * 2 + h, t_lines)]
    d_gather = Gather(net, wires, d_own, d_piece)
    w_gather = Gather(net, wires, w_own, w_piece)
    t_gather = Gather(net, wires, t_own, t_piece)
    d_gather.begin_z()
    for item in smalls:
        item.relay(0)
    pair.wait_recv()
    own32 = wide[:, mine].astype(jnp.float32)
    sib32 = fresh[...].astype(jnp.float32)
    first = net.c == 0
    joined[...] = jnp.concatenate(
        [jnp.where(first, own32, sib32), jnp.where(first, sib32, own32)], axis=0
    ).astype(low)
    for k in range(1, planes):
        for item in smalls:
            item.spread(k)
        for item in smalls:
            item.relay(k)
    w_gather.begin_z()
    for h in range(2):
        keep(w_own(h), w_piece(net.chip(0), h))
        keep(d_own(h), d_piece(net.chip(0), h))
    for k in range(planes):
        for item in smalls:
            item.close(k)
    heavy = [w_gather, d_gather]
    for item in heavy:
        item.spread(0)
    steps = [partial(item.relay, 0) for item in heavy]
    for k in range(1, planes):
        steps += [partial(item.spread, k) for item in heavy]
        steps += [partial(item.relay, k) for item in heavy]
    for k in range(planes):
        steps += [partial(item.close, k) for item in heavy]

    def pump(count):
        for _ in range(min(count, len(steps))):
            steps.pop(0)()

    for item in smalls:
        item.finish()
    for copy in copies[:2]:
        copy.wait()

    lines = width // devices
    small = gen_rows.shape[0] // devices
    groups = r_size // small
    shape = (gen_rows.shape[0], devices * r_size)
    row = lax.broadcasted_iota(jnp.int32, shape, 0)
    column = lax.broadcasted_iota(jnp.int32, shape, 1)
    for q in range(groups):
        source = lax.div(row, small) * r_size + q * small + lax.rem(row, small)
        gen_rows[:, pl.ds(q * r_cols, r_cols)] = dot_nn(
            (column == source).astype(low), g_rows[...]
        ).astype(low)
    gen_down[...] = g_tail[:, pl.ds(0, t_size - 16), :].reshape(gen_down.shape)
    tail = g_tail[:, pl.ds(t_size - 16, 16), :].reshape(devices * 16, 128)
    shape = (devices * 16, devices * 16)
    row = lax.broadcasted_iota(jnp.int32, shape, 0)
    column = lax.broadcasted_iota(jnp.int32, shape, 1)
    source = lax.rem(row, devices) * 16 + lax.div(row, devices)
    tail = dot_nn((column == source).astype(low), tail).astype(low)
    part = lambda i: tail[i * devices : (i + 1) * devices]
    vecs[...] = jnp.zeros_like(vecs)
    for i in range(5):
        vecs[pl.ds(i, 1), pl.ds(0, width)] = join_lanes(part(i), lines)
    vecs[pl.ds(5, 1), :] = join_lanes(part(5), hidden // devices)
    for i in (6, 7):
        vecs[pl.ds(i, 1), pl.ds(0, dec_width)] = join_lanes(part(i), dec_width // devices)
    gen_vec[...] = jnp.zeros_like(gen_vec)
    for i in range(6):
        gen_vec[pl.ds(i, 1), pl.ds(0, gen_rows.shape[0])] = join_lanes(part(8 + i), small)
    gen_vec[pl.ds(6, 1), :] = join_lanes(part(14), up_size // devices)

    pump(2)
    operands = gen_parts(gen_rows, gen_down, gen_vec, wave_code[...], up_size)
    seq = operands[0]
    final = gen_layer(*operands, LAT + NWAVE + 1)
    feature = (final[LAT : LAT + NWAVE] + seq[LAT : LAT + NWAVE]).astype(low)
    feature_out[...] = feature
    source = final[LAT + NWAVE : LAT + NWAVE + 8].astype(low)
    source_out[...] = source
    own = (dot_nn(feature, weight[...]) + weight_bias[...].astype(jnp.float32)).astype(low)
    for h in range(2):
        table[tile_rows(me * 2 + h, t_lines), :] = own[:, h * width : (h + 1) * width]
    t_gather.begin_z()
    t_gather.spread(0)
    pump(2)

    bias_at = gen_rows.shape[1] - gen_rows.shape[0] - width
    conv = dot_nn(source, gen_rows[:, pl.ds(bias_at, width)])[:1]
    t_gather.relay(0)
    grid_lane = lax.broadcasted_iota(jnp.int32, (rows, GRID), 1)
    for i, spot in enumerate((lax.div(visible[...], GRID), lax.rem(visible[...], GRID))):
        half = pl.ds(i * (width // 2), width // 2)
        picked = jnp.dot(
            (spot == grid_lane).astype(jnp.float32),
            places[...],
            precision=HIGH,
            preferred_element_type=jnp.float32,
        )
        start[:, half] = picked + conv[:, i * (width // 2) : (i + 1) * (width // 2)]
    t_gather.spread(1)
    t_gather.relay(1)
    pump(2)
    seen = rows // chips
    span = 256
    bands_pix = pixels.shape[1]
    pix = bands_pix // (waves.shape[1] // (table.shape[0] // NWAVE))

    def slot_block(i, _):
        shape = (span, bands_pix)
        line = lax.broadcasted_iota(jnp.int32, shape, 0) + i * span
        column = lax.broadcasted_iota(jnp.int32, shape, 1)
        count = slots.shape[0] // NWAVE
        same = lax.div(line, NWAVE) == lax.rem(column, count)
        for chip in range(chips):
            wave = waves[pl.ds(chip, 1), :]
            chosen = same & (lax.rem(line, NWAVE) == wave)
            slots[tile_rows(i, span), pl.ds(chip * seen, seen)] = ndot(
                chosen.astype(jnp.float32).astype(low), pixels[pl.ds(chip * seen, seen), :]
            ).astype(low)
        return 0

    blocks = slots.shape[0] // span
    lax.fori_loop(0, blocks // 2, slot_block, 0)
    for k in range(2, planes):
        t_gather.spread(k)
        t_gather.relay(k)
    pump(2)
    lax.fori_loop(blocks // 2, blocks, slot_block, 0)
    keep(slots, slots_out)
    pump(4)
    for k in range(planes):
        t_gather.close(k)
    pump(2)
    t_gather.finish()
    keep(table, table_out)
    wide_span = 512

    def embed(i, _):
        at = tile_rows(i, wide_span)
        start[...] += tdot(slots[at, :], table[at, :])
        return 0

    lax.fori_loop(0, slots.shape[0] // wide_span, embed, 0)
    pump(len(steps))
    for item in heavy:
        item.finish()
    for copy in copies[2:]:
        copy.wait()
    wires.drain()


def prepare(planes, sizes, *args):
    (rows, width, hidden, dec_width, chips, up_size) = sizes
    devices = planes * 8
    low, full = jnp.bfloat16, jnp.float32
    s_rows, s_tail, qkv, up, out, dec, down = args[:7]
    gen_width = args[13].shape[1]
    cols = qkv.shape[1] + up.shape[1] + out.shape[1] + dec.shape[1]
    shard = qkv.shape[0]
    slots = args[7].shape[1] // width * devices * NWAVE
    copies = 5 * gather_copies(planes) + 1
    shapes = (
        ((width, cols), low),
        ((hidden, width), low),
        ((slots, width), low),
        ((slots, rows), low),
        ((rows, width), full),
        ((gen_width, s_rows.shape[1] * s_rows.shape[0] * devices // gen_width), low),
        ((up_size, gen_width), low),
        ((8, up_size), full),
        ((8, hidden), full),
        ((NWAVE, gen_width), low),
        ((8, gen_width), low),
    )
    return pl.pallas_call(
        partial(prepare_kernel, planes, sizes),
        out_shape=tuple(jax.ShapeDtypeStruct(shape, dtype) for shape, dtype in shapes),
        in_specs=[VMEM] * 14,
        out_specs=[ANY] * 4 + [VMEM] * 7,
        scratch_shapes=[
            pltpu.VMEM((devices * s_rows.shape[0], s_rows.shape[1]), low),
            pltpu.VMEM((devices,) + s_tail.shape, low),
            pltpu.VMEM((slots, width), low),
            pltpu.VMEM((slots, rows), low),
            pltpu.VMEM((shard, cols), low),
            pltpu.VMEM((shard, cols // 2), low),
            pltpu.VMEM((2 * shard, cols // 2), low),
            pltpu.SemaphoreType.DMA((copies,)),
            pltpu.SemaphoreType.DMA((copies,)),
            pltpu.SemaphoreType.DMA((8,)),
        ],
        compiler_params=pltpu.CompilerParams(
            collective_id=0, has_side_effects=True, vmem_limit_bytes=60 * 2**20
        ),
    )(*args)


def forward_kernel(sizes, *refs):
    (rows, width, hidden, dec_width, chips, patches) = sizes
    (start, wide, down, vecs, visible, order) = refs[:6]
    (
        ordered, normed_out, joint_out, probs_out, context_out, middle_out, normed2_out,
        activ_out, slope_out, ending_out,
    ) = refs[6:16]
    (
        w_qkv, w_out, w_up, w_down, w_dec, normed, joint, probs, context, middle, normed2,
        activ, slope, ending, total, load_sem, keep_sem,
    ) = refs[16:]
    low = jnp.bfloat16
    seen = rows // chips
    loads, kept = [], []
    spans = ((0, 3 * width), (3 * width + hidden, width), (3 * width, hidden))
    spans += ((4 * width + hidden, dec_width),)
    for (at, size), dst in zip(spans, (w_qkv, w_out, w_up, w_dec)):
        loads.append((wide.at[:, pl.ds(at, size)], dst))
    loads.append((down, w_down))
    loads = [
        pltpu.make_async_copy(src, dst, load_sem.at[i]) for i, (src, dst) in enumerate(loads)
    ]
    for copy in loads:
        copy.start()

    def keep(src, dst):
        copy = pltpu.make_async_copy(src, dst, keep_sem.at[len(kept)])
        copy.start()
        kept.append(copy)

    def norm_into(src, dst, row):
        gain = vecs[pl.ds(row, 1), pl.ds(0, width)]
        shift = vecs[pl.ds(row + 1, 1), pl.ds(0, width)]

        def block(i, _):
            at = tile_rows(i, BLOCK)
            dst[at, :] = norm_rows(src[at, :], gain, shift).astype(low)
            return 0

        lax.fori_loop(0, rows // BLOCK, block, 0)

    norm_into(start, normed, 0)
    keep(normed, normed_out)
    loads[0].wait()

    def project(i, _):
        lane = pl.ds(pl.multiple_of(i * width, 128), width)
        joint[:, lane] = dot_nn(normed[...], w_qkv[:, lane]).astype(low)
        return 0

    lax.fori_loop(0, 3, project, 0)
    keep(joint, joint_out)
    pairs = width // 128
    head = width // HEADS
    scale = 1.0 / math.sqrt(head)
    odd = lax.broadcasted_iota(jnp.int32, (1, 128), 1) >= head

    def attend(n, _):
        at = tile_rows(lax.div(n, pairs), seen)
        pair = lax.rem(n, pairs)
        query, key, value = [
            joint[at, pl.ds(pl.multiple_of(pair * 128 + i * width, 128), 128)] for i in range(3)
        ]
        zero = jnp.zeros_like(query)
        parts = []
        for h in range(2):
            mine = odd if h else jnp.logical_not(odd)
            scores = ndot(jnp.where(mine, query, zero), key) * scale
            raised = jnp.exp(scores - jnp.max(scores, axis=-1, keepdims=True))
            prob = (raised / jnp.sum(raised, axis=-1, keepdims=True)).astype(low)
            probs[2 * n + h] = prob
            parts.append(dot_nn(prob, value))
        lane = pl.ds(pl.multiple_of(pair * 128, 128), 128)
        context[at, lane] = jnp.where(odd, parts[1], parts[0]).astype(low)
        return 0

    lax.fori_loop(0, chips * pairs, attend, 0)
    keep(probs, probs_out)
    keep(context, context_out)
    loads[1].wait()
    middle[...] = start[...] + dot_nn(context[...], w_out[...])
    keep(middle, middle_out)
    norm_into(middle, normed2, 2)
    keep(normed2, normed2_out)
    total[...] = middle[...] + vecs[pl.ds(4, 1), pl.ds(0, width)]
    loads[2].wait()
    loads[4].wait()

    def feed(t, _):
        at = tile_rows(t, FT)
        upper = dot_nn(normed2[...], w_up[:, at]) + vecs[pl.ds(5, 1), at]
        bell = 0.5 * (1.0 + lax.erf(upper * math.sqrt(0.5)))
        active = (upper * bell).astype(low)
        activ[:, at] = active
        tilt = upper * jnp.exp(-0.5 * upper * upper) * (1.0 / math.sqrt(2.0 * math.pi))
        slope[:, at] = (bell + tilt).astype(low)
        total[...] += dot_nn(active, w_down[at, :])
        return 0

    lax.fori_loop(0, hidden // FT, feed, 0)
    keep(activ, activ_out)
    keep(slope, slope_out)
    ending[...] = total[...].astype(low)
    keep(ending, ending_out)
    loads[3].wait()
    decoded = dot_nn(ending[...], w_dec[...]) + vecs[pl.ds(6, 1), pl.ds(0, dec_width)]
    total[:, pl.ds(0, dec_width)] = decoded
    mask = vecs[pl.ds(7, 1), pl.ds(0, dec_width)]
    blocks, _, lines, _ = ordered.shape
    for chip in range(chips):
        at = pl.ds(chip * seen, seen)
        chosen = (order[...] == visible[pl.ds(chip, 1), :]).astype(jnp.float32)
        found = jnp.sum(chosen, axis=1, keepdims=True) > 0.0
        placed = dot_nn(chosen.astype(low), total[at, pl.ds(0, dec_width)].astype(low))
        placed = jnp.where(found, placed, mask).astype(low)
        ordered[:, chip] = placed.reshape(blocks, lines, dec_width)
    for copy in kept:
        copy.wait()


def forward(sizes, devices, *args):
    (rows, width, hidden, dec_width, chips, patches) = sizes
    low, full = jnp.bfloat16, jnp.float32
    seen = rows // chips
    heads = chips * HEADS
    shapes = (
        ((devices, chips, patches // devices, dec_width), low),
        ((rows, width), low),
        ((rows, 3 * width), low),
        ((heads, seen, seen), low),
        ((rows, width), low),
        ((rows, width), full),
        ((rows, width), low),
        ((rows, hidden), low),
        ((rows, hidden), low),
        ((rows, width), low),
    )
    return pl.pallas_call(
        partial(forward_kernel, sizes),
        out_shape=tuple(jax.ShapeDtypeStruct(shape, dtype) for shape, dtype in shapes),
        in_specs=[VMEM, ANY, ANY] + [VMEM] * 3,
        out_specs=[VMEM] + [ANY] * 9,
        scratch_shapes=[
            pltpu.VMEM((width, 3 * width), low),
            pltpu.VMEM((width, width), low),
            pltpu.VMEM((width, hidden), low),
            pltpu.VMEM((hidden, width), low),
            pltpu.VMEM((width, dec_width), low),
        ]
        + [pltpu.VMEM(shape, dtype) for shape, dtype in shapes[1:]]
        + [
            pltpu.VMEM((rows, width), full),
            pltpu.SemaphoreType.DMA((5,)),
            pltpu.SemaphoreType.DMA((9,)),
        ],
        compiler_params=pltpu.CompilerParams(
            has_side_effects=True, vmem_limit_bytes=60 * 2**20
        ),
    )(*args)


def gen_back(
    gen_rows, gen_down, gen_vec, wave_code, length, grad_feature, grad_source, sums, put_up, put_down
):
    up_size, width = gen_down.shape
    size = width // GHEADS
    scale = 1.0 / math.sqrt(size)
    total = lambda value: jnp.sum(value, axis=0, keepdims=True)
    chunk = up_size // 4

    def dot(left, right, dims):
        return lax.dot_general(
            left.astype(jnp.bfloat16),
            right.astype(jnp.bfloat16),
            (dims, ((), ())),
            preferred_element_type=jnp.float32,
        )

    nn = lambda left, right: dot(left, right, ((1,), (0,)))
    nt = lambda left, right: dot(left, right, ((1,), (1,)))
    tn = lambda left, right: dot(left, right, ((0,), (0,)))
    seq = gen_seq_of(gen_rows, wave_code, up_size)
    full = jnp.float32
    qkv = gen_rows[:, pl.ds(up_size, 3 * width)].astype(full)
    out = gen_rows[:, pl.ds(up_size + 3 * width, width)].astype(full)
    out_bias, gain1, shift1, down_bias, gain2, _ = [
        gen_vec[pl.ds(i, 1), pl.ds(0, width)] for i in range(6)
    ]
    joint = nn(seq, qkv)
    query, key, value = [joint[:, i * width : (i + 1) * width] for i in range(3)]
    lane = lax.broadcasted_iota(jnp.int32, (1, width), 1)
    spot = lax.broadcasted_iota(jnp.int32, (1, seq.shape[0]), 1)
    masks = [(lax.div(lane, size) == h).astype(full) for h in range(GHEADS)]
    probs = []
    context = jnp.zeros_like(seq)
    for mine in masks:
        scores = jnp.where(spot < length, nt(query * mine, key) * scale, -1e30)
        raised = jnp.exp(scores - jnp.max(scores, axis=-1, keepdims=True))
        probs.append(raised / jnp.sum(raised, axis=-1, keepdims=True))
        context = context + nn(probs[-1], value * mine)
    first = seq + nn(context, out) + out_bias
    mixed = norm_rows(first, gain1, shift1)

    def piece(i):
        at = pl.ds(pl.multiple_of(i * chunk, chunk), chunk)
        up = gen_rows[:, at].astype(full)
        down = gen_down[at, :].astype(full)
        inner = nn(mixed, up) + gen_vec[pl.ds(6, 1), at]
        return up, down, inner, 0.5 * (1.0 + lax.erf(inner * math.sqrt(0.5)))

    def ahead(i, so_far):
        _, down, inner, bell = piece(i)
        return so_far + nn(inner * bell, down)

    second = lax.fori_loop(0, 4, ahead, mixed + down_bias)
    rest = seq.shape[0] - LAT - NWAVE
    zeros = jnp.zeros((LAT, width), full)
    grad = jnp.concatenate([zeros, grad_feature, grad_source], axis=0)
    through, terms = norm_back(grad, second, gain2)
    g_gain2, g_shift2, g_down_bias = total(terms), total(grad), total(through)

    def behind(i, so_far):
        up, down, inner, bell = piece(i)
        put_down(i, tn(inner * bell, through))
        slope = bell + inner * jnp.exp(-0.5 * inner * inner) * (1.0 / math.sqrt(2.0 * math.pi))
        g_inner = nt(through, down) * slope
        put_up(i, tn(mixed, g_inner))
        sums[pl.ds(6, 1), pl.ds(pl.multiple_of(i * chunk, chunk), chunk)] = total(g_inner)
        return so_far + nt(g_inner, up)

    g_mixed = lax.fori_loop(0, 4, behind, through)
    through, terms = norm_back(g_mixed, first, gain1)
    g_gain1, g_shift1, g_out_bias = total(terms), total(g_mixed), total(through)
    g_out = tn(context, through)
    g_context = nt(through, out)
    g_query = g_key = g_value = jnp.zeros_like(seq)
    for mine, prob in zip(masks, probs):
        g_head = g_context * mine
        g_prob = nt(g_head, value)
        g_value = g_value + tn(prob, g_head)
        g_score = prob * (g_prob - jnp.sum(prob * g_prob, axis=-1, keepdims=True)) * scale
        g_query = g_query + nn(g_score, key * mine)
        g_key = g_key + tn(g_score, query * mine)
    g_joint = jnp.concatenate([g_query, g_key, g_value], axis=1)
    direct = jnp.concatenate([zeros, grad_feature, jnp.zeros((rest, width), full)], axis=0)
    g_seq = through + nt(g_joint, qkv) + direct
    thin = (g_out_bias, g_gain1, g_shift1, g_down_bias, g_gain2, g_shift2)
    return g_seq, tn(seq, g_joint), g_out, thin


def on_device_plain(
    pixels,
    sensor,
    band_wave,
    visible,
    block_order,
    pre_gain,
    pre_shift,
    qkv_weight,
    out_weight,
    mid_gain,
    mid_shift,
    up_weight,
    up_bias,
    down_weight,
    down_bias,
    dec_weight,
    dec_bias,
    mask_token,
    gen_tokens,
    gen_qkv,
    gen_out,
    gen_out_bias,
    gen_gain1,
    gen_shift1,
    gen_up,
    gen_up_bias,
    gen_down,
    gen_down_bias,
    gen_gain2,
    gen_shift2,
    kernel_weight,
    kernel_bias,
    bias_weight,
    cotangent,
):
    fetched = (
        lax.all_gather(pre_gain, AXES, axis=0, tiled=True),
        lax.all_gather(pre_shift, AXES, axis=0, tiled=True),
        lax.all_gather(qkv_weight, AXES, axis=0, tiled=True),
        lax.all_gather(out_weight, AXES, axis=0, tiled=True),
        lax.all_gather(mid_gain, AXES, axis=0, tiled=True),
        lax.all_gather(mid_shift, AXES, axis=0, tiled=True),
        lax.all_gather(up_weight, AXES, axis=0, tiled=True),
        lax.all_gather(up_bias, AXES, axis=0, tiled=True),
        lax.all_gather(down_weight, AXES, axis=0, tiled=True),
        lax.all_gather(down_bias, AXES, axis=0, tiled=True),
        lax.all_gather(dec_weight, AXES, axis=0, tiled=True),
        lax.all_gather(dec_bias, AXES, axis=0, tiled=True),
        lax.all_gather(mask_token, AXES, axis=0, tiled=True),
        lax.all_gather(gen_tokens, AXES, axis=1, tiled=True),
        lax.all_gather(gen_qkv, AXES, axis=0, tiled=True),
        lax.all_gather(gen_out, AXES, axis=0, tiled=True),
        lax.all_gather(gen_out_bias, AXES, axis=0, tiled=True),
        lax.all_gather(gen_gain1, AXES, axis=0, tiled=True),
        lax.all_gather(gen_shift1, AXES, axis=0, tiled=True),
        lax.all_gather(gen_up, AXES, axis=0, tiled=True),
        lax.all_gather(gen_up_bias, AXES, axis=0, tiled=True),
        lax.all_gather(gen_down, AXES, axis=0, tiled=True),
        lax.all_gather(gen_down_bias, AXES, axis=0, tiled=True),
        lax.all_gather(gen_gain2, AXES, axis=0, tiled=True),
        lax.all_gather(gen_shift2, AXES, axis=0, tiled=True),
        lax.all_gather(kernel_weight, AXES, axis=1, tiled=True),
        lax.all_gather(kernel_bias, AXES, axis=0, tiled=True),
        lax.all_gather(bias_weight, AXES, axis=0, tiled=True),
    )
    full_kernel = fetched[25]
    full_kernel_bias = fetched[26]
    full_bias_weight = fetched[27]
    (
        full_pre_gain,
        full_pre_shift,
        full_qkv,
        full_out,
        full_mid_gain,
        full_mid_shift,
        full_up,
        full_up_bias,
        full_down,
        full_down_bias,
        full_dec,
        full_dec_bias,
        full_mask,
    ) = fetched[:13]
    core32 = tuple((item.astype(jnp.float32) for item in fetched[13:25]))
    chips, seen, bands, pix = pixels.shape
    width = full_qkv.shape[0]
    head_dim = width // HEADS
    scale = 1.0 / math.sqrt(head_dim)
    dec_width = full_dec.shape[1]
    rows = chips * seen
    wave_code = lax.optimization_barrier(
        sincos(jnp.arange(NWAVE, dtype=jnp.float32), WD // 2).astype(jnp.bfloat16)
    ).astype(jnp.float32)
    (feature, source), core_back = jax.vjp(partial(gen_core, wave_code), *core32)
    feature_low = feature.astype(jnp.bfloat16)
    source_low = source.astype(jnp.bfloat16)
    conv_bias = jnp.dot(source_low[None, :], full_bias_weight, preferred_element_type=jnp.float32)[
        0
    ]
    kernels = (
        jnp.dot(feature_low, full_kernel, preferred_element_type=jnp.float32)
        + full_kernel_bias.astype(jnp.float32)[None, :]
    ).astype(jnp.bfloat16)
    valid = band_valid(sensor, bands)
    onehot = (band_wave[:, :, None] == jnp.arange(NWAVE, dtype=jnp.int32)[None, None, :]).astype(
        jnp.float32
    )
    place = place_code(visible, width)
    band_kernels = jnp.einsum(
        "cbw,wk->cbk", onehot.astype(jnp.bfloat16), kernels, preferred_element_type=jnp.float32
    ).astype(jnp.bfloat16)
    band_kernels = band_kernels.reshape(chips, bands, pix, width)
    masked = pixels * valid.astype(jnp.bfloat16)[:, None, :, None]
    embedded = jnp.einsum(
        "cvbp,cbpd->cvd", masked, band_kernels, preferred_element_type=jnp.float32
    )
    start = (embedded + conv_bias + place).reshape(rows, width)
    pre_gain32 = full_pre_gain.astype(jnp.float32)
    pre_shift32 = full_pre_shift.astype(jnp.float32)
    normed = norm_rows(start, pre_gain32, pre_shift32).astype(jnp.bfloat16)
    joint = jnp.dot(normed, full_qkv, preferred_element_type=jnp.float32).astype(jnp.bfloat16)
    joint = joint.reshape(chips, seen, 3, HEADS, head_dim)
    queries = joint[:, :, 0]
    keys = joint[:, :, 1]
    values = joint[:, :, 2]
    scores = (
        jnp.einsum("cqhe,ckhe->chqk", queries, keys, preferred_element_type=jnp.float32) * scale
    )
    peak = jnp.max(scores, axis=-1, keepdims=True)
    expd = jnp.exp(scores - peak)
    total = jnp.sum(expd, axis=-1, keepdims=True)
    probs = (expd / total).astype(jnp.bfloat16)
    log_total = peak + jnp.log(total)
    context = jnp.einsum("chqk,ckhe->cqhe", probs, values, preferred_element_type=jnp.float32)
    context = context.astype(jnp.bfloat16).reshape(rows, width)
    attended = jnp.dot(context, full_out, preferred_element_type=jnp.float32)
    middle = start + attended
    mid_gain32 = full_mid_gain.astype(jnp.float32)
    mid_shift32 = full_mid_shift.astype(jnp.float32)
    normed2 = norm_rows(middle, mid_gain32, mid_shift32).astype(jnp.bfloat16)
    upper = jnp.dot(normed2, full_up, preferred_element_type=jnp.float32) + full_up_bias.astype(
        jnp.float32
    )
    activ = exact_gelu(upper).astype(jnp.bfloat16)
    branch = jnp.dot(activ, full_down, preferred_element_type=jnp.float32) + full_down_bias.astype(
        jnp.float32
    )
    ending = (middle + branch).astype(jnp.bfloat16)
    decoded = jnp.dot(ending, full_dec, preferred_element_type=jnp.float32) + full_dec_bias.astype(
        jnp.float32
    )
    decoded = decoded.astype(jnp.bfloat16).reshape(chips, seen, dec_width)
    chip_ids = jnp.arange(chips, dtype=jnp.int32)[:, None]
    canvas = jnp.broadcast_to(full_mask, (chips, PATCH, dec_width))
    canvas = canvas.at[chip_ids, visible].set(decoded)
    ordered = jnp.take(canvas, block_order, axis=1)
    decoder_in = lax.all_to_all(ordered, AXES, split_axis=1, concat_axis=0, tiled=True)
    returned = lax.all_to_all(cotangent, AXES, split_axis=0, concat_axis=1, tiled=True)
    (
        full_pre_gain,
        full_pre_shift,
        full_qkv,
        full_out,
        full_mid_gain,
        full_mid_shift,
        full_up,
        full_up_bias,
        full_down,
        full_down_bias,
        full_dec,
        full_dec_bias,
        full_mask,
    ) = (
        lax.all_gather(pre_gain, AXES, axis=0, tiled=True),
        lax.all_gather(pre_shift, AXES, axis=0, tiled=True),
        lax.all_gather(qkv_weight, AXES, axis=0, tiled=True),
        lax.all_gather(out_weight, AXES, axis=0, tiled=True),
        lax.all_gather(mid_gain, AXES, axis=0, tiled=True),
        lax.all_gather(mid_shift, AXES, axis=0, tiled=True),
        lax.all_gather(up_weight, AXES, axis=0, tiled=True),
        lax.all_gather(up_bias, AXES, axis=0, tiled=True),
        lax.all_gather(down_weight, AXES, axis=0, tiled=True),
        lax.all_gather(down_bias, AXES, axis=0, tiled=True),
        lax.all_gather(dec_weight, AXES, axis=0, tiled=True),
        lax.all_gather(dec_bias, AXES, axis=0, tiled=True),
        lax.all_gather(mask_token, AXES, axis=0, tiled=True),
    )
    restored = jnp.zeros_like(returned).at[:, block_order].set(returned)
    seen_grad = jnp.take_along_axis(restored, visible[:, :, None], axis=1)
    grad_mask = jnp.sum(restored.astype(jnp.float32), axis=(0, 1)) - jnp.sum(
        seen_grad.astype(jnp.float32), axis=(0, 1)
    )
    grad_rows = seen_grad.reshape(rows, dec_width)
    grad_dec_weight = tdot(ending, grad_rows)
    grad_dec_bias = jnp.sum(grad_rows.astype(jnp.float32), axis=0)
    grad_ending = ndot(grad_rows, full_dec)
    grad_branch = grad_ending.astype(jnp.bfloat16)
    grad_down_bias = jnp.sum(grad_branch.astype(jnp.float32), axis=0)
    grad_down_weight = tdot(activ, grad_branch)
    grad_activ = ndot(grad_branch, full_down)
    gelu_out, gelu_back = jax.vjp(exact_gelu, upper)
    grad_upper = gelu_back(grad_activ)[0].astype(jnp.bfloat16)
    grad_up_bias = jnp.sum(grad_upper.astype(jnp.float32), axis=0)
    grad_up_weight = tdot(normed2, grad_upper)
    grad_normed2 = ndot(grad_upper, full_up)
    norm_out, norm_back = jax.vjp(norm_rows, middle, mid_gain32, mid_shift32)
    through_mid, grad_mid_gain, grad_mid_shift = norm_back(grad_normed2)
    grad_middle = grad_ending + through_mid
    grad_attended = grad_middle.astype(jnp.bfloat16)
    grad_out_weight = tdot(context, grad_attended)
    grad_context = (
        ndot(grad_attended, full_out).astype(jnp.bfloat16).reshape(chips, seen, HEADS, head_dim)
    )
    again_scores = (
        jnp.einsum("cqhe,ckhe->chqk", queries, keys, preferred_element_type=jnp.float32) * scale
    )
    probs_full = jnp.exp(again_scores - log_total)
    probs_low = probs_full.astype(jnp.bfloat16)
    grad_values = jnp.einsum(
        "chqk,cqhe->ckhe", probs_low, grad_context, preferred_element_type=jnp.float32
    ).astype(jnp.bfloat16)
    grad_probs = jnp.einsum(
        "cqhe,ckhe->chqk", grad_context, values, preferred_element_type=jnp.float32
    )
    row_dot = jnp.sum(probs_full * grad_probs, axis=-1, keepdims=True)
    grad_scores = (probs_full * (grad_probs - row_dot)).astype(jnp.bfloat16)
    grad_queries = (
        jnp.einsum("chqk,ckhe->cqhe", grad_scores, keys, preferred_element_type=jnp.float32) * scale
    ).astype(jnp.bfloat16)
    grad_keys = (
        jnp.einsum("chqk,cqhe->ckhe", grad_scores, queries, preferred_element_type=jnp.float32)
        * scale
    ).astype(jnp.bfloat16)
    grad_joint = jnp.stack([grad_queries, grad_keys, grad_values], axis=2).reshape(rows, 3 * width)
    grad_qkv_weight = tdot(normed, grad_joint)
    grad_normed = ndot(grad_joint, full_qkv)
    first_out, first_back = jax.vjp(norm_rows, start, pre_gain32, pre_shift32)
    through_pre, grad_pre_gain, grad_pre_shift = first_back(grad_normed)
    grad_start = grad_middle + through_pre
    grad_conv_part = jnp.sum(grad_start, axis=0)
    grad_embedded = grad_start.astype(jnp.bfloat16).reshape(chips, seen, width)
    grad_band = jnp.einsum(
        "cvbp,cvd->cbpd", masked, grad_embedded, preferred_element_type=jnp.float32
    )
    grad_band = grad_band.reshape(chips, bands, pix * width)
    grad_pixels = jnp.einsum(
        "cvd,cbpd->cvbp", grad_embedded, band_kernels, preferred_element_type=jnp.float32
    )
    grad_pixels = grad_pixels * valid[:, None, :, None]
    grad_kernels_part = jnp.einsum("cbw,cbk->wk", onehot, grad_band, precision=HIGH)
    kernel_sum, grad_conv = lax.psum((grad_kernels_part, grad_conv_part), AXES)
    kernel_low = kernel_sum.astype(jnp.bfloat16)
    own_low = own_part(kernel_low, 1)
    grad_kernel_weight = tdot(feature_low, own_low)
    grad_kernel_bias = jnp.sum(own_low.astype(jnp.float32), axis=0)
    grad_feature = ndot(kernel_low, full_kernel)
    grad_bias_weight = own_part(source_low.astype(jnp.float32)[:, None] * grad_conv[None, :], 0)
    grad_source = jnp.dot(full_bias_weight.astype(jnp.float32), grad_conv, precision=HIGH)
    core_grads = core_back((grad_feature, grad_source))
    summed = (
        lax.psum_scatter(grad_pre_gain, AXES, scatter_dimension=0, tiled=True),
        lax.psum_scatter(grad_pre_shift, AXES, scatter_dimension=0, tiled=True),
        lax.psum_scatter(grad_qkv_weight, AXES, scatter_dimension=0, tiled=True),
        lax.psum_scatter(grad_out_weight, AXES, scatter_dimension=0, tiled=True),
        lax.psum_scatter(grad_mid_gain, AXES, scatter_dimension=0, tiled=True),
        lax.psum_scatter(grad_mid_shift, AXES, scatter_dimension=0, tiled=True),
        lax.psum_scatter(grad_up_weight, AXES, scatter_dimension=0, tiled=True),
        lax.psum_scatter(grad_up_bias, AXES, scatter_dimension=0, tiled=True),
        lax.psum_scatter(grad_down_weight, AXES, scatter_dimension=0, tiled=True),
        lax.psum_scatter(grad_down_bias, AXES, scatter_dimension=0, tiled=True),
        lax.psum_scatter(grad_dec_weight, AXES, scatter_dimension=0, tiled=True),
        lax.psum_scatter(grad_dec_bias, AXES, scatter_dimension=0, tiled=True),
        lax.psum_scatter(grad_mask, AXES, scatter_dimension=0, tiled=True),
    )
    return (
        decoder_in,
        grad_pixels,
        summed[0],
        summed[1],
        summed[2],
        summed[3],
        summed[4],
        summed[5],
        summed[6],
        summed[7],
        summed[8],
        summed[9],
        summed[10],
        summed[11],
        summed[12],
        own_part(core_grads[0], 1),
        own_part(core_grads[1], 0),
        own_part(core_grads[2], 0),
        own_part(core_grads[3], 0),
        own_part(core_grads[4], 0),
        own_part(core_grads[5], 0),
        own_part(core_grads[6], 0),
        own_part(core_grads[7], 0),
        own_part(core_grads[8], 0),
        own_part(core_grads[9], 0),
        own_part(core_grads[10], 0),
        own_part(core_grads[11], 0),
        grad_kernel_weight,
        grad_kernel_bias,
        grad_bias_weight,
    )


def on_device(
    pixels,
    sensor,
    band_wave,
    visible,
    block_order,
    pre_gain,
    pre_shift,
    qkv_weight,
    out_weight,
    mid_gain,
    mid_shift,
    up_weight,
    up_bias,
    down_weight,
    down_bias,
    dec_weight,
    dec_bias,
    mask_token,
    gen_tokens,
    gen_qkv,
    gen_out,
    gen_out_bias,
    gen_gain1,
    gen_shift1,
    gen_up,
    gen_up_bias,
    gen_down,
    gen_down_bias,
    gen_gain2,
    gen_shift2,
    kernel_weight,
    kernel_bias,
    bias_weight,
    cotangent,
):
    arguments = (
        pixels,
        sensor,
        band_wave,
        visible,
        block_order,
        pre_gain,
        pre_shift,
        qkv_weight,
        out_weight,
        mid_gain,
        mid_shift,
        up_weight,
        up_bias,
        down_weight,
        down_bias,
        dec_weight,
        dec_bias,
        mask_token,
        gen_tokens,
        gen_qkv,
        gen_out,
        gen_out_bias,
        gen_gain1,
        gen_shift1,
        gen_up,
        gen_up_bias,
        gen_down,
        gen_down_bias,
        gen_gain2,
        gen_shift2,
        kernel_weight,
        kernel_bias,
        bias_weight,
        cotangent,
    )
    planes = lax.axis_size("dp") // 2
    devices = planes * 8
    if lax.axis_size("fsdp") != 4 or planes & (planes - 1) or pre_gain.shape[0] % 8:
        return on_device_plain(*arguments)
    low = jnp.bfloat16
    chips, seen, bands, pix = pixels.shape
    width = qkv_weight.shape[0] * devices
    hidden_width = up_weight.shape[1]
    head_dim = width // HEADS
    scale = 1.0 / math.sqrt(head_dim)
    dec_width = dec_weight.shape[1]
    rows = chips * seen
    gen_width = gen_qkv.shape[0] * devices
    up_size = gen_up.shape[1]
    tokens = jnp.pad(gen_tokens.T, ((0, 0), (0, gen_width - 1)))
    small = jnp.concatenate(
        [gen_up, gen_qkv, gen_out, tokens[:, :gen_width], bias_weight, tokens[:, gen_width:]],
        axis=1,
    )
    groups = 16 // small.shape[0]
    small = small.reshape(small.shape[0], groups, -1)
    small = jnp.swapaxes(small, 0, 1).reshape(16, -1)
    vectors = (
        pre_gain, pre_shift, mid_gain, mid_shift, down_bias, up_bias, dec_bias, mask_token,
        gen_out_bias, gen_gain1, gen_shift1, gen_down_bias, gen_gain2, gen_shift2, gen_up_bias,
        jnp.zeros_like(gen_gain1),
    )
    vectors = jnp.stack([jnp.pad(item, (0, 128 - item.shape[0])) for item in vectors])
    tail = jnp.concatenate([gen_down, vectors], axis=0)
    wave_code = lax.optimization_barrier(
        sincos(jnp.arange(NWAVE, dtype=jnp.float32), gen_width // 2).astype(low)
    ).astype(jnp.float32)
    valid = band_valid(sensor, bands)
    wave_rows = jnp.repeat(jnp.where(valid > 0, band_wave, -1), pix, axis=1)
    (
        full_wide, full_down, kernels, slots, start, gen_rows, gen_down_full, gen_vec, vecs,
        feature_low, source_low,
    ) = prepare(
        planes,
        (rows, width, hidden_width, dec_width, chips, up_size),
        small,
        tail,
        qkv_weight,
        up_weight,
        out_weight,
        dec_weight,
        down_weight,
        kernel_weight,
        kernel_bias.reshape(1, -1),
        pixels.reshape(rows, bands * pix),
        wave_rows,
        visible.reshape(rows, 1),
        sincos(jnp.arange(GRID, dtype=jnp.float32), width // 4),
        wave_code,
    )
    full_wide, cotangent = lax.optimization_barrier((full_wide, cotangent))
    onehot = (band_wave[:, :, None] == jnp.arange(NWAVE, dtype=jnp.int32)[None, None, :]).astype(
        low
    )
    band_kernels = jnp.einsum(
        "cbw,pwd->cbpd",
        onehot,
        kernels.reshape(pix, NWAVE, width),
        preferred_element_type=jnp.float32,
    ).astype(low)
    sizes = (rows, width, hidden_width, dec_width, chips, PATCH)
    (
        ordered, normed, joint, probs, context, middle, normed2, activ, slope, ending,
    ) = forward(
        sizes,
        devices,
        start,
        full_wide,
        full_down,
        vecs,
        visible,
        block_order.reshape(PATCH, 1),
    )
    share = PATCH // devices
    trade = partial(lax.all_to_all, axis_name=AXES, split_axis=0, concat_axis=0, tiled=True)
    decoder_in = trade(ordered).reshape(devices * chips, share, dec_width)
    returned = trade(cotangent.reshape(devices, chips, share, dec_width))
    spot = jnp.arange(chips, dtype=jnp.int32) * PATCH
    wide_order = block_order.reshape(devices, 1, share) + spot[None, :, None]
    (
        sum_dec, sum_up, sum_oq, sum_down, grad_kernel_weight, grad_kernel_bias, sum_all,
        gen_wide, gen_tall, gen_seq, gen_lines, grad_bias_weight, grad_embedded,
    ) = backward(
        planes,
        sizes,
        returned.reshape(chips * PATCH, dec_width),
        (visible + spot[:, None]).reshape(rows, 1),
        wide_order.reshape(1, chips * PATCH),
        ending,
        full_wide,
        full_down,
        activ,
        slope,
        normed2,
        middle,
        context,
        joint,
        probs,
        normed,
        start,
        slots,
        vecs,
        kernel_weight,
        feature_low,
        source_low,
        gen_rows,
        gen_down_full,
        gen_vec,
        wave_code,
    )
    grad_embedded = grad_embedded.reshape(chips, seen, width)
    grad_pixels = jnp.einsum(
        "cvd,cbpd->cvbp", grad_embedded, band_kernels, preferred_element_type=jnp.float32
    )
    grad_pixels = grad_pixels * valid[:, None, :, None]
    small = gen_qkv.shape[0]
    gen_at = (0, up_size, up_size + 3 * gen_width, up_size + 4 * gen_width)
    gen_cut = lambda i: gen_wide[:small, gen_at[i] : gen_at[i + 1]]
    grad_tokens = jnp.concatenate(
        [gen_seq[:LAT, :small], gen_seq[LAT + NWAVE : LAT + NWAVE + 1, :small]], axis=0
    )
    gen_line = lambda i: own_part(gen_lines[i, :gen_width], 0)
    flat = sum_all[NWAVE + width // 128 :].reshape(-1)
    vec = []
    at = 0
    for size in (width,) * 5 + (hidden_width, dec_width, dec_width):
        vec.append(own_part(flat[at : at + size], 0))
        at += size
    summed = (
        vec[0], vec[1], sum_oq[:, width:], sum_oq[:, :width], vec[2], vec[3], sum_up, vec[5],
        sum_down, vec[4], sum_dec, vec[6], vec[7],
    )
    return (
        decoder_in,
        grad_pixels,
        summed[0],
        summed[1],
        summed[2],
        summed[3],
        summed[4],
        summed[5],
        summed[6],
        summed[7],
        summed[8],
        summed[9],
        summed[10],
        summed[11],
        summed[12],
        grad_tokens,
        gen_cut(1),
        gen_cut(2),
        gen_line(0),
        gen_line(1),
        gen_line(2),
        gen_cut(0),
        own_part(gen_lines[6], 0),
        gen_tall,
        gen_line(3),
        gen_line(4),
        gen_line(5),
        grad_kernel_weight,
        grad_kernel_bias.reshape(-1),
        grad_bias_weight[:small],
    )


def solution(mesh):
    in_specs = (
        P(AXES, None, None, None),
        P(AXES),
        P(AXES, None),
        P(AXES, None),
        P(),
        P(AXES),
        P(AXES),
        P(AXES, None),
        P(AXES, None),
        P(AXES),
        P(AXES),
        P(AXES, None),
        P(AXES),
        P(AXES, None),
        P(AXES),
        P(AXES, None),
        P(AXES),
        P(AXES),
        P(None, AXES),
        P(AXES, None),
        P(AXES, None),
        P(AXES),
        P(AXES),
        P(AXES),
        P(AXES, None),
        P(AXES),
        P(AXES, None),
        P(AXES),
        P(AXES),
        P(AXES),
        P(None, AXES),
        P(AXES),
        P(AXES, None),
        P(None, AXES, None),
    )
    out_specs = (
        P(None, AXES, None),
        P(AXES, None, None, None),
        P(AXES),
        P(AXES),
        P(AXES, None),
        P(AXES, None),
        P(AXES),
        P(AXES),
        P(AXES, None),
        P(AXES),
        P(AXES, None),
        P(AXES),
        P(AXES, None),
        P(AXES),
        P(AXES),
        P(None, AXES),
        P(AXES, None),
        P(AXES, None),
        P(AXES),
        P(AXES),
        P(AXES),
        P(AXES, None),
        P(AXES),
        P(AXES, None),
        P(AXES),
        P(AXES),
        P(AXES),
        P(None, AXES),
        P(AXES),
        P(AXES, None),
    )
    return jax.shard_map(
        on_device, mesh=mesh, in_specs=in_specs, out_specs=out_specs, check_vma=False
    )
```

```python
from functools import partial
import math

import jax
import jax.numpy as jnp
import numpy as np
from jax import lax
from jax.experimental import pallas as pl
from jax.experimental.pallas import tpu as pltpu
from jax.sharding import PartitionSpec as P

HEADS = 12
WD = 128
GHEADS = 4
LAT = 128
NWAVE = 32
GRID = 32
PATCH = 1024


EPS = 1e-05
AXES = ("dp", "fsdp")
BAND_DROP = (0, 6, 9, 7)
HIGH = lax.Precision.HIGHEST


def sincos(values, count):
    freq = jnp.exp(jnp.arange(count, dtype=jnp.float32) * (-math.log(10000.0) / count))
    angle = values[..., None] * freq
    return jnp.concatenate([jnp.sin(angle), jnp.cos(angle)], axis=-1)


def code_table(count, size):
    freq = np.exp(np.arange(size, dtype=np.float32) * np.float32(-math.log(10000.0) / size))
    angle = np.arange(count, dtype=np.float32)[:, None] * freq.astype(np.float32)
    return np.concatenate([np.sin(angle), np.cos(angle)], axis=-1).astype(np.float32)


def norm_rows(rows, gain, shift):
    mean = jnp.mean(rows, axis=-1, keepdims=True)
    centred = rows - mean
    spread = jnp.mean(centred * centred, axis=-1, keepdims=True)
    return centred * lax.rsqrt(spread + EPS) * gain + shift


def exact_gelu(values):
    return jax.nn.gelu(values, approximate=False)


def band_valid(sensor, bands):
    drops = jnp.array(BAND_DROP, jnp.int32)
    picked = jnp.where(
        sensor[:, None] == jnp.arange(4, dtype=jnp.int32)[None, :], drops[None, :], 0
    )
    count = bands - jnp.sum(picked, axis=1)
    return (jnp.arange(bands, dtype=jnp.int32)[None, :] < count[:, None]).astype(jnp.float32)


def place_code(visible, width):
    row = (visible // GRID).astype(jnp.float32)
    col = (visible % GRID).astype(jnp.float32)
    return jnp.concatenate([sincos(row, width // 4), sincos(col, width // 4)], axis=-1)


def gen_core(
    wave_code,
    tokens,
    gen_qkv,
    gen_out,
    gen_out_bias,
    gen_gain1,
    gen_shift1,
    gen_up,
    gen_up_bias,
    gen_down,
    gen_down_bias,
    gen_gain2,
    gen_shift2,
):
    sequence = jnp.concatenate([tokens[:LAT], wave_code, tokens[LAT:]], axis=0)
    length = sequence.shape[0]
    width = sequence.shape[1]
    head_dim = width // GHEADS
    joint = jnp.dot(sequence, gen_qkv, precision=HIGH).reshape(length, 3, GHEADS, head_dim)
    scores = jnp.einsum("qhe,khe->hqk", joint[:, 0], joint[:, 1], precision=HIGH) / math.sqrt(
        head_dim
    )
    probs = jax.nn.softmax(scores, axis=-1)
    context = jnp.einsum("hqk,khe->qhe", probs, joint[:, 2], precision=HIGH).reshape(length, width)
    mixed = norm_rows(
        sequence + jnp.dot(context, gen_out, precision=HIGH) + gen_out_bias, gen_gain1, gen_shift1
    )
    hidden = jax.nn.gelu(jnp.dot(mixed, gen_up, precision=HIGH) + gen_up_bias, approximate=False)
    final = norm_rows(
        mixed + jnp.dot(hidden, gen_down, precision=HIGH) + gen_down_bias, gen_gain2, gen_shift2
    )
    feature = final[LAT : LAT + NWAVE] + sequence[LAT : LAT + NWAVE]
    return (feature, final[length - 1])


def own_part(full, dim):
    count = lax.axis_size("dp") * lax.axis_size("fsdp")
    index = lax.axis_index("dp") * lax.axis_size("fsdp") + lax.axis_index("fsdp")
    piece = full.shape[dim] // count
    return lax.dynamic_slice_in_dim(full, index * piece, piece, dim)


def tdot(left, right):
    return lax.dot_general(
        left, right, (((0,), (0,)), ((), ())), preferred_element_type=jnp.float32
    )


def ndot(left, right):
    return lax.dot_general(
        left, right, (((1,), (1,)), ((), ())), preferred_element_type=jnp.float32
    )


MESH_ID = pl.DeviceIdType.MESH
ANY = pl.BlockSpec(memory_space=pl.ANY)
VMEM = pl.BlockSpec(memory_space=pltpu.VMEM)


class Net:
    def __init__(self, planes):
        dp, fs = lax.axis_index("dp"), lax.axis_index("fsdp")
        self.planes = planes
        self.z, self.x = lax.div(dp, 2), lax.rem(dp, 2)
        self.y, self.c = lax.div(fs, 2), lax.rem(fs, 2)
        self.sib = self.at(self.z, self.x, self.y, 1 - self.c)
        self.nx = self.at(self.z, 1 - self.x, self.y, self.c)
        self.ny = self.at(self.z, self.x, 1 - self.y, self.c)

    def at(self, z, x, y, c):
        return (z * 2 + x, y * 2 + c)

    def plane(self, k):
        return lax.rem(self.z + k, self.planes)

    def zpeer(self, k):
        return self.at(self.plane(k), self.x, self.y, self.c)

    def chip(self, k, dx=0, dy=0):
        x = 1 - self.x if dx else self.x
        y = 1 - self.y if dy else self.y
        return self.plane(k) * 4 + x * 2 + y

    def greet(self):
        barrier = pltpu.get_barrier_semaphore()
        partners = [self.sib, self.nx, self.ny]
        partners += [self.zpeer(k) for k in range(1, self.planes)]
        for partner in partners:
            pl.semaphore_signal(barrier, inc=1, device_id=partner, device_id_type=MESH_ID)
        pl.semaphore_wait(barrier, len(partners))


class Wires:
    def __init__(self, send, recv):
        self.send, self.recv, self.used, self.started = send, recv, 0, []

    def push(self, src, dst, device):
        index = self.used
        self.used += 1
        copy = pltpu.make_async_remote_copy(
            src_ref=src,
            dst_ref=dst,
            send_sem=self.send.at[index],
            recv_sem=self.recv.at[index],
            device_id=device,
            device_id_type=MESH_ID,
        )
        copy.start()
        self.started.append(copy)
        return copy

    def drain(self):
        for copy in self.started:
            copy.wait_send()


class Gather:
    def __init__(self, net, wires, own, piece):
        self.net, self.wires, self.own, self.piece = net, wires, own, piece
        self.z_in, self.first, self.second, self.twins = {}, {}, {}, []

    def near(self, h):
        return self.net.ny if h else self.net.nx

    def far(self, h):
        return self.net.nx if h else self.net.ny

    def share(self, chip, h, src=None):
        spot = self.piece(chip, h)
        self.twins.append(self.wires.push(spot if src is None else src, spot, self.net.sib))

    def begin_z(self):
        for k in range(1, self.net.planes):
            for h in range(2):
                spot = self.piece(self.net.chip(0), h)
                self.z_in[k, h] = self.wires.push(self.own(h), spot, self.net.zpeer(k))

    def spread(self, k):
        back = (self.net.planes - k) % self.net.planes
        for h in range(2):
            if k:
                self.z_in[k, h].wait_recv()
            spot = self.piece(self.net.chip(back), h)
            src = self.own(h) if k == 0 else spot
            self.first[k, h] = self.wires.push(src, spot, self.near(h))
            self.second[k, h, 0] = self.wires.push(src, spot, self.far(h))
            self.share(self.net.chip(back), h, src)

    def relay(self, k):
        back = (self.net.planes - k) % self.net.planes
        for h in range(2):
            self.first[k, h].wait_recv()
            chip = self.net.chip(back, dx=h == 0, dy=h == 1)
            spot = self.piece(chip, h)
            self.second[k, h, 1] = self.wires.push(spot, spot, self.far(h))
            self.share(chip, h)

    def close(self, k):
        back = (self.net.planes - k) % self.net.planes
        for h in range(2):
            for hop in range(2):
                self.second[k, h, hop].wait_recv()
                chip = self.net.chip(back, dx=hop == 1 or h == 1, dy=hop == 1 or h == 0)
                self.share(chip, h)

    def finish(self):
        for copy in self.twins:
            copy.wait_recv()


def gather_copies(planes):
    return 2 * (planes - 1) + 4 * planes + 2 * planes + 8 * planes


class Reduce:
    def __init__(self, net, wires, part, held, near_in, far_in, z_in):
        self.net, self.wires, self.part, self.held = net, wires, part, held
        self.near_in, self.far_in, self.z_in = near_in, far_in, z_in
        self.pairs, self.near, self.far, self.along = {}, {}, {}, {}

    def add(self, spot, other):
        size = 16 if spot.shape[0] % 16 == 0 else 8

        def some(i, _):
            at = pl.ds(pl.multiple_of(i * size, size), size)
            total = spot[at].astype(jnp.float32) + other[at].astype(jnp.float32)
            spot[at] = total.astype(spot.dtype)
            return 0

        lax.fori_loop(0, spot.shape[0] // size, some, 0)

    def begin(self, k):
        for dx in range(2):
            for dy in range(2):
                for h in range(2):
                    chip = self.net.chip(k, dx, dy)
                    self.pairs[k, dx, dy, h] = self.wires.push(
                        self.part(chip, 1 - self.net.c, h), self.held.at[chip, h], self.net.sib
                    )

    def stage0(self, k):
        for dx, dy in ((1, 1), (0, 1), (1, 0), (0, 0)):
            for h in range(2):
                self.pairs[k, dx, dy, h].wait_recv()
                chip = self.net.chip(k, dx, dy)
                self.add(self.held.at[chip, h], self.part(chip, self.net.c, h))
                if (dy if h == 0 else dx) == 1:
                    other = dx if h == 0 else dy
                    self.near[k, h, other] = self.wires.push(
                        self.held.at[chip, h],
                        self.near_in.at[k, h, other],
                        self.net.ny if h == 0 else self.net.nx,
                    )

    def stage1(self, k):
        for h in range(2):
            for other in (1, 0):
                self.near[k, h, other].wait_recv()
                chip = self.net.chip(k, other, 0) if h == 0 else self.net.chip(k, 0, other)
                self.add(self.held.at[chip, h], self.near_in.at[k, h, other])
                if other:
                    self.far[k, h] = self.wires.push(
                        self.held.at[chip, h],
                        self.far_in.at[k, h],
                        self.net.nx if h == 0 else self.net.ny,
                    )

    def stage2(self, k):
        for h in range(2):
            self.far[k, h].wait_recv()
            spot = self.held.at[self.net.chip(k), h]
            self.add(spot, self.far_in.at[k, h])
            if k:
                self.along[k, h] = self.wires.push(spot, self.z_in.at[k - 1, h], self.net.zpeer(k))

    def total(self, h):
        value = self.held[self.net.chip(0), h].astype(jnp.float32)
        for k in range(1, self.net.planes):
            self.along[k, h].wait_recv()
            value = value + self.z_in[k - 1, h].astype(jnp.float32)
        return value


def reduce_copies(planes):
    return 8 * planes + 4 * planes + 2 * planes + 2 * (planes - 1)


def reduce_scratch(planes, rows, cols, dtype):
    return [
        pltpu.VMEM((planes * 4, 2, rows, cols), dtype),
        pltpu.VMEM((planes, 2, 2, rows, cols), dtype),
        pltpu.VMEM((planes, 2, rows, cols), dtype),
        pltpu.VMEM((planes - 1, 2, rows, cols), dtype),
    ]


def dot_nn(left, right):
    return jnp.dot(left, right, preferred_element_type=jnp.float32)


class Trade:
    def __init__(self, src, dst, send, recv, local):
        self.src, self.dst, self.send, self.recv = src, dst, send, recv
        self.count = src.shape[0]
        self.me = lax.axis_index("dp") * 4 + lax.axis_index("fsdp")
        self.own = pltpu.make_async_copy(src.at[self.me], dst.at[self.me], local)

    def place(self, i):
        to = lax.rem(self.me + i, self.count)
        return to, (lax.div(to, 4), lax.rem(to, 4))

    def greet(self):
        barrier = pltpu.get_barrier_semaphore()

        def call(i, _):
            pl.semaphore_signal(
                barrier, inc=1, device_id=self.place(i)[1], device_id_type=MESH_ID
            )
            return 0

        lax.fori_loop(1, self.count, call, 0)
        pl.semaphore_wait(barrier, self.count - 1)

    def copy(self, i):
        to, device = self.place(i)
        return pltpu.make_async_remote_copy(
            src_ref=self.src.at[to],
            dst_ref=self.dst.at[self.me],
            send_sem=self.send.at[i],
            recv_sem=self.recv.at[i],
            device_id=device,
            device_id_type=MESH_ID,
        )

    def begin(self, part=0, parts=1):
        def go(i, _):
            self.copy(i).start()
            return 0

        cuts = [1 + (self.count - 1) * p // parts for p in (part, part + 1)]
        lax.fori_loop(*cuts, go, 0)
        if part == 0:
            self.own.start()

    def finish(self):
        def end(i, _):
            self.copy(i).wait()
            return 0

        lax.fori_loop(1, self.count, end, 0)
        self.own.wait()


class Pump:
    def __init__(self):
        self.units, self.at, self.last = [], 0, False

    def put(self, item, order):
        for k in order:
            item.begin(k)
        self.units += [(item, k) for k in order]

    def step(self, count=1):
        for _ in range(count):
            if self.at >= len(self.units) and not self.last:
                return
            for stage, lag in enumerate(LAGS):
                at = self.at - lag
                if 0 <= at < len(self.units):
                    item, k = self.units[at]
                    (item.stage0, item.stage1, item.stage2)[stage](k)
            self.at += 1

    def until(self, item):
        self.last = True
        last = max(i for i, unit in enumerate(self.units) if unit[0] is item)
        while self.at <= last + LAGS[2]:
            self.step()


def tile_rows(i, size):
    return pl.ds(pl.multiple_of(i * size, size), size)


def norm_back(grad, rows, gain):
    mean = jnp.mean(rows, axis=-1, keepdims=True)
    centred = rows - mean
    spread = jnp.mean(centred * centred, axis=-1, keepdims=True)
    inverse = lax.rsqrt(spread + EPS)
    unit = centred * inverse
    scaled = grad * gain
    inner = scaled - jnp.mean(scaled, axis=-1, keepdims=True)
    inner = inner - unit * jnp.mean(scaled * unit, axis=-1, keepdims=True)
    return inverse * inner, grad * unit


def lay_lines(box, at, value):
    for i in range(value.shape[1] // 128):
        box[0, pl.ds(at + i, 1), :] = value[:, i * 128 : (i + 1) * 128]
    return at + value.shape[1] // 128


def box_lines(waves, width, hidden, dec_width):
    used = waves + (6 * width + hidden + 2 * dec_width) // 128
    return used + (-used) % 8


FT = 256
TRADES = 1
LAGS = (0, 3, 6)
NORM_STEPS = 2
HEAD_STEPS = 1
FEED_STEPS = 1
BLOCK = 128


def backward_kernel(planes, steps, sizes, *refs):
    (rows, width, hidden, dec_width, chips, patches) = sizes
    devices = planes * 8
    seen = rows // chips
    (
        blocks, returned, visible, order, ending, wide, down, activ, slope, normed2, middle, context,
        joint, probs, normed, start, slots, gains, weight, feature, source, gen_rows, gen_down,
        gen_vec, wave_code,
    ) = refs[:25]
    (
        dec_out, up_out, oq_out, down_out, kw_out, kb_out, all_out, gen_wide, gen_tall, gen_seq,
        gen_lines, bias_out, embed_out, decoder_out,
    ) = refs[25:39]
    scratch = refs[39:61]
    (
        big, left, w_down, w_up, t_activ, t_slope, resid, w_sq, t_joint, t_probs,
        g_dec, g_up, g_down, g_oq, g_table, run, back, g_low, g_joint, v_sums,
        f_dec, f_up, f_oq, hand_dec, hand_up, hand_oq, box, send, recv, trade_send, trade_recv, tile_sem, load_sem,
    ) = refs[61:]
    loads = {}

    def load(name, src, dst):
        copy = pltpu.make_async_copy(src, dst, load_sem.at[len(loads)])
        copy.start()
        loads[name] = copy

    up_at, out_at, dec_at = 3 * width, 3 * width + hidden, 4 * width + hidden
    load("returned", returned, big)
    w_dec = w_sq.at[0, :, pl.ds(0, dec_width)]
    load("dec", wide.at[:, pl.ds(dec_at, dec_width)], w_dec)
    load("ending", ending, left.at[0])

    def tile_copies(t):
        slot = lax.rem(t, 2)
        at = tile_rows(t, FT)
        return (
            pltpu.make_async_copy(down.at[at], w_down.at[slot], tile_sem.at[slot, 0]),
            pltpu.make_async_copy(
                wide.at[:, pl.ds(pl.multiple_of(up_at + t * FT, 128), FT)],
                w_up.at[slot],
                tile_sem.at[slot, 1],
            ),
            pltpu.make_async_copy(activ.at[:, at], t_activ.at[slot], tile_sem.at[slot, 2]),
            pltpu.make_async_copy(slope.at[:, at], t_slope.at[slot], tile_sem.at[slot, 3]),
        )

    for copy in tile_copies(0):
        copy.start()
    load("normed2", normed2, left.at[1])
    load("middle", middle, resid)
    load("query", wide.at[:, pl.ds(0, width)], w_sq.at[1])

    net = Net(planes)
    trade = Trade(blocks, decoder_out, trade_send, trade_recv, load_sem.at[15])
    trade.greet()
    trade.begin(0, TRADES)
    wires = Wires(send, recv)
    pump = Pump()
    shard = width // (devices // 2)
    w_rows = lambda chip: pl.ds(pl.multiple_of(chip * shard, 16), shard)

    def quarter(ref, size):
        return lambda chip, c, h: ref.at[
            w_rows(chip), pl.ds(pl.multiple_of((c * 2 + h) * size, 128), size)
        ]

    def stripe(ref, size):
        return lambda chip, c, h: ref.at[
            pl.ds(pl.multiple_of(((chip * 2 + c) * 2 + h) * size, 16), size)
        ]

    q_dec, q_up = dec_width // 4, hidden // 8
    d_rows = hidden // devices // 2
    t_rows = g_table.shape[0] // devices // 2
    parts = (
        quarter(g_dec, q_dec),
        quarter(g_up.at[0], q_up),
        quarter(g_up.at[1], q_up),
        stripe(g_down, d_rows),
        stripe(g_table, t_rows),
        lambda chip, c, h: g_oq.at[c * 2 + h, w_rows(chip)],
    )
    lands = [scratch[i * 4 : i * 4 + 4] for i in range(5)]
    lands.append((scratch[20], lands[3][1], lands[3][2], scratch[21]))
    dec, up0, up1, downs, tables, oq = [
        Reduce(net, wires, part, *land) for part, land in zip(parts, lands)
    ]
    away = list(range(1, planes)) + [0]

    loads["returned"].wait()
    grad_mask = jnp.zeros((8, dec_width), jnp.float32)
    spread = big.reshape(devices, chips, patches // devices, dec_width)
    for chip in range(chips):
        got = spread[:, chip].reshape(patches, dec_width)
        chosen = (order[...] == visible[pl.ds(chip, 1), :]).astype(jnp.float32)
        picked = tdot(chosen.astype(jnp.bfloat16), got)
        g_joint[pl.ds(chip * seen, seen), pl.ds(0, dec_width)] = picked.astype(jnp.bfloat16)
        left_out = 1.0 - jnp.sum(chosen, axis=1, keepdims=True)
        left_out = jnp.broadcast_to(left_out, (patches, 8)).astype(jnp.bfloat16)
        grad_mask = grad_mask + tdot(left_out, got)
    v_sums[pl.ds(7, 1), pl.ds(dec_width, dec_width)] = grad_mask[:1]
    load("slots", slots, big)
    grad_rows = g_joint[:, pl.ds(0, dec_width)]
    v_sums[pl.ds(7, 1), pl.ds(0, dec_width)] = jnp.sum(
        grad_rows.astype(jnp.float32), axis=0, keepdims=True
    )
    loads["ending"].wait()

    def dec_part(i, _):
        at = tile_rows(i, FT)
        g_dec[at, :] = tdot(left[0, :, at], grad_rows).astype(jnp.bfloat16)
        return 0

    lax.fori_loop(0, width // FT, dec_part, 0)
    pump.put(dec, away)
    loads["dec"].wait()

    def end_part(i, _):
        at = tile_rows(i, FT)
        run[at, :] = ndot(g_joint[at, pl.ds(0, dec_width)], w_dec[...])
        g_low[at, :] = run[at, :].astype(jnp.bfloat16)
        return 0

    lax.fori_loop(0, rows // FT, end_part, 0)
    load("out", wide.at[:, pl.ds(out_at, width)], w_sq.at[0])
    load("context", context, left.at[0])
    back[...] = jnp.zeros_like(back)
    v_sums[pl.ds(0, 1), pl.ds(0, width)] = jnp.sum(
        g_low[...].astype(jnp.float32), axis=0, keepdims=True
    )
    loads["normed2"].wait()
    tiles = hidden // FT

    parts_sent = [1]

    def trade_more():
        if parts_sent[0] < TRADES:
            trade.begin(parts_sent[0], TRADES)
            parts_sent[0] += 1

    def feed(t, _):
        slot = lax.rem(t, 2)

        @pl.when(t + 1 < tiles)
        def _():
            for copy in tile_copies(t + 1):
                copy.start()

        for copy in tile_copies(t):
            copy.wait()
        grad = ndot(g_low[...], w_down[slot])
        grad_upper = (grad * t_slope[slot].astype(jnp.float32)).astype(jnp.bfloat16)
        at = tile_rows(t, FT)
        v_sums[pl.ds(1, 1), at] = jnp.sum(
            grad_upper.astype(jnp.float32), axis=0, keepdims=True
        )
        g_down[at, :] = tdot(t_activ[slot], g_low[...]).astype(jnp.bfloat16)
        g_up[lax.div(t, tiles // 2), :, tile_rows(lax.rem(t, tiles // 2), FT)] = tdot(
            left[1], grad_upper
        ).astype(jnp.bfloat16)
        for i in range(rows // FT):
            part = pl.ds(i * FT, FT)
            back[part, :] += ndot(grad_upper[i * FT : (i + 1) * FT], w_up[slot])
        return 0

    for i in range(0, tiles, 2):
        lax.fori_loop(i, i + 2, feed, 0)
        if i + 2 == tiles // 2:
            pump.put(up0, away)
        if i + 2 < tiles:
            trade_more()
            pump.step(FEED_STEPS)
    pump.put(up1, away)
    pump.put(downs, away)
    load("normed", normed, left.at[1])
    loads["middle"].wait()

    def through_norm(gain_row, sums_at):
        gain = gains[pl.ds(gain_row, 1), pl.ds(0, width)]

        def block(i, sums):
            at = tile_rows(i, BLOCK)
            grad = back[at, :]
            inner, terms = norm_back(grad, resid[at, :], gain)
            run[at, :] += inner
            return (
                sums[0] + jnp.sum(terms, axis=0, keepdims=True),
                sums[1] + jnp.sum(grad, axis=0, keepdims=True),
            )

        zero = jnp.zeros((1, width), jnp.float32)
        sums = lax.fori_loop(0, rows // BLOCK, block, (zero, zero))
        v_sums[pl.ds(sums_at, 1), pl.ds(0, width)] = sums[0]
        v_sums[pl.ds(sums_at + 1, 1), pl.ds(0, width)] = sums[1]

    through_norm(2, 2)
    pump.step(NORM_STEPS)
    load("start", start, resid)
    g_low[...] = run[...].astype(jnp.bfloat16)
    loads["context"].wait()
    loads["out"].wait()

    def out_part(i, _):
        at = tile_rows(i, FT)
        g_oq[0, at, :] = tdot(left[0, :, at], g_low[...]).astype(jnp.bfloat16)
        return 0

    lax.fori_loop(0, width // FT, out_part, 0)

    def context_part(i, _):
        at = tile_rows(i, FT)
        g_low[at, :] = ndot(g_low[at, :], w_sq[0]).astype(jnp.bfloat16)
        return 0

    lax.fori_loop(0, rows // FT, context_part, 0)
    load("key", wide.at[:, pl.ds(width, width)], w_sq.at[0])
    pump.step(2)

    pairs = width // 128
    head = width // HEADS
    scale = 1.0 / math.sqrt(head)
    odd = lax.broadcasted_iota(jnp.int32, (1, 128), 1) >= head

    def pair_copies(n):
        slot = lax.rem(n, 2)
        at = tile_rows(lax.div(n, pairs), seen)
        copies = [
            pltpu.make_async_copy(probs.at[pl.ds(2 * n, 2)], t_probs.at[slot], tile_sem.at[slot, 0])
        ]
        for i in range(3):
            lane = pl.ds(pl.multiple_of(lax.rem(n, pairs) * 128 + i * width, 128), 128)
            copies.append(
                pltpu.make_async_copy(
                    joint.at[at, lane], t_joint.at[slot, i], tile_sem.at[slot, i + 1]
                )
            )
        return copies

    for copy in pair_copies(0):
        copy.start()

    def attend(n, _):
        slot = lax.rem(n, 2)

        @pl.when(n + 1 < chips * pairs)
        def _():
            for copy in pair_copies(n + 1):
                copy.start()

        for copy in pair_copies(n):
            copy.wait()
        chip = lax.div(n, pairs)
        pair = lax.rem(n, pairs)
        at = tile_rows(chip, seen)
        lanes = [
            pl.ds(pl.multiple_of(pair * 128 + i * width, 128), 128) for i in range(3)
        ]
        query, key, value = [t_joint[slot, i] for i in range(3)]
        grad = g_low[at, lanes[0]]
        zero = jnp.zeros_like(grad)
        totals = [None, None, None]
        for h in range(2):
            mine = odd if h else jnp.logical_not(odd)
            grad_h = jnp.where(mine, grad, zero)
            query_h = jnp.where(mine, query, zero)
            key_h = jnp.where(mine, key, zero)
            prob = t_probs[slot, h]
            prob32 = prob.astype(jnp.float32)
            grad_prob = ndot(grad_h, value)
            row_dot = jnp.sum(prob32 * grad_prob, axis=-1, keepdims=True)
            grad_score = (prob32 * (grad_prob - row_dot)).astype(jnp.bfloat16)
            terms = (dot_nn(grad_score, key_h), tdot(grad_score, query_h), tdot(prob, grad_h))
            totals = [new if old is None else old + new for old, new in zip(totals, terms)]
        g_joint[at, lanes[0]] = (totals[0] * scale).astype(jnp.bfloat16)
        g_joint[at, lanes[1]] = (totals[1] * scale).astype(jnp.bfloat16)
        g_joint[at, lanes[2]] = totals[2].astype(jnp.bfloat16)
        return 0

    for i in range(0, chips * pairs, 2):
        lax.fori_loop(i, i + 2, attend, 0)
        trade_more()
        pump.step(HEAD_STEPS)

    loads["normed"].wait()
    def joint_part(i, _):
        which, at = lax.div(i, width // FT), tile_rows(lax.rem(i, width // FT), FT)
        lane = pl.ds(pl.multiple_of(which * width, 128), width)
        g_oq[which + 1, at, :] = tdot(left[1, :, at], g_joint[:, lane]).astype(jnp.bfloat16)
        return 0

    lax.fori_loop(0, 3 * width // FT, joint_part, 0)
    value = pltpu.make_async_copy(
        wide.at[:, pl.ds(2 * width, width)], w_sq.at[1], load_sem.at[len(loads)]
    )
    back[...] = jnp.zeros_like(back)

    def joint_back(i, _):
        for j, copy in enumerate((loads["query"], loads["key"], value)):

            @pl.when(i == j)
            def _():
                copy.wait()

        lane = pl.ds(pl.multiple_of(i * width, 128), width)

        def some(j, _):
            at = tile_rows(j, FT)
            back[at, :] += ndot(g_joint[at, lane], w_sq[lax.rem(i + 1, 2)])
            return 0

        lax.fori_loop(0, rows // FT, some, 0)

        @pl.when(i == 0)
        def _():
            value.start()

        return 0

    lax.fori_loop(0, 3, joint_back, 0)
    pump.step(1)
    loads["start"].wait()
    through_norm(0, 4)
    g_low[...] = run[...].astype(jnp.bfloat16)
    conv = jnp.sum(run[...], axis=0, keepdims=True)
    embed = pltpu.make_async_copy(g_low, embed_out, tile_sem.at[0, 1])
    embed.start()
    loads["slots"].wait()
    span = 512

    def table_block(i, _):
        at = tile_rows(i, span)
        g_table[at, :] = dot_nn(big[at, :], g_low[...]).astype(jnp.bfloat16)
        return 0

    lax.fori_loop(0, g_table.shape[0] // span, table_block, 0)
    pump.put(tables, away)
    pump.put(oq, away)

    waves = t_rows
    lines = width // 128
    box[0, pl.ds(waves, box.shape[1] - waves), :] = jnp.zeros(
        (box.shape[1] - waves, 128), jnp.float32
    )
    at = lay_lines(box, waves, conv)
    for line in (4, 5, 2, 3, 0):
        at = lay_lines(box, at, v_sums[pl.ds(line, 1), pl.ds(0, width)])
    at = lay_lines(box, at, v_sums[pl.ds(1, 1), :])
    lay_lines(box, at, v_sums[pl.ds(7, 1), pl.ds(0, 2 * dec_width)])

    while parts_sent[0] < TRADES:
        trade_more()
    pump.until(tables)
    held = tables.held
    partial_sum = jnp.zeros((waves, 128), jnp.float32)
    for h in range(2):
        own = tables.total(h).astype(jnp.bfloat16)
        cols = pl.ds(h * width, width)
        kw_out[:, cols] = tdot(feature[...], own)
        kb_out[:, cols] = jnp.sum(own.astype(jnp.float32), axis=0, keepdims=True)
        partial_sum = partial_sum + ndot(own, weight[:, cols])
    box[0, pl.ds(0, waves), :] = partial_sum
    peers = [net.sib, net.nx, net.ny]
    for bit in range(steps):
        step = 1 << bit
        up = lax.rem(lax.div(net.z, step), 2) == 0
        peers.append(net.at(jnp.where(up, net.z + step, net.z - step), net.x, net.y, net.c))
    for i, peer in enumerate(peers):
        hop = wires.push(box.at[2 * i], box.at[2 * i + 1], peer)
        pump.step(1)
        hop.wait_recv()
        box[2 * i + 2] = box[2 * i] + box[2 * i + 1]
    end = box.at[2 * len(peers)]
    all_out[...] = end[...]
    me = net.chip(0) * 2 + net.c
    conv = jnp.concatenate(
        [end[pl.ds(waves + i, 1), :] for i in range(lines)], axis=1
    )
    gen_width = gen_rows.shape[0]
    up_size = gen_down.shape[0]
    bias_at = gen_rows.shape[1] - gen_width - width
    grad_source = lax.dot_general(
        jnp.broadcast_to(conv, (8, width)),
        gen_rows[:, pl.ds(bias_at, width)].astype(jnp.float32),
        (((1,), (1,)), ((), ())),
        precision=HIGH,
        preferred_element_type=jnp.float32,
    )
    top = lax.broadcasted_iota(jnp.int32, (8, gen_width), 0)
    grad_source = jnp.where(top == 0, grad_source, 0.0)
    pump.step(1)
    small = gen_width // devices
    lane = lax.broadcasted_iota(jnp.int32, (8, gen_width), 1)
    pick = ((lane == me * small + top) & (top < small)).astype(jnp.float32)
    exact = partial(
        lax.dot_general, precision=HIGH, preferred_element_type=jnp.float32
    )
    rows_of = lambda value: exact(pick, value, (((1,), (0,)), ((), ())))
    lanes_of = lambda value: exact(value, pick, (((1,), (1,)), ((), ())))
    chunk = up_size // 4

    def put_up(i, value):
        gen_wide[:, pl.ds(pl.multiple_of(i * chunk, chunk), chunk)] = rows_of(value)

    def put_down(i, value):
        back[:, pl.ds(pl.multiple_of(i * gen_width, gen_width), gen_width)] = value

    g_seq, g_qkv, g_out, thin = gen_back(
        gen_rows, gen_down, gen_vec, wave_code[...], LAT + NWAVE + 1, end[pl.ds(0, waves), :],
        grad_source, v_sums, put_up, put_down,
    )
    pump.step(2)
    gen_wide[:, pl.ds(up_size, 3 * gen_width)] = rows_of(g_qkv)
    gen_wide[:, pl.ds(up_size + 3 * gen_width, gen_width)] = rows_of(g_out)
    tall = up_size // devices
    per = devices // 4
    gen_tall[...] = back[
        tile_rows(lax.rem(me, per), tall),
        pl.ds(pl.multiple_of(lax.div(me, per) * gen_width, 128), gen_width),
    ]
    gen_seq[...] = lanes_of(g_seq)
    for i, value in enumerate(thin):
        gen_lines[pl.ds(i, 1), pl.ds(0, gen_width)] = value
    gen_lines[pl.ds(6, 1), :] = v_sums[pl.ds(6, 1), pl.ds(0, up_size)]
    own_source = jnp.sum(
        pick * source[pl.ds(0, 1), :].astype(jnp.float32), axis=1, keepdims=True
    )
    bias_out[...] = own_source * conv
    pump.until(oq)
    half = shard // 2
    own_rows = pl.ds(pl.multiple_of(net.c * half, 8), half)
    their_rows = pl.ds(pl.multiple_of((1 - net.c) * half, 8), half)
    jobs = (
        (dec, f_dec, hand_dec, dec_out, 0, q_dec),
        (up0, f_up.at[0], hand_up.at[0], up_out, 0, q_up),
        (up1, f_up.at[1], hand_up.at[1], up_out, hidden // 2, q_up),
        (oq, f_oq, hand_oq, oq_out, 0, width),
    )
    swaps = []
    for item, final, hand, out, base, size in jobs:
        for h in range(2):
            final[h] = item.total(h)
            swaps.append(wires.push(final.at[h, their_rows], hand.at[h], net.sib))
    for h in range(2):
        down_out[pl.ds(h * d_rows, d_rows)] = downs.total(h)
    for item, final, hand, out, base, size in jobs:
        for h in range(2):
            own = pl.ds(pl.multiple_of(base + (net.c * 2 + h) * size, 128), size)
            other = pl.ds(pl.multiple_of(base + ((1 - net.c) * 2 + h) * size, 128), size)
            out[:, own] = final[h, own_rows]
            swaps.pop(0).wait_recv()
            out[:, other] = hand[h]
    embed.wait()
    trade.finish()
    wires.drain()


def backward(planes, sizes, *args):
    (rows, width, hidden, dec_width, chips, patches) = sizes
    devices = planes * 8
    steps = (planes - 1).bit_length()
    low, full = jnp.bfloat16, jnp.float32
    shard = width // (devices // 2)
    q_dec, q_up = dec_width // 4, hidden // 8
    d_rows = hidden // devices // 2
    slots = args[16].shape[0]
    t_rows = slots // devices // 2
    box_rows = box_lines(t_rows, width, hidden, dec_width)
    up_size, gen_width = args[22].shape
    copies = 6 * reduce_copies(planes) + 3 + steps + 8
    scratch = []
    for shape in (
        (shard, q_dec), (shard, q_up), (shard, q_up), (d_rows, width), (t_rows, width),
    ):
        scratch += reduce_scratch(planes, *shape, low)
    assert d_rows == shard
    last = reduce_scratch(planes, shard, width, low)
    scratch += [last[0], last[3]]
    scratch += [
        pltpu.VMEM((chips * patches, dec_width), low),
        pltpu.VMEM((2, rows, width), low),
        pltpu.VMEM((2, FT, width), low),
        pltpu.VMEM((2, width, FT), low),
        pltpu.VMEM((2, rows, FT), low),
        pltpu.VMEM((2, rows, FT), low),
        pltpu.VMEM((rows, width), full),
        pltpu.VMEM((2, width, width), low),
        pltpu.VMEM((2, 3, rows // chips, 128), low),
        pltpu.VMEM((2, 2, rows // chips, rows // chips), low),
        pltpu.VMEM((width, dec_width), low),
        pltpu.VMEM((2, width, hidden // 2), low),
        pltpu.VMEM((hidden, width), low),
        pltpu.VMEM((4, width, width), low),
        pltpu.VMEM((slots, width), low),
        pltpu.VMEM((rows, width), full),
        pltpu.VMEM((rows, width), full),
        pltpu.VMEM((rows, width), low),
        pltpu.VMEM((rows, 3 * width), low),
        pltpu.VMEM((8, hidden), full),
        pltpu.VMEM((2, shard, q_dec), full),
        pltpu.VMEM((2, 2, shard, q_up), full),
        pltpu.VMEM((2, shard, width), full),
        pltpu.VMEM((2, shard // 2, q_dec), full),
        pltpu.VMEM((2, 2, shard // 2, q_up), full),
        pltpu.VMEM((2, shard // 2, width), full),
        pltpu.VMEM((2 * (3 + steps) + 1, box_rows, 128), full),
        pltpu.SemaphoreType.DMA((copies,)),
        pltpu.SemaphoreType.DMA((copies,)),
        pltpu.SemaphoreType.DMA((devices,)),
        pltpu.SemaphoreType.DMA((devices,)),
        pltpu.SemaphoreType.DMA((2, 4)),
        pltpu.SemaphoreType.DMA((16,)),
    ]
    shapes = (
        ((width // devices, dec_width), full),
        ((width // devices, hidden), full),
        ((width // devices, 4 * width), full),
        ((hidden // devices, width), full),
        ((args[19].shape[1], 2 * width), full),
        ((1, 2 * width), full),
        ((box_rows, 128), full),
        ((8, up_size + 4 * gen_width), full),
        ((up_size // devices, gen_width), full),
        ((args[24].shape[0] + gen_width + 8, 8), full),
        ((8, up_size), full),
        ((8, width), full),
        ((rows, width), low),
        (args[0].shape, low),
    )
    spots = [ANY, ANY, VMEM, VMEM] + [ANY] * 13 + [VMEM] * 8
    return pl.pallas_call(
        partial(backward_kernel, planes, steps, sizes),
        out_shape=tuple(jax.ShapeDtypeStruct(shape, dtype) for shape, dtype in shapes),
        in_specs=spots,
        out_specs=[VMEM] * 12 + [ANY] * 2,
        scratch_shapes=scratch,
        compiler_params=pltpu.CompilerParams(
            collective_id=2, has_side_effects=True, vmem_limit_bytes=125 * 2**19
        ),
    )(*args)


CHUNK = 896


def gen_layer(
    seq, qkv, out, out_bias, gain1, shift1, up, up_bias, down, down_bias, gain2, shift2, length
):
    width = seq.shape[1]
    size = width // GHEADS

    def times(left, right):
        return jnp.dot(left, right, precision=HIGH, preferred_element_type=jnp.float32)

    joint = times(seq, qkv)
    query, key, value = [joint[:, i * width : (i + 1) * width] for i in range(3)]
    lane = lax.broadcasted_iota(jnp.int32, (1, width), 1)
    spot = lax.broadcasted_iota(jnp.int32, (1, seq.shape[0]), 1)
    context = jnp.zeros_like(seq)
    for h in range(GHEADS):
        mine = (lax.div(lane, size) == h).astype(jnp.float32)
        scores = lax.dot_general(
            query * mine,
            key,
            (((1,), (1,)), ((), ())),
            precision=HIGH,
            preferred_element_type=jnp.float32,
        ) * (1.0 / math.sqrt(size))
        scores = jnp.where(spot < length, scores, -1e30)
        peak = lax.stop_gradient(jnp.max(scores, axis=-1, keepdims=True))
        raised = jnp.exp(scores - peak)
        probs = raised / jnp.sum(raised, axis=-1, keepdims=True)
        context = context + times(probs, value * mine)
    mixed = norm_rows(seq + times(context, out) + out_bias, gain1, shift1)
    inner = times(mixed, up) + up_bias
    hidden = 0.5 * inner * (1.0 + lax.erf(inner * math.sqrt(0.5)))
    return norm_rows(mixed + times(hidden, down) + down_bias, gain2, shift2)


def gen_seq_of(gen_rows, wave_code, up_size):
    width = gen_rows.shape[0]
    full = jnp.float32
    tokens = gen_rows[:, pl.ds(up_size + 4 * width, width)].astype(full).T
    last = gen_rows[:, pl.ds(gen_rows.shape[1] - width, width)].astype(full).T
    return jnp.concatenate([tokens, wave_code, last[:8]], axis=0)


def gen_parts(gen_rows, gen_down, gen_vec, wave_code, up_size):
    width = gen_rows.shape[0]
    full = jnp.float32
    at = up_size
    up = gen_rows[:, pl.ds(0, up_size)].astype(full)
    qkv = gen_rows[:, pl.ds(at, 3 * width)].astype(full)
    out = gen_rows[:, pl.ds(at + 3 * width, width)].astype(full)
    seq = gen_seq_of(gen_rows, wave_code, up_size)
    vec = [gen_vec[pl.ds(i, 1), pl.ds(0, width)] for i in range(6)]
    up_bias = gen_vec[pl.ds(6, 1), :]
    down = gen_down[...].astype(full)
    return (seq, qkv, out, vec[0], vec[1], vec[2], up, up_bias, down, vec[3], vec[4], vec[5])


def join_lanes(parts, size):
    owners = parts.shape[0]
    shape = (128, owners * size)
    lane = lax.broadcasted_iota(jnp.int32, shape, 0)
    column = lax.broadcasted_iota(jnp.int32, shape, 1)
    spread = dot_nn(parts, (lax.rem(column, size) == lane).astype(parts.dtype))
    shape = (owners, owners * size)
    row = lax.broadcasted_iota(jnp.int32, shape, 0)
    column = lax.broadcasted_iota(jnp.int32, shape, 1)
    return jnp.sum(
        jnp.where(lax.div(column, size) == row, spread, 0.0), axis=0, keepdims=True
    )


def prepare_kernel(planes, sizes, *refs):
    (rows, width, hidden, dec_width, chips, up_size) = sizes
    devices = planes * 8
    (
        qkv, up, out, dec, down, weight, weight_bias, pixels, sensor, waves, visible, places,
        wave_code, gen_up, gen_qkv, gen_out, bias_weight, gen_tokens, gen_low,
    ) = refs[:19]
    thin = refs[19:34]
    (
        wide_out, down_out, table_out, slots_out, start, gen_rows, gen_down, gen_vec, vecs,
        feature_out, source_out,
    ) = refs[34:45]
    (
        g_rows, g_tail, table, slots, wide, fresh, joined, rows32, tail32, s_rows, s_tail, send,
        recv, local,
    ) = refs[45:]
    net = Net(planes)
    net.greet()
    wires = Wires(send, recv)
    me = net.chip(0) * 2 + net.c
    low = jnp.bfloat16
    copies = []

    def keep(src, dst):
        copy = pltpu.make_async_copy(src, dst, local.at[len(copies)])
        copy.start()
        copies.append(copy)

    small = gen_up.shape[0]
    gen_width = gen_out.shape[1]
    shape = (gen_tokens.shape[0], 2 * gen_width)
    row = lax.broadcasted_iota(jnp.int32, shape, 0)
    column = lax.broadcasted_iota(jnp.int32, shape, 1)
    turned = tdot(gen_tokens[...], (row == column).astype(low))
    line = jnp.concatenate(
        [item[...].astype(jnp.float32) for item in (gen_up, gen_qkv, gen_out)]
        + [turned[:, :gen_width], bias_weight[...].astype(jnp.float32), turned[:, gen_width:]],
        axis=1,
    )
    for q in range(16 // small):
        rows32[pl.ds(q * small, small), :] = line[:, q * CHUNK : (q + 1) * CHUNK]
    s_rows[...] = rows32[...].astype(low)
    tail32[...] = jnp.zeros_like(tail32)
    for i, item in enumerate(thin):
        tail32[pl.ds(i, 1), pl.ds(0, item.shape[1])] = item[...].astype(jnp.float32)
    s_tail[pl.ds(0, gen_low.shape[0]), :] = gen_low[...]
    s_tail[pl.ds(gen_low.shape[0], 16), :] = tail32[...].astype(low)
    r_size, r_cols = s_rows.shape
    r_cut = (r_cols // 256) * 128 + 128
    r_span = lambda h: pl.ds(r_cut * h, r_cols - r_cut if h else r_cut)
    t_size = s_tail.shape[0]
    t_cut = (t_size // 32) * 16 + 16
    t_span = lambda h: pl.ds(t_cut * h, t_size - t_cut if h else t_cut)
    smalls = [
        Gather(
            net,
            wires,
            lambda h: s_rows.at[:, r_span(h)],
            lambda chip, h: g_rows.at[tile_rows(chip * 2 + net.c, r_size), r_span(h)],
        ),
        Gather(
            net,
            wires,
            lambda h: s_tail.at[t_span(h)],
            lambda chip, h: g_tail.at[chip * 2 + net.c, t_span(h)],
        ),
    ]
    for item in smalls:
        item.begin_z()
        item.spread(0)
    keep(s_rows, g_rows.at[tile_rows(me, r_size)])
    keep(s_tail, g_tail.at[me])

    at = 0
    for item in (qkv, up, out, dec):
        wide[:, pl.ds(at, item.shape[1])] = item[...]
        at += item.shape[1]
    w_cols = at // 2
    quarter = w_cols // 2
    shard = wide.shape[0]
    mine = pl.ds(pl.multiple_of(net.c * w_cols, 128), w_cols)
    theirs = pl.ds(pl.multiple_of((1 - net.c) * w_cols, 128), w_cols)
    pair = wires.push(wide.at[:, theirs], fresh, net.sib)
    d_rows = down.shape[0]
    d_half = d_rows // 2
    d_own = lambda h: down.at[pl.ds(h * d_half, d_half)]
    d_piece = lambda chip, h: down_out.at[
        pl.ds(pl.multiple_of((chip * 2 + net.c) * d_rows + h * d_half, 16), d_half)
    ]
    w_own = lambda h: joined.at[:, pl.ds(h * quarter, quarter)]
    w_piece = lambda chip, h: wide_out.at[
        pl.ds(pl.multiple_of(chip * 2 * shard, 16), 2 * shard),
        pl.ds(pl.multiple_of((net.c * 2 + h) * quarter, 128), quarter),
    ]
    t_lines = table.shape[0] // devices // 2
    t_piece = lambda chip, h: table.at[tile_rows((chip * 2 + net.c) * 2 + h, t_lines)]
    t_own = lambda h: table.at[tile_rows(me * 2 + h, t_lines)]
    d_gather = Gather(net, wires, d_own, d_piece)
    w_gather = Gather(net, wires, w_own, w_piece)
    t_gather = Gather(net, wires, t_own, t_piece)
    d_gather.begin_z()
    for item in smalls:
        item.relay(0)
    pair.wait_recv()
    own32 = wide[:, mine].astype(jnp.float32)
    sib32 = fresh[...].astype(jnp.float32)
    first = net.c == 0
    joined[...] = jnp.concatenate(
        [jnp.where(first, own32, sib32), jnp.where(first, sib32, own32)], axis=0
    ).astype(low)
    for k in range(1, planes):
        for item in smalls:
            item.spread(k)
        for item in smalls:
            item.relay(k)
    w_gather.begin_z()
    for h in range(2):
        keep(w_own(h), w_piece(net.chip(0), h))
        keep(d_own(h), d_piece(net.chip(0), h))
    for k in range(planes):
        for item in smalls:
            item.close(k)
    heavy = [w_gather, d_gather]
    for item in heavy:
        item.spread(0)
    steps = [partial(item.relay, 0) for item in heavy]
    for k in range(1, planes):
        steps += [partial(item.spread, k) for item in heavy]
        steps += [partial(item.relay, k) for item in heavy]
    for k in range(planes):
        steps += [partial(item.close, k) for item in heavy]

    def pump(count):
        for _ in range(min(count, len(steps))):
            steps.pop(0)()

    for item in smalls:
        item.finish()
    for copy in copies[:2]:
        copy.wait()

    lines = width // devices
    groups = r_size // small
    shape = (gen_rows.shape[0], devices * r_size)
    row = lax.broadcasted_iota(jnp.int32, shape, 0)
    column = lax.broadcasted_iota(jnp.int32, shape, 1)
    for q in range(groups):
        source = lax.div(row, small) * r_size + q * small + lax.rem(row, small)
        gen_rows[:, pl.ds(q * r_cols, r_cols)] = dot_nn(
            (column == source).astype(low), g_rows[...]
        ).astype(low)
    gen_down[...] = g_tail[:, pl.ds(0, t_size - 16), :].reshape(gen_down.shape)
    tail = g_tail[:, pl.ds(t_size - 16, 16), :].reshape(devices * 16, 128)
    shape = (devices * 16, devices * 16)
    row = lax.broadcasted_iota(jnp.int32, shape, 0)
    column = lax.broadcasted_iota(jnp.int32, shape, 1)
    source = lax.rem(row, devices) * 16 + lax.div(row, devices)
    tail = dot_nn((column == source).astype(low), tail).astype(low)
    part = lambda i: tail[i * devices : (i + 1) * devices]
    vecs[...] = jnp.zeros_like(vecs)
    for i in range(5):
        vecs[pl.ds(i, 1), pl.ds(0, width)] = join_lanes(part(i), lines)
    vecs[pl.ds(5, 1), :] = join_lanes(part(5), hidden // devices)
    for i in (6, 7):
        vecs[pl.ds(i, 1), pl.ds(0, dec_width)] = join_lanes(part(i), dec_width // devices)
    gen_vec[...] = jnp.zeros_like(gen_vec)
    for i in range(6):
        gen_vec[pl.ds(i, 1), pl.ds(0, gen_rows.shape[0])] = join_lanes(part(8 + i), small)
    gen_vec[pl.ds(6, 1), :] = join_lanes(part(14), up_size // devices)

    pump(2)
    operands = gen_parts(gen_rows, gen_down, gen_vec, wave_code[...], up_size)
    seq = operands[0]
    final = gen_layer(*operands, LAT + NWAVE + 1)
    feature = (final[LAT : LAT + NWAVE] + seq[LAT : LAT + NWAVE]).astype(low)
    feature_out[...] = feature
    source = final[LAT + NWAVE : LAT + NWAVE + 8].astype(low)
    source_out[...] = source
    own = (dot_nn(feature, weight[...]) + weight_bias[...].astype(jnp.float32)).astype(low)
    for h in range(2):
        table[tile_rows(me * 2 + h, t_lines), :] = own[:, h * width : (h + 1) * width]
    t_gather.begin_z()
    t_gather.spread(0)
    pump(2)

    bias_at = gen_rows.shape[1] - gen_rows.shape[0] - width
    conv = dot_nn(source, gen_rows[:, pl.ds(bias_at, width)])[:1]
    t_gather.relay(0)
    seen = rows // chips
    grid_line = lax.broadcasted_iota(jnp.int32, (GRID, seen), 0)
    for chip in range(chips):
        patch = visible[pl.ds(chip, 1), :]
        for i, spot in enumerate((lax.div(patch, GRID), lax.rem(patch, GRID))):
            half = pl.ds(i * (width // 2), width // 2)
            picked = lax.dot_general(
                (spot == grid_line).astype(jnp.float32),
                places[...],
                (((0,), (0,)), ((), ())),
                precision=HIGH,
                preferred_element_type=jnp.float32,
            )
            start[pl.ds(chip * seen, seen), half] = (
                picked + conv[:, i * (width // 2) : (i + 1) * (width // 2)]
            )
    t_gather.spread(1)
    t_gather.relay(1)
    pump(2)
    span = 256
    bands_pix = pixels.shape[1]
    bands = waves.shape[1]
    band_of = lax.div(lax.broadcasted_iota(jnp.int32, (1, bands_pix), 1), bands_pix // bands)
    wave_lines = []
    for chip in range(chips):
        drop = jnp.zeros((1, 1), jnp.int32)
        for i, less in enumerate(BAND_DROP):
            drop = jnp.where(sensor[pl.ds(chip, 1), :] == i, less, drop)
        wave = jnp.full((1, bands_pix), -1, jnp.int32)
        for i in range(bands):
            wave = jnp.where(band_of == i, waves[pl.ds(chip, 1), pl.ds(i, 1)], wave)
        wave_lines.append(jnp.where(band_of < bands - drop, wave, -1))

    def slot_block(i, _):
        shape = (span, bands_pix)
        line = lax.broadcasted_iota(jnp.int32, shape, 0) + i * span
        column = lax.broadcasted_iota(jnp.int32, shape, 1)
        count = slots.shape[0] // NWAVE
        same = lax.div(line, NWAVE) == lax.rem(column, count)
        for chip in range(chips):
            chosen = same & (lax.rem(line, NWAVE) == wave_lines[chip])
            slots[tile_rows(i, span), pl.ds(chip * seen, seen)] = ndot(
                chosen.astype(jnp.float32).astype(low), pixels[pl.ds(chip * seen, seen), :]
            ).astype(low)
        return 0

    blocks = slots.shape[0] // span
    lax.fori_loop(0, blocks // 2, slot_block, 0)
    for k in range(2, planes):
        t_gather.spread(k)
        t_gather.relay(k)
    pump(2)
    lax.fori_loop(blocks // 2, blocks, slot_block, 0)
    keep(slots, slots_out)
    pump(4)
    for k in range(planes):
        t_gather.close(k)
    pump(2)
    t_gather.finish()
    keep(table, table_out)
    wide_span = 512

    def embed(i, _):
        at = tile_rows(i, wide_span)
        start[...] += tdot(slots[at, :], table[at, :])
        return 0

    lax.fori_loop(0, slots.shape[0] // wide_span, embed, 0)
    pump(len(steps))
    for item in heavy:
        item.finish()
    for copy in copies[2:]:
        copy.wait()
    wires.drain()


def prepare(planes, sizes, *args):
    (rows, width, hidden, dec_width, chips, up_size) = sizes
    devices = planes * 8
    low, full = jnp.bfloat16, jnp.float32
    qkv, up, out, dec, down = args[:5]
    gen_width = args[12].shape[1]
    tail = args[18].shape[0] + 16
    cols = qkv.shape[1] + up.shape[1] + out.shape[1] + dec.shape[1]
    shard = qkv.shape[0]
    slots = args[5].shape[1] // width * devices * NWAVE
    copies = 5 * gather_copies(planes) + 1
    shapes = (
        ((width, cols), low),
        ((hidden, width), low),
        ((slots, width), low),
        ((slots, rows), low),
        ((rows, width), full),
        ((gen_width, CHUNK * 16 * devices // gen_width), low),
        ((up_size, gen_width), low),
        ((8, up_size), full),
        ((8, hidden), full),
        ((NWAVE, gen_width), low),
        ((8, gen_width), low),
    )
    return pl.pallas_call(
        partial(prepare_kernel, planes, sizes),
        out_shape=tuple(jax.ShapeDtypeStruct(shape, dtype) for shape, dtype in shapes),
        in_specs=[VMEM] * len(args),
        out_specs=[ANY] * 4 + [VMEM] * 7,
        scratch_shapes=[
            pltpu.VMEM((devices * 16, CHUNK), low),
            pltpu.VMEM((devices, tail, 128), low),
            pltpu.VMEM((slots, width), low),
            pltpu.VMEM((slots, rows), low),
            pltpu.VMEM((shard, cols), low),
            pltpu.VMEM((shard, cols // 2), low),
            pltpu.VMEM((2 * shard, cols // 2), low),
            pltpu.VMEM((16, CHUNK), full),
            pltpu.VMEM((16, 128), full),
            pltpu.VMEM((16, CHUNK), low),
            pltpu.VMEM((tail, 128), low),
            pltpu.SemaphoreType.DMA((copies,)),
            pltpu.SemaphoreType.DMA((copies,)),
            pltpu.SemaphoreType.DMA((8,)),
        ],
        compiler_params=pltpu.CompilerParams(
            collective_id=0, has_side_effects=True, vmem_limit_bytes=60 * 2**20
        ),
    )(*args)


def forward_kernel(sizes, *refs):
    (rows, width, hidden, dec_width, chips, patches) = sizes
    (cotangent, start, wide, down, vecs, visible, order) = refs[:7]
    (
        ordered, returned, normed_out, joint_out, probs_out, context_out, middle_out, normed2_out,
        activ_out, slope_out, ending_out,
    ) = refs[7:18]
    (
        w_qkv, w_out, w_up, w_down, w_dec, normed, joint, probs, context, middle, normed2,
        activ, slope, ending, total, load_sem, keep_sem, send, recv,
    ) = refs[18:]
    low = jnp.bfloat16
    seen = rows // chips
    trade = Trade(cotangent, returned, send, recv, load_sem.at[5])
    trade.greet()
    trade.begin()
    loads, kept = [], []
    spans = ((0, 3 * width), (3 * width + hidden, width), (3 * width, hidden))
    spans += ((4 * width + hidden, dec_width),)
    for (at, size), dst in zip(spans, (w_qkv, w_out, w_up, w_dec)):
        loads.append((wide.at[:, pl.ds(at, size)], dst))
    loads.append((down, w_down))
    loads = [
        pltpu.make_async_copy(src, dst, load_sem.at[i]) for i, (src, dst) in enumerate(loads)
    ]
    for copy in loads:
        copy.start()

    def keep(src, dst):
        copy = pltpu.make_async_copy(src, dst, keep_sem.at[len(kept)])
        copy.start()
        kept.append(copy)

    def norm_into(src, dst, row):
        gain = vecs[pl.ds(row, 1), pl.ds(0, width)]
        shift = vecs[pl.ds(row + 1, 1), pl.ds(0, width)]

        def block(i, _):
            at = tile_rows(i, BLOCK)
            dst[at, :] = norm_rows(src[at, :], gain, shift).astype(low)
            return 0

        lax.fori_loop(0, rows // BLOCK, block, 0)

    norm_into(start, normed, 0)
    keep(normed, normed_out)
    loads[0].wait()

    def project(i, _):
        lane = pl.ds(pl.multiple_of(i * width, 128), width)
        joint[:, lane] = dot_nn(normed[...], w_qkv[:, lane]).astype(low)
        return 0

    lax.fori_loop(0, 3, project, 0)
    keep(joint, joint_out)
    pairs = width // 128
    head = width // HEADS
    scale = 1.0 / math.sqrt(head)
    odd = lax.broadcasted_iota(jnp.int32, (1, 128), 1) >= head

    def attend(n, _):
        at = tile_rows(lax.div(n, pairs), seen)
        pair = lax.rem(n, pairs)
        query, key, value = [
            joint[at, pl.ds(pl.multiple_of(pair * 128 + i * width, 128), 128)] for i in range(3)
        ]
        zero = jnp.zeros_like(query)
        parts = []
        for h in range(2):
            mine = odd if h else jnp.logical_not(odd)
            scores = ndot(jnp.where(mine, query, zero), key) * scale
            raised = jnp.exp(scores - jnp.max(scores, axis=-1, keepdims=True))
            prob = (raised / jnp.sum(raised, axis=-1, keepdims=True)).astype(low)
            probs[2 * n + h] = prob
            parts.append(dot_nn(prob, value))
        lane = pl.ds(pl.multiple_of(pair * 128, 128), 128)
        context[at, lane] = jnp.where(odd, parts[1], parts[0]).astype(low)
        return 0

    lax.fori_loop(0, chips * pairs, attend, 0)
    keep(probs, probs_out)
    keep(context, context_out)
    loads[1].wait()
    middle[...] = start[...] + dot_nn(context[...], w_out[...])
    keep(middle, middle_out)
    norm_into(middle, normed2, 2)
    keep(normed2, normed2_out)
    total[...] = middle[...] + vecs[pl.ds(4, 1), pl.ds(0, width)]
    loads[2].wait()
    loads[4].wait()

    def feed(t, _):
        at = tile_rows(t, FT)
        upper = dot_nn(normed2[...], w_up[:, at]) + vecs[pl.ds(5, 1), at]
        bell = 0.5 * (1.0 + lax.erf(upper * math.sqrt(0.5)))
        active = (upper * bell).astype(low)
        activ[:, at] = active
        tilt = upper * jnp.exp(-0.5 * upper * upper) * (1.0 / math.sqrt(2.0 * math.pi))
        slope[:, at] = (bell + tilt).astype(low)
        total[...] += dot_nn(active, w_down[at, :])
        return 0

    lax.fori_loop(0, hidden // FT, feed, 0)
    keep(activ, activ_out)
    keep(slope, slope_out)
    ending[...] = total[...].astype(low)
    keep(ending, ending_out)
    loads[3].wait()
    decoded = dot_nn(ending[...], w_dec[...]) + vecs[pl.ds(6, 1), pl.ds(0, dec_width)]
    total[:, pl.ds(0, dec_width)] = decoded
    mask = vecs[pl.ds(7, 1), pl.ds(0, dec_width)]
    blocks, _, lines, _ = ordered.shape
    for chip in range(chips):
        at = pl.ds(chip * seen, seen)
        chosen = (order[...] == visible[pl.ds(chip, 1), :]).astype(jnp.float32)
        found = jnp.sum(chosen, axis=1, keepdims=True) > 0.0
        placed = dot_nn(chosen.astype(low), total[at, pl.ds(0, dec_width)].astype(low))
        placed = jnp.where(found, placed, mask).astype(low)
        ordered[:, chip] = placed.reshape(blocks, lines, dec_width)
    for copy in kept:
        copy.wait()
    trade.finish()


def forward(sizes, devices, *args):
    (rows, width, hidden, dec_width, chips, patches) = sizes
    low, full = jnp.bfloat16, jnp.float32
    seen = rows // chips
    heads = chips * HEADS
    shapes = (
        ((devices, chips, patches // devices, dec_width), low),
        (args[0].shape, low),
        ((rows, width), low),
        ((rows, 3 * width), low),
        ((heads, seen, seen), low),
        ((rows, width), low),
        ((rows, width), full),
        ((rows, width), low),
        ((rows, hidden), low),
        ((rows, hidden), low),
        ((rows, width), low),
    )
    return pl.pallas_call(
        partial(forward_kernel, sizes),
        out_shape=tuple(jax.ShapeDtypeStruct(shape, dtype) for shape, dtype in shapes),
        in_specs=[ANY, VMEM, ANY, ANY] + [VMEM] * 3,
        out_specs=[VMEM] + [ANY] * 10,
        scratch_shapes=[
            pltpu.VMEM((width, 3 * width), low),
            pltpu.VMEM((width, width), low),
            pltpu.VMEM((width, hidden), low),
            pltpu.VMEM((hidden, width), low),
            pltpu.VMEM((width, dec_width), low),
        ]
        + [pltpu.VMEM(shape, dtype) for shape, dtype in shapes[2:]]
        + [
            pltpu.VMEM((rows, width), full),
            pltpu.SemaphoreType.DMA((6,)),
            pltpu.SemaphoreType.DMA((9,)),
            pltpu.SemaphoreType.DMA((devices,)),
            pltpu.SemaphoreType.DMA((devices,)),
        ],
        compiler_params=pltpu.CompilerParams(
            collective_id=1, has_side_effects=True, vmem_limit_bytes=60 * 2**20
        ),
    )(*args)


def gen_back(
    gen_rows, gen_down, gen_vec, wave_code, length, grad_feature, grad_source, sums, put_up, put_down
):
    up_size, width = gen_down.shape
    size = width // GHEADS
    scale = 1.0 / math.sqrt(size)
    total = lambda value: jnp.sum(value, axis=0, keepdims=True)
    chunk = up_size // 4

    def dot(left, right, dims):
        return lax.dot_general(
            left.astype(jnp.bfloat16),
            right.astype(jnp.bfloat16),
            (dims, ((), ())),
            preferred_element_type=jnp.float32,
        )

    nn = lambda left, right: dot(left, right, ((1,), (0,)))
    nt = lambda left, right: dot(left, right, ((1,), (1,)))
    tn = lambda left, right: dot(left, right, ((0,), (0,)))
    seq = gen_seq_of(gen_rows, wave_code, up_size)
    full = jnp.float32
    qkv = gen_rows[:, pl.ds(up_size, 3 * width)].astype(full)
    out = gen_rows[:, pl.ds(up_size + 3 * width, width)].astype(full)
    out_bias, gain1, shift1, down_bias, gain2, _ = [
        gen_vec[pl.ds(i, 1), pl.ds(0, width)] for i in range(6)
    ]
    joint = nn(seq, qkv)
    query, key, value = [joint[:, i * width : (i + 1) * width] for i in range(3)]
    lane = lax.broadcasted_iota(jnp.int32, (1, width), 1)
    spot = lax.broadcasted_iota(jnp.int32, (1, seq.shape[0]), 1)
    masks = [(lax.div(lane, size) == h).astype(full) for h in range(GHEADS)]
    probs = []
    context = jnp.zeros_like(seq)
    for mine in masks:
        scores = jnp.where(spot < length, nt(query * mine, key) * scale, -1e30)
        raised = jnp.exp(scores - jnp.max(scores, axis=-1, keepdims=True))
        probs.append(raised / jnp.sum(raised, axis=-1, keepdims=True))
        context = context + nn(probs[-1], value * mine)
    first = seq + nn(context, out) + out_bias
    mixed = norm_rows(first, gain1, shift1)

    def piece(i):
        at = pl.ds(pl.multiple_of(i * chunk, chunk), chunk)
        up = gen_rows[:, at].astype(full)
        down = gen_down[at, :].astype(full)
        inner = nn(mixed, up) + gen_vec[pl.ds(6, 1), at]
        return up, down, inner, 0.5 * (1.0 + lax.erf(inner * math.sqrt(0.5)))

    def ahead(i, so_far):
        _, down, inner, bell = piece(i)
        return so_far + nn(inner * bell, down)

    second = lax.fori_loop(0, 4, ahead, mixed + down_bias)
    rest = seq.shape[0] - LAT - NWAVE
    zeros = jnp.zeros((LAT, width), full)
    grad = jnp.concatenate([zeros, grad_feature, grad_source], axis=0)
    through, terms = norm_back(grad, second, gain2)
    g_gain2, g_shift2, g_down_bias = total(terms), total(grad), total(through)

    def behind(i, so_far):
        up, down, inner, bell = piece(i)
        put_down(i, tn(inner * bell, through))
        slope = bell + inner * jnp.exp(-0.5 * inner * inner) * (1.0 / math.sqrt(2.0 * math.pi))
        g_inner = nt(through, down) * slope
        put_up(i, tn(mixed, g_inner))
        sums[pl.ds(6, 1), pl.ds(pl.multiple_of(i * chunk, chunk), chunk)] = total(g_inner)
        return so_far + nt(g_inner, up)

    g_mixed = lax.fori_loop(0, 4, behind, through)
    through, terms = norm_back(g_mixed, first, gain1)
    g_gain1, g_shift1, g_out_bias = total(terms), total(g_mixed), total(through)
    g_out = tn(context, through)
    g_context = nt(through, out)
    g_query = g_key = g_value = jnp.zeros_like(seq)
    for mine, prob in zip(masks, probs):
        g_head = g_context * mine
        g_prob = nt(g_head, value)
        g_value = g_value + tn(prob, g_head)
        g_score = prob * (g_prob - jnp.sum(prob * g_prob, axis=-1, keepdims=True)) * scale
        g_query = g_query + nn(g_score, key * mine)
        g_key = g_key + tn(g_score, query * mine)
    g_joint = jnp.concatenate([g_query, g_key, g_value], axis=1)
    direct = jnp.concatenate([zeros, grad_feature, jnp.zeros((rest, width), full)], axis=0)
    g_seq = through + nt(g_joint, qkv) + direct
    thin = (g_out_bias, g_gain1, g_shift1, g_down_bias, g_gain2, g_shift2)
    return g_seq, tn(seq, g_joint), g_out, thin


def hand_out_kernel(planes, sizes, *refs):
    (width, hidden, dec_width, small) = sizes
    devices = planes * 8
    (
        s_dec, s_up, s_oq, s_down, kernels, kernel_sums, lines, g_wide, g_tall, g_seq, g_lines,
        g_bias,
    ) = refs[40:52]
    copies = [
        pltpu.make_async_copy(refs[i], refs[40 + i], refs[52].at[i]) for i in range(12)
    ]
    for copy in copies:
        copy.start()
    for copy in copies:
        copy.wait()
    outs = refs[12:40]
    (
        pre_gain, pre_shift, qkv, out, mid_gain, mid_shift, up, up_bias, down, down_bias, dec,
        dec_bias, mask, tokens, gen_qkv, gen_out, gen_out_bias, gain1, shift1, gen_up,
        gen_up_bias, gen_down, gen_down_bias, gain2, shift2, kernel_weight, kernel_bias, bias,
    ) = outs
    me = lax.axis_index("dp") * 4 + lax.axis_index("fsdp")
    qkv[...] = s_oq[:, pl.ds(width, 3 * width)]
    out[...] = s_oq[:, pl.ds(0, width)]
    up[...] = s_up[...]
    down[...] = s_down[...]
    dec[...] = s_dec[...]
    kernel_weight[...] = kernels[...]
    kernel_bias[...] = kernel_sums[...]
    gen_down[...] = g_tall[...]
    up_size = gen_up.shape[1]
    gen_width = gen_out.shape[1]
    gen_up[...] = g_wide[pl.ds(0, small), pl.ds(0, up_size)]
    gen_qkv[...] = g_wide[pl.ds(0, small), pl.ds(up_size, 3 * gen_width)]
    gen_out[...] = g_wide[pl.ds(0, small), pl.ds(up_size + 3 * gen_width, gen_width)]
    tokens[pl.ds(0, LAT), :] = g_seq[pl.ds(0, LAT), pl.ds(0, small)]
    tokens[pl.ds(LAT, 1), :] = g_seq[pl.ds(LAT + NWAVE, 1), pl.ds(0, small)]
    bias[...] = g_bias[pl.ds(0, small), :]

    def own(values, part):
        shape = (values.shape[1], 128)
        row = lax.broadcasted_iota(jnp.int32, shape, 0)
        lane = lax.broadcasted_iota(jnp.int32, shape, 1)
        pick = ((row == me * part + lane) & (lane < part)).astype(jnp.float32)
        return jnp.dot(values, pick, precision=HIGH, preferred_element_type=jnp.float32)

    at = NWAVE + width // 128

    def row_of(size):
        nonlocal at
        count = size // 128
        row = jnp.concatenate([lines[pl.ds(at + i, 1), :] for i in range(count)], axis=1)
        at += count
        return row

    def rows_of(sizes_):
        rows = [row_of(size) for size in sizes_]
        rows.append(jnp.zeros((8 - len(rows), rows[0].shape[1]), jnp.float32))
        return jnp.concatenate(rows, axis=0)

    def split(values, part, refs_):
        mine = own(values, part)
        for i, ref in enumerate(refs_):
            ref[...] = mine[i : i + 1, :part]

    split(rows_of((width,) * 5), width // devices, (pre_gain, pre_shift, mid_gain, mid_shift, down_bias))
    split(rows_of((hidden,)), hidden // devices, (up_bias,))
    split(rows_of((dec_width,) * 2), dec_width // devices, (dec_bias, mask))
    split(
        g_lines[:, pl.ds(0, gen_width)],
        small,
        (gen_out_bias, gain1, shift1, gen_down_bias, gain2, shift2),
    )
    split(
        jnp.concatenate(
            [g_lines[pl.ds(6, 1), :], jnp.zeros((7, up_size), jnp.float32)], axis=0
        ),
        up_size // devices,
        (gen_up_bias,),
    )


def hand_out(planes, sizes, *args):
    (width, hidden, dec_width, small) = sizes
    devices = planes * 8
    up_size = args[10].shape[1]
    gen_width = args[8].shape[1]
    wide, thin = width // devices, (1, width // devices)
    row = lambda size: (1, size // devices)
    shapes = (
        thin, thin, (wide, 3 * width), (wide, width), thin, thin, (wide, hidden), row(hidden),
        (hidden // devices, width), thin, (wide, dec_width), row(dec_width), row(dec_width),
        (LAT + 1, small), (small, 3 * gen_width), (small, gen_width), (1, small), (1, small),
        (1, small), (small, up_size), row(up_size), (up_size // devices, gen_width), (1, small),
        (1, small), (1, small), args[4].shape, args[5].shape, (small, width),
    )
    return pl.pallas_call(
        partial(hand_out_kernel, planes, sizes),
        out_shape=tuple(jax.ShapeDtypeStruct(shape, jnp.float32) for shape in shapes),
        in_specs=[ANY] * 12,
        out_specs=[VMEM] * 28,
        scratch_shapes=[pltpu.VMEM(item.shape, item.dtype) for item in args]
        + [pltpu.SemaphoreType.DMA((12,))],
        compiler_params=pltpu.CompilerParams(vmem_limit_bytes=60 * 2**20),
    )(*args)


def on_device_plain(
    pixels,
    sensor,
    band_wave,
    visible,
    block_order,
    pre_gain,
    pre_shift,
    qkv_weight,
    out_weight,
    mid_gain,
    mid_shift,
    up_weight,
    up_bias,
    down_weight,
    down_bias,
    dec_weight,
    dec_bias,
    mask_token,
    gen_tokens,
    gen_qkv,
    gen_out,
    gen_out_bias,
    gen_gain1,
    gen_shift1,
    gen_up,
    gen_up_bias,
    gen_down,
    gen_down_bias,
    gen_gain2,
    gen_shift2,
    kernel_weight,
    kernel_bias,
    bias_weight,
    cotangent,
):
    fetched = (
        lax.all_gather(pre_gain, AXES, axis=0, tiled=True),
        lax.all_gather(pre_shift, AXES, axis=0, tiled=True),
        lax.all_gather(qkv_weight, AXES, axis=0, tiled=True),
        lax.all_gather(out_weight, AXES, axis=0, tiled=True),
        lax.all_gather(mid_gain, AXES, axis=0, tiled=True),
        lax.all_gather(mid_shift, AXES, axis=0, tiled=True),
        lax.all_gather(up_weight, AXES, axis=0, tiled=True),
        lax.all_gather(up_bias, AXES, axis=0, tiled=True),
        lax.all_gather(down_weight, AXES, axis=0, tiled=True),
        lax.all_gather(down_bias, AXES, axis=0, tiled=True),
        lax.all_gather(dec_weight, AXES, axis=0, tiled=True),
        lax.all_gather(dec_bias, AXES, axis=0, tiled=True),
        lax.all_gather(mask_token, AXES, axis=0, tiled=True),
        lax.all_gather(gen_tokens, AXES, axis=1, tiled=True),
        lax.all_gather(gen_qkv, AXES, axis=0, tiled=True),
        lax.all_gather(gen_out, AXES, axis=0, tiled=True),
        lax.all_gather(gen_out_bias, AXES, axis=0, tiled=True),
        lax.all_gather(gen_gain1, AXES, axis=0, tiled=True),
        lax.all_gather(gen_shift1, AXES, axis=0, tiled=True),
        lax.all_gather(gen_up, AXES, axis=0, tiled=True),
        lax.all_gather(gen_up_bias, AXES, axis=0, tiled=True),
        lax.all_gather(gen_down, AXES, axis=0, tiled=True),
        lax.all_gather(gen_down_bias, AXES, axis=0, tiled=True),
        lax.all_gather(gen_gain2, AXES, axis=0, tiled=True),
        lax.all_gather(gen_shift2, AXES, axis=0, tiled=True),
        lax.all_gather(kernel_weight, AXES, axis=1, tiled=True),
        lax.all_gather(kernel_bias, AXES, axis=0, tiled=True),
        lax.all_gather(bias_weight, AXES, axis=0, tiled=True),
    )
    full_kernel = fetched[25]
    full_kernel_bias = fetched[26]
    full_bias_weight = fetched[27]
    (
        full_pre_gain,
        full_pre_shift,
        full_qkv,
        full_out,
        full_mid_gain,
        full_mid_shift,
        full_up,
        full_up_bias,
        full_down,
        full_down_bias,
        full_dec,
        full_dec_bias,
        full_mask,
    ) = fetched[:13]
    core32 = tuple((item.astype(jnp.float32) for item in fetched[13:25]))
    chips, seen, bands, pix = pixels.shape
    width = full_qkv.shape[0]
    head_dim = width // HEADS
    scale = 1.0 / math.sqrt(head_dim)
    dec_width = full_dec.shape[1]
    rows = chips * seen
    wave_code = lax.optimization_barrier(
        sincos(jnp.arange(NWAVE, dtype=jnp.float32), WD // 2).astype(jnp.bfloat16)
    ).astype(jnp.float32)
    (feature, source), core_back = jax.vjp(partial(gen_core, wave_code), *core32)
    feature_low = feature.astype(jnp.bfloat16)
    source_low = source.astype(jnp.bfloat16)
    conv_bias = jnp.dot(source_low[None, :], full_bias_weight, preferred_element_type=jnp.float32)[
        0
    ]
    kernels = (
        jnp.dot(feature_low, full_kernel, preferred_element_type=jnp.float32)
        + full_kernel_bias.astype(jnp.float32)[None, :]
    ).astype(jnp.bfloat16)
    valid = band_valid(sensor, bands)
    onehot = (band_wave[:, :, None] == jnp.arange(NWAVE, dtype=jnp.int32)[None, None, :]).astype(
        jnp.float32
    )
    place = place_code(visible, width)
    band_kernels = jnp.einsum(
        "cbw,wk->cbk", onehot.astype(jnp.bfloat16), kernels, preferred_element_type=jnp.float32
    ).astype(jnp.bfloat16)
    band_kernels = band_kernels.reshape(chips, bands, pix, width)
    masked = pixels * valid.astype(jnp.bfloat16)[:, None, :, None]
    embedded = jnp.einsum(
        "cvbp,cbpd->cvd", masked, band_kernels, preferred_element_type=jnp.float32
    )
    start = (embedded + conv_bias + place).reshape(rows, width)
    pre_gain32 = full_pre_gain.astype(jnp.float32)
    pre_shift32 = full_pre_shift.astype(jnp.float32)
    normed = norm_rows(start, pre_gain32, pre_shift32).astype(jnp.bfloat16)
    joint = jnp.dot(normed, full_qkv, preferred_element_type=jnp.float32).astype(jnp.bfloat16)
    joint = joint.reshape(chips, seen, 3, HEADS, head_dim)
    queries = joint[:, :, 0]
    keys = joint[:, :, 1]
    values = joint[:, :, 2]
    scores = (
        jnp.einsum("cqhe,ckhe->chqk", queries, keys, preferred_element_type=jnp.float32) * scale
    )
    peak = jnp.max(scores, axis=-1, keepdims=True)
    expd = jnp.exp(scores - peak)
    total = jnp.sum(expd, axis=-1, keepdims=True)
    probs = (expd / total).astype(jnp.bfloat16)
    log_total = peak + jnp.log(total)
    context = jnp.einsum("chqk,ckhe->cqhe", probs, values, preferred_element_type=jnp.float32)
    context = context.astype(jnp.bfloat16).reshape(rows, width)
    attended = jnp.dot(context, full_out, preferred_element_type=jnp.float32)
    middle = start + attended
    mid_gain32 = full_mid_gain.astype(jnp.float32)
    mid_shift32 = full_mid_shift.astype(jnp.float32)
    normed2 = norm_rows(middle, mid_gain32, mid_shift32).astype(jnp.bfloat16)
    upper = jnp.dot(normed2, full_up, preferred_element_type=jnp.float32) + full_up_bias.astype(
        jnp.float32
    )
    activ = exact_gelu(upper).astype(jnp.bfloat16)
    branch = jnp.dot(activ, full_down, preferred_element_type=jnp.float32) + full_down_bias.astype(
        jnp.float32
    )
    ending = (middle + branch).astype(jnp.bfloat16)
    decoded = jnp.dot(ending, full_dec, preferred_element_type=jnp.float32) + full_dec_bias.astype(
        jnp.float32
    )
    decoded = decoded.astype(jnp.bfloat16).reshape(chips, seen, dec_width)
    chip_ids = jnp.arange(chips, dtype=jnp.int32)[:, None]
    canvas = jnp.broadcast_to(full_mask, (chips, PATCH, dec_width))
    canvas = canvas.at[chip_ids, visible].set(decoded)
    ordered = jnp.take(canvas, block_order, axis=1)
    decoder_in = lax.all_to_all(ordered, AXES, split_axis=1, concat_axis=0, tiled=True)
    returned = lax.all_to_all(cotangent, AXES, split_axis=0, concat_axis=1, tiled=True)
    (
        full_pre_gain,
        full_pre_shift,
        full_qkv,
        full_out,
        full_mid_gain,
        full_mid_shift,
        full_up,
        full_up_bias,
        full_down,
        full_down_bias,
        full_dec,
        full_dec_bias,
        full_mask,
    ) = (
        lax.all_gather(pre_gain, AXES, axis=0, tiled=True),
        lax.all_gather(pre_shift, AXES, axis=0, tiled=True),
        lax.all_gather(qkv_weight, AXES, axis=0, tiled=True),
        lax.all_gather(out_weight, AXES, axis=0, tiled=True),
        lax.all_gather(mid_gain, AXES, axis=0, tiled=True),
        lax.all_gather(mid_shift, AXES, axis=0, tiled=True),
        lax.all_gather(up_weight, AXES, axis=0, tiled=True),
        lax.all_gather(up_bias, AXES, axis=0, tiled=True),
        lax.all_gather(down_weight, AXES, axis=0, tiled=True),
        lax.all_gather(down_bias, AXES, axis=0, tiled=True),
        lax.all_gather(dec_weight, AXES, axis=0, tiled=True),
        lax.all_gather(dec_bias, AXES, axis=0, tiled=True),
        lax.all_gather(mask_token, AXES, axis=0, tiled=True),
    )
    restored = jnp.zeros_like(returned).at[:, block_order].set(returned)
    seen_grad = jnp.take_along_axis(restored, visible[:, :, None], axis=1)
    grad_mask = jnp.sum(restored.astype(jnp.float32), axis=(0, 1)) - jnp.sum(
        seen_grad.astype(jnp.float32), axis=(0, 1)
    )
    grad_rows = seen_grad.reshape(rows, dec_width)
    grad_dec_weight = tdot(ending, grad_rows)
    grad_dec_bias = jnp.sum(grad_rows.astype(jnp.float32), axis=0)
    grad_ending = ndot(grad_rows, full_dec)
    grad_branch = grad_ending.astype(jnp.bfloat16)
    grad_down_bias = jnp.sum(grad_branch.astype(jnp.float32), axis=0)
    grad_down_weight = tdot(activ, grad_branch)
    grad_activ = ndot(grad_branch, full_down)
    gelu_out, gelu_back = jax.vjp(exact_gelu, upper)
    grad_upper = gelu_back(grad_activ)[0].astype(jnp.bfloat16)
    grad_up_bias = jnp.sum(grad_upper.astype(jnp.float32), axis=0)
    grad_up_weight = tdot(normed2, grad_upper)
    grad_normed2 = ndot(grad_upper, full_up)
    norm_out, norm_back = jax.vjp(norm_rows, middle, mid_gain32, mid_shift32)
    through_mid, grad_mid_gain, grad_mid_shift = norm_back(grad_normed2)
    grad_middle = grad_ending + through_mid
    grad_attended = grad_middle.astype(jnp.bfloat16)
    grad_out_weight = tdot(context, grad_attended)
    grad_context = (
        ndot(grad_attended, full_out).astype(jnp.bfloat16).reshape(chips, seen, HEADS, head_dim)
    )
    again_scores = (
        jnp.einsum("cqhe,ckhe->chqk", queries, keys, preferred_element_type=jnp.float32) * scale
    )
    probs_full = jnp.exp(again_scores - log_total)
    probs_low = probs_full.astype(jnp.bfloat16)
    grad_values = jnp.einsum(
        "chqk,cqhe->ckhe", probs_low, grad_context, preferred_element_type=jnp.float32
    ).astype(jnp.bfloat16)
    grad_probs = jnp.einsum(
        "cqhe,ckhe->chqk", grad_context, values, preferred_element_type=jnp.float32
    )
    row_dot = jnp.sum(probs_full * grad_probs, axis=-1, keepdims=True)
    grad_scores = (probs_full * (grad_probs - row_dot)).astype(jnp.bfloat16)
    grad_queries = (
        jnp.einsum("chqk,ckhe->cqhe", grad_scores, keys, preferred_element_type=jnp.float32) * scale
    ).astype(jnp.bfloat16)
    grad_keys = (
        jnp.einsum("chqk,cqhe->ckhe", grad_scores, queries, preferred_element_type=jnp.float32)
        * scale
    ).astype(jnp.bfloat16)
    grad_joint = jnp.stack([grad_queries, grad_keys, grad_values], axis=2).reshape(rows, 3 * width)
    grad_qkv_weight = tdot(normed, grad_joint)
    grad_normed = ndot(grad_joint, full_qkv)
    first_out, first_back = jax.vjp(norm_rows, start, pre_gain32, pre_shift32)
    through_pre, grad_pre_gain, grad_pre_shift = first_back(grad_normed)
    grad_start = grad_middle + through_pre
    grad_conv_part = jnp.sum(grad_start, axis=0)
    grad_embedded = grad_start.astype(jnp.bfloat16).reshape(chips, seen, width)
    grad_band = jnp.einsum(
        "cvbp,cvd->cbpd", masked, grad_embedded, preferred_element_type=jnp.float32
    )
    grad_band = grad_band.reshape(chips, bands, pix * width)
    grad_pixels = jnp.einsum(
        "cvd,cbpd->cvbp", grad_embedded, band_kernels, preferred_element_type=jnp.float32
    )
    grad_pixels = grad_pixels * valid[:, None, :, None]
    grad_kernels_part = jnp.einsum("cbw,cbk->wk", onehot, grad_band, precision=HIGH)
    kernel_sum, grad_conv = lax.psum((grad_kernels_part, grad_conv_part), AXES)
    kernel_low = kernel_sum.astype(jnp.bfloat16)
    own_low = own_part(kernel_low, 1)
    grad_kernel_weight = tdot(feature_low, own_low)
    grad_kernel_bias = jnp.sum(own_low.astype(jnp.float32), axis=0)
    grad_feature = ndot(kernel_low, full_kernel)
    grad_bias_weight = own_part(source_low.astype(jnp.float32)[:, None] * grad_conv[None, :], 0)
    grad_source = jnp.dot(full_bias_weight.astype(jnp.float32), grad_conv, precision=HIGH)
    core_grads = core_back((grad_feature, grad_source))
    summed = (
        lax.psum_scatter(grad_pre_gain, AXES, scatter_dimension=0, tiled=True),
        lax.psum_scatter(grad_pre_shift, AXES, scatter_dimension=0, tiled=True),
        lax.psum_scatter(grad_qkv_weight, AXES, scatter_dimension=0, tiled=True),
        lax.psum_scatter(grad_out_weight, AXES, scatter_dimension=0, tiled=True),
        lax.psum_scatter(grad_mid_gain, AXES, scatter_dimension=0, tiled=True),
        lax.psum_scatter(grad_mid_shift, AXES, scatter_dimension=0, tiled=True),
        lax.psum_scatter(grad_up_weight, AXES, scatter_dimension=0, tiled=True),
        lax.psum_scatter(grad_up_bias, AXES, scatter_dimension=0, tiled=True),
        lax.psum_scatter(grad_down_weight, AXES, scatter_dimension=0, tiled=True),
        lax.psum_scatter(grad_down_bias, AXES, scatter_dimension=0, tiled=True),
        lax.psum_scatter(grad_dec_weight, AXES, scatter_dimension=0, tiled=True),
        lax.psum_scatter(grad_dec_bias, AXES, scatter_dimension=0, tiled=True),
        lax.psum_scatter(grad_mask, AXES, scatter_dimension=0, tiled=True),
    )
    return (
        decoder_in,
        grad_pixels,
        summed[0],
        summed[1],
        summed[2],
        summed[3],
        summed[4],
        summed[5],
        summed[6],
        summed[7],
        summed[8],
        summed[9],
        summed[10],
        summed[11],
        summed[12],
        own_part(core_grads[0], 1),
        own_part(core_grads[1], 0),
        own_part(core_grads[2], 0),
        own_part(core_grads[3], 0),
        own_part(core_grads[4], 0),
        own_part(core_grads[5], 0),
        own_part(core_grads[6], 0),
        own_part(core_grads[7], 0),
        own_part(core_grads[8], 0),
        own_part(core_grads[9], 0),
        own_part(core_grads[10], 0),
        own_part(core_grads[11], 0),
        grad_kernel_weight,
        grad_kernel_bias,
        grad_bias_weight,
    )


def on_device(
    pixels,
    sensor,
    band_wave,
    visible,
    block_order,
    pre_gain,
    pre_shift,
    qkv_weight,
    out_weight,
    mid_gain,
    mid_shift,
    up_weight,
    up_bias,
    down_weight,
    down_bias,
    dec_weight,
    dec_bias,
    mask_token,
    gen_tokens,
    gen_qkv,
    gen_out,
    gen_out_bias,
    gen_gain1,
    gen_shift1,
    gen_up,
    gen_up_bias,
    gen_down,
    gen_down_bias,
    gen_gain2,
    gen_shift2,
    kernel_weight,
    kernel_bias,
    bias_weight,
    cotangent,
):
    arguments = (
        pixels,
        sensor,
        band_wave,
        visible,
        block_order,
        pre_gain,
        pre_shift,
        qkv_weight,
        out_weight,
        mid_gain,
        mid_shift,
        up_weight,
        up_bias,
        down_weight,
        down_bias,
        dec_weight,
        dec_bias,
        mask_token,
        gen_tokens,
        gen_qkv,
        gen_out,
        gen_out_bias,
        gen_gain1,
        gen_shift1,
        gen_up,
        gen_up_bias,
        gen_down,
        gen_down_bias,
        gen_gain2,
        gen_shift2,
        kernel_weight,
        kernel_bias,
        bias_weight,
        cotangent,
    )
    planes = lax.axis_size("dp") // 2
    devices = planes * 8
    if lax.axis_size("fsdp") != 4 or planes & (planes - 1) or pre_gain.shape[0] % 8:
        return on_device_plain(*arguments)
    low = jnp.bfloat16
    chips, seen, bands, pix = pixels.shape
    width = qkv_weight.shape[0] * devices
    hidden_width = up_weight.shape[1]
    head_dim = width // HEADS
    scale = 1.0 / math.sqrt(head_dim)
    dec_width = dec_weight.shape[1]
    rows = chips * seen
    gen_width = gen_qkv.shape[0] * devices
    up_size = gen_up.shape[1]
    thin = (
        pre_gain, pre_shift, mid_gain, mid_shift, down_bias, up_bias, dec_bias, mask_token,
        gen_out_bias, gen_gain1, gen_shift1, gen_down_bias, gen_gain2, gen_shift2, gen_up_bias,
    )
    thin = tuple(item.reshape(1, -1) for item in thin)
    wave_code = jnp.asarray(code_table(NWAVE, gen_width // 2).astype(low).astype(np.float32))
    valid = band_valid(sensor, bands)
    (
        full_wide, full_down, kernels, slots, start, gen_rows, gen_down_full, gen_vec, vecs,
        feature_low, source_low,
    ) = prepare(
        planes,
        (rows, width, hidden_width, dec_width, chips, up_size),
        qkv_weight,
        up_weight,
        out_weight,
        dec_weight,
        down_weight,
        kernel_weight,
        kernel_bias.reshape(1, -1),
        pixels.reshape(rows, bands * pix),
        sensor.reshape(chips, 1),
        band_wave,
        visible,
        jnp.asarray(code_table(GRID, width // 4)),
        wave_code,
        gen_up,
        gen_qkv,
        gen_out,
        bias_weight,
        gen_tokens,
        gen_down,
        *thin,
    )
    onehot = (band_wave[:, :, None] == jnp.arange(NWAVE, dtype=jnp.int32)[None, None, :]).astype(
        low
    )
    band_kernels = jnp.einsum(
        "cbw,pwd->cbpd",
        onehot,
        kernels.reshape(pix, NWAVE, width),
        preferred_element_type=jnp.float32,
    ).astype(low)
    sizes = (rows, width, hidden_width, dec_width, chips, PATCH)
    share = PATCH // devices
    order = block_order.reshape(PATCH, 1)
    (
        ordered, returned, normed, joint, probs, context, middle, normed2, activ, slope, ending,
    ) = forward(
        sizes,
        devices,
        cotangent.reshape(devices, chips, share, dec_width),
        start,
        full_wide,
        full_down,
        vecs,
        visible,
        order,
    )
    (
        sum_dec, sum_up, sum_oq, sum_down, grad_kernel_weight, grad_kernel_bias, sum_all,
        gen_wide, gen_tall, gen_seq, gen_lines, grad_bias_weight, grad_embedded, decoder_in,
    ) = backward(
        planes,
        sizes,
        ordered,
        returned.reshape(chips * PATCH, dec_width),
        visible,
        order,
        ending,
        full_wide,
        full_down,
        activ,
        slope,
        normed2,
        middle,
        context,
        joint,
        probs,
        normed,
        start,
        slots,
        vecs,
        kernel_weight,
        feature_low,
        source_low,
        gen_rows,
        gen_down_full,
        gen_vec,
        wave_code,
    )
    handed = hand_out(
        planes,
        (width, hidden_width, dec_width, gen_qkv.shape[0]),
        sum_dec, sum_up, sum_oq, sum_down, grad_kernel_weight, grad_kernel_bias, sum_all,
        gen_wide, gen_tall, gen_seq, gen_lines, grad_bias_weight,
    )
    flat = (0, 1, 4, 5, 7, 9, 11, 12, 16, 17, 18, 20, 22, 23, 24, 26)
    handed = [item.reshape(-1) if i in flat else item for i, item in enumerate(handed)]
    grad_embedded = grad_embedded.reshape(chips, seen, width)
    grad_pixels = jnp.einsum(
        "cvd,cbpd->cvbp", grad_embedded, band_kernels, preferred_element_type=jnp.float32
    )
    grad_pixels = grad_pixels * valid[:, None, :, None]
    decoder_in = decoder_in.reshape(devices * chips, share, dec_width)
    return (decoder_in, grad_pixels) + tuple(handed)


def solution(mesh):
    in_specs = (
        P(AXES, None, None, None),
        P(AXES),
        P(AXES, None),
        P(AXES, None),
        P(),
        P(AXES),
        P(AXES),
        P(AXES, None),
        P(AXES, None),
        P(AXES),
        P(AXES),
        P(AXES, None),
        P(AXES),
        P(AXES, None),
        P(AXES),
        P(AXES, None),
        P(AXES),
        P(AXES),
        P(None, AXES),
        P(AXES, None),
        P(AXES, None),
        P(AXES),
        P(AXES),
        P(AXES),
        P(AXES, None),
        P(AXES),
        P(AXES, None),
        P(AXES),
        P(AXES),
        P(AXES),
        P(None, AXES),
        P(AXES),
        P(AXES, None),
        P(None, AXES, None),
    )
    out_specs = (
        P(None, AXES, None),
        P(AXES, None, None, None),
        P(AXES),
        P(AXES),
        P(AXES, None),
        P(AXES, None),
        P(AXES),
        P(AXES),
        P(AXES, None),
        P(AXES),
        P(AXES, None),
        P(AXES),
        P(AXES, None),
        P(AXES),
        P(AXES),
        P(None, AXES),
        P(AXES, None),
        P(AXES, None),
        P(AXES),
        P(AXES),
        P(AXES),
        P(AXES, None),
        P(AXES),
        P(AXES, None),
        P(AXES),
        P(AXES),
        P(AXES),
        P(None, AXES),
        P(AXES),
        P(AXES, None),
    )
    return jax.shard_map(
        on_device, mesh=mesh, in_specs=in_specs, out_specs=out_specs, check_vma=False
    )
```

```python
from functools import partial
import math

import jax
import jax.numpy as jnp
import numpy as np
from jax import lax
from jax.experimental import pallas as pl
from jax.experimental.pallas import tpu as pltpu
from jax.sharding import PartitionSpec as P

HEADS = 12
WD = 128
GHEADS = 4
LAT = 128
NWAVE = 32
GRID = 32
PATCH = 1024


EPS = 1e-05
AXES = ("dp", "fsdp")
BAND_DROP = (0, 6, 9, 7)
HIGH = lax.Precision.HIGHEST


def sincos(values, count):
    freq = jnp.exp(jnp.arange(count, dtype=jnp.float32) * (-math.log(10000.0) / count))
    angle = values[..., None] * freq
    return jnp.concatenate([jnp.sin(angle), jnp.cos(angle)], axis=-1)


def code_table(count, size):
    freq = np.exp(np.arange(size, dtype=np.float32) * np.float32(-math.log(10000.0) / size))
    angle = np.arange(count, dtype=np.float32)[:, None] * freq.astype(np.float32)
    return np.concatenate([np.sin(angle), np.cos(angle)], axis=-1).astype(np.float32)


def norm_rows(rows, gain, shift):
    mean = jnp.mean(rows, axis=-1, keepdims=True)
    centred = rows - mean
    spread = jnp.mean(centred * centred, axis=-1, keepdims=True)
    return centred * lax.rsqrt(spread + EPS) * gain + shift


def exact_gelu(values):
    return jax.nn.gelu(values, approximate=False)


def band_valid(sensor, bands):
    drops = jnp.array(BAND_DROP, jnp.int32)
    picked = jnp.where(
        sensor[:, None] == jnp.arange(4, dtype=jnp.int32)[None, :], drops[None, :], 0
    )
    count = bands - jnp.sum(picked, axis=1)
    return (jnp.arange(bands, dtype=jnp.int32)[None, :] < count[:, None]).astype(jnp.float32)


def place_code(visible, width):
    row = (visible // GRID).astype(jnp.float32)
    col = (visible % GRID).astype(jnp.float32)
    return jnp.concatenate([sincos(row, width // 4), sincos(col, width // 4)], axis=-1)


def gen_core(
    wave_code,
    tokens,
    gen_qkv,
    gen_out,
    gen_out_bias,
    gen_gain1,
    gen_shift1,
    gen_up,
    gen_up_bias,
    gen_down,
    gen_down_bias,
    gen_gain2,
    gen_shift2,
):
    sequence = jnp.concatenate([tokens[:LAT], wave_code, tokens[LAT:]], axis=0)
    length = sequence.shape[0]
    width = sequence.shape[1]
    head_dim = width // GHEADS
    joint = jnp.dot(sequence, gen_qkv, precision=HIGH).reshape(length, 3, GHEADS, head_dim)
    scores = jnp.einsum("qhe,khe->hqk", joint[:, 0], joint[:, 1], precision=HIGH) / math.sqrt(
        head_dim
    )
    probs = jax.nn.softmax(scores, axis=-1)
    context = jnp.einsum("hqk,khe->qhe", probs, joint[:, 2], precision=HIGH).reshape(length, width)
    mixed = norm_rows(
        sequence + jnp.dot(context, gen_out, precision=HIGH) + gen_out_bias, gen_gain1, gen_shift1
    )
    hidden = jax.nn.gelu(jnp.dot(mixed, gen_up, precision=HIGH) + gen_up_bias, approximate=False)
    final = norm_rows(
        mixed + jnp.dot(hidden, gen_down, precision=HIGH) + gen_down_bias, gen_gain2, gen_shift2
    )
    feature = final[LAT : LAT + NWAVE] + sequence[LAT : LAT + NWAVE]
    return (feature, final[length - 1])


def own_part(full, dim):
    count = lax.axis_size("dp") * lax.axis_size("fsdp")
    index = lax.axis_index("dp") * lax.axis_size("fsdp") + lax.axis_index("fsdp")
    piece = full.shape[dim] // count
    return lax.dynamic_slice_in_dim(full, index * piece, piece, dim)


def tdot(left, right):
    return lax.dot_general(
        left, right, (((0,), (0,)), ((), ())), preferred_element_type=jnp.float32
    )


def ndot(left, right):
    return lax.dot_general(
        left, right, (((1,), (1,)), ((), ())), preferred_element_type=jnp.float32
    )


MESH_ID = pl.DeviceIdType.MESH
ANY = pl.BlockSpec(memory_space=pl.ANY)
VMEM = pl.BlockSpec(memory_space=pltpu.VMEM)


class Net:
    def __init__(self, planes):
        dp, fs = lax.axis_index("dp"), lax.axis_index("fsdp")
        self.planes = planes
        self.z, self.x = lax.div(dp, 2), lax.rem(dp, 2)
        self.y, self.c = lax.div(fs, 2), lax.rem(fs, 2)
        self.sib = self.at(self.z, self.x, self.y, 1 - self.c)
        self.nx = self.at(self.z, 1 - self.x, self.y, self.c)
        self.ny = self.at(self.z, self.x, 1 - self.y, self.c)

    def at(self, z, x, y, c):
        return (z * 2 + x, y * 2 + c)

    def plane(self, k):
        return lax.rem(self.z + k, self.planes)

    def zpeer(self, k):
        return self.at(self.plane(k), self.x, self.y, self.c)

    def chip(self, k, dx=0, dy=0):
        x = 1 - self.x if dx else self.x
        y = 1 - self.y if dy else self.y
        return self.plane(k) * 4 + x * 2 + y

    def greet(self):
        barrier = pltpu.get_barrier_semaphore()
        partners = [self.sib, self.nx, self.ny]
        partners += [self.zpeer(k) for k in range(1, self.planes)]
        for partner in partners:
            pl.semaphore_signal(barrier, inc=1, device_id=partner, device_id_type=MESH_ID)
        pl.semaphore_wait(barrier, len(partners))


class Wires:
    def __init__(self, send, recv):
        self.send, self.recv, self.used, self.started = send, recv, 0, []

    def push(self, src, dst, device):
        index = self.used
        self.used += 1
        copy = pltpu.make_async_remote_copy(
            src_ref=src,
            dst_ref=dst,
            send_sem=self.send.at[index],
            recv_sem=self.recv.at[index],
            device_id=device,
            device_id_type=MESH_ID,
        )
        copy.start()
        self.started.append(copy)
        return copy

    def drain(self):
        for copy in self.started:
            copy.wait_send()


class Gather:
    def __init__(self, net, wires, own, piece):
        self.net, self.wires, self.own, self.piece = net, wires, own, piece
        self.z_in, self.first, self.second, self.twins = {}, {}, {}, []

    def near(self, h):
        return self.net.ny if h else self.net.nx

    def far(self, h):
        return self.net.nx if h else self.net.ny

    def share(self, chip, h, src=None):
        spot = self.piece(chip, h)
        self.twins.append(self.wires.push(spot if src is None else src, spot, self.net.sib))

    def begin_z(self):
        for k in range(1, self.net.planes):
            for h in range(2):
                spot = self.piece(self.net.chip(0), h)
                self.z_in[k, h] = self.wires.push(self.own(h), spot, self.net.zpeer(k))

    def spread(self, k):
        back = (self.net.planes - k) % self.net.planes
        for h in range(2):
            if k:
                self.z_in[k, h].wait_recv()
            spot = self.piece(self.net.chip(back), h)
            src = self.own(h) if k == 0 else spot
            self.first[k, h] = self.wires.push(src, spot, self.near(h))
            self.second[k, h, 0] = self.wires.push(src, spot, self.far(h))
            self.share(self.net.chip(back), h, src)

    def relay(self, k):
        back = (self.net.planes - k) % self.net.planes
        for h in range(2):
            self.first[k, h].wait_recv()
            chip = self.net.chip(back, dx=h == 0, dy=h == 1)
            spot = self.piece(chip, h)
            self.second[k, h, 1] = self.wires.push(spot, spot, self.far(h))
            self.share(chip, h)

    def close(self, k):
        back = (self.net.planes - k) % self.net.planes
        for h in range(2):
            for hop in range(2):
                self.second[k, h, hop].wait_recv()
                chip = self.net.chip(back, dx=hop == 1 or h == 1, dy=hop == 1 or h == 0)
                self.share(chip, h)

    def finish(self):
        for copy in self.twins:
            copy.wait_recv()


def gather_copies(planes):
    return 2 * (planes - 1) + 4 * planes + 2 * planes + 8 * planes


class Reduce:
    def __init__(self, net, wires, part, held, near_in, far_in, z_in):
        self.net, self.wires, self.part, self.held = net, wires, part, held
        self.near_in, self.far_in, self.z_in = near_in, far_in, z_in
        self.pairs, self.near, self.far, self.along = {}, {}, {}, {}

    def add(self, spot, other):
        size = 16 if spot.shape[0] % 16 == 0 else 8

        def some(i, _):
            at = pl.ds(pl.multiple_of(i * size, size), size)
            total = spot[at].astype(jnp.float32) + other[at].astype(jnp.float32)
            spot[at] = total.astype(spot.dtype)
            return 0

        lax.fori_loop(0, spot.shape[0] // size, some, 0)

    def begin(self, k):
        for dx in range(2):
            for dy in range(2):
                for h in range(2):
                    chip = self.net.chip(k, dx, dy)
                    self.pairs[k, dx, dy, h] = self.wires.push(
                        self.part(chip, 1 - self.net.c, h), self.held.at[chip, h], self.net.sib
                    )

    def stage0(self, k):
        for dx, dy in ((1, 1), (0, 1), (1, 0), (0, 0)):
            for h in range(2):
                self.pairs[k, dx, dy, h].wait_recv()
                chip = self.net.chip(k, dx, dy)
                self.add(self.held.at[chip, h], self.part(chip, self.net.c, h))
                if (dy if h == 0 else dx) == 1:
                    other = dx if h == 0 else dy
                    self.near[k, h, other] = self.wires.push(
                        self.held.at[chip, h],
                        self.near_in.at[k, h, other],
                        self.net.ny if h == 0 else self.net.nx,
                    )

    def stage1(self, k):
        for h in range(2):
            for other in (1, 0):
                self.near[k, h, other].wait_recv()
                chip = self.net.chip(k, other, 0) if h == 0 else self.net.chip(k, 0, other)
                self.add(self.held.at[chip, h], self.near_in.at[k, h, other])
                if other:
                    self.far[k, h] = self.wires.push(
                        self.held.at[chip, h],
                        self.far_in.at[k, h],
                        self.net.nx if h == 0 else self.net.ny,
                    )

    def stage2(self, k):
        for h in range(2):
            self.far[k, h].wait_recv()
            spot = self.held.at[self.net.chip(k), h]
            self.add(spot, self.far_in.at[k, h])
            if k:
                self.along[k, h] = self.wires.push(spot, self.z_in.at[k - 1, h], self.net.zpeer(k))

    def total(self, h):
        value = self.held[self.net.chip(0), h].astype(jnp.float32)
        for k in range(1, self.net.planes):
            self.along[k, h].wait_recv()
            value = value + self.z_in[k - 1, h].astype(jnp.float32)
        return value


def reduce_copies(planes):
    return 8 * planes + 4 * planes + 2 * planes + 2 * (planes - 1)


def reduce_scratch(planes, rows, cols, dtype):
    return [
        pltpu.VMEM((planes * 4, 2, rows, cols), dtype),
        pltpu.VMEM((planes, 2, 2, rows, cols), dtype),
        pltpu.VMEM((planes, 2, rows, cols), dtype),
        pltpu.VMEM((planes - 1, 2, rows, cols), dtype),
    ]


def dot_nn(left, right):
    return jnp.dot(left, right, preferred_element_type=jnp.float32)


class Trade:
    def __init__(self, src, dst, send, recv, local):
        self.src, self.dst, self.send, self.recv = src, dst, send, recv
        self.count = src.shape[0]
        self.me = lax.axis_index("dp") * 4 + lax.axis_index("fsdp")
        self.own = pltpu.make_async_copy(src.at[self.me], dst.at[self.me], local)

    def place(self, i):
        to = lax.rem(self.me + i, self.count)
        return to, (lax.div(to, 4), lax.rem(to, 4))

    def greet(self):
        barrier = pltpu.get_barrier_semaphore()

        def call(i, _):
            pl.semaphore_signal(
                barrier, inc=1, device_id=self.place(i)[1], device_id_type=MESH_ID
            )
            return 0

        lax.fori_loop(1, self.count, call, 0)
        pl.semaphore_wait(barrier, self.count - 1)

    def copy(self, i):
        to, device = self.place(i)
        return pltpu.make_async_remote_copy(
            src_ref=self.src.at[to],
            dst_ref=self.dst.at[self.me],
            send_sem=self.send.at[i],
            recv_sem=self.recv.at[i],
            device_id=device,
            device_id_type=MESH_ID,
        )

    def begin(self, part=0, parts=1):
        def go(i, _):
            self.copy(i).start()
            return 0

        cuts = [1 + (self.count - 1) * p // parts for p in (part, part + 1)]
        lax.fori_loop(*cuts, go, 0)
        if part == 0:
            self.own.start()

    def finish(self):
        def end(i, _):
            self.copy(i).wait()
            return 0

        lax.fori_loop(1, self.count, end, 0)
        self.own.wait()


class Pump:
    def __init__(self):
        self.units, self.at, self.last = [], 0, False

    def put(self, item, order):
        for k in order:
            item.begin(k)
        self.units += [(item, k) for k in order]

    def step(self, count=1):
        for _ in range(count):
            if self.at >= len(self.units) and not self.last:
                return
            for stage, lag in enumerate(LAGS):
                at = self.at - lag
                if 0 <= at < len(self.units) and self.units[at]:
                    item, k = self.units[at]
                    (item.stage0, item.stage1, item.stage2)[stage](k)
            self.at += 1

    def until(self, item):
        self.last = True
        last = max(i for i, unit in enumerate(self.units) if unit and unit[0] is item)
        while self.at <= last + LAGS[2]:
            self.step()


def tile_rows(i, size):
    return pl.ds(pl.multiple_of(i * size, size), size)


def norm_back(grad, rows, gain):
    mean = jnp.mean(rows, axis=-1, keepdims=True)
    centred = rows - mean
    spread = jnp.mean(centred * centred, axis=-1, keepdims=True)
    inverse = lax.rsqrt(spread + EPS)
    unit = centred * inverse
    scaled = grad * gain
    inner = scaled - jnp.mean(scaled, axis=-1, keepdims=True)
    inner = inner - unit * jnp.mean(scaled * unit, axis=-1, keepdims=True)
    return inverse * inner, grad * unit


def lay_lines(box, at, value):
    for i in range(value.shape[1] // 128):
        box[0, pl.ds(at + i, 1), :] = value[:, i * 128 : (i + 1) * 128]
    return at + value.shape[1] // 128


def box_lines(waves, width, hidden, dec_width):
    used = waves + (6 * width + hidden + 2 * dec_width) // 128
    return used + (-used) % 8


FT = 256
TRADES = 1
LAGS = (0, 3, 6)
BUBBLES = 3
NORM_STEPS = 2
HEAD_STEPS = 1
FEED_STEPS = 1
BLOCK = 128


def backward_kernel(planes, steps, sizes, *refs):
    (rows, width, hidden, dec_width, chips, patches) = sizes
    devices = planes * 8
    seen = rows // chips
    (
        blocks, returned, visible, order, ending, wide, down, activ, slope, normed2, middle, context,
        joint, probs, normed, start, slots, gains, weight, feature, source, gen_rows, gen_down,
        gen_vec, wave_code,
    ) = refs[:25]
    (
        dec_out, up_out, oq_out, down_out, kw_out, kb_out, all_out, gen_wide, gen_tall, gen_seq,
        gen_lines, bias_out, embed_out, decoder_out,
    ) = refs[25:39]
    scratch = refs[39:61]
    (
        big, left, w_down, w_up, t_activ, t_slope, resid, w_sq, t_joint, t_probs,
        g_dec, g_up, g_down, g_oq, g_table, run, back, g_low, g_joint, v_sums,
        f_dec, f_up, f_oq, hand_dec, hand_up, hand_oq, box, send, recv, trade_send, trade_recv, tile_sem, load_sem,
    ) = refs[61:]
    loads = {}

    def load(name, src, dst):
        copy = pltpu.make_async_copy(src, dst, load_sem.at[len(loads)])
        copy.start()
        loads[name] = copy

    up_at, out_at, dec_at = 3 * width, 3 * width + hidden, 4 * width + hidden
    load("returned", returned, big)
    w_dec = w_sq.at[0, :, pl.ds(0, dec_width)]
    load("dec", wide.at[:, pl.ds(dec_at, dec_width)], w_dec)
    load("ending", ending, left.at[0])

    def tile_copies(t):
        slot = lax.rem(t, 2)
        at = tile_rows(t, FT)
        return (
            pltpu.make_async_copy(down.at[at], w_down.at[slot], tile_sem.at[slot, 0]),
            pltpu.make_async_copy(
                wide.at[:, pl.ds(pl.multiple_of(up_at + t * FT, 128), FT)],
                w_up.at[slot],
                tile_sem.at[slot, 1],
            ),
            pltpu.make_async_copy(activ.at[:, at], t_activ.at[slot], tile_sem.at[slot, 2]),
            pltpu.make_async_copy(slope.at[:, at], t_slope.at[slot], tile_sem.at[slot, 3]),
        )

    for copy in tile_copies(0):
        copy.start()
    load("normed2", normed2, left.at[1])
    load("middle", middle, resid)
    load("query", wide.at[:, pl.ds(0, width)], w_sq.at[1])

    net = Net(planes)
    trade = Trade(blocks, decoder_out, trade_send, trade_recv, load_sem.at[15])
    trade.greet()
    trade.begin(0, TRADES)
    wires = Wires(send, recv)
    pump = Pump()
    shard = width // (devices // 2)
    w_rows = lambda chip: pl.ds(pl.multiple_of(chip * shard, 16), shard)

    def quarter(ref, size):
        return lambda chip, c, h: ref.at[
            w_rows(chip), pl.ds(pl.multiple_of((c * 2 + h) * size, 128), size)
        ]

    def stripe(ref, size):
        return lambda chip, c, h: ref.at[
            pl.ds(pl.multiple_of(((chip * 2 + c) * 2 + h) * size, 16), size)
        ]

    q_dec, q_up = dec_width // 4, hidden // 8
    d_rows = hidden // devices // 2
    t_rows = g_table.shape[0] // devices // 2
    parts = (
        quarter(g_dec, q_dec),
        quarter(g_up.at[0], q_up),
        quarter(g_up.at[1], q_up),
        stripe(g_down, d_rows),
        stripe(g_table, t_rows),
        lambda chip, c, h: g_oq.at[c * 2 + h, w_rows(chip)],
    )
    lands = [scratch[i * 4 : i * 4 + 4] for i in range(5)]
    lands.append((scratch[20], lands[3][1], lands[3][2], scratch[21]))
    dec, up0, up1, downs, tables, oq = [
        Reduce(net, wires, part, *land) for part, land in zip(parts, lands)
    ]
    away = list(range(1, planes)) + [0]

    loads["returned"].wait()
    grad_mask = jnp.zeros((8, dec_width), jnp.float32)
    spread = big.reshape(devices, chips, patches // devices, dec_width)
    for chip in range(chips):
        got = spread[:, chip].reshape(patches, dec_width)
        chosen = (order[...] == visible[pl.ds(chip, 1), :]).astype(jnp.float32)
        picked = tdot(chosen.astype(jnp.bfloat16), got)
        g_joint[pl.ds(chip * seen, seen), pl.ds(0, dec_width)] = picked.astype(jnp.bfloat16)
        left_out = 1.0 - jnp.sum(chosen, axis=1, keepdims=True)
        left_out = jnp.broadcast_to(left_out, (patches, 8)).astype(jnp.bfloat16)
        grad_mask = grad_mask + tdot(left_out, got)
    v_sums[pl.ds(7, 1), pl.ds(dec_width, dec_width)] = grad_mask[:1]
    load("slots", slots, big)
    grad_rows = g_joint[:, pl.ds(0, dec_width)]
    v_sums[pl.ds(7, 1), pl.ds(0, dec_width)] = jnp.sum(
        grad_rows.astype(jnp.float32), axis=0, keepdims=True
    )
    loads["ending"].wait()

    def dec_part(i, _):
        at = tile_rows(i, FT)
        g_dec[at, :] = tdot(left[0, :, at], grad_rows).astype(jnp.bfloat16)
        return 0

    lax.fori_loop(0, width // FT, dec_part, 0)
    pump.put(dec, away)
    loads["dec"].wait()

    def end_part(i, _):
        at = tile_rows(i, FT)
        run[at, :] = ndot(g_joint[at, pl.ds(0, dec_width)], w_dec[...])
        g_low[at, :] = run[at, :].astype(jnp.bfloat16)
        return 0

    lax.fori_loop(0, rows // FT, end_part, 0)
    load("out", wide.at[:, pl.ds(out_at, width)], w_sq.at[0])
    load("context", context, left.at[0])
    back[...] = jnp.zeros_like(back)
    v_sums[pl.ds(0, 1), pl.ds(0, width)] = jnp.sum(
        g_low[...].astype(jnp.float32), axis=0, keepdims=True
    )
    loads["normed2"].wait()
    tiles = hidden // FT

    parts_sent = [1]

    def trade_more():
        if parts_sent[0] < TRADES:
            trade.begin(parts_sent[0], TRADES)
            parts_sent[0] += 1

    def feed(t, _):
        slot = lax.rem(t, 2)

        @pl.when(t + 1 < tiles)
        def _():
            for copy in tile_copies(t + 1):
                copy.start()

        for copy in tile_copies(t):
            copy.wait()
        grad = ndot(g_low[...], w_down[slot])
        grad_upper = (grad * t_slope[slot].astype(jnp.float32)).astype(jnp.bfloat16)
        at = tile_rows(t, FT)
        v_sums[pl.ds(1, 1), at] = jnp.sum(
            grad_upper.astype(jnp.float32), axis=0, keepdims=True
        )
        g_down[at, :] = tdot(t_activ[slot], g_low[...]).astype(jnp.bfloat16)
        g_up[lax.div(t, tiles // 2), :, tile_rows(lax.rem(t, tiles // 2), FT)] = tdot(
            left[1], grad_upper
        ).astype(jnp.bfloat16)
        for i in range(rows // FT):
            part = pl.ds(i * FT, FT)
            back[part, :] += ndot(grad_upper[i * FT : (i + 1) * FT], w_up[slot])
        return 0

    for i in range(0, tiles, 2):
        lax.fori_loop(i, i + 2, feed, 0)
        if i + 2 == tiles // 2:
            pump.put(up0, away)
        if i + 2 < tiles:
            trade_more()
            pump.step(FEED_STEPS)
    pump.put(up1, away)
    pump.put(downs, away)
    load("normed", normed, left.at[1])
    loads["middle"].wait()

    def through_norm(gain_row, sums_at):
        gain = gains[pl.ds(gain_row, 1), pl.ds(0, width)]

        def block(i, sums):
            at = tile_rows(i, BLOCK)
            grad = back[at, :]
            inner, terms = norm_back(grad, resid[at, :], gain)
            run[at, :] += inner
            return (
                sums[0] + jnp.sum(terms, axis=0, keepdims=True),
                sums[1] + jnp.sum(grad, axis=0, keepdims=True),
            )

        zero = jnp.zeros((1, width), jnp.float32)
        sums = lax.fori_loop(0, rows // BLOCK, block, (zero, zero))
        v_sums[pl.ds(sums_at, 1), pl.ds(0, width)] = sums[0]
        v_sums[pl.ds(sums_at + 1, 1), pl.ds(0, width)] = sums[1]

    through_norm(2, 2)
    pump.step(NORM_STEPS)
    load("start", start, resid)
    g_low[...] = run[...].astype(jnp.bfloat16)
    loads["context"].wait()
    loads["out"].wait()

    def out_part(i, _):
        at = tile_rows(i, FT)
        g_oq[0, at, :] = tdot(left[0, :, at], g_low[...]).astype(jnp.bfloat16)
        return 0

    lax.fori_loop(0, width // FT, out_part, 0)

    def context_part(i, _):
        at = tile_rows(i, FT)
        g_low[at, :] = ndot(g_low[at, :], w_sq[0]).astype(jnp.bfloat16)
        return 0

    lax.fori_loop(0, rows // FT, context_part, 0)
    load("key", wide.at[:, pl.ds(width, width)], w_sq.at[0])
    pump.step(2)

    pairs = width // 128
    head = width // HEADS
    scale = 1.0 / math.sqrt(head)
    odd = lax.broadcasted_iota(jnp.int32, (1, 128), 1) >= head

    def pair_copies(n):
        slot = lax.rem(n, 2)
        at = tile_rows(lax.div(n, pairs), seen)
        copies = [
            pltpu.make_async_copy(probs.at[pl.ds(2 * n, 2)], t_probs.at[slot], tile_sem.at[slot, 0])
        ]
        for i in range(3):
            lane = pl.ds(pl.multiple_of(lax.rem(n, pairs) * 128 + i * width, 128), 128)
            copies.append(
                pltpu.make_async_copy(
                    joint.at[at, lane], t_joint.at[slot, i], tile_sem.at[slot, i + 1]
                )
            )
        return copies

    for copy in pair_copies(0):
        copy.start()

    def attend(n, _):
        slot = lax.rem(n, 2)

        @pl.when(n + 1 < chips * pairs)
        def _():
            for copy in pair_copies(n + 1):
                copy.start()

        for copy in pair_copies(n):
            copy.wait()
        chip = lax.div(n, pairs)
        pair = lax.rem(n, pairs)
        at = tile_rows(chip, seen)
        lanes = [
            pl.ds(pl.multiple_of(pair * 128 + i * width, 128), 128) for i in range(3)
        ]
        query, key, value = [t_joint[slot, i] for i in range(3)]
        grad = g_low[at, lanes[0]]
        zero = jnp.zeros_like(grad)
        totals = [None, None, None]
        for h in range(2):
            mine = odd if h else jnp.logical_not(odd)
            grad_h = jnp.where(mine, grad, zero)
            query_h = jnp.where(mine, query, zero)
            key_h = jnp.where(mine, key, zero)
            prob = t_probs[slot, h]
            prob32 = prob.astype(jnp.float32)
            grad_prob = ndot(grad_h, value)
            row_dot = jnp.sum(prob32 * grad_prob, axis=-1, keepdims=True)
            grad_score = (prob32 * (grad_prob - row_dot)).astype(jnp.bfloat16)
            terms = (dot_nn(grad_score, key_h), tdot(grad_score, query_h), tdot(prob, grad_h))
            totals = [new if old is None else old + new for old, new in zip(totals, terms)]
        g_joint[at, lanes[0]] = (totals[0] * scale).astype(jnp.bfloat16)
        g_joint[at, lanes[1]] = (totals[1] * scale).astype(jnp.bfloat16)
        g_joint[at, lanes[2]] = totals[2].astype(jnp.bfloat16)
        return 0

    for i in range(0, chips * pairs, 2):
        lax.fori_loop(i, i + 2, attend, 0)
        trade_more()
        pump.step(HEAD_STEPS)

    loads["normed"].wait()
    def joint_part(i, _):
        which, at = lax.div(i, width // FT), tile_rows(lax.rem(i, width // FT), FT)
        lane = pl.ds(pl.multiple_of(which * width, 128), width)
        g_oq[which + 1, at, :] = tdot(left[1, :, at], g_joint[:, lane]).astype(jnp.bfloat16)
        return 0

    lax.fori_loop(0, 3 * width // FT, joint_part, 0)
    value = pltpu.make_async_copy(
        wide.at[:, pl.ds(2 * width, width)], w_sq.at[1], load_sem.at[len(loads)]
    )
    back[...] = jnp.zeros_like(back)

    def joint_back(i, _):
        for j, copy in enumerate((loads["query"], loads["key"], value)):

            @pl.when(i == j)
            def _():
                copy.wait()

        lane = pl.ds(pl.multiple_of(i * width, 128), width)

        def some(j, _):
            at = tile_rows(j, FT)
            back[at, :] += ndot(g_joint[at, lane], w_sq[lax.rem(i + 1, 2)])
            return 0

        lax.fori_loop(0, rows // FT, some, 0)

        @pl.when(i == 0)
        def _():
            value.start()

        return 0

    lax.fori_loop(0, 3, joint_back, 0)
    pump.step(1)
    loads["start"].wait()
    through_norm(0, 4)
    g_low[...] = run[...].astype(jnp.bfloat16)
    conv = jnp.sum(run[...], axis=0, keepdims=True)
    embed = pltpu.make_async_copy(g_low, embed_out, tile_sem.at[0, 1])
    embed.start()
    loads["slots"].wait()
    span = 512

    def table_block(i, _):
        at = tile_rows(i, span)
        g_table[at, :] = dot_nn(big[at, :], g_low[...]).astype(jnp.bfloat16)
        return 0

    lax.fori_loop(0, g_table.shape[0] // span, table_block, 0)
    pump.put(tables, away)
    pump.units += [None] * BUBBLES
    pump.put(oq, away)

    waves = t_rows
    lines = width // 128
    box[0, pl.ds(waves, box.shape[1] - waves), :] = jnp.zeros(
        (box.shape[1] - waves, 128), jnp.float32
    )
    at = lay_lines(box, waves, conv)
    for line in (4, 5, 2, 3, 0):
        at = lay_lines(box, at, v_sums[pl.ds(line, 1), pl.ds(0, width)])
    at = lay_lines(box, at, v_sums[pl.ds(1, 1), :])
    lay_lines(box, at, v_sums[pl.ds(7, 1), pl.ds(0, 2 * dec_width)])

    while parts_sent[0] < TRADES:
        trade_more()
    pump.until(tables)
    held = tables.held
    partial_sum = jnp.zeros((waves, 128), jnp.float32)
    for h in range(2):
        own = tables.total(h).astype(jnp.bfloat16)
        cols = pl.ds(h * width, width)
        kw_out[:, cols] = tdot(feature[...], own)
        kb_out[:, cols] = jnp.sum(own.astype(jnp.float32), axis=0, keepdims=True)
        partial_sum = partial_sum + ndot(own, weight[:, cols])
    box[0, pl.ds(0, waves), :] = partial_sum
    peers = [net.sib, net.nx, net.ny]
    for bit in range(steps):
        step = 1 << bit
        up = lax.rem(lax.div(net.z, step), 2) == 0
        peers.append(net.at(jnp.where(up, net.z + step, net.z - step), net.x, net.y, net.c))
    for i, peer in enumerate(peers):
        hop = wires.push(box.at[2 * i], box.at[2 * i + 1], peer)
        pump.step(1)
        hop.wait_recv()
        box[2 * i + 2] = box[2 * i] + box[2 * i + 1]
    end = box.at[2 * len(peers)]
    all_out[...] = end[...]
    me = net.chip(0) * 2 + net.c
    conv = jnp.concatenate(
        [end[pl.ds(waves + i, 1), :] for i in range(lines)], axis=1
    )
    gen_width = gen_rows.shape[0]
    up_size = gen_down.shape[0]
    bias_at = gen_rows.shape[1] - gen_width - width
    grad_source = lax.dot_general(
        jnp.broadcast_to(conv, (8, width)),
        gen_rows[:, pl.ds(bias_at, width)].astype(jnp.float32),
        (((1,), (1,)), ((), ())),
        precision=HIGH,
        preferred_element_type=jnp.float32,
    )
    top = lax.broadcasted_iota(jnp.int32, (8, gen_width), 0)
    grad_source = jnp.where(top == 0, grad_source, 0.0)
    pump.step(1)
    small = gen_width // devices
    lane = lax.broadcasted_iota(jnp.int32, (8, gen_width), 1)
    pick = ((lane == me * small + top) & (top < small)).astype(jnp.float32)
    exact = partial(
        lax.dot_general, precision=HIGH, preferred_element_type=jnp.float32
    )
    rows_of = lambda value: exact(pick, value, (((1,), (0,)), ((), ())))
    lanes_of = lambda value: exact(value, pick, (((1,), (1,)), ((), ())))
    chunk = up_size // 4

    def put_up(i, value):
        gen_wide[:, pl.ds(pl.multiple_of(i * chunk, chunk), chunk)] = rows_of(value)

    def put_down(i, value):
        back[:, pl.ds(pl.multiple_of(i * gen_width, gen_width), gen_width)] = value

    g_seq, g_qkv, g_out, thin = gen_back(
        gen_rows, gen_down, gen_vec, wave_code[...], LAT + NWAVE + 1, end[pl.ds(0, waves), :],
        grad_source, v_sums, put_up, put_down,
    )
    pump.step(2)
    gen_wide[:, pl.ds(up_size, 3 * gen_width)] = rows_of(g_qkv)
    gen_wide[:, pl.ds(up_size + 3 * gen_width, gen_width)] = rows_of(g_out)
    tall = up_size // devices
    per = devices // 4
    gen_tall[...] = back[
        tile_rows(lax.rem(me, per), tall),
        pl.ds(pl.multiple_of(lax.div(me, per) * gen_width, 128), gen_width),
    ]
    gen_seq[...] = lanes_of(g_seq)
    for i, value in enumerate(thin):
        gen_lines[pl.ds(i, 1), pl.ds(0, gen_width)] = value
    gen_lines[pl.ds(6, 1), :] = v_sums[pl.ds(6, 1), pl.ds(0, up_size)]
    own_source = jnp.sum(
        pick * source[pl.ds(0, 1), :].astype(jnp.float32), axis=1, keepdims=True
    )
    bias_out[...] = own_source * conv
    pump.until(oq)
    half = shard // 2
    own_rows = pl.ds(pl.multiple_of(net.c * half, 8), half)
    their_rows = pl.ds(pl.multiple_of((1 - net.c) * half, 8), half)
    jobs = (
        (dec, f_dec, hand_dec, dec_out, 0, q_dec),
        (up0, f_up.at[0], hand_up.at[0], up_out, 0, q_up),
        (up1, f_up.at[1], hand_up.at[1], up_out, hidden // 2, q_up),
        (oq, f_oq, hand_oq, oq_out, 0, width),
    )
    swaps = []
    for item, final, hand, out, base, size in jobs:
        for h in range(2):
            final[h] = item.total(h)
            swaps.append(wires.push(final.at[h, their_rows], hand.at[h], net.sib))
    for h in range(2):
        down_out[pl.ds(h * d_rows, d_rows)] = downs.total(h)
    for item, final, hand, out, base, size in jobs:
        for h in range(2):
            own = pl.ds(pl.multiple_of(base + (net.c * 2 + h) * size, 128), size)
            other = pl.ds(pl.multiple_of(base + ((1 - net.c) * 2 + h) * size, 128), size)
            out[:, own] = final[h, own_rows]
            swaps.pop(0).wait_recv()
            out[:, other] = hand[h]
    embed.wait()
    trade.finish()
    wires.drain()


def backward(planes, sizes, *args):
    (rows, width, hidden, dec_width, chips, patches) = sizes
    devices = planes * 8
    steps = (planes - 1).bit_length()
    low, full = jnp.bfloat16, jnp.float32
    shard = width // (devices // 2)
    q_dec, q_up = dec_width // 4, hidden // 8
    d_rows = hidden // devices // 2
    slots = args[16].shape[0]
    t_rows = slots // devices // 2
    box_rows = box_lines(t_rows, width, hidden, dec_width)
    up_size, gen_width = args[22].shape
    copies = 6 * reduce_copies(planes) + 3 + steps + 8
    scratch = []
    for shape in (
        (shard, q_dec), (shard, q_up), (shard, q_up), (d_rows, width), (t_rows, width),
    ):
        scratch += reduce_scratch(planes, *shape, low)
    assert d_rows == shard
    last = reduce_scratch(planes, shard, width, low)
    scratch += [last[0], last[3]]
    scratch += [
        pltpu.VMEM((chips * patches, dec_width), low),
        pltpu.VMEM((2, rows, width), low),
        pltpu.VMEM((2, FT, width), low),
        pltpu.VMEM((2, width, FT), low),
        pltpu.VMEM((2, rows, FT), low),
        pltpu.VMEM((2, rows, FT), low),
        pltpu.VMEM((rows, width), full),
        pltpu.VMEM((2, width, width), low),
        pltpu.VMEM((2, 3, rows // chips, 128), low),
        pltpu.VMEM((2, 2, rows // chips, rows // chips), low),
        pltpu.VMEM((width, dec_width), low),
        pltpu.VMEM((2, width, hidden // 2), low),
        pltpu.VMEM((hidden, width), low),
        pltpu.VMEM((4, width, width), low),
        pltpu.VMEM((slots, width), low),
        pltpu.VMEM((rows, width), full),
        pltpu.VMEM((rows, width), full),
        pltpu.VMEM((rows, width), low),
        pltpu.VMEM((rows, 3 * width), low),
        pltpu.VMEM((8, hidden), full),
        pltpu.VMEM((2, shard, q_dec), full),
        pltpu.VMEM((2, 2, shard, q_up), full),
        pltpu.VMEM((2, shard, width), full),
        pltpu.VMEM((2, shard // 2, q_dec), full),
        pltpu.VMEM((2, 2, shard // 2, q_up), full),
        pltpu.VMEM((2, shard // 2, width), full),
        pltpu.VMEM((2 * (3 + steps) + 1, box_rows, 128), full),
        pltpu.SemaphoreType.DMA((copies,)),
        pltpu.SemaphoreType.DMA((copies,)),
        pltpu.SemaphoreType.DMA((devices,)),
        pltpu.SemaphoreType.DMA((devices,)),
        pltpu.SemaphoreType.DMA((2, 4)),
        pltpu.SemaphoreType.DMA((16,)),
    ]
    shapes = (
        ((width // devices, dec_width), full),
        ((width // devices, hidden), full),
        ((width // devices, 4 * width), full),
        ((hidden // devices, width), full),
        ((args[19].shape[1], 2 * width), full),
        ((1, 2 * width), full),
        ((box_rows, 128), full),
        ((8, up_size + 4 * gen_width), full),
        ((up_size // devices, gen_width), full),
        ((args[24].shape[0] + gen_width + 8, 8), full),
        ((8, up_size), full),
        ((8, width), full),
        ((rows, width), low),
        (args[0].shape, low),
    )
    spots = [ANY, ANY, VMEM, VMEM] + [ANY] * 13 + [VMEM] * 8
    return pl.pallas_call(
        partial(backward_kernel, planes, steps, sizes),
        out_shape=tuple(jax.ShapeDtypeStruct(shape, dtype) for shape, dtype in shapes),
        in_specs=spots,
        out_specs=[VMEM] * 12 + [ANY] * 2,
        scratch_shapes=scratch,
        compiler_params=pltpu.CompilerParams(
            collective_id=2, has_side_effects=True, vmem_limit_bytes=125 * 2**19
        ),
    )(*args)


CHUNK = 896
TRADE_PARTS = 1


def gen_layer(
    seq, qkv, out, out_bias, gain1, shift1, up, up_bias, down, down_bias, gain2, shift2, length
):
    width = seq.shape[1]
    size = width // GHEADS

    def times(left, right):
        return jnp.dot(left, right, precision=HIGH, preferred_element_type=jnp.float32)

    joint = times(seq, qkv)
    query, key, value = [joint[:, i * width : (i + 1) * width] for i in range(3)]
    lane = lax.broadcasted_iota(jnp.int32, (1, width), 1)
    spot = lax.broadcasted_iota(jnp.int32, (1, seq.shape[0]), 1)
    context = jnp.zeros_like(seq)
    for h in range(GHEADS):
        mine = (lax.div(lane, size) == h).astype(jnp.float32)
        scores = lax.dot_general(
            query * mine,
            key,
            (((1,), (1,)), ((), ())),
            precision=HIGH,
            preferred_element_type=jnp.float32,
        ) * (1.0 / math.sqrt(size))
        scores = jnp.where(spot < length, scores, -1e30)
        peak = lax.stop_gradient(jnp.max(scores, axis=-1, keepdims=True))
        raised = jnp.exp(scores - peak)
        probs = raised / jnp.sum(raised, axis=-1, keepdims=True)
        context = context + times(probs, value * mine)
    mixed = norm_rows(seq + times(context, out) + out_bias, gain1, shift1)
    inner = times(mixed, up) + up_bias
    hidden = 0.5 * inner * (1.0 + lax.erf(inner * math.sqrt(0.5)))
    return norm_rows(mixed + times(hidden, down) + down_bias, gain2, shift2)


def gen_seq_of(gen_rows, wave_code, up_size):
    width = gen_rows.shape[0]
    full = jnp.float32
    tokens = gen_rows[:, pl.ds(up_size + 4 * width, width)].astype(full).T
    last = gen_rows[:, pl.ds(gen_rows.shape[1] - width, width)].astype(full).T
    return jnp.concatenate([tokens, wave_code, last[:8]], axis=0)


def gen_parts(gen_rows, gen_down, gen_vec, wave_code, up_size):
    width = gen_rows.shape[0]
    full = jnp.float32
    at = up_size
    up = gen_rows[:, pl.ds(0, up_size)].astype(full)
    qkv = gen_rows[:, pl.ds(at, 3 * width)].astype(full)
    out = gen_rows[:, pl.ds(at + 3 * width, width)].astype(full)
    seq = gen_seq_of(gen_rows, wave_code, up_size)
    vec = [gen_vec[pl.ds(i, 1), pl.ds(0, width)] for i in range(6)]
    up_bias = gen_vec[pl.ds(6, 1), :]
    down = gen_down[...].astype(full)
    return (seq, qkv, out, vec[0], vec[1], vec[2], up, up_bias, down, vec[3], vec[4], vec[5])


def join_lanes(parts, size):
    owners = parts.shape[0]
    shape = (128, owners * size)
    lane = lax.broadcasted_iota(jnp.int32, shape, 0)
    column = lax.broadcasted_iota(jnp.int32, shape, 1)
    spread = dot_nn(parts, (lax.rem(column, size) == lane).astype(parts.dtype))
    shape = (owners, owners * size)
    row = lax.broadcasted_iota(jnp.int32, shape, 0)
    column = lax.broadcasted_iota(jnp.int32, shape, 1)
    return jnp.sum(
        jnp.where(lax.div(column, size) == row, spread, 0.0), axis=0, keepdims=True
    )


def prepare_kernel(planes, sizes, *refs):
    (rows, width, hidden, dec_width, chips, up_size, patches) = sizes
    devices = planes * 8
    (
        qkv, up, out, dec, down, weight, weight_bias, pixels, sensor, waves, visible, places,
        wave_code, gen_up, gen_qkv, gen_out, bias_weight, gen_tokens, gen_low, cotangent, order,
    ) = refs[:21]
    thin = refs[21:36]
    (
        wide_out, down_out, table_out, slots_out, returned, normed_out, joint_out, probs_out,
        context_out, middle_out, normed2_out, activ_out, slope_out, ending_out, start_out, ordered,
        gen_rows, gen_down, gen_vec, vecs, feature_out, source_out,
    ) = refs[36:58]
    (
        g_rows, g_tail, table, slots, wide, fresh, joined, rows32, tail32, s_rows, s_tail, w_qkv,
        w_out, w_up, w_down, w_dec, normed, joint, probs, context, middle, normed2, activ, slope,
        ending, start, total, send, recv, trade_send, trade_recv, local, load_sem, keep_sem,
    ) = refs[58:]
    net = Net(planes)
    trade = Trade(cotangent, returned, trade_send, trade_recv, load_sem.at[5])
    trade.greet()
    sent = [0]

    def trade_more(count=1):
        for _ in range(count):
            if sent[0] < TRADE_PARTS:
                trade.begin(sent[0], TRADE_PARTS)
                sent[0] += 1

    seen = rows // chips
    loads, stashed = [], []
    spans = ((0, 3 * width), (3 * width + hidden, width), (3 * width, hidden))
    spans += ((4 * width + hidden, dec_width),)
    for (at, size), dst in zip(spans, (w_qkv, w_out, w_up, w_dec)):
        loads.append((wide_out.at[:, pl.ds(at, size)], dst))
    loads.append((down_out, w_down))
    loads = [
        pltpu.make_async_copy(src, dst, load_sem.at[i]) for i, (src, dst) in enumerate(loads)
    ]

    def stash(src, dst):
        copy = pltpu.make_async_copy(src, dst, keep_sem.at[len(stashed)])
        copy.start()
        stashed.append(copy)

    wires = Wires(send, recv)
    me = net.chip(0) * 2 + net.c
    low = jnp.bfloat16
    copies = []

    def keep(src, dst):
        copy = pltpu.make_async_copy(src, dst, local.at[len(copies)])
        copy.start()
        copies.append(copy)

    small = gen_up.shape[0]
    gen_width = gen_out.shape[1]
    shape = (gen_tokens.shape[0], 2 * gen_width)
    row = lax.broadcasted_iota(jnp.int32, shape, 0)
    column = lax.broadcasted_iota(jnp.int32, shape, 1)
    turned = tdot(gen_tokens[...], (row == column).astype(low))
    line = jnp.concatenate(
        [item[...].astype(jnp.float32) for item in (gen_up, gen_qkv, gen_out)]
        + [turned[:, :gen_width], bias_weight[...].astype(jnp.float32), turned[:, gen_width:]],
        axis=1,
    )
    for q in range(16 // small):
        rows32[pl.ds(q * small, small), :] = line[:, q * CHUNK : (q + 1) * CHUNK]
    s_rows[...] = rows32[...].astype(low)
    tail32[...] = jnp.zeros_like(tail32)
    for i, item in enumerate(thin):
        tail32[pl.ds(i, 1), pl.ds(0, item.shape[1])] = item[...].astype(jnp.float32)
    s_tail[pl.ds(0, gen_low.shape[0]), :] = gen_low[...]
    s_tail[pl.ds(gen_low.shape[0], 16), :] = tail32[...].astype(low)
    r_size, r_cols = s_rows.shape
    r_cut = (r_cols // 256) * 128 + 128
    r_span = lambda h: pl.ds(r_cut * h, r_cols - r_cut if h else r_cut)
    t_size = s_tail.shape[0]
    t_cut = (t_size // 32) * 16 + 16
    t_span = lambda h: pl.ds(t_cut * h, t_size - t_cut if h else t_cut)
    smalls = [
        Gather(
            net,
            wires,
            lambda h: s_rows.at[:, r_span(h)],
            lambda chip, h: g_rows.at[tile_rows(chip * 2 + net.c, r_size), r_span(h)],
        ),
        Gather(
            net,
            wires,
            lambda h: s_tail.at[t_span(h)],
            lambda chip, h: g_tail.at[chip * 2 + net.c, t_span(h)],
        ),
    ]
    for item in smalls:
        item.begin_z()
        item.spread(0)
    keep(s_rows, g_rows.at[tile_rows(me, r_size)])
    keep(s_tail, g_tail.at[me])

    at = 0
    for item in (qkv, up, out, dec):
        wide[:, pl.ds(at, item.shape[1])] = item[...]
        at += item.shape[1]
    w_cols = at // 2
    quarter = w_cols // 2
    shard = wide.shape[0]
    mine = pl.ds(pl.multiple_of(net.c * w_cols, 128), w_cols)
    theirs = pl.ds(pl.multiple_of((1 - net.c) * w_cols, 128), w_cols)
    pair = wires.push(wide.at[:, theirs], fresh, net.sib)
    d_rows = down.shape[0]
    d_half = d_rows // 2
    d_own = lambda h: down.at[pl.ds(h * d_half, d_half)]
    d_piece = lambda chip, h: down_out.at[
        pl.ds(pl.multiple_of((chip * 2 + net.c) * d_rows + h * d_half, 16), d_half)
    ]
    w_own = lambda h: joined.at[:, pl.ds(h * quarter, quarter)]
    w_piece = lambda chip, h: wide_out.at[
        pl.ds(pl.multiple_of(chip * 2 * shard, 16), 2 * shard),
        pl.ds(pl.multiple_of((net.c * 2 + h) * quarter, 128), quarter),
    ]
    t_lines = table.shape[0] // devices // 2
    t_piece = lambda chip, h: table.at[tile_rows((chip * 2 + net.c) * 2 + h, t_lines)]
    t_own = lambda h: table.at[tile_rows(me * 2 + h, t_lines)]
    d_gather = Gather(net, wires, d_own, d_piece)
    w_gather = Gather(net, wires, w_own, w_piece)
    t_gather = Gather(net, wires, t_own, t_piece)
    d_gather.begin_z()
    for item in smalls:
        item.relay(0)
    pair.wait_recv()
    own32 = wide[:, mine].astype(jnp.float32)
    sib32 = fresh[...].astype(jnp.float32)
    first = net.c == 0
    joined[...] = jnp.concatenate(
        [jnp.where(first, own32, sib32), jnp.where(first, sib32, own32)], axis=0
    ).astype(low)
    for k in range(1, planes):
        for item in smalls:
            item.spread(k)
        for item in smalls:
            item.relay(k)
    w_gather.begin_z()
    for h in range(2):
        keep(w_own(h), w_piece(net.chip(0), h))
        keep(d_own(h), d_piece(net.chip(0), h))
    for k in range(planes):
        for item in smalls:
            item.close(k)
    w_gather.spread(0)
    d_gather.spread(0)
    steps = [partial(w_gather.relay, 0)]
    for k in range(1, planes):
        steps += [partial(w_gather.spread, k), partial(w_gather.relay, k)]
    steps.append(partial(d_gather.relay, 0))
    for k in range(1, planes):
        steps += [partial(d_gather.spread, k), partial(d_gather.relay, k)]
        steps.append(partial(w_gather.close, k - 1))
    steps.append(partial(w_gather.close, planes - 1))
    steps += [partial(d_gather.close, k) for k in range(planes)]

    def pump(count):
        for _ in range(min(count, len(steps))):
            steps.pop(0)()

    for item in smalls:
        item.finish()
    for copy in copies[:2]:
        copy.wait()

    lines = width // devices
    groups = r_size // small
    shape = (gen_rows.shape[0], devices * r_size)
    row = lax.broadcasted_iota(jnp.int32, shape, 0)
    column = lax.broadcasted_iota(jnp.int32, shape, 1)
    for q in range(groups):
        source = lax.div(row, small) * r_size + q * small + lax.rem(row, small)
        gen_rows[:, pl.ds(q * r_cols, r_cols)] = dot_nn(
            (column == source).astype(low), g_rows[...]
        ).astype(low)
    gen_down[...] = g_tail[:, pl.ds(0, t_size - 16), :].reshape(gen_down.shape)
    tail = g_tail[:, pl.ds(t_size - 16, 16), :].reshape(devices * 16, 128)
    shape = (devices * 16, devices * 16)
    row = lax.broadcasted_iota(jnp.int32, shape, 0)
    column = lax.broadcasted_iota(jnp.int32, shape, 1)
    source = lax.rem(row, devices) * 16 + lax.div(row, devices)
    tail = dot_nn((column == source).astype(low), tail).astype(low)
    part = lambda i: tail[i * devices : (i + 1) * devices]
    vecs[...] = jnp.zeros_like(vecs)
    for i in range(5):
        vecs[pl.ds(i, 1), pl.ds(0, width)] = join_lanes(part(i), lines)
    vecs[pl.ds(5, 1), :] = join_lanes(part(5), hidden // devices)
    for i in (6, 7):
        vecs[pl.ds(i, 1), pl.ds(0, dec_width)] = join_lanes(part(i), dec_width // devices)
    gen_vec[...] = jnp.zeros_like(gen_vec)
    for i in range(6):
        gen_vec[pl.ds(i, 1), pl.ds(0, gen_rows.shape[0])] = join_lanes(part(8 + i), small)
    gen_vec[pl.ds(6, 1), :] = join_lanes(part(14), up_size // devices)

    pump(2)
    operands = gen_parts(gen_rows, gen_down, gen_vec, wave_code[...], up_size)
    seq = operands[0]
    final = gen_layer(*operands, LAT + NWAVE + 1)
    feature = (final[LAT : LAT + NWAVE] + seq[LAT : LAT + NWAVE]).astype(low)
    feature_out[...] = feature
    source = final[LAT + NWAVE : LAT + NWAVE + 8].astype(low)
    source_out[...] = source
    own = (dot_nn(feature, weight[...]) + weight_bias[...].astype(jnp.float32)).astype(low)
    for h in range(2):
        table[tile_rows(me * 2 + h, t_lines), :] = own[:, h * width : (h + 1) * width]
    t_gather.begin_z()
    t_gather.spread(0)
    pump(2)

    bias_at = gen_rows.shape[1] - gen_rows.shape[0] - width
    conv = dot_nn(source, gen_rows[:, pl.ds(bias_at, width)])[:1]
    t_gather.relay(0)
    grid_line = lax.broadcasted_iota(jnp.int32, (GRID, seen), 0)
    for chip in range(chips):
        patch = visible[pl.ds(chip, 1), :]
        for i, spot in enumerate((lax.div(patch, GRID), lax.rem(patch, GRID))):
            half = pl.ds(i * (width // 2), width // 2)
            picked = lax.dot_general(
                (spot == grid_line).astype(jnp.float32),
                places[...],
                (((0,), (0,)), ((), ())),
                precision=HIGH,
                preferred_element_type=jnp.float32,
            )
            start[pl.ds(chip * seen, seen), half] = (
                picked + conv[:, i * (width // 2) : (i + 1) * (width // 2)]
            )
    t_gather.spread(1)
    t_gather.relay(1)
    pump(2)
    span = 256
    bands_pix = pixels.shape[1]
    bands = waves.shape[1]
    band_of = lax.div(lax.broadcasted_iota(jnp.int32, (1, bands_pix), 1), bands_pix // bands)
    wave_lines = []
    for chip in range(chips):
        drop = jnp.zeros((1, 1), jnp.int32)
        for i, less in enumerate(BAND_DROP):
            drop = jnp.where(sensor[pl.ds(chip, 1), :] == i, less, drop)
        wave = jnp.full((1, bands_pix), -1, jnp.int32)
        for i in range(bands):
            wave = jnp.where(band_of == i, waves[pl.ds(chip, 1), pl.ds(i, 1)], wave)
        wave_lines.append(jnp.where(band_of < bands - drop, wave, -1))

    def slot_block(i, _):
        shape = (span, bands_pix)
        line = lax.broadcasted_iota(jnp.int32, shape, 0) + i * span
        column = lax.broadcasted_iota(jnp.int32, shape, 1)
        count = slots.shape[0] // NWAVE
        same = lax.div(line, NWAVE) == lax.rem(column, count)
        for chip in range(chips):
            chosen = same & (lax.rem(line, NWAVE) == wave_lines[chip])
            slots[tile_rows(i, span), pl.ds(chip * seen, seen)] = ndot(
                chosen.astype(jnp.float32).astype(low), pixels[pl.ds(chip * seen, seen), :]
            ).astype(low)
        return 0

    blocks = slots.shape[0] // span
    lax.fori_loop(0, blocks // 2, slot_block, 0)
    for k in range(2, planes):
        t_gather.spread(k)
        t_gather.relay(k)
    pump(2)
    lax.fori_loop(blocks // 2, blocks, slot_block, 0)
    keep(slots, slots_out)
    pump(4)
    for k in range(planes):
        t_gather.close(k)
    pump(2)
    t_gather.finish()
    keep(table, table_out)
    wide_span = 512

    def embed(i, _):
        at = tile_rows(i, wide_span)
        start[...] += tdot(slots[at, :], table[at, :])
        return 0

    lax.fori_loop(0, slots.shape[0] // wide_span, embed, 0)
    stash(start, start_out)
    while len(steps) > planes:
        pump(1)

    def norm_into(src, dst, row):
        gain = vecs[pl.ds(row, 1), pl.ds(0, width)]
        shift = vecs[pl.ds(row + 1, 1), pl.ds(0, width)]

        def block(i, _):
            at = tile_rows(i, BLOCK)
            dst[at, :] = norm_rows(src[at, :], gain, shift).astype(low)
            return 0

        lax.fori_loop(0, rows // BLOCK, block, 0)

    trade_more(TRADE_PARTS)
    norm_into(start, normed, 0)
    for copy in copies[2:6]:
        copy.wait()
    w_gather.finish()
    for copy in loads[:4]:
        copy.start()
    stash(normed, normed_out)
    loads[0].wait()

    def project(i, _):
        lane = pl.ds(pl.multiple_of(i * width, 128), width)
        joint[:, lane] = dot_nn(normed[...], w_qkv[:, lane]).astype(low)
        return 0

    lax.fori_loop(0, 3, project, 0)
    pump(2)
    stash(joint, joint_out)
    pairs = width // 128
    head = width // HEADS
    scale = 1.0 / math.sqrt(head)
    odd = lax.broadcasted_iota(jnp.int32, (1, 128), 1) >= head

    def attend(n, _):
        at = tile_rows(lax.div(n, pairs), seen)
        pair = lax.rem(n, pairs)
        query, key, value = [
            joint[at, pl.ds(pl.multiple_of(pair * 128 + i * width, 128), 128)] for i in range(3)
        ]
        zero = jnp.zeros_like(query)
        parts = []
        for h in range(2):
            mine = odd if h else jnp.logical_not(odd)
            scores = ndot(jnp.where(mine, query, zero), key) * scale
            raised = jnp.exp(scores - jnp.max(scores, axis=-1, keepdims=True))
            prob = (raised / jnp.sum(raised, axis=-1, keepdims=True)).astype(low)
            probs[2 * n + h] = prob
            parts.append(dot_nn(prob, value))
        lane = pl.ds(pl.multiple_of(pair * 128, 128), 128)
        context[at, lane] = jnp.where(odd, parts[1], parts[0]).astype(low)
        return 0

    for i in range(0, chips * pairs, 3):
        lax.fori_loop(i, i + 3, attend, 0)
        pump(1)
    stash(probs, probs_out)
    stash(context, context_out)
    loads[1].wait()
    middle[...] = start[...] + dot_nn(context[...], w_out[...])
    stash(middle, middle_out)
    norm_into(middle, normed2, 2)
    stash(normed2, normed2_out)
    total[...] = middle[...] + vecs[pl.ds(4, 1), pl.ds(0, width)]
    pump(len(steps))
    d_gather.finish()
    loads[4].start()
    loads[2].wait()
    loads[4].wait()

    def feed(t, _):
        at = tile_rows(t, FT)
        upper = dot_nn(normed2[...], w_up[:, at]) + vecs[pl.ds(5, 1), at]
        bell = 0.5 * (1.0 + lax.erf(upper * math.sqrt(0.5)))
        active = (upper * bell).astype(low)
        activ[:, at] = active
        tilt = upper * jnp.exp(-0.5 * upper * upper) * (1.0 / math.sqrt(2.0 * math.pi))
        slope[:, at] = (bell + tilt).astype(low)
        total[...] += dot_nn(active, w_down[at, :])
        return 0

    lax.fori_loop(0, hidden // FT, feed, 0)
    stash(activ, activ_out)
    stash(slope, slope_out)
    ending[...] = total[...].astype(low)
    stash(ending, ending_out)
    loads[3].wait()
    decoded = dot_nn(ending[...], w_dec[...]) + vecs[pl.ds(6, 1), pl.ds(0, dec_width)]
    total[:, pl.ds(0, dec_width)] = decoded
    mask = vecs[pl.ds(7, 1), pl.ds(0, dec_width)]
    blocks, _, lines, _ = ordered.shape
    for chip in range(chips):
        at = pl.ds(chip * seen, seen)
        chosen = (order[...] == visible[pl.ds(chip, 1), :]).astype(jnp.float32)
        found = jnp.sum(chosen, axis=1, keepdims=True) > 0.0
        placed = dot_nn(chosen.astype(low), total[at, pl.ds(0, dec_width)].astype(low))
        placed = jnp.where(found, placed, mask).astype(low)
        ordered[:, chip] = placed.reshape(blocks, lines, dec_width)
    for copy in copies[6:] + stashed:
        copy.wait()
    trade_more(TRADE_PARTS)
    trade.finish()
    wires.drain()


def prepare(planes, sizes, *args):
    (rows, width, hidden, dec_width, chips, up_size, patches) = sizes
    seen = rows // chips
    heads = chips * HEADS
    devices = planes * 8
    low, full = jnp.bfloat16, jnp.float32
    qkv, up, out, dec, down = args[:5]
    gen_width = args[12].shape[1]
    tail = args[18].shape[0] + 16
    cols = qkv.shape[1] + up.shape[1] + out.shape[1] + dec.shape[1]
    shard = qkv.shape[0]
    slots = args[5].shape[1] // width * devices * NWAVE
    copies = 5 * gather_copies(planes) + 1
    shapes = (
        ((width, cols), low),
        ((hidden, width), low),
        ((slots, width), low),
        ((slots, rows), low),
        (args[19].shape, low),
        ((rows, width), low),
        ((rows, 3 * width), low),
        ((heads, seen, seen), low),
        ((rows, width), low),
        ((rows, width), full),
        ((rows, width), low),
        ((rows, hidden), low),
        ((rows, hidden), low),
        ((rows, width), low),
        ((rows, width), full),
        ((devices, chips, patches // devices, dec_width), low),
        ((gen_width, CHUNK * 16 * devices // gen_width), low),
        ((up_size, gen_width), low),
        ((8, up_size), full),
        ((8, hidden), full),
        ((NWAVE, gen_width), low),
        ((8, gen_width), low),
    )
    return pl.pallas_call(
        partial(prepare_kernel, planes, sizes),
        out_shape=tuple(jax.ShapeDtypeStruct(shape, dtype) for shape, dtype in shapes),
        in_specs=[VMEM] * 19 + [ANY] + [VMEM] * (len(args) - 20),
        out_specs=[ANY] * 15 + [VMEM] * 7,
        scratch_shapes=[
            pltpu.VMEM((devices * 16, CHUNK), low),
            pltpu.VMEM((devices, tail, 128), low),
            pltpu.VMEM((slots, width), low),
            pltpu.VMEM((slots, rows), low),
            pltpu.VMEM((shard, cols), low),
            pltpu.VMEM((shard, cols // 2), low),
            pltpu.VMEM((2 * shard, cols // 2), low),
            pltpu.VMEM((16, CHUNK), full),
            pltpu.VMEM((16, 128), full),
            pltpu.VMEM((16, CHUNK), low),
            pltpu.VMEM((tail, 128), low),
            pltpu.VMEM((width, 3 * width), low),
            pltpu.VMEM((width, width), low),
            pltpu.VMEM((width, hidden), low),
            pltpu.VMEM((hidden, width), low),
            pltpu.VMEM((width, dec_width), low),
        ]
        + [pltpu.VMEM(shape, dtype) for shape, dtype in shapes[5:15]]
        + [
            pltpu.VMEM((rows, width), full),
            pltpu.SemaphoreType.DMA((copies,)),
            pltpu.SemaphoreType.DMA((copies,)),
            pltpu.SemaphoreType.DMA((devices,)),
            pltpu.SemaphoreType.DMA((devices,)),
            pltpu.SemaphoreType.DMA((8,)),
            pltpu.SemaphoreType.DMA((6,)),
            pltpu.SemaphoreType.DMA((10,)),
        ],
        compiler_params=pltpu.CompilerParams(
            collective_id=0, has_side_effects=True, vmem_limit_bytes=60 * 2**20
        ),
    )(*args)


def gen_back(
    gen_rows, gen_down, gen_vec, wave_code, length, grad_feature, grad_source, sums, put_up, put_down
):
    up_size, width = gen_down.shape
    size = width // GHEADS
    scale = 1.0 / math.sqrt(size)
    total = lambda value: jnp.sum(value, axis=0, keepdims=True)
    chunk = up_size // 4

    def dot(left, right, dims):
        return lax.dot_general(
            left.astype(jnp.bfloat16),
            right.astype(jnp.bfloat16),
            (dims, ((), ())),
            preferred_element_type=jnp.float32,
        )

    nn = lambda left, right: dot(left, right, ((1,), (0,)))
    nt = lambda left, right: dot(left, right, ((1,), (1,)))
    tn = lambda left, right: dot(left, right, ((0,), (0,)))
    seq = gen_seq_of(gen_rows, wave_code, up_size)
    full = jnp.float32
    qkv = gen_rows[:, pl.ds(up_size, 3 * width)].astype(full)
    out = gen_rows[:, pl.ds(up_size + 3 * width, width)].astype(full)
    out_bias, gain1, shift1, down_bias, gain2, _ = [
        gen_vec[pl.ds(i, 1), pl.ds(0, width)] for i in range(6)
    ]
    joint = nn(seq, qkv)
    query, key, value = [joint[:, i * width : (i + 1) * width] for i in range(3)]
    lane = lax.broadcasted_iota(jnp.int32, (1, width), 1)
    spot = lax.broadcasted_iota(jnp.int32, (1, seq.shape[0]), 1)
    masks = [(lax.div(lane, size) == h).astype(full) for h in range(GHEADS)]
    probs = []
    context = jnp.zeros_like(seq)
    for mine in masks:
        scores = jnp.where(spot < length, nt(query * mine, key) * scale, -1e30)
        raised = jnp.exp(scores - jnp.max(scores, axis=-1, keepdims=True))
        probs.append(raised / jnp.sum(raised, axis=-1, keepdims=True))
        context = context + nn(probs[-1], value * mine)
    first = seq + nn(context, out) + out_bias
    mixed = norm_rows(first, gain1, shift1)

    def piece(i):
        at = pl.ds(pl.multiple_of(i * chunk, chunk), chunk)
        up = gen_rows[:, at].astype(full)
        down = gen_down[at, :].astype(full)
        inner = nn(mixed, up) + gen_vec[pl.ds(6, 1), at]
        return up, down, inner, 0.5 * (1.0 + lax.erf(inner * math.sqrt(0.5)))

    def ahead(i, so_far):
        _, down, inner, bell = piece(i)
        return so_far + nn(inner * bell, down)

    second = lax.fori_loop(0, 4, ahead, mixed + down_bias)
    rest = seq.shape[0] - LAT - NWAVE
    zeros = jnp.zeros((LAT, width), full)
    grad = jnp.concatenate([zeros, grad_feature, grad_source], axis=0)
    through, terms = norm_back(grad, second, gain2)
    g_gain2, g_shift2, g_down_bias = total(terms), total(grad), total(through)

    def behind(i, so_far):
        up, down, inner, bell = piece(i)
        put_down(i, tn(inner * bell, through))
        slope = bell + inner * jnp.exp(-0.5 * inner * inner) * (1.0 / math.sqrt(2.0 * math.pi))
        g_inner = nt(through, down) * slope
        put_up(i, tn(mixed, g_inner))
        sums[pl.ds(6, 1), pl.ds(pl.multiple_of(i * chunk, chunk), chunk)] = total(g_inner)
        return so_far + nt(g_inner, up)

    g_mixed = lax.fori_loop(0, 4, behind, through)
    through, terms = norm_back(g_mixed, first, gain1)
    g_gain1, g_shift1, g_out_bias = total(terms), total(g_mixed), total(through)
    g_out = tn(context, through)
    g_context = nt(through, out)
    g_query = g_key = g_value = jnp.zeros_like(seq)
    for mine, prob in zip(masks, probs):
        g_head = g_context * mine
        g_prob = nt(g_head, value)
        g_value = g_value + tn(prob, g_head)
        g_score = prob * (g_prob - jnp.sum(prob * g_prob, axis=-1, keepdims=True)) * scale
        g_query = g_query + nn(g_score, key * mine)
        g_key = g_key + tn(g_score, query * mine)
    g_joint = jnp.concatenate([g_query, g_key, g_value], axis=1)
    direct = jnp.concatenate([zeros, grad_feature, jnp.zeros((rest, width), full)], axis=0)
    g_seq = through + nt(g_joint, qkv) + direct
    thin = (g_out_bias, g_gain1, g_shift1, g_down_bias, g_gain2, g_shift2)
    return g_seq, tn(seq, g_joint), g_out, thin


def hand_out_kernel(planes, sizes, *refs):
    (width, hidden, dec_width, small) = sizes
    devices = planes * 8
    (
        s_dec, s_up, s_oq, s_down, kernels, kernel_sums, lines, g_wide, g_tall, g_seq, g_lines,
        g_bias,
    ) = refs[40:52]
    copies = [
        pltpu.make_async_copy(refs[i], refs[40 + i], refs[52].at[i]) for i in range(12)
    ]
    for copy in copies:
        copy.start()
    for copy in copies:
        copy.wait()
    outs = refs[12:40]
    (
        pre_gain, pre_shift, qkv, out, mid_gain, mid_shift, up, up_bias, down, down_bias, dec,
        dec_bias, mask, tokens, gen_qkv, gen_out, gen_out_bias, gain1, shift1, gen_up,
        gen_up_bias, gen_down, gen_down_bias, gain2, shift2, kernel_weight, kernel_bias, bias,
    ) = outs
    me = lax.axis_index("dp") * 4 + lax.axis_index("fsdp")
    qkv[...] = s_oq[:, pl.ds(width, 3 * width)]
    out[...] = s_oq[:, pl.ds(0, width)]
    up[...] = s_up[...]
    down[...] = s_down[...]
    dec[...] = s_dec[...]
    kernel_weight[...] = kernels[...]
    kernel_bias[...] = kernel_sums[...]
    gen_down[...] = g_tall[...]
    up_size = gen_up.shape[1]
    gen_width = gen_out.shape[1]
    gen_up[...] = g_wide[pl.ds(0, small), pl.ds(0, up_size)]
    gen_qkv[...] = g_wide[pl.ds(0, small), pl.ds(up_size, 3 * gen_width)]
    gen_out[...] = g_wide[pl.ds(0, small), pl.ds(up_size + 3 * gen_width, gen_width)]
    tokens[pl.ds(0, LAT), :] = g_seq[pl.ds(0, LAT), pl.ds(0, small)]
    tokens[pl.ds(LAT, 1), :] = g_seq[pl.ds(LAT + NWAVE, 1), pl.ds(0, small)]
    bias[...] = g_bias[pl.ds(0, small), :]

    def own(values, part):
        shape = (values.shape[1], 128)
        row = lax.broadcasted_iota(jnp.int32, shape, 0)
        lane = lax.broadcasted_iota(jnp.int32, shape, 1)
        pick = ((row == me * part + lane) & (lane < part)).astype(jnp.float32)
        return jnp.dot(values, pick, precision=HIGH, preferred_element_type=jnp.float32)

    at = NWAVE + width // 128

    def row_of(size):
        nonlocal at
        count = size // 128
        row = jnp.concatenate([lines[pl.ds(at + i, 1), :] for i in range(count)], axis=1)
        at += count
        return row

    def rows_of(sizes_):
        rows = [row_of(size) for size in sizes_]
        rows.append(jnp.zeros((8 - len(rows), rows[0].shape[1]), jnp.float32))
        return jnp.concatenate(rows, axis=0)

    def split(values, part, refs_):
        mine = own(values, part)
        for i, ref in enumerate(refs_):
            ref[...] = mine[i : i + 1, :part]

    split(rows_of((width,) * 5), width // devices, (pre_gain, pre_shift, mid_gain, mid_shift, down_bias))
    split(rows_of((hidden,)), hidden // devices, (up_bias,))
    split(rows_of((dec_width,) * 2), dec_width // devices, (dec_bias, mask))
    split(
        g_lines[:, pl.ds(0, gen_width)],
        small,
        (gen_out_bias, gain1, shift1, gen_down_bias, gain2, shift2),
    )
    split(
        jnp.concatenate(
            [g_lines[pl.ds(6, 1), :], jnp.zeros((7, up_size), jnp.float32)], axis=0
        ),
        up_size // devices,
        (gen_up_bias,),
    )


def hand_out(planes, sizes, *args):
    (width, hidden, dec_width, small) = sizes
    devices = planes * 8
    up_size = args[10].shape[1]
    gen_width = args[8].shape[1]
    wide, thin = width // devices, (1, width // devices)
    row = lambda size: (1, size // devices)
    shapes = (
        thin, thin, (wide, 3 * width), (wide, width), thin, thin, (wide, hidden), row(hidden),
        (hidden // devices, width), thin, (wide, dec_width), row(dec_width), row(dec_width),
        (LAT + 1, small), (small, 3 * gen_width), (small, gen_width), (1, small), (1, small),
        (1, small), (small, up_size), row(up_size), (up_size // devices, gen_width), (1, small),
        (1, small), (1, small), args[4].shape, args[5].shape, (small, width),
    )
    return pl.pallas_call(
        partial(hand_out_kernel, planes, sizes),
        out_shape=tuple(jax.ShapeDtypeStruct(shape, jnp.float32) for shape in shapes),
        in_specs=[ANY] * 12,
        out_specs=[VMEM] * 28,
        scratch_shapes=[pltpu.VMEM(item.shape, item.dtype) for item in args]
        + [pltpu.SemaphoreType.DMA((12,))],
        compiler_params=pltpu.CompilerParams(vmem_limit_bytes=60 * 2**20),
    )(*args)


def on_device_plain(
    pixels,
    sensor,
    band_wave,
    visible,
    block_order,
    pre_gain,
    pre_shift,
    qkv_weight,
    out_weight,
    mid_gain,
    mid_shift,
    up_weight,
    up_bias,
    down_weight,
    down_bias,
    dec_weight,
    dec_bias,
    mask_token,
    gen_tokens,
    gen_qkv,
    gen_out,
    gen_out_bias,
    gen_gain1,
    gen_shift1,
    gen_up,
    gen_up_bias,
    gen_down,
    gen_down_bias,
    gen_gain2,
    gen_shift2,
    kernel_weight,
    kernel_bias,
    bias_weight,
    cotangent,
):
    fetched = (
        lax.all_gather(pre_gain, AXES, axis=0, tiled=True),
        lax.all_gather(pre_shift, AXES, axis=0, tiled=True),
        lax.all_gather(qkv_weight, AXES, axis=0, tiled=True),
        lax.all_gather(out_weight, AXES, axis=0, tiled=True),
        lax.all_gather(mid_gain, AXES, axis=0, tiled=True),
        lax.all_gather(mid_shift, AXES, axis=0, tiled=True),
        lax.all_gather(up_weight, AXES, axis=0, tiled=True),
        lax.all_gather(up_bias, AXES, axis=0, tiled=True),
        lax.all_gather(down_weight, AXES, axis=0, tiled=True),
        lax.all_gather(down_bias, AXES, axis=0, tiled=True),
        lax.all_gather(dec_weight, AXES, axis=0, tiled=True),
        lax.all_gather(dec_bias, AXES, axis=0, tiled=True),
        lax.all_gather(mask_token, AXES, axis=0, tiled=True),
        lax.all_gather(gen_tokens, AXES, axis=1, tiled=True),
        lax.all_gather(gen_qkv, AXES, axis=0, tiled=True),
        lax.all_gather(gen_out, AXES, axis=0, tiled=True),
        lax.all_gather(gen_out_bias, AXES, axis=0, tiled=True),
        lax.all_gather(gen_gain1, AXES, axis=0, tiled=True),
        lax.all_gather(gen_shift1, AXES, axis=0, tiled=True),
        lax.all_gather(gen_up, AXES, axis=0, tiled=True),
        lax.all_gather(gen_up_bias, AXES, axis=0, tiled=True),
        lax.all_gather(gen_down, AXES, axis=0, tiled=True),
        lax.all_gather(gen_down_bias, AXES, axis=0, tiled=True),
        lax.all_gather(gen_gain2, AXES, axis=0, tiled=True),
        lax.all_gather(gen_shift2, AXES, axis=0, tiled=True),
        lax.all_gather(kernel_weight, AXES, axis=1, tiled=True),
        lax.all_gather(kernel_bias, AXES, axis=0, tiled=True),
        lax.all_gather(bias_weight, AXES, axis=0, tiled=True),
    )
    full_kernel = fetched[25]
    full_kernel_bias = fetched[26]
    full_bias_weight = fetched[27]
    (
        full_pre_gain,
        full_pre_shift,
        full_qkv,
        full_out,
        full_mid_gain,
        full_mid_shift,
        full_up,
        full_up_bias,
        full_down,
        full_down_bias,
        full_dec,
        full_dec_bias,
        full_mask,
    ) = fetched[:13]
    core32 = tuple((item.astype(jnp.float32) for item in fetched[13:25]))
    chips, seen, bands, pix = pixels.shape
    width = full_qkv.shape[0]
    head_dim = width // HEADS
    scale = 1.0 / math.sqrt(head_dim)
    dec_width = full_dec.shape[1]
    rows = chips * seen
    wave_code = lax.optimization_barrier(
        sincos(jnp.arange(NWAVE, dtype=jnp.float32), WD // 2).astype(jnp.bfloat16)
    ).astype(jnp.float32)
    (feature, source), core_back = jax.vjp(partial(gen_core, wave_code), *core32)
    feature_low = feature.astype(jnp.bfloat16)
    source_low = source.astype(jnp.bfloat16)
    conv_bias = jnp.dot(source_low[None, :], full_bias_weight, preferred_element_type=jnp.float32)[
        0
    ]
    kernels = (
        jnp.dot(feature_low, full_kernel, preferred_element_type=jnp.float32)
        + full_kernel_bias.astype(jnp.float32)[None, :]
    ).astype(jnp.bfloat16)
    valid = band_valid(sensor, bands)
    onehot = (band_wave[:, :, None] == jnp.arange(NWAVE, dtype=jnp.int32)[None, None, :]).astype(
        jnp.float32
    )
    place = place_code(visible, width)
    band_kernels = jnp.einsum(
        "cbw,wk->cbk", onehot.astype(jnp.bfloat16), kernels, preferred_element_type=jnp.float32
    ).astype(jnp.bfloat16)
    band_kernels = band_kernels.reshape(chips, bands, pix, width)
    masked = pixels * valid.astype(jnp.bfloat16)[:, None, :, None]
    embedded = jnp.einsum(
        "cvbp,cbpd->cvd", masked, band_kernels, preferred_element_type=jnp.float32
    )
    start = (embedded + conv_bias + place).reshape(rows, width)
    pre_gain32 = full_pre_gain.astype(jnp.float32)
    pre_shift32 = full_pre_shift.astype(jnp.float32)
    normed = norm_rows(start, pre_gain32, pre_shift32).astype(jnp.bfloat16)
    joint = jnp.dot(normed, full_qkv, preferred_element_type=jnp.float32).astype(jnp.bfloat16)
    joint = joint.reshape(chips, seen, 3, HEADS, head_dim)
    queries = joint[:, :, 0]
    keys = joint[:, :, 1]
    values = joint[:, :, 2]
    scores = (
        jnp.einsum("cqhe,ckhe->chqk", queries, keys, preferred_element_type=jnp.float32) * scale
    )
    peak = jnp.max(scores, axis=-1, keepdims=True)
    expd = jnp.exp(scores - peak)
    total = jnp.sum(expd, axis=-1, keepdims=True)
    probs = (expd / total).astype(jnp.bfloat16)
    log_total = peak + jnp.log(total)
    context = jnp.einsum("chqk,ckhe->cqhe", probs, values, preferred_element_type=jnp.float32)
    context = context.astype(jnp.bfloat16).reshape(rows, width)
    attended = jnp.dot(context, full_out, preferred_element_type=jnp.float32)
    middle = start + attended
    mid_gain32 = full_mid_gain.astype(jnp.float32)
    mid_shift32 = full_mid_shift.astype(jnp.float32)
    normed2 = norm_rows(middle, mid_gain32, mid_shift32).astype(jnp.bfloat16)
    upper = jnp.dot(normed2, full_up, preferred_element_type=jnp.float32) + full_up_bias.astype(
        jnp.float32
    )
    activ = exact_gelu(upper).astype(jnp.bfloat16)
    branch = jnp.dot(activ, full_down, preferred_element_type=jnp.float32) + full_down_bias.astype(
        jnp.float32
    )
    ending = (middle + branch).astype(jnp.bfloat16)
    decoded = jnp.dot(ending, full_dec, preferred_element_type=jnp.float32) + full_dec_bias.astype(
        jnp.float32
    )
    decoded = decoded.astype(jnp.bfloat16).reshape(chips, seen, dec_width)
    chip_ids = jnp.arange(chips, dtype=jnp.int32)[:, None]
    canvas = jnp.broadcast_to(full_mask, (chips, PATCH, dec_width))
    canvas = canvas.at[chip_ids, visible].set(decoded)
    ordered = jnp.take(canvas, block_order, axis=1)
    decoder_in = lax.all_to_all(ordered, AXES, split_axis=1, concat_axis=0, tiled=True)
    returned = lax.all_to_all(cotangent, AXES, split_axis=0, concat_axis=1, tiled=True)
    (
        full_pre_gain,
        full_pre_shift,
        full_qkv,
        full_out,
        full_mid_gain,
        full_mid_shift,
        full_up,
        full_up_bias,
        full_down,
        full_down_bias,
        full_dec,
        full_dec_bias,
        full_mask,
    ) = (
        lax.all_gather(pre_gain, AXES, axis=0, tiled=True),
        lax.all_gather(pre_shift, AXES, axis=0, tiled=True),
        lax.all_gather(qkv_weight, AXES, axis=0, tiled=True),
        lax.all_gather(out_weight, AXES, axis=0, tiled=True),
        lax.all_gather(mid_gain, AXES, axis=0, tiled=True),
        lax.all_gather(mid_shift, AXES, axis=0, tiled=True),
        lax.all_gather(up_weight, AXES, axis=0, tiled=True),
        lax.all_gather(up_bias, AXES, axis=0, tiled=True),
        lax.all_gather(down_weight, AXES, axis=0, tiled=True),
        lax.all_gather(down_bias, AXES, axis=0, tiled=True),
        lax.all_gather(dec_weight, AXES, axis=0, tiled=True),
        lax.all_gather(dec_bias, AXES, axis=0, tiled=True),
        lax.all_gather(mask_token, AXES, axis=0, tiled=True),
    )
    restored = jnp.zeros_like(returned).at[:, block_order].set(returned)
    seen_grad = jnp.take_along_axis(restored, visible[:, :, None], axis=1)
    grad_mask = jnp.sum(restored.astype(jnp.float32), axis=(0, 1)) - jnp.sum(
        seen_grad.astype(jnp.float32), axis=(0, 1)
    )
    grad_rows = seen_grad.reshape(rows, dec_width)
    grad_dec_weight = tdot(ending, grad_rows)
    grad_dec_bias = jnp.sum(grad_rows.astype(jnp.float32), axis=0)
    grad_ending = ndot(grad_rows, full_dec)
    grad_branch = grad_ending.astype(jnp.bfloat16)
    grad_down_bias = jnp.sum(grad_branch.astype(jnp.float32), axis=0)
    grad_down_weight = tdot(activ, grad_branch)
    grad_activ = ndot(grad_branch, full_down)
    gelu_out, gelu_back = jax.vjp(exact_gelu, upper)
    grad_upper = gelu_back(grad_activ)[0].astype(jnp.bfloat16)
    grad_up_bias = jnp.sum(grad_upper.astype(jnp.float32), axis=0)
    grad_up_weight = tdot(normed2, grad_upper)
    grad_normed2 = ndot(grad_upper, full_up)
    norm_out, norm_back = jax.vjp(norm_rows, middle, mid_gain32, mid_shift32)
    through_mid, grad_mid_gain, grad_mid_shift = norm_back(grad_normed2)
    grad_middle = grad_ending + through_mid
    grad_attended = grad_middle.astype(jnp.bfloat16)
    grad_out_weight = tdot(context, grad_attended)
    grad_context = (
        ndot(grad_attended, full_out).astype(jnp.bfloat16).reshape(chips, seen, HEADS, head_dim)
    )
    again_scores = (
        jnp.einsum("cqhe,ckhe->chqk", queries, keys, preferred_element_type=jnp.float32) * scale
    )
    probs_full = jnp.exp(again_scores - log_total)
    probs_low = probs_full.astype(jnp.bfloat16)
    grad_values = jnp.einsum(
        "chqk,cqhe->ckhe", probs_low, grad_context, preferred_element_type=jnp.float32
    ).astype(jnp.bfloat16)
    grad_probs = jnp.einsum(
        "cqhe,ckhe->chqk", grad_context, values, preferred_element_type=jnp.float32
    )
    row_dot = jnp.sum(probs_full * grad_probs, axis=-1, keepdims=True)
    grad_scores = (probs_full * (grad_probs - row_dot)).astype(jnp.bfloat16)
    grad_queries = (
        jnp.einsum("chqk,ckhe->cqhe", grad_scores, keys, preferred_element_type=jnp.float32) * scale
    ).astype(jnp.bfloat16)
    grad_keys = (
        jnp.einsum("chqk,cqhe->ckhe", grad_scores, queries, preferred_element_type=jnp.float32)
        * scale
    ).astype(jnp.bfloat16)
    grad_joint = jnp.stack([grad_queries, grad_keys, grad_values], axis=2).reshape(rows, 3 * width)
    grad_qkv_weight = tdot(normed, grad_joint)
    grad_normed = ndot(grad_joint, full_qkv)
    first_out, first_back = jax.vjp(norm_rows, start, pre_gain32, pre_shift32)
    through_pre, grad_pre_gain, grad_pre_shift = first_back(grad_normed)
    grad_start = grad_middle + through_pre
    grad_conv_part = jnp.sum(grad_start, axis=0)
    grad_embedded = grad_start.astype(jnp.bfloat16).reshape(chips, seen, width)
    grad_band = jnp.einsum(
        "cvbp,cvd->cbpd", masked, grad_embedded, preferred_element_type=jnp.float32
    )
    grad_band = grad_band.reshape(chips, bands, pix * width)
    grad_pixels = jnp.einsum(
        "cvd,cbpd->cvbp", grad_embedded, band_kernels, preferred_element_type=jnp.float32
    )
    grad_pixels = grad_pixels * valid[:, None, :, None]
    grad_kernels_part = jnp.einsum("cbw,cbk->wk", onehot, grad_band, precision=HIGH)
    kernel_sum, grad_conv = lax.psum((grad_kernels_part, grad_conv_part), AXES)
    kernel_low = kernel_sum.astype(jnp.bfloat16)
    own_low = own_part(kernel_low, 1)
    grad_kernel_weight = tdot(feature_low, own_low)
    grad_kernel_bias = jnp.sum(own_low.astype(jnp.float32), axis=0)
    grad_feature = ndot(kernel_low, full_kernel)
    grad_bias_weight = own_part(source_low.astype(jnp.float32)[:, None] * grad_conv[None, :], 0)
    grad_source = jnp.dot(full_bias_weight.astype(jnp.float32), grad_conv, precision=HIGH)
    core_grads = core_back((grad_feature, grad_source))
    summed = (
        lax.psum_scatter(grad_pre_gain, AXES, scatter_dimension=0, tiled=True),
        lax.psum_scatter(grad_pre_shift, AXES, scatter_dimension=0, tiled=True),
        lax.psum_scatter(grad_qkv_weight, AXES, scatter_dimension=0, tiled=True),
        lax.psum_scatter(grad_out_weight, AXES, scatter_dimension=0, tiled=True),
        lax.psum_scatter(grad_mid_gain, AXES, scatter_dimension=0, tiled=True),
        lax.psum_scatter(grad_mid_shift, AXES, scatter_dimension=0, tiled=True),
        lax.psum_scatter(grad_up_weight, AXES, scatter_dimension=0, tiled=True),
        lax.psum_scatter(grad_up_bias, AXES, scatter_dimension=0, tiled=True),
        lax.psum_scatter(grad_down_weight, AXES, scatter_dimension=0, tiled=True),
        lax.psum_scatter(grad_down_bias, AXES, scatter_dimension=0, tiled=True),
        lax.psum_scatter(grad_dec_weight, AXES, scatter_dimension=0, tiled=True),
        lax.psum_scatter(grad_dec_bias, AXES, scatter_dimension=0, tiled=True),
        lax.psum_scatter(grad_mask, AXES, scatter_dimension=0, tiled=True),
    )
    return (
        decoder_in,
        grad_pixels,
        summed[0],
        summed[1],
        summed[2],
        summed[3],
        summed[4],
        summed[5],
        summed[6],
        summed[7],
        summed[8],
        summed[9],
        summed[10],
        summed[11],
        summed[12],
        own_part(core_grads[0], 1),
        own_part(core_grads[1], 0),
        own_part(core_grads[2], 0),
        own_part(core_grads[3], 0),
        own_part(core_grads[4], 0),
        own_part(core_grads[5], 0),
        own_part(core_grads[6], 0),
        own_part(core_grads[7], 0),
        own_part(core_grads[8], 0),
        own_part(core_grads[9], 0),
        own_part(core_grads[10], 0),
        own_part(core_grads[11], 0),
        grad_kernel_weight,
        grad_kernel_bias,
        grad_bias_weight,
    )


def on_device(
    pixels,
    sensor,
    band_wave,
    visible,
    block_order,
    pre_gain,
    pre_shift,
    qkv_weight,
    out_weight,
    mid_gain,
    mid_shift,
    up_weight,
    up_bias,
    down_weight,
    down_bias,
    dec_weight,
    dec_bias,
    mask_token,
    gen_tokens,
    gen_qkv,
    gen_out,
    gen_out_bias,
    gen_gain1,
    gen_shift1,
    gen_up,
    gen_up_bias,
    gen_down,
    gen_down_bias,
    gen_gain2,
    gen_shift2,
    kernel_weight,
    kernel_bias,
    bias_weight,
    cotangent,
):
    arguments = (
        pixels,
        sensor,
        band_wave,
        visible,
        block_order,
        pre_gain,
        pre_shift,
        qkv_weight,
        out_weight,
        mid_gain,
        mid_shift,
        up_weight,
        up_bias,
        down_weight,
        down_bias,
        dec_weight,
        dec_bias,
        mask_token,
        gen_tokens,
        gen_qkv,
        gen_out,
        gen_out_bias,
        gen_gain1,
        gen_shift1,
        gen_up,
        gen_up_bias,
        gen_down,
        gen_down_bias,
        gen_gain2,
        gen_shift2,
        kernel_weight,
        kernel_bias,
        bias_weight,
        cotangent,
    )
    planes = lax.axis_size("dp") // 2
    devices = planes * 8
    if lax.axis_size("fsdp") != 4 or planes & (planes - 1) or pre_gain.shape[0] % 8:
        return on_device_plain(*arguments)
    low = jnp.bfloat16
    chips, seen, bands, pix = pixels.shape
    width = qkv_weight.shape[0] * devices
    hidden_width = up_weight.shape[1]
    head_dim = width // HEADS
    scale = 1.0 / math.sqrt(head_dim)
    dec_width = dec_weight.shape[1]
    rows = chips * seen
    gen_width = gen_qkv.shape[0] * devices
    up_size = gen_up.shape[1]
    thin = (
        pre_gain, pre_shift, mid_gain, mid_shift, down_bias, up_bias, dec_bias, mask_token,
        gen_out_bias, gen_gain1, gen_shift1, gen_down_bias, gen_gain2, gen_shift2, gen_up_bias,
    )
    thin = tuple(item.reshape(1, -1) for item in thin)
    wave_code = jnp.asarray(code_table(NWAVE, gen_width // 2).astype(low).astype(np.float32))
    valid = band_valid(sensor, bands)
    sizes = (rows, width, hidden_width, dec_width, chips, PATCH)
    share = PATCH // devices
    order = block_order.reshape(PATCH, 1)
    (
        full_wide, full_down, kernels, slots, returned, normed, joint, probs, context, middle,
        normed2, activ, slope, ending, start, ordered, gen_rows, gen_down_full, gen_vec, vecs,
        feature_low, source_low,
    ) = prepare(
        planes,
        (rows, width, hidden_width, dec_width, chips, up_size, PATCH),
        qkv_weight,
        up_weight,
        out_weight,
        dec_weight,
        down_weight,
        kernel_weight,
        kernel_bias.reshape(1, -1),
        pixels.reshape(rows, bands * pix),
        sensor.reshape(chips, 1),
        band_wave,
        visible,
        jnp.asarray(code_table(GRID, width // 4)),
        wave_code,
        gen_up,
        gen_qkv,
        gen_out,
        bias_weight,
        gen_tokens,
        gen_down,
        cotangent.reshape(devices, chips, share, dec_width),
        order,
        *thin,
    )
    onehot = (band_wave[:, :, None] == jnp.arange(NWAVE, dtype=jnp.int32)[None, None, :]).astype(
        low
    )
    band_kernels = jnp.einsum(
        "cbw,pwd->cbpd",
        onehot,
        kernels.reshape(pix, NWAVE, width),
        preferred_element_type=jnp.float32,
    ).astype(low)
    (
        sum_dec, sum_up, sum_oq, sum_down, grad_kernel_weight, grad_kernel_bias, sum_all,
        gen_wide, gen_tall, gen_seq, gen_lines, grad_bias_weight, grad_embedded, decoder_in,
    ) = backward(
        planes,
        sizes,
        ordered,
        returned.reshape(chips * PATCH, dec_width),
        visible,
        order,
        ending,
        full_wide,
        full_down,
        activ,
        slope,
        normed2,
        middle,
        context,
        joint,
        probs,
        normed,
        start,
        slots,
        vecs,
        kernel_weight,
        feature_low,
        source_low,
        gen_rows,
        gen_down_full,
        gen_vec,
        wave_code,
    )
    handed = hand_out(
        planes,
        (width, hidden_width, dec_width, gen_qkv.shape[0]),
        sum_dec, sum_up, sum_oq, sum_down, grad_kernel_weight, grad_kernel_bias, sum_all,
        gen_wide, gen_tall, gen_seq, gen_lines, grad_bias_weight,
    )
    flat = (0, 1, 4, 5, 7, 9, 11, 12, 16, 17, 18, 20, 22, 23, 24, 26)
    handed = [item.reshape(-1) if i in flat else item for i, item in enumerate(handed)]
    grad_embedded = grad_embedded.reshape(chips, seen, width)
    grad_pixels = jnp.einsum(
        "cvd,cbpd->cvbp", grad_embedded, band_kernels, preferred_element_type=jnp.float32
    )
    grad_pixels = grad_pixels * valid[:, None, :, None]
    decoder_in = decoder_in.reshape(devices * chips, share, dec_width)
    return (decoder_in, grad_pixels) + tuple(handed)


def solution(mesh):
    in_specs = (
        P(AXES, None, None, None),
        P(AXES),
        P(AXES, None),
        P(AXES, None),
        P(),
        P(AXES),
        P(AXES),
        P(AXES, None),
        P(AXES, None),
        P(AXES),
        P(AXES),
        P(AXES, None),
        P(AXES),
        P(AXES, None),
        P(AXES),
        P(AXES, None),
        P(AXES),
        P(AXES),
        P(None, AXES),
        P(AXES, None),
        P(AXES, None),
        P(AXES),
        P(AXES),
        P(AXES),
        P(AXES, None),
        P(AXES),
        P(AXES, None),
        P(AXES),
        P(AXES),
        P(AXES),
        P(None, AXES),
        P(AXES),
        P(AXES, None),
        P(None, AXES, None),
    )
    out_specs = (
        P(None, AXES, None),
        P(AXES, None, None, None),
        P(AXES),
        P(AXES),
        P(AXES, None),
        P(AXES, None),
        P(AXES),
        P(AXES),
        P(AXES, None),
        P(AXES),
        P(AXES, None),
        P(AXES),
        P(AXES, None),
        P(AXES),
        P(AXES),
        P(None, AXES),
        P(AXES, None),
        P(AXES, None),
        P(AXES),
        P(AXES),
        P(AXES),
        P(AXES, None),
        P(AXES),
        P(AXES, None),
        P(AXES),
        P(AXES),
        P(AXES),
        P(None, AXES),
        P(AXES),
        P(AXES, None),
    )
    return jax.shard_map(
        on_device, mesh=mesh, in_specs=in_specs, out_specs=out_specs, check_vma=False
    )
```

```python
from functools import partial
import math

import jax
import jax.numpy as jnp
import numpy as np
from jax import lax
from jax.experimental import pallas as pl
from jax.experimental.pallas import tpu as pltpu
from jax.sharding import PartitionSpec as P

HEADS = 12
WD = 128
GHEADS = 4
LAT = 128
NWAVE = 32
GRID = 32
PATCH = 1024


EPS = 1e-05
AXES = ("dp", "fsdp")
BAND_DROP = (0, 6, 9, 7)
HIGH = lax.Precision.HIGHEST


def sincos(values, count):
    freq = jnp.exp(jnp.arange(count, dtype=jnp.float32) * (-math.log(10000.0) / count))
    angle = values[..., None] * freq
    return jnp.concatenate([jnp.sin(angle), jnp.cos(angle)], axis=-1)


def code_table(count, size):
    freq = np.exp(np.arange(size, dtype=np.float32) * np.float32(-math.log(10000.0) / size))
    angle = np.arange(count, dtype=np.float32)[:, None] * freq.astype(np.float32)
    return np.concatenate([np.sin(angle), np.cos(angle)], axis=-1).astype(np.float32)


def norm_rows(rows, gain, shift):
    mean = jnp.mean(rows, axis=-1, keepdims=True)
    centred = rows - mean
    spread = jnp.mean(centred * centred, axis=-1, keepdims=True)
    return centred * lax.rsqrt(spread + EPS) * gain + shift


def exact_gelu(values):
    return jax.nn.gelu(values, approximate=False)


def band_valid(sensor, bands):
    drops = jnp.array(BAND_DROP, jnp.int32)
    picked = jnp.where(
        sensor[:, None] == jnp.arange(4, dtype=jnp.int32)[None, :], drops[None, :], 0
    )
    count = bands - jnp.sum(picked, axis=1)
    return (jnp.arange(bands, dtype=jnp.int32)[None, :] < count[:, None]).astype(jnp.float32)


def place_code(visible, width):
    row = (visible // GRID).astype(jnp.float32)
    col = (visible % GRID).astype(jnp.float32)
    return jnp.concatenate([sincos(row, width // 4), sincos(col, width // 4)], axis=-1)


def gen_core(
    wave_code,
    tokens,
    gen_qkv,
    gen_out,
    gen_out_bias,
    gen_gain1,
    gen_shift1,
    gen_up,
    gen_up_bias,
    gen_down,
    gen_down_bias,
    gen_gain2,
    gen_shift2,
):
    sequence = jnp.concatenate([tokens[:LAT], wave_code, tokens[LAT:]], axis=0)
    length = sequence.shape[0]
    width = sequence.shape[1]
    head_dim = width // GHEADS
    joint = jnp.dot(sequence, gen_qkv, precision=HIGH).reshape(length, 3, GHEADS, head_dim)
    scores = jnp.einsum("qhe,khe->hqk", joint[:, 0], joint[:, 1], precision=HIGH) / math.sqrt(
        head_dim
    )
    probs = jax.nn.softmax(scores, axis=-1)
    context = jnp.einsum("hqk,khe->qhe", probs, joint[:, 2], precision=HIGH).reshape(length, width)
    mixed = norm_rows(
        sequence + jnp.dot(context, gen_out, precision=HIGH) + gen_out_bias, gen_gain1, gen_shift1
    )
    hidden = jax.nn.gelu(jnp.dot(mixed, gen_up, precision=HIGH) + gen_up_bias, approximate=False)
    final = norm_rows(
        mixed + jnp.dot(hidden, gen_down, precision=HIGH) + gen_down_bias, gen_gain2, gen_shift2
    )
    feature = final[LAT : LAT + NWAVE] + sequence[LAT : LAT + NWAVE]
    return (feature, final[length - 1])


def own_part(full, dim):
    count = lax.axis_size("dp") * lax.axis_size("fsdp")
    index = lax.axis_index("dp") * lax.axis_size("fsdp") + lax.axis_index("fsdp")
    piece = full.shape[dim] // count
    return lax.dynamic_slice_in_dim(full, index * piece, piece, dim)


def tdot(left, right):
    return lax.dot_general(
        left, right, (((0,), (0,)), ((), ())), preferred_element_type=jnp.float32
    )


def ndot(left, right):
    return lax.dot_general(
        left, right, (((1,), (1,)), ((), ())), preferred_element_type=jnp.float32
    )


MESH_ID = pl.DeviceIdType.MESH
ANY = pl.BlockSpec(memory_space=pl.ANY)
VMEM = pl.BlockSpec(memory_space=pltpu.VMEM)


class Net:
    def __init__(self, planes):
        dp, fs = lax.axis_index("dp"), lax.axis_index("fsdp")
        self.planes = planes
        self.z, self.x = lax.div(dp, 2), lax.rem(dp, 2)
        self.y, self.c = lax.div(fs, 2), lax.rem(fs, 2)
        self.sib = self.at(self.z, self.x, self.y, 1 - self.c)
        self.nx = self.at(self.z, 1 - self.x, self.y, self.c)
        self.ny = self.at(self.z, self.x, 1 - self.y, self.c)

    def at(self, z, x, y, c):
        return (z * 2 + x, y * 2 + c)

    def plane(self, k):
        return lax.rem(self.z + k, self.planes)

    def zpeer(self, k):
        return self.at(self.plane(k), self.x, self.y, self.c)

    def chip(self, k, dx=0, dy=0):
        x = 1 - self.x if dx else self.x
        y = 1 - self.y if dy else self.y
        return self.plane(k) * 4 + x * 2 + y

    def greet(self):
        barrier = pltpu.get_barrier_semaphore()
        partners = [self.sib, self.nx, self.ny]
        partners += [self.zpeer(k) for k in range(1, self.planes)]
        for partner in partners:
            pl.semaphore_signal(barrier, inc=1, device_id=partner, device_id_type=MESH_ID)
        pl.semaphore_wait(barrier, len(partners))


class Wires:
    def __init__(self, send, recv):
        self.send, self.recv, self.used, self.started = send, recv, 0, []

    def push(self, src, dst, device):
        index = self.used
        self.used += 1
        copy = pltpu.make_async_remote_copy(
            src_ref=src,
            dst_ref=dst,
            send_sem=self.send.at[index],
            recv_sem=self.recv.at[index],
            device_id=device,
            device_id_type=MESH_ID,
        )
        copy.start()
        self.started.append(copy)
        return copy

    def drain(self):
        for copy in self.started:
            copy.wait_send()


class Gather:
    def __init__(self, net, wires, own, piece):
        self.net, self.wires, self.own, self.piece = net, wires, own, piece
        self.z_in, self.first, self.second, self.twins = {}, {}, {}, []

    def near(self, h):
        return self.net.ny if h else self.net.nx

    def far(self, h):
        return self.net.nx if h else self.net.ny

    def share(self, chip, h, src=None):
        spot = self.piece(chip, h)
        self.twins.append(self.wires.push(spot if src is None else src, spot, self.net.sib))

    def begin_z(self):
        for k in range(1, self.net.planes):
            for h in range(2):
                spot = self.piece(self.net.chip(0), h)
                self.z_in[k, h] = self.wires.push(self.own(h), spot, self.net.zpeer(k))

    def spread(self, k):
        back = (self.net.planes - k) % self.net.planes
        for h in range(2):
            if k:
                self.z_in[k, h].wait_recv()
            spot = self.piece(self.net.chip(back), h)
            src = self.own(h) if k == 0 else spot
            self.first[k, h] = self.wires.push(src, spot, self.near(h))
            self.second[k, h, 0] = self.wires.push(src, spot, self.far(h))
            self.share(self.net.chip(back), h, src)

    def relay(self, k):
        back = (self.net.planes - k) % self.net.planes
        for h in range(2):
            self.first[k, h].wait_recv()
            chip = self.net.chip(back, dx=h == 0, dy=h == 1)
            spot = self.piece(chip, h)
            self.second[k, h, 1] = self.wires.push(spot, spot, self.far(h))
            self.share(chip, h)

    def close(self, k):
        back = (self.net.planes - k) % self.net.planes
        for h in range(2):
            for hop in range(2):
                self.second[k, h, hop].wait_recv()
                chip = self.net.chip(back, dx=hop == 1 or h == 1, dy=hop == 1 or h == 0)
                self.share(chip, h)

    def finish(self):
        for copy in self.twins:
            copy.wait_recv()


def gather_copies(planes):
    return 2 * (planes - 1) + 4 * planes + 2 * planes + 8 * planes


class Reduce:
    def __init__(self, net, wires, part, held, near_in, far_in, z_in):
        self.net, self.wires, self.part, self.held = net, wires, part, held
        self.near_in, self.far_in, self.z_in = near_in, far_in, z_in
        self.pairs, self.near, self.far, self.along = {}, {}, {}, {}

    def add(self, spot, other):
        size = 16 if spot.shape[0] % 16 == 0 else 8

        def some(i, _):
            at = pl.ds(pl.multiple_of(i * size, size), size)
            total = spot[at].astype(jnp.float32) + other[at].astype(jnp.float32)
            spot[at] = total.astype(spot.dtype)
            return 0

        lax.fori_loop(0, spot.shape[0] // size, some, 0)

    def begin(self, k):
        for dx in range(2):
            for dy in range(2):
                for h in range(2):
                    chip = self.net.chip(k, dx, dy)
                    self.pairs[k, dx, dy, h] = self.wires.push(
                        self.part(chip, 1 - self.net.c, h), self.held.at[chip, h], self.net.sib
                    )

    def stage0(self, k):
        for dx, dy in ((1, 1), (0, 1), (1, 0), (0, 0)):
            for h in range(2):
                self.pairs[k, dx, dy, h].wait_recv()
                chip = self.net.chip(k, dx, dy)
                self.add(self.held.at[chip, h], self.part(chip, self.net.c, h))
                if (dy if h == 0 else dx) == 1:
                    other = dx if h == 0 else dy
                    self.near[k, h, other] = self.wires.push(
                        self.held.at[chip, h],
                        self.near_in.at[k, h, other],
                        self.net.ny if h == 0 else self.net.nx,
                    )

    def stage1(self, k):
        for h in range(2):
            for other in (1, 0):
                self.near[k, h, other].wait_recv()
                chip = self.net.chip(k, other, 0) if h == 0 else self.net.chip(k, 0, other)
                self.add(self.held.at[chip, h], self.near_in.at[k, h, other])
                if other:
                    self.far[k, h] = self.wires.push(
                        self.held.at[chip, h],
                        self.far_in.at[k, h],
                        self.net.nx if h == 0 else self.net.ny,
                    )

    def stage2(self, k):
        for h in range(2):
            self.far[k, h].wait_recv()
            spot = self.held.at[self.net.chip(k), h]
            self.add(spot, self.far_in.at[k, h])
            if k:
                self.along[k, h] = self.wires.push(spot, self.z_in.at[k - 1, h], self.net.zpeer(k))

    def total(self, h):
        value = self.held[self.net.chip(0), h].astype(jnp.float32)
        for k in range(1, self.net.planes):
            self.along[k, h].wait_recv()
            value = value + self.z_in[k - 1, h].astype(jnp.float32)
        return value


def reduce_copies(planes):
    return 8 * planes + 4 * planes + 2 * planes + 2 * (planes - 1)


def reduce_scratch(planes, rows, cols, dtype):
    return [
        pltpu.VMEM((planes * 4, 2, rows, cols), dtype),
        pltpu.VMEM((planes, 2, 2, rows, cols), dtype),
        pltpu.VMEM((planes, 2, rows, cols), dtype),
        pltpu.VMEM((planes - 1, 2, rows, cols), dtype),
    ]


def dot_nn(left, right):
    return jnp.dot(left, right, preferred_element_type=jnp.float32)


class Trade:
    def __init__(self, src, dst, send, recv, local):
        self.src, self.dst, self.send, self.recv = src, dst, send, recv
        self.count = src.shape[0]
        self.me = lax.axis_index("dp") * 4 + lax.axis_index("fsdp")
        self.own = pltpu.make_async_copy(src.at[self.me], dst.at[self.me], local)

    def place(self, i):
        to = lax.rem(self.me + i, self.count)
        return to, (lax.div(to, 4), lax.rem(to, 4))

    def greet(self):
        barrier = pltpu.get_barrier_semaphore()

        def call(i, _):
            pl.semaphore_signal(
                barrier, inc=1, device_id=self.place(i)[1], device_id_type=MESH_ID
            )
            return 0

        lax.fori_loop(1, self.count, call, 0)
        pl.semaphore_wait(barrier, self.count - 1)

    def copy(self, i):
        to, device = self.place(i)
        return pltpu.make_async_remote_copy(
            src_ref=self.src.at[to],
            dst_ref=self.dst.at[self.me],
            send_sem=self.send.at[i],
            recv_sem=self.recv.at[i],
            device_id=device,
            device_id_type=MESH_ID,
        )

    def begin(self, part=0, parts=1):
        def go(i, _):
            self.copy(i).start()
            return 0

        cuts = [1 + (self.count - 1) * p // parts for p in (part, part + 1)]
        lax.fori_loop(*cuts, go, 0)
        if part == 0:
            self.own.start()

    def finish(self):
        def end(i, _):
            self.copy(i).wait()
            return 0

        lax.fori_loop(1, self.count, end, 0)
        self.own.wait()


class Pump:
    def __init__(self):
        self.units, self.at, self.last = [], 0, False

    def put(self, item, order):
        for k in order:
            item.begin(k)
        self.units += [(item, k) for k in order]

    def step(self, count=1):
        for _ in range(count):
            if self.at >= len(self.units) and not self.last:
                return
            for stage, lag in enumerate(LAGS):
                at = self.at - lag
                if 0 <= at < len(self.units) and self.units[at]:
                    item, k = self.units[at]
                    (item.stage0, item.stage1, item.stage2)[stage](k)
            self.at += 1

    def until(self, item):
        self.last = True
        last = max(i for i, unit in enumerate(self.units) if unit and unit[0] is item)
        while self.at <= last + LAGS[2]:
            self.step()


def order_column(order):
    turned = order[...].astype(jnp.float32).T
    column = [turned[:, i : i + 1] for i in range(turned.shape[1])]
    return jnp.concatenate(column, axis=0).astype(jnp.int32)


def tile_rows(i, size):
    return pl.ds(pl.multiple_of(i * size, size), size)


def norm_back(grad, rows, gain):
    mean = jnp.mean(rows, axis=-1, keepdims=True)
    centred = rows - mean
    spread = jnp.mean(centred * centred, axis=-1, keepdims=True)
    inverse = lax.rsqrt(spread + EPS)
    unit = centred * inverse
    scaled = grad * gain
    inner = scaled - jnp.mean(scaled, axis=-1, keepdims=True)
    inner = inner - unit * jnp.mean(scaled * unit, axis=-1, keepdims=True)
    return inverse * inner, grad * unit


def lay_lines(box, at, value):
    for i in range(value.shape[1] // 128):
        box[0, pl.ds(at + i, 1), :] = value[:, i * 128 : (i + 1) * 128]
    return at + value.shape[1] // 128


def box_lines(waves, width, hidden, dec_width):
    used = waves + (6 * width + hidden + 2 * dec_width) // 128
    return used + (-used) % 8


FT = 256
TRADES = 1
LAGS = (0, 3, 6)
BUBBLES = 3
HOP_STEPS = 1
NORM_STEPS = 2
HEAD_STEPS = 1
FEED_STEPS = 1
BLOCK = 128


def backward_kernel(planes, steps, sizes, *refs):
    (rows, width, hidden, dec_width, chips, patches) = sizes
    devices = planes * 8
    seen = rows // chips
    (
        blocks, returned, visible, order, ending, wide, down, activ, slope, normed2, middle, context,
        joint, probs, normed, start, slots, gains, weight, feature, source, gen_rows, gen_down,
        gen_vec, wave_code,
    ) = refs[:25]
    (
        dec_out, up_out, oq_out, down_out, kw_out, kb_out, all_out, gen_wide, gen_tall, gen_seq,
        gen_lines, bias_out, embed_out, decoder_out,
    ) = refs[25:39]
    scratch = refs[39:61]
    (
        big, left, w_down, w_up, t_activ, t_slope, resid, w_sq, t_joint, t_probs,
        g_dec, g_up, g_down, g_oq, g_table, run, back, g_low, g_joint, v_sums,
        f_dec, f_up, f_oq, hand_dec, hand_up, hand_oq, box, send, recv, trade_send, trade_recv, tile_sem, load_sem,
    ) = refs[61:]
    loads = {}

    def load(name, src, dst):
        copy = pltpu.make_async_copy(src, dst, load_sem.at[len(loads)])
        copy.start()
        loads[name] = copy

    up_at, out_at, dec_at = 3 * width, 3 * width + hidden, 4 * width + hidden
    load("returned", returned, big)
    w_dec = w_sq.at[0, :, pl.ds(0, dec_width)]
    load("dec", wide.at[:, pl.ds(dec_at, dec_width)], w_dec)
    load("ending", ending, left.at[0])

    def tile_copies(t):
        slot = lax.rem(t, 2)
        at = tile_rows(t, FT)
        return (
            pltpu.make_async_copy(down.at[at], w_down.at[slot], tile_sem.at[slot, 0]),
            pltpu.make_async_copy(
                wide.at[:, pl.ds(pl.multiple_of(up_at + t * FT, 128), FT)],
                w_up.at[slot],
                tile_sem.at[slot, 1],
            ),
            pltpu.make_async_copy(activ.at[:, at], t_activ.at[slot], tile_sem.at[slot, 2]),
            pltpu.make_async_copy(slope.at[:, at], t_slope.at[slot], tile_sem.at[slot, 3]),
        )

    for copy in tile_copies(0):
        copy.start()
    load("normed2", normed2, left.at[1])
    load("middle", middle, resid)
    load("query", wide.at[:, pl.ds(0, width)], w_sq.at[1])

    net = Net(planes)
    trade = Trade(blocks, decoder_out, trade_send, trade_recv, load_sem.at[15])
    trade.greet()
    trade.begin(0, TRADES)
    wires = Wires(send, recv)
    pump = Pump()
    shard = width // (devices // 2)
    w_rows = lambda chip: pl.ds(pl.multiple_of(chip * shard, 16), shard)

    def quarter(ref, size):
        return lambda chip, c, h: ref.at[
            w_rows(chip), pl.ds(pl.multiple_of((c * 2 + h) * size, 128), size)
        ]

    def stripe(ref, size):
        return lambda chip, c, h: ref.at[
            pl.ds(pl.multiple_of(((chip * 2 + c) * 2 + h) * size, 16), size)
        ]

    q_dec, q_up = dec_width // 4, hidden // 8
    d_rows = hidden // devices // 2
    t_rows = g_table.shape[0] // devices // 2
    parts = (
        quarter(g_dec, q_dec),
        quarter(g_up.at[0], q_up),
        quarter(g_up.at[1], q_up),
        stripe(g_down, d_rows),
        stripe(g_table, t_rows),
        lambda chip, c, h: g_oq.at[c * 2 + h, w_rows(chip)],
    )
    lands = [scratch[i * 4 : i * 4 + 4] for i in range(5)]
    lands.append((scratch[20], lands[3][1], lands[3][2], scratch[21]))
    dec, up0, up1, downs, tables, oq = [
        Reduce(net, wires, part, *land) for part, land in zip(parts, lands)
    ]
    away = list(range(1, planes)) + [0]

    loads["returned"].wait()
    grad_mask = jnp.zeros((8, dec_width), jnp.float32)
    column = order_column(order)
    spread = big.reshape(devices, chips, patches // devices, dec_width)
    for chip in range(chips):
        got = spread[:, chip].reshape(patches, dec_width)
        chosen = (column == visible[pl.ds(chip, 1), :]).astype(jnp.float32)
        picked = tdot(chosen.astype(jnp.bfloat16), got)
        g_joint[pl.ds(chip * seen, seen), pl.ds(0, dec_width)] = picked.astype(jnp.bfloat16)
        left_out = 1.0 - jnp.sum(chosen, axis=1, keepdims=True)
        left_out = jnp.broadcast_to(left_out, (patches, 8)).astype(jnp.bfloat16)
        grad_mask = grad_mask + tdot(left_out, got)
    v_sums[pl.ds(7, 1), pl.ds(dec_width, dec_width)] = grad_mask[:1]
    load("slots", slots, big)
    grad_rows = g_joint[:, pl.ds(0, dec_width)]
    v_sums[pl.ds(7, 1), pl.ds(0, dec_width)] = jnp.sum(
        grad_rows.astype(jnp.float32), axis=0, keepdims=True
    )
    loads["ending"].wait()

    def dec_part(i, _):
        at = tile_rows(i, FT)
        g_dec[at, :] = tdot(left[0, :, at], grad_rows).astype(jnp.bfloat16)
        return 0

    lax.fori_loop(0, width // FT, dec_part, 0)
    pump.put(dec, away)
    loads["dec"].wait()

    def end_part(i, _):
        at = tile_rows(i, FT)
        run[at, :] = ndot(g_joint[at, pl.ds(0, dec_width)], w_dec[...])
        g_low[at, :] = run[at, :].astype(jnp.bfloat16)
        return 0

    lax.fori_loop(0, rows // FT, end_part, 0)
    load("out", wide.at[:, pl.ds(out_at, width)], w_sq.at[0])
    load("context", context, left.at[0])
    back[...] = jnp.zeros_like(back)
    v_sums[pl.ds(0, 1), pl.ds(0, width)] = jnp.sum(
        g_low[...].astype(jnp.float32), axis=0, keepdims=True
    )
    loads["normed2"].wait()
    tiles = hidden // FT

    parts_sent = [1]

    def trade_more():
        if parts_sent[0] < TRADES:
            trade.begin(parts_sent[0], TRADES)
            parts_sent[0] += 1

    def feed(t, _):
        slot = lax.rem(t, 2)

        @pl.when(t + 1 < tiles)
        def _():
            for copy in tile_copies(t + 1):
                copy.start()

        for copy in tile_copies(t):
            copy.wait()
        grad = ndot(g_low[...], w_down[slot])
        grad_upper = (grad * t_slope[slot].astype(jnp.float32)).astype(jnp.bfloat16)
        at = tile_rows(t, FT)
        v_sums[pl.ds(1, 1), at] = jnp.sum(
            grad_upper.astype(jnp.float32), axis=0, keepdims=True
        )
        g_down[at, :] = tdot(t_activ[slot], g_low[...]).astype(jnp.bfloat16)
        g_up[lax.div(t, tiles // 2), :, tile_rows(lax.rem(t, tiles // 2), FT)] = tdot(
            left[1], grad_upper
        ).astype(jnp.bfloat16)
        for i in range(rows // FT):
            part = pl.ds(i * FT, FT)
            back[part, :] += ndot(grad_upper[i * FT : (i + 1) * FT], w_up[slot])
        return 0

    for i in range(0, tiles, 2):
        lax.fori_loop(i, i + 2, feed, 0)
        if i + 2 == tiles // 2:
            pump.put(up0, away)
        if i + 2 < tiles:
            trade_more()
            pump.step(FEED_STEPS)
    pump.put(up1, away)
    pump.put(downs, away)
    load("normed", normed, left.at[1])
    loads["middle"].wait()

    def through_norm(gain_row, sums_at):
        gain = gains[pl.ds(gain_row, 1), pl.ds(0, width)]

        def block(i, sums):
            at = tile_rows(i, BLOCK)
            grad = back[at, :]
            inner, terms = norm_back(grad, resid[at, :], gain)
            run[at, :] += inner
            return (
                sums[0] + jnp.sum(terms, axis=0, keepdims=True),
                sums[1] + jnp.sum(grad, axis=0, keepdims=True),
            )

        zero = jnp.zeros((1, width), jnp.float32)
        sums = lax.fori_loop(0, rows // BLOCK, block, (zero, zero))
        v_sums[pl.ds(sums_at, 1), pl.ds(0, width)] = sums[0]
        v_sums[pl.ds(sums_at + 1, 1), pl.ds(0, width)] = sums[1]

    through_norm(2, 2)
    pump.step(NORM_STEPS)
    load("start", start, resid)
    g_low[...] = run[...].astype(jnp.bfloat16)
    loads["context"].wait()
    loads["out"].wait()

    def out_part(i, _):
        at = tile_rows(i, FT)
        g_oq[0, at, :] = tdot(left[0, :, at], g_low[...]).astype(jnp.bfloat16)
        return 0

    lax.fori_loop(0, width // FT, out_part, 0)

    def context_part(i, _):
        at = tile_rows(i, FT)
        g_low[at, :] = ndot(g_low[at, :], w_sq[0]).astype(jnp.bfloat16)
        return 0

    lax.fori_loop(0, rows // FT, context_part, 0)
    load("key", wide.at[:, pl.ds(width, width)], w_sq.at[0])
    pump.step(2)

    pairs = width // 128
    head = width // HEADS
    scale = 1.0 / math.sqrt(head)
    odd = lax.broadcasted_iota(jnp.int32, (1, 128), 1) >= head

    def pair_copies(n):
        slot = lax.rem(n, 2)
        at = tile_rows(lax.div(n, pairs), seen)
        copies = [
            pltpu.make_async_copy(probs.at[pl.ds(2 * n, 2)], t_probs.at[slot], tile_sem.at[slot, 0])
        ]
        for i in range(3):
            lane = pl.ds(pl.multiple_of(lax.rem(n, pairs) * 128 + i * width, 128), 128)
            copies.append(
                pltpu.make_async_copy(
                    joint.at[at, lane], t_joint.at[slot, i], tile_sem.at[slot, i + 1]
                )
            )
        return copies

    for copy in pair_copies(0):
        copy.start()

    def attend(n, _):
        slot = lax.rem(n, 2)

        @pl.when(n + 1 < chips * pairs)
        def _():
            for copy in pair_copies(n + 1):
                copy.start()

        for copy in pair_copies(n):
            copy.wait()
        chip = lax.div(n, pairs)
        pair = lax.rem(n, pairs)
        at = tile_rows(chip, seen)
        lanes = [
            pl.ds(pl.multiple_of(pair * 128 + i * width, 128), 128) for i in range(3)
        ]
        query, key, value = [t_joint[slot, i] for i in range(3)]
        grad = g_low[at, lanes[0]]
        zero = jnp.zeros_like(grad)
        totals = [None, None, None]
        for h in range(2):
            mine = odd if h else jnp.logical_not(odd)
            grad_h = jnp.where(mine, grad, zero)
            query_h = jnp.where(mine, query, zero)
            key_h = jnp.where(mine, key, zero)
            prob = t_probs[slot, h]
            prob32 = prob.astype(jnp.float32)
            grad_prob = ndot(grad_h, value)
            row_dot = jnp.sum(prob32 * grad_prob, axis=-1, keepdims=True)
            grad_score = (prob32 * (grad_prob - row_dot)).astype(jnp.bfloat16)
            terms = (dot_nn(grad_score, key_h), tdot(grad_score, query_h), tdot(prob, grad_h))
            totals = [new if old is None else old + new for old, new in zip(totals, terms)]
        g_joint[at, lanes[0]] = (totals[0] * scale).astype(jnp.bfloat16)
        g_joint[at, lanes[1]] = (totals[1] * scale).astype(jnp.bfloat16)
        g_joint[at, lanes[2]] = totals[2].astype(jnp.bfloat16)
        return 0

    for i in range(0, chips * pairs, 2):
        lax.fori_loop(i, i + 2, attend, 0)
        trade_more()
        pump.step(HEAD_STEPS)

    loads["normed"].wait()
    def joint_part(i, _):
        which, at = lax.div(i, width // FT), tile_rows(lax.rem(i, width // FT), FT)
        lane = pl.ds(pl.multiple_of(which * width, 128), width)
        g_oq[which + 1, at, :] = tdot(left[1, :, at], g_joint[:, lane]).astype(jnp.bfloat16)
        return 0

    lax.fori_loop(0, 3 * width // FT, joint_part, 0)
    value = pltpu.make_async_copy(
        wide.at[:, pl.ds(2 * width, width)], w_sq.at[1], load_sem.at[len(loads)]
    )
    back[...] = jnp.zeros_like(back)

    def joint_back(i, _):
        for j, copy in enumerate((loads["query"], loads["key"], value)):

            @pl.when(i == j)
            def _():
                copy.wait()

        lane = pl.ds(pl.multiple_of(i * width, 128), width)

        def some(j, _):
            at = tile_rows(j, FT)
            back[at, :] += ndot(g_joint[at, lane], w_sq[lax.rem(i + 1, 2)])
            return 0

        lax.fori_loop(0, rows // FT, some, 0)

        @pl.when(i == 0)
        def _():
            value.start()

        return 0

    lax.fori_loop(0, 3, joint_back, 0)
    pump.step(1)
    loads["start"].wait()
    through_norm(0, 4)
    g_low[...] = run[...].astype(jnp.bfloat16)
    conv = jnp.sum(run[...], axis=0, keepdims=True)
    embed = pltpu.make_async_copy(g_low, embed_out, tile_sem.at[0, 1])
    embed.start()
    loads["slots"].wait()
    span = 512

    def table_block(i, _):
        at = tile_rows(i, span)
        g_table[at, :] = dot_nn(big[at, :], g_low[...]).astype(jnp.bfloat16)
        return 0

    lax.fori_loop(0, g_table.shape[0] // span, table_block, 0)
    pump.put(tables, away)
    pump.units += [None] * BUBBLES
    pump.put(oq, away)

    waves = t_rows
    lines = width // 128
    box[0, pl.ds(waves, box.shape[1] - waves), :] = jnp.zeros(
        (box.shape[1] - waves, 128), jnp.float32
    )
    at = lay_lines(box, waves, conv)
    for line in (4, 5, 2, 3, 0):
        at = lay_lines(box, at, v_sums[pl.ds(line, 1), pl.ds(0, width)])
    at = lay_lines(box, at, v_sums[pl.ds(1, 1), :])
    lay_lines(box, at, v_sums[pl.ds(7, 1), pl.ds(0, 2 * dec_width)])

    while parts_sent[0] < TRADES:
        trade_more()
    pump.until(tables)
    held = tables.held
    partial_sum = jnp.zeros((waves, 128), jnp.float32)
    for h in range(2):
        own = tables.total(h).astype(jnp.bfloat16)
        cols = pl.ds(h * width, width)
        kw_out[:, cols] = tdot(feature[...], own)
        kb_out[:, cols] = jnp.sum(own.astype(jnp.float32), axis=0, keepdims=True)
        partial_sum = partial_sum + ndot(own, weight[:, cols])
    box[0, pl.ds(0, waves), :] = partial_sum
    peers = [net.sib, net.nx, net.ny]
    for bit in range(steps):
        step = 1 << bit
        up = lax.rem(lax.div(net.z, step), 2) == 0
        peers.append(net.at(jnp.where(up, net.z + step, net.z - step), net.x, net.y, net.c))
    for i, peer in enumerate(peers):
        hop = wires.push(box.at[2 * i], box.at[2 * i + 1], peer)
        pump.step(HOP_STEPS)
        hop.wait_recv()
        box[2 * i + 2] = box[2 * i] + box[2 * i + 1]
    end = box.at[2 * len(peers)]
    all_out[...] = end[...]
    me = net.chip(0) * 2 + net.c
    conv = jnp.concatenate(
        [end[pl.ds(waves + i, 1), :] for i in range(lines)], axis=1
    )
    gen_width = gen_rows.shape[0]
    up_size = gen_down.shape[0]
    bias_at = gen_rows.shape[1] - gen_width - width
    grad_source = lax.dot_general(
        jnp.broadcast_to(conv, (8, width)),
        gen_rows[:, pl.ds(bias_at, width)].astype(jnp.float32),
        (((1,), (1,)), ((), ())),
        precision=HIGH,
        preferred_element_type=jnp.float32,
    )
    top = lax.broadcasted_iota(jnp.int32, (8, gen_width), 0)
    grad_source = jnp.where(top == 0, grad_source, 0.0)
    pump.step(1)
    small = gen_width // devices
    lane = lax.broadcasted_iota(jnp.int32, (8, gen_width), 1)
    pick = ((lane == me * small + top) & (top < small)).astype(jnp.float32)
    exact = partial(
        lax.dot_general, precision=HIGH, preferred_element_type=jnp.float32
    )
    rows_of = lambda value: exact(pick, value, (((1,), (0,)), ((), ())))
    lanes_of = lambda value: exact(value, pick, (((1,), (1,)), ((), ())))
    chunk = up_size // 4

    def put_up(i, value):
        gen_wide[:, pl.ds(pl.multiple_of(i * chunk, chunk), chunk)] = rows_of(value)

    def put_down(i, value):
        back[:, pl.ds(pl.multiple_of(i * gen_width, gen_width), gen_width)] = value

    g_seq, g_qkv, g_out, thin = gen_back(
        gen_rows, gen_down, gen_vec, wave_code[...], LAT + NWAVE + 1, end[pl.ds(0, waves), :],
        grad_source, v_sums, put_up, put_down,
    )
    pump.step(2)
    gen_wide[:, pl.ds(up_size, 3 * gen_width)] = rows_of(g_qkv)
    gen_wide[:, pl.ds(up_size + 3 * gen_width, gen_width)] = rows_of(g_out)
    tall = up_size // devices
    per = devices // 4
    gen_tall[...] = back[
        tile_rows(lax.rem(me, per), tall),
        pl.ds(pl.multiple_of(lax.div(me, per) * gen_width, 128), gen_width),
    ]
    gen_seq[...] = lanes_of(g_seq)
    for i, value in enumerate(thin):
        gen_lines[pl.ds(i, 1), pl.ds(0, gen_width)] = value
    gen_lines[pl.ds(6, 1), :] = v_sums[pl.ds(6, 1), pl.ds(0, up_size)]
    own_source = jnp.sum(
        pick * source[pl.ds(0, 1), :].astype(jnp.float32), axis=1, keepdims=True
    )
    bias_out[...] = own_source * conv
    pump.until(oq)
    half = shard // 2
    own_rows = pl.ds(pl.multiple_of(net.c * half, 8), half)
    their_rows = pl.ds(pl.multiple_of((1 - net.c) * half, 8), half)
    jobs = (
        (dec, f_dec, hand_dec, dec_out, 0, q_dec),
        (up0, f_up.at[0], hand_up.at[0], up_out, 0, q_up),
        (up1, f_up.at[1], hand_up.at[1], up_out, hidden // 2, q_up),
        (oq, f_oq, hand_oq, oq_out, 0, width),
    )
    swaps = []
    for item, final, hand, out, base, size in jobs:
        for h in range(2):
            final[h] = item.total(h)
            swaps.append(wires.push(final.at[h, their_rows], hand.at[h], net.sib))
    for h in range(2):
        down_out[pl.ds(h * d_rows, d_rows)] = downs.total(h)
    for item, final, hand, out, base, size in jobs:
        for h in range(2):
            own = pl.ds(pl.multiple_of(base + (net.c * 2 + h) * size, 128), size)
            other = pl.ds(pl.multiple_of(base + ((1 - net.c) * 2 + h) * size, 128), size)
            out[:, own] = final[h, own_rows]
            swaps.pop(0).wait_recv()
            out[:, other] = hand[h]
    embed.wait()
    trade.finish()
    wires.drain()


def backward(planes, sizes, *args):
    (rows, width, hidden, dec_width, chips, patches) = sizes
    devices = planes * 8
    steps = (planes - 1).bit_length()
    low, full = jnp.bfloat16, jnp.float32
    shard = width // (devices // 2)
    q_dec, q_up = dec_width // 4, hidden // 8
    d_rows = hidden // devices // 2
    slots = args[16].shape[0]
    t_rows = slots // devices // 2
    box_rows = box_lines(t_rows, width, hidden, dec_width)
    up_size, gen_width = args[22].shape
    copies = 6 * reduce_copies(planes) + 3 + steps + 8
    scratch = []
    for shape in (
        (shard, q_dec), (shard, q_up), (shard, q_up), (d_rows, width), (t_rows, width),
    ):
        scratch += reduce_scratch(planes, *shape, low)
    assert d_rows == shard
    last = reduce_scratch(planes, shard, width, low)
    scratch += [last[0], last[3]]
    scratch += [
        pltpu.VMEM((chips * patches, dec_width), low),
        pltpu.VMEM((2, rows, width), low),
        pltpu.VMEM((2, FT, width), low),
        pltpu.VMEM((2, width, FT), low),
        pltpu.VMEM((2, rows, FT), low),
        pltpu.VMEM((2, rows, FT), low),
        pltpu.VMEM((rows, width), full),
        pltpu.VMEM((2, width, width), low),
        pltpu.VMEM((2, 3, rows // chips, 128), low),
        pltpu.VMEM((2, 2, rows // chips, rows // chips), low),
        pltpu.VMEM((width, dec_width), low),
        pltpu.VMEM((2, width, hidden // 2), low),
        pltpu.VMEM((hidden, width), low),
        pltpu.VMEM((4, width, width), low),
        pltpu.VMEM((slots, width), low),
        pltpu.VMEM((rows, width), full),
        pltpu.VMEM((rows, width), full),
        pltpu.VMEM((rows, width), low),
        pltpu.VMEM((rows, 3 * width), low),
        pltpu.VMEM((8, hidden), full),
        pltpu.VMEM((2, shard, q_dec), full),
        pltpu.VMEM((2, 2, shard, q_up), full),
        pltpu.VMEM((2, shard, width), full),
        pltpu.VMEM((2, shard // 2, q_dec), full),
        pltpu.VMEM((2, 2, shard // 2, q_up), full),
        pltpu.VMEM((2, shard // 2, width), full),
        pltpu.VMEM((2 * (3 + steps) + 1, box_rows, 128), full),
        pltpu.SemaphoreType.DMA((copies,)),
        pltpu.SemaphoreType.DMA((copies,)),
        pltpu.SemaphoreType.DMA((devices,)),
        pltpu.SemaphoreType.DMA((devices,)),
        pltpu.SemaphoreType.DMA((2, 4)),
        pltpu.SemaphoreType.DMA((16,)),
    ]
    shapes = (
        ((width // devices, dec_width), full),
        ((width // devices, hidden), full),
        ((width // devices, 4 * width), full),
        ((hidden // devices, width), full),
        ((args[19].shape[1], 2 * width), full),
        ((1, 2 * width), full),
        ((box_rows, 128), full),
        ((8, up_size + 4 * gen_width), full),
        ((up_size // devices, gen_width), full),
        ((args[24].shape[0] + gen_width + 8, 8), full),
        ((8, up_size), full),
        ((8, width), full),
        ((rows, width), low),
        (args[0].shape, low),
    )
    spots = [ANY, ANY, VMEM, VMEM] + [ANY] * 13 + [VMEM] * 8
    return pl.pallas_call(
        partial(backward_kernel, planes, steps, sizes),
        out_shape=tuple(jax.ShapeDtypeStruct(shape, dtype) for shape, dtype in shapes),
        in_specs=spots,
        out_specs=[VMEM] * 12 + [ANY] * 2,
        scratch_shapes=scratch,
        compiler_params=pltpu.CompilerParams(
            collective_id=2, has_side_effects=True, vmem_limit_bytes=125 * 2**19
        ),
    )(*args)


CHUNK = 896
TRADE_PARTS = 1


def gen_layer(
    seq, qkv, out, out_bias, gain1, shift1, up, up_bias, down, down_bias, gain2, shift2, length
):
    width = seq.shape[1]
    size = width // GHEADS

    def times(left, right):
        return jnp.dot(left, right, precision=HIGH, preferred_element_type=jnp.float32)

    joint = times(seq, qkv)
    query, key, value = [joint[:, i * width : (i + 1) * width] for i in range(3)]
    lane = lax.broadcasted_iota(jnp.int32, (1, width), 1)
    spot = lax.broadcasted_iota(jnp.int32, (1, seq.shape[0]), 1)
    context = jnp.zeros_like(seq)
    for h in range(GHEADS):
        mine = (lax.div(lane, size) == h).astype(jnp.float32)
        scores = lax.dot_general(
            query * mine,
            key,
            (((1,), (1,)), ((), ())),
            precision=HIGH,
            preferred_element_type=jnp.float32,
        ) * (1.0 / math.sqrt(size))
        scores = jnp.where(spot < length, scores, -1e30)
        peak = lax.stop_gradient(jnp.max(scores, axis=-1, keepdims=True))
        raised = jnp.exp(scores - peak)
        probs = raised / jnp.sum(raised, axis=-1, keepdims=True)
        context = context + times(probs, value * mine)
    mixed = norm_rows(seq + times(context, out) + out_bias, gain1, shift1)
    inner = times(mixed, up) + up_bias
    hidden = 0.5 * inner * (1.0 + lax.erf(inner * math.sqrt(0.5)))
    return norm_rows(mixed + times(hidden, down) + down_bias, gain2, shift2)


def gen_seq_of(gen_rows, wave_code, up_size):
    width = gen_rows.shape[0]
    full = jnp.float32
    tokens = gen_rows[:, pl.ds(up_size + 4 * width, width)].astype(full).T
    last = gen_rows[:, pl.ds(gen_rows.shape[1] - width, width)].astype(full).T
    return jnp.concatenate([tokens, wave_code, last[:8]], axis=0)


def gen_parts(gen_rows, gen_down, gen_vec, wave_code, up_size):
    width = gen_rows.shape[0]
    full = jnp.float32
    at = up_size
    up = gen_rows[:, pl.ds(0, up_size)].astype(full)
    qkv = gen_rows[:, pl.ds(at, 3 * width)].astype(full)
    out = gen_rows[:, pl.ds(at + 3 * width, width)].astype(full)
    seq = gen_seq_of(gen_rows, wave_code, up_size)
    vec = [gen_vec[pl.ds(i, 1), pl.ds(0, width)] for i in range(6)]
    up_bias = gen_vec[pl.ds(6, 1), :]
    down = gen_down[...].astype(full)
    return (seq, qkv, out, vec[0], vec[1], vec[2], up, up_bias, down, vec[3], vec[4], vec[5])


def join_lanes(parts, size):
    owners = parts.shape[0]
    shape = (128, owners * size)
    lane = lax.broadcasted_iota(jnp.int32, shape, 0)
    column = lax.broadcasted_iota(jnp.int32, shape, 1)
    spread = dot_nn(parts, (lax.rem(column, size) == lane).astype(parts.dtype))
    shape = (owners, owners * size)
    row = lax.broadcasted_iota(jnp.int32, shape, 0)
    column = lax.broadcasted_iota(jnp.int32, shape, 1)
    return jnp.sum(
        jnp.where(lax.div(column, size) == row, spread, 0.0), axis=0, keepdims=True
    )


def prepare_kernel(planes, sizes, *refs):
    (rows, width, hidden, dec_width, chips, up_size, patches) = sizes
    devices = planes * 8
    (
        qkv, up, out, dec, down, weight, weight_bias, pixels, sensor, waves, visible, places,
        wave_code, gen_up, gen_qkv, gen_out, bias_weight, gen_tokens, gen_low, cotangent, order,
    ) = refs[:21]
    thin = refs[21:36]
    (
        wide_out, down_out, table_out, slots_out, returned, normed_out, joint_out, probs_out,
        context_out, middle_out, normed2_out, activ_out, slope_out, ending_out, start_out, ordered,
        gen_rows, gen_down, gen_vec, vecs, feature_out, source_out,
    ) = refs[36:58]
    (
        g_rows, g_tail, table, slots, wide, fresh, joined, rows32, tail32, s_rows, s_tail, w_qkv,
        w_out, w_up, w_down, w_dec, normed, joint, probs, context, middle, normed2, activ, slope,
        ending, start, total, send, recv, trade_send, trade_recv, local, load_sem, keep_sem,
    ) = refs[58:]
    net = Net(planes)
    trade = Trade(cotangent, returned, trade_send, trade_recv, load_sem.at[5])
    trade.greet()
    sent = [0]

    def trade_more(count=1):
        for _ in range(count):
            if sent[0] < TRADE_PARTS:
                trade.begin(sent[0], TRADE_PARTS)
                sent[0] += 1

    seen = rows // chips
    loads, stashed = [], []
    spans = ((0, 3 * width), (3 * width + hidden, width), (3 * width, hidden))
    spans += ((4 * width + hidden, dec_width),)
    for (at, size), dst in zip(spans, (w_qkv, w_out, w_up, w_dec)):
        loads.append((wide_out.at[:, pl.ds(at, size)], dst))
    loads.append((down_out, w_down))
    loads = [
        pltpu.make_async_copy(src, dst, load_sem.at[i]) for i, (src, dst) in enumerate(loads)
    ]

    def stash(src, dst):
        copy = pltpu.make_async_copy(src, dst, keep_sem.at[len(stashed)])
        copy.start()
        stashed.append(copy)

    wires = Wires(send, recv)
    me = net.chip(0) * 2 + net.c
    low = jnp.bfloat16
    copies = []

    def keep(src, dst):
        copy = pltpu.make_async_copy(src, dst, local.at[len(copies)])
        copy.start()
        copies.append(copy)

    small = gen_up.shape[0]
    gen_width = gen_out.shape[1]
    turned = gen_tokens[...].astype(jnp.float32)
    turned = jnp.concatenate(
        [turned, jnp.zeros((small, 2 * gen_width - turned.shape[1]), jnp.float32)], axis=1
    )
    line = jnp.concatenate(
        [item[...].astype(jnp.float32) for item in (gen_up, gen_qkv, gen_out)]
        + [turned[:, :gen_width], bias_weight[...].astype(jnp.float32), turned[:, gen_width:]],
        axis=1,
    )
    for q in range(16 // small):
        rows32[pl.ds(q * small, small), :] = line[:, q * CHUNK : (q + 1) * CHUNK]
    s_rows[...] = rows32[...].astype(low)
    tail32[...] = jnp.zeros_like(tail32)
    for i, item in enumerate(thin):
        tail32[pl.ds(i, 1), pl.ds(0, item.shape[1])] = item[...].astype(jnp.float32)
    s_tail[pl.ds(0, gen_low.shape[0]), :] = gen_low[...]
    s_tail[pl.ds(gen_low.shape[0], 16), :] = tail32[...].astype(low)
    r_size, r_cols = s_rows.shape
    r_cut = (r_cols // 256) * 128 + 128
    r_span = lambda h: pl.ds(r_cut * h, r_cols - r_cut if h else r_cut)
    t_size = s_tail.shape[0]
    t_cut = (t_size // 32) * 16 + 16
    t_span = lambda h: pl.ds(t_cut * h, t_size - t_cut if h else t_cut)
    smalls = [
        Gather(
            net,
            wires,
            lambda h: s_rows.at[:, r_span(h)],
            lambda chip, h: g_rows.at[tile_rows(chip * 2 + net.c, r_size), r_span(h)],
        ),
        Gather(
            net,
            wires,
            lambda h: s_tail.at[t_span(h)],
            lambda chip, h: g_tail.at[chip * 2 + net.c, t_span(h)],
        ),
    ]
    for item in smalls:
        item.begin_z()
        item.spread(0)
    keep(s_rows, g_rows.at[tile_rows(me, r_size)])
    keep(s_tail, g_tail.at[me])

    at = 0
    for item in (qkv, up, out, dec):
        wide[:, pl.ds(at, item.shape[1])] = item[...]
        at += item.shape[1]
    w_cols = at // 2
    quarter = w_cols // 2
    shard = wide.shape[0]
    mine = pl.ds(pl.multiple_of(net.c * w_cols, 128), w_cols)
    theirs = pl.ds(pl.multiple_of((1 - net.c) * w_cols, 128), w_cols)
    pair = wires.push(wide.at[:, theirs], fresh, net.sib)
    d_rows = down.shape[0]
    d_half = d_rows // 2
    d_own = lambda h: down.at[pl.ds(h * d_half, d_half)]
    d_piece = lambda chip, h: down_out.at[
        pl.ds(pl.multiple_of((chip * 2 + net.c) * d_rows + h * d_half, 16), d_half)
    ]
    w_own = lambda h: joined.at[:, pl.ds(h * quarter, quarter)]
    w_piece = lambda chip, h: wide_out.at[
        pl.ds(pl.multiple_of(chip * 2 * shard, 16), 2 * shard),
        pl.ds(pl.multiple_of((net.c * 2 + h) * quarter, 128), quarter),
    ]
    t_lines = table.shape[0] // devices // 2
    t_piece = lambda chip, h: table.at[tile_rows((chip * 2 + net.c) * 2 + h, t_lines)]
    t_own = lambda h: table.at[tile_rows(me * 2 + h, t_lines)]
    d_gather = Gather(net, wires, d_own, d_piece)
    w_gather = Gather(net, wires, w_own, w_piece)
    t_gather = Gather(net, wires, t_own, t_piece)
    d_gather.begin_z()
    for item in smalls:
        item.relay(0)
    pair.wait_recv()
    own32 = wide[:, mine].astype(jnp.float32)
    sib32 = fresh[...].astype(jnp.float32)
    first = net.c == 0
    joined[...] = jnp.concatenate(
        [jnp.where(first, own32, sib32), jnp.where(first, sib32, own32)], axis=0
    ).astype(low)
    for k in range(1, planes):
        for item in smalls:
            item.spread(k)
        for item in smalls:
            item.relay(k)
    w_gather.begin_z()
    for h in range(2):
        keep(w_own(h), w_piece(net.chip(0), h))
        keep(d_own(h), d_piece(net.chip(0), h))
    for k in range(planes):
        for item in smalls:
            item.close(k)
    w_gather.spread(0)
    d_gather.spread(0)
    steps = [partial(w_gather.relay, 0)]
    for k in range(1, planes):
        steps += [partial(w_gather.spread, k), partial(w_gather.relay, k)]
    steps.append(partial(d_gather.relay, 0))
    for k in range(1, planes):
        steps += [partial(d_gather.spread, k), partial(d_gather.relay, k)]
        steps.append(partial(w_gather.close, k - 1))
    steps.append(partial(w_gather.close, planes - 1))
    steps += [partial(d_gather.close, k) for k in range(planes)]

    def pump(count):
        for _ in range(min(count, len(steps))):
            steps.pop(0)()

    for item in smalls:
        item.finish()
    for copy in copies[:2]:
        copy.wait()

    lines = width // devices
    groups = r_size // small
    shape = (gen_rows.shape[0], devices * r_size)
    row = lax.broadcasted_iota(jnp.int32, shape, 0)
    column = lax.broadcasted_iota(jnp.int32, shape, 1)
    for q in range(groups):
        source = lax.div(row, small) * r_size + q * small + lax.rem(row, small)
        gen_rows[:, pl.ds(q * r_cols, r_cols)] = dot_nn(
            (column == source).astype(low), g_rows[...]
        ).astype(low)
    gen_down[...] = g_tail[:, pl.ds(0, t_size - 16), :].reshape(gen_down.shape)
    tail = g_tail[:, pl.ds(t_size - 16, 16), :].reshape(devices * 16, 128)
    shape = (devices * 16, devices * 16)
    row = lax.broadcasted_iota(jnp.int32, shape, 0)
    column = lax.broadcasted_iota(jnp.int32, shape, 1)
    source = lax.rem(row, devices) * 16 + lax.div(row, devices)
    tail = dot_nn((column == source).astype(low), tail).astype(low)
    part = lambda i: tail[i * devices : (i + 1) * devices]
    vecs[...] = jnp.zeros_like(vecs)
    for i in range(5):
        vecs[pl.ds(i, 1), pl.ds(0, width)] = join_lanes(part(i), lines)
    vecs[pl.ds(5, 1), :] = join_lanes(part(5), hidden // devices)
    for i in (6, 7):
        vecs[pl.ds(i, 1), pl.ds(0, dec_width)] = join_lanes(part(i), dec_width // devices)
    gen_vec[...] = jnp.zeros_like(gen_vec)
    for i in range(6):
        gen_vec[pl.ds(i, 1), pl.ds(0, gen_rows.shape[0])] = join_lanes(part(8 + i), small)
    gen_vec[pl.ds(6, 1), :] = join_lanes(part(14), up_size // devices)

    pump(2)
    operands = gen_parts(gen_rows, gen_down, gen_vec, wave_code[...], up_size)
    seq = operands[0]
    final = gen_layer(*operands, LAT + NWAVE + 1)
    feature = (final[LAT : LAT + NWAVE] + seq[LAT : LAT + NWAVE]).astype(low)
    feature_out[...] = feature
    source = final[LAT + NWAVE : LAT + NWAVE + 8].astype(low)
    source_out[...] = source
    own = (dot_nn(feature, weight[...]) + weight_bias[...].astype(jnp.float32)).astype(low)
    for h in range(2):
        table[tile_rows(me * 2 + h, t_lines), :] = own[:, h * width : (h + 1) * width]
    t_gather.begin_z()
    t_gather.spread(0)
    pump(2)

    bias_at = gen_rows.shape[1] - gen_rows.shape[0] - width
    conv = dot_nn(source, gen_rows[:, pl.ds(bias_at, width)])[:1]
    t_gather.relay(0)
    grid_line = lax.broadcasted_iota(jnp.int32, (GRID, seen), 0)
    for chip in range(chips):
        patch = visible[pl.ds(chip, 1), :]
        for i, spot in enumerate((lax.div(patch, GRID), lax.rem(patch, GRID))):
            half = pl.ds(i * (width // 2), width // 2)
            picked = lax.dot_general(
                (spot == grid_line).astype(jnp.float32),
                places[...],
                (((0,), (0,)), ((), ())),
                precision=HIGH,
                preferred_element_type=jnp.float32,
            )
            start[pl.ds(chip * seen, seen), half] = (
                picked + conv[:, i * (width // 2) : (i + 1) * (width // 2)]
            )
    t_gather.spread(1)
    t_gather.relay(1)
    pump(2)
    span = 256
    bands_pix = pixels.shape[1]
    bands = waves.shape[1]
    band_of = lax.div(lax.broadcasted_iota(jnp.int32, (1, bands_pix), 1), bands_pix // bands)
    wave_lines = []
    for chip in range(chips):
        drop = jnp.zeros((1, 1), jnp.int32)
        for i, less in enumerate(BAND_DROP):
            drop = jnp.where(sensor[:, pl.ds(chip, 1)] == i, less, drop)
        wave = jnp.full((1, bands_pix), -1, jnp.int32)
        for i in range(bands):
            wave = jnp.where(band_of == i, waves[pl.ds(chip, 1), pl.ds(i, 1)], wave)
        wave_lines.append(jnp.where(band_of < bands - drop, wave, -1))

    def slot_block(i, _):
        shape = (span, bands_pix)
        line = lax.broadcasted_iota(jnp.int32, shape, 0) + i * span
        column = lax.broadcasted_iota(jnp.int32, shape, 1)
        count = slots.shape[0] // NWAVE
        same = lax.div(line, NWAVE) == lax.rem(column, count)
        for chip in range(chips):
            chosen = same & (lax.rem(line, NWAVE) == wave_lines[chip])
            slots[tile_rows(i, span), pl.ds(chip * seen, seen)] = dot_nn(
                chosen.astype(jnp.float32).astype(low), pixels[chip]
            ).astype(low)
        return 0

    blocks = slots.shape[0] // span
    lax.fori_loop(0, blocks // 2, slot_block, 0)
    for k in range(2, planes):
        t_gather.spread(k)
        t_gather.relay(k)
    pump(2)
    lax.fori_loop(blocks // 2, blocks, slot_block, 0)
    keep(slots, slots_out)
    pump(4)
    for k in range(planes):
        t_gather.close(k)
    pump(2)
    t_gather.finish()
    keep(table, table_out)
    wide_span = 512

    def embed(i, _):
        at = tile_rows(i, wide_span)
        start[...] += tdot(slots[at, :], table[at, :])
        return 0

    lax.fori_loop(0, slots.shape[0] // wide_span, embed, 0)
    stash(start, start_out)
    while len(steps) > planes:
        pump(1)

    def norm_into(src, dst, row):
        gain = vecs[pl.ds(row, 1), pl.ds(0, width)]
        shift = vecs[pl.ds(row + 1, 1), pl.ds(0, width)]

        def block(i, _):
            at = tile_rows(i, BLOCK)
            dst[at, :] = norm_rows(src[at, :], gain, shift).astype(low)
            return 0

        lax.fori_loop(0, rows // BLOCK, block, 0)

    norm_into(start, normed, 0)
    for copy in copies[2:6]:
        copy.wait()
    w_gather.finish()
    trade_more(TRADE_PARTS)
    for copy in loads[:4]:
        copy.start()
    stash(normed, normed_out)
    loads[0].wait()

    def project(i, _):
        lane = pl.ds(pl.multiple_of(i * width, 128), width)
        joint[:, lane] = dot_nn(normed[...], w_qkv[:, lane]).astype(low)
        return 0

    lax.fori_loop(0, 3, project, 0)
    pump(2)
    stash(joint, joint_out)
    pairs = width // 128
    head = width // HEADS
    scale = 1.0 / math.sqrt(head)
    odd = lax.broadcasted_iota(jnp.int32, (1, 128), 1) >= head

    def attend(n, _):
        at = tile_rows(lax.div(n, pairs), seen)
        pair = lax.rem(n, pairs)
        query, key, value = [
            joint[at, pl.ds(pl.multiple_of(pair * 128 + i * width, 128), 128)] for i in range(3)
        ]
        zero = jnp.zeros_like(query)
        parts = []
        for h in range(2):
            mine = odd if h else jnp.logical_not(odd)
            scores = ndot(jnp.where(mine, query, zero), key) * scale
            raised = jnp.exp(scores - jnp.max(scores, axis=-1, keepdims=True))
            prob = (raised / jnp.sum(raised, axis=-1, keepdims=True)).astype(low)
            probs[2 * n + h] = prob
            parts.append(dot_nn(prob, value))
        lane = pl.ds(pl.multiple_of(pair * 128, 128), 128)
        context[at, lane] = jnp.where(odd, parts[1], parts[0]).astype(low)
        return 0

    for i in range(0, chips * pairs, 3):
        lax.fori_loop(i, i + 3, attend, 0)
        pump(1)
    stash(probs, probs_out)
    stash(context, context_out)
    loads[1].wait()
    middle[...] = start[...] + dot_nn(context[...], w_out[...])
    stash(middle, middle_out)
    norm_into(middle, normed2, 2)
    stash(normed2, normed2_out)
    total[...] = middle[...] + vecs[pl.ds(4, 1), pl.ds(0, width)]
    pump(len(steps))
    d_gather.finish()
    loads[4].start()
    loads[2].wait()
    loads[4].wait()

    def feed(t, _):
        at = tile_rows(t, FT)
        upper = dot_nn(normed2[...], w_up[:, at]) + vecs[pl.ds(5, 1), at]
        bell = 0.5 * (1.0 + lax.erf(upper * math.sqrt(0.5)))
        active = (upper * bell).astype(low)
        activ[:, at] = active
        tilt = upper * jnp.exp(-0.5 * upper * upper) * (1.0 / math.sqrt(2.0 * math.pi))
        slope[:, at] = (bell + tilt).astype(low)
        total[...] += dot_nn(active, w_down[at, :])
        return 0

    lax.fori_loop(0, hidden // FT, feed, 0)
    stash(activ, activ_out)
    stash(slope, slope_out)
    ending[...] = total[...].astype(low)
    stash(ending, ending_out)
    loads[3].wait()
    decoded = dot_nn(ending[...], w_dec[...]) + vecs[pl.ds(6, 1), pl.ds(0, dec_width)]
    total[:, pl.ds(0, dec_width)] = decoded
    mask = vecs[pl.ds(7, 1), pl.ds(0, dec_width)]
    blocks, _, lines, _ = ordered.shape
    column = order_column(order)
    for chip in range(chips):
        at = pl.ds(chip * seen, seen)
        chosen = (column == visible[pl.ds(chip, 1), :]).astype(jnp.float32)
        found = jnp.sum(chosen, axis=1, keepdims=True) > 0.0
        placed = dot_nn(chosen.astype(low), total[at, pl.ds(0, dec_width)].astype(low))
        placed = jnp.where(found, placed, mask).astype(low)
        ordered[:, chip] = placed.reshape(blocks, lines, dec_width)
    for copy in copies[6:] + stashed:
        copy.wait()
    trade_more(TRADE_PARTS)
    trade.finish()
    wires.drain()


def prepare(planes, sizes, *args):
    (rows, width, hidden, dec_width, chips, up_size, patches) = sizes
    seen = rows // chips
    heads = chips * HEADS
    devices = planes * 8
    low, full = jnp.bfloat16, jnp.float32
    qkv, up, out, dec, down = args[:5]
    gen_width = args[12].shape[1]
    tail = args[18].shape[0] + 16
    cols = qkv.shape[1] + up.shape[1] + out.shape[1] + dec.shape[1]
    shard = qkv.shape[0]
    slots = args[5].shape[1] // width * devices * NWAVE
    copies = 5 * gather_copies(planes) + 1
    shapes = (
        ((width, cols), low),
        ((hidden, width), low),
        ((slots, width), low),
        ((slots, rows), low),
        (args[19].shape, low),
        ((rows, width), low),
        ((rows, 3 * width), low),
        ((heads, seen, seen), low),
        ((rows, width), low),
        ((rows, width), full),
        ((rows, width), low),
        ((rows, hidden), low),
        ((rows, hidden), low),
        ((rows, width), low),
        ((rows, width), full),
        ((devices, chips, patches // devices, dec_width), low),
        ((gen_width, CHUNK * 16 * devices // gen_width), low),
        ((up_size, gen_width), low),
        ((8, up_size), full),
        ((8, hidden), full),
        ((NWAVE, gen_width), low),
        ((8, gen_width), low),
    )
    return pl.pallas_call(
        partial(prepare_kernel, planes, sizes),
        out_shape=tuple(jax.ShapeDtypeStruct(shape, dtype) for shape, dtype in shapes),
        in_specs=[VMEM] * 19 + [ANY] + [VMEM] * (len(args) - 20),
        out_specs=[ANY] * 15 + [VMEM] * 7,
        scratch_shapes=[
            pltpu.VMEM((devices * 16, CHUNK), low),
            pltpu.VMEM((devices, tail, 128), low),
            pltpu.VMEM((slots, width), low),
            pltpu.VMEM((slots, rows), low),
            pltpu.VMEM((shard, cols), low),
            pltpu.VMEM((shard, cols // 2), low),
            pltpu.VMEM((2 * shard, cols // 2), low),
            pltpu.VMEM((16, CHUNK), full),
            pltpu.VMEM((16, 128), full),
            pltpu.VMEM((16, CHUNK), low),
            pltpu.VMEM((tail, 128), low),
            pltpu.VMEM((width, 3 * width), low),
            pltpu.VMEM((width, width), low),
            pltpu.VMEM((width, hidden), low),
            pltpu.VMEM((hidden, width), low),
            pltpu.VMEM((width, dec_width), low),
        ]
        + [pltpu.VMEM(shape, dtype) for shape, dtype in shapes[5:15]]
        + [
            pltpu.VMEM((rows, width), full),
            pltpu.SemaphoreType.DMA((copies,)),
            pltpu.SemaphoreType.DMA((copies,)),
            pltpu.SemaphoreType.DMA((devices,)),
            pltpu.SemaphoreType.DMA((devices,)),
            pltpu.SemaphoreType.DMA((8,)),
            pltpu.SemaphoreType.DMA((6,)),
            pltpu.SemaphoreType.DMA((10,)),
        ],
        compiler_params=pltpu.CompilerParams(
            collective_id=0, has_side_effects=True, vmem_limit_bytes=60 * 2**20
        ),
    )(*args)


def gen_back(
    gen_rows, gen_down, gen_vec, wave_code, length, grad_feature, grad_source, sums, put_up, put_down
):
    up_size, width = gen_down.shape
    size = width // GHEADS
    scale = 1.0 / math.sqrt(size)
    total = lambda value: jnp.sum(value, axis=0, keepdims=True)
    chunk = up_size // 4

    def dot(left, right, dims):
        return lax.dot_general(
            left.astype(jnp.bfloat16),
            right.astype(jnp.bfloat16),
            (dims, ((), ())),
            preferred_element_type=jnp.float32,
        )

    nn = lambda left, right: dot(left, right, ((1,), (0,)))
    nt = lambda left, right: dot(left, right, ((1,), (1,)))
    tn = lambda left, right: dot(left, right, ((0,), (0,)))
    seq = gen_seq_of(gen_rows, wave_code, up_size)
    full = jnp.float32
    qkv = gen_rows[:, pl.ds(up_size, 3 * width)].astype(full)
    out = gen_rows[:, pl.ds(up_size + 3 * width, width)].astype(full)
    out_bias, gain1, shift1, down_bias, gain2, _ = [
        gen_vec[pl.ds(i, 1), pl.ds(0, width)] for i in range(6)
    ]
    joint = nn(seq, qkv)
    query, key, value = [joint[:, i * width : (i + 1) * width] for i in range(3)]
    lane = lax.broadcasted_iota(jnp.int32, (1, width), 1)
    spot = lax.broadcasted_iota(jnp.int32, (1, seq.shape[0]), 1)
    masks = [(lax.div(lane, size) == h).astype(full) for h in range(GHEADS)]
    probs = []
    context = jnp.zeros_like(seq)
    for mine in masks:
        scores = jnp.where(spot < length, nt(query * mine, key) * scale, -1e30)
        raised = jnp.exp(scores - jnp.max(scores, axis=-1, keepdims=True))
        probs.append(raised / jnp.sum(raised, axis=-1, keepdims=True))
        context = context + nn(probs[-1], value * mine)
    first = seq + nn(context, out) + out_bias
    mixed = norm_rows(first, gain1, shift1)

    def piece(i):
        at = pl.ds(pl.multiple_of(i * chunk, chunk), chunk)
        up = gen_rows[:, at].astype(full)
        down = gen_down[at, :].astype(full)
        inner = nn(mixed, up) + gen_vec[pl.ds(6, 1), at]
        return up, down, inner, 0.5 * (1.0 + lax.erf(inner * math.sqrt(0.5)))

    def ahead(i, so_far):
        _, down, inner, bell = piece(i)
        return so_far + nn(inner * bell, down)

    second = lax.fori_loop(0, 4, ahead, mixed + down_bias)
    rest = seq.shape[0] - LAT - NWAVE
    zeros = jnp.zeros((LAT, width), full)
    grad = jnp.concatenate([zeros, grad_feature, grad_source], axis=0)
    through, terms = norm_back(grad, second, gain2)
    g_gain2, g_shift2, g_down_bias = total(terms), total(grad), total(through)

    def behind(i, so_far):
        up, down, inner, bell = piece(i)
        put_down(i, tn(inner * bell, through))
        slope = bell + inner * jnp.exp(-0.5 * inner * inner) * (1.0 / math.sqrt(2.0 * math.pi))
        g_inner = nt(through, down) * slope
        put_up(i, tn(mixed, g_inner))
        sums[pl.ds(6, 1), pl.ds(pl.multiple_of(i * chunk, chunk), chunk)] = total(g_inner)
        return so_far + nt(g_inner, up)

    g_mixed = lax.fori_loop(0, 4, behind, through)
    through, terms = norm_back(g_mixed, first, gain1)
    g_gain1, g_shift1, g_out_bias = total(terms), total(g_mixed), total(through)
    g_out = tn(context, through)
    g_context = nt(through, out)
    g_query = g_key = g_value = jnp.zeros_like(seq)
    for mine, prob in zip(masks, probs):
        g_head = g_context * mine
        g_prob = nt(g_head, value)
        g_value = g_value + tn(prob, g_head)
        g_score = prob * (g_prob - jnp.sum(prob * g_prob, axis=-1, keepdims=True)) * scale
        g_query = g_query + nn(g_score, key * mine)
        g_key = g_key + tn(g_score, query * mine)
    g_joint = jnp.concatenate([g_query, g_key, g_value], axis=1)
    direct = jnp.concatenate([zeros, grad_feature, jnp.zeros((rest, width), full)], axis=0)
    g_seq = through + nt(g_joint, qkv) + direct
    thin = (g_out_bias, g_gain1, g_shift1, g_down_bias, g_gain2, g_shift2)
    return g_seq, tn(seq, g_joint), g_out, thin


def hand_out_kernel(planes, sizes, *refs):
    (width, hidden, dec_width, small) = sizes
    devices = planes * 8
    (
        s_dec, s_up, s_oq, s_down, kernels, kernel_sums, lines, g_wide, g_tall, g_seq, g_lines,
        g_bias,
    ) = refs[40:52]
    copies = [
        pltpu.make_async_copy(refs[i], refs[40 + i], refs[52].at[i]) for i in range(12)
    ]
    for copy in copies:
        copy.start()
    for copy in copies:
        copy.wait()
    outs = refs[12:40]
    (
        pre_gain, pre_shift, qkv, out, mid_gain, mid_shift, up, up_bias, down, down_bias, dec,
        dec_bias, mask, tokens, gen_qkv, gen_out, gen_out_bias, gain1, shift1, gen_up,
        gen_up_bias, gen_down, gen_down_bias, gain2, shift2, kernel_weight, kernel_bias, bias,
    ) = outs
    me = lax.axis_index("dp") * 4 + lax.axis_index("fsdp")
    qkv[...] = s_oq[:, pl.ds(width, 3 * width)]
    out[...] = s_oq[:, pl.ds(0, width)]
    up[...] = s_up[...]
    down[...] = s_down[...]
    dec[...] = s_dec[...]
    kernel_weight[...] = kernels[...]
    for i in range(kernel_bias.shape[0]):
        kernel_bias[pl.ds(i, 1), :] = kernel_sums[:, i * 128 : (i + 1) * 128]
    gen_down[...] = g_tall[...]
    up_size = gen_up.shape[1]
    gen_width = gen_out.shape[1]
    gen_up[...] = g_wide[pl.ds(0, small), pl.ds(0, up_size)]
    gen_qkv[...] = g_wide[pl.ds(0, small), pl.ds(up_size, 3 * gen_width)]
    gen_out[...] = g_wide[pl.ds(0, small), pl.ds(up_size + 3 * gen_width, gen_width)]
    tokens[pl.ds(0, LAT), :] = g_seq[pl.ds(0, LAT), pl.ds(0, small)]
    tokens[pl.ds(LAT, 1), :] = g_seq[pl.ds(LAT + NWAVE, 1), pl.ds(0, small)]
    bias[...] = g_bias[pl.ds(0, small), :]

    def own(values, part):
        shape = (values.shape[1], 128)
        row = lax.broadcasted_iota(jnp.int32, shape, 0)
        lane = lax.broadcasted_iota(jnp.int32, shape, 1)
        pick = ((row == me * part + lane) & (lane < part)).astype(jnp.float32)
        return jnp.dot(values, pick, precision=HIGH, preferred_element_type=jnp.float32)

    at = NWAVE + width // 128

    def row_of(size):
        nonlocal at
        count = size // 128
        row = jnp.concatenate([lines[pl.ds(at + i, 1), :] for i in range(count)], axis=1)
        at += count
        return row

    def rows_of(sizes_):
        rows = [row_of(size) for size in sizes_]
        rows.append(jnp.zeros((8 - len(rows), rows[0].shape[1]), jnp.float32))
        return jnp.concatenate(rows, axis=0)

    def split(values, part, refs_):
        mine = own(values, part)
        for i, ref in enumerate(refs_):
            ref[...] = mine[i : i + 1, :part]

    split(rows_of((width,) * 5), width // devices, (pre_gain, pre_shift, mid_gain, mid_shift, down_bias))
    split(rows_of((hidden,)), hidden // devices, (up_bias,))
    split(rows_of((dec_width,) * 2), dec_width // devices, (dec_bias, mask))
    split(
        g_lines[:, pl.ds(0, gen_width)],
        small,
        (gen_out_bias, gain1, shift1, gen_down_bias, gain2, shift2),
    )
    split(
        jnp.concatenate(
            [g_lines[pl.ds(6, 1), :], jnp.zeros((7, up_size), jnp.float32)], axis=0
        ),
        up_size // devices,
        (gen_up_bias,),
    )


def hand_out(planes, sizes, *args):
    (width, hidden, dec_width, small) = sizes
    devices = planes * 8
    up_size = args[10].shape[1]
    gen_width = args[8].shape[1]
    wide, thin = width // devices, (1, width // devices)
    row = lambda size: (1, size // devices)
    shapes = (
        thin, thin, (wide, 3 * width), (wide, width), thin, thin, (wide, hidden), row(hidden),
        (hidden // devices, width), thin, (wide, dec_width), row(dec_width), row(dec_width),
        (LAT + 1, small), (small, 3 * gen_width), (small, gen_width), (1, small), (1, small),
        (1, small), (small, up_size), row(up_size), (up_size // devices, gen_width), (1, small),
        (1, small), (1, small), args[4].shape, (args[5].shape[1] // 128, 128), (small, width),
    )
    return pl.pallas_call(
        partial(hand_out_kernel, planes, sizes),
        out_shape=tuple(jax.ShapeDtypeStruct(shape, jnp.float32) for shape in shapes),
        in_specs=[ANY] * 12,
        out_specs=[VMEM] * 28,
        scratch_shapes=[pltpu.VMEM(item.shape, item.dtype) for item in args]
        + [pltpu.SemaphoreType.DMA((12,))],
        compiler_params=pltpu.CompilerParams(vmem_limit_bytes=60 * 2**20),
    )(*args)


def on_device_plain(
    pixels,
    sensor,
    band_wave,
    visible,
    block_order,
    pre_gain,
    pre_shift,
    qkv_weight,
    out_weight,
    mid_gain,
    mid_shift,
    up_weight,
    up_bias,
    down_weight,
    down_bias,
    dec_weight,
    dec_bias,
    mask_token,
    gen_tokens,
    gen_qkv,
    gen_out,
    gen_out_bias,
    gen_gain1,
    gen_shift1,
    gen_up,
    gen_up_bias,
    gen_down,
    gen_down_bias,
    gen_gain2,
    gen_shift2,
    kernel_weight,
    kernel_bias,
    bias_weight,
    cotangent,
):
    fetched = (
        lax.all_gather(pre_gain, AXES, axis=0, tiled=True),
        lax.all_gather(pre_shift, AXES, axis=0, tiled=True),
        lax.all_gather(qkv_weight, AXES, axis=0, tiled=True),
        lax.all_gather(out_weight, AXES, axis=0, tiled=True),
        lax.all_gather(mid_gain, AXES, axis=0, tiled=True),
        lax.all_gather(mid_shift, AXES, axis=0, tiled=True),
        lax.all_gather(up_weight, AXES, axis=0, tiled=True),
        lax.all_gather(up_bias, AXES, axis=0, tiled=True),
        lax.all_gather(down_weight, AXES, axis=0, tiled=True),
        lax.all_gather(down_bias, AXES, axis=0, tiled=True),
        lax.all_gather(dec_weight, AXES, axis=0, tiled=True),
        lax.all_gather(dec_bias, AXES, axis=0, tiled=True),
        lax.all_gather(mask_token, AXES, axis=0, tiled=True),
        lax.all_gather(gen_tokens, AXES, axis=1, tiled=True),
        lax.all_gather(gen_qkv, AXES, axis=0, tiled=True),
        lax.all_gather(gen_out, AXES, axis=0, tiled=True),
        lax.all_gather(gen_out_bias, AXES, axis=0, tiled=True),
        lax.all_gather(gen_gain1, AXES, axis=0, tiled=True),
        lax.all_gather(gen_shift1, AXES, axis=0, tiled=True),
        lax.all_gather(gen_up, AXES, axis=0, tiled=True),
        lax.all_gather(gen_up_bias, AXES, axis=0, tiled=True),
        lax.all_gather(gen_down, AXES, axis=0, tiled=True),
        lax.all_gather(gen_down_bias, AXES, axis=0, tiled=True),
        lax.all_gather(gen_gain2, AXES, axis=0, tiled=True),
        lax.all_gather(gen_shift2, AXES, axis=0, tiled=True),
        lax.all_gather(kernel_weight, AXES, axis=1, tiled=True),
        lax.all_gather(kernel_bias, AXES, axis=0, tiled=True),
        lax.all_gather(bias_weight, AXES, axis=0, tiled=True),
    )
    full_kernel = fetched[25]
    full_kernel_bias = fetched[26]
    full_bias_weight = fetched[27]
    (
        full_pre_gain,
        full_pre_shift,
        full_qkv,
        full_out,
        full_mid_gain,
        full_mid_shift,
        full_up,
        full_up_bias,
        full_down,
        full_down_bias,
        full_dec,
        full_dec_bias,
        full_mask,
    ) = fetched[:13]
    core32 = tuple((item.astype(jnp.float32) for item in fetched[13:25]))
    chips, seen, bands, pix = pixels.shape
    width = full_qkv.shape[0]
    head_dim = width // HEADS
    scale = 1.0 / math.sqrt(head_dim)
    dec_width = full_dec.shape[1]
    rows = chips * seen
    wave_code = lax.optimization_barrier(
        sincos(jnp.arange(NWAVE, dtype=jnp.float32), WD // 2).astype(jnp.bfloat16)
    ).astype(jnp.float32)
    (feature, source), core_back = jax.vjp(partial(gen_core, wave_code), *core32)
    feature_low = feature.astype(jnp.bfloat16)
    source_low = source.astype(jnp.bfloat16)
    conv_bias = jnp.dot(source_low[None, :], full_bias_weight, preferred_element_type=jnp.float32)[
        0
    ]
    kernels = (
        jnp.dot(feature_low, full_kernel, preferred_element_type=jnp.float32)
        + full_kernel_bias.astype(jnp.float32)[None, :]
    ).astype(jnp.bfloat16)
    valid = band_valid(sensor, bands)
    onehot = (band_wave[:, :, None] == jnp.arange(NWAVE, dtype=jnp.int32)[None, None, :]).astype(
        jnp.float32
    )
    place = place_code(visible, width)
    band_kernels = jnp.einsum(
        "cbw,wk->cbk", onehot.astype(jnp.bfloat16), kernels, preferred_element_type=jnp.float32
    ).astype(jnp.bfloat16)
    band_kernels = band_kernels.reshape(chips, bands, pix, width)
    masked = pixels * valid.astype(jnp.bfloat16)[:, None, :, None]
    embedded = jnp.einsum(
        "cvbp,cbpd->cvd", masked, band_kernels, preferred_element_type=jnp.float32
    )
    start = (embedded + conv_bias + place).reshape(rows, width)
    pre_gain32 = full_pre_gain.astype(jnp.float32)
    pre_shift32 = full_pre_shift.astype(jnp.float32)
    normed = norm_rows(start, pre_gain32, pre_shift32).astype(jnp.bfloat16)
    joint = jnp.dot(normed, full_qkv, preferred_element_type=jnp.float32).astype(jnp.bfloat16)
    joint = joint.reshape(chips, seen, 3, HEADS, head_dim)
    queries = joint[:, :, 0]
    keys = joint[:, :, 1]
    values = joint[:, :, 2]
    scores = (
        jnp.einsum("cqhe,ckhe->chqk", queries, keys, preferred_element_type=jnp.float32) * scale
    )
    peak = jnp.max(scores, axis=-1, keepdims=True)
    expd = jnp.exp(scores - peak)
    total = jnp.sum(expd, axis=-1, keepdims=True)
    probs = (expd / total).astype(jnp.bfloat16)
    log_total = peak + jnp.log(total)
    context = jnp.einsum("chqk,ckhe->cqhe", probs, values, preferred_element_type=jnp.float32)
    context = context.astype(jnp.bfloat16).reshape(rows, width)
    attended = jnp.dot(context, full_out, preferred_element_type=jnp.float32)
    middle = start + attended
    mid_gain32 = full_mid_gain.astype(jnp.float32)
    mid_shift32 = full_mid_shift.astype(jnp.float32)
    normed2 = norm_rows(middle, mid_gain32, mid_shift32).astype(jnp.bfloat16)
    upper = jnp.dot(normed2, full_up, preferred_element_type=jnp.float32) + full_up_bias.astype(
        jnp.float32
    )
    activ = exact_gelu(upper).astype(jnp.bfloat16)
    branch = jnp.dot(activ, full_down, preferred_element_type=jnp.float32) + full_down_bias.astype(
        jnp.float32
    )
    ending = (middle + branch).astype(jnp.bfloat16)
    decoded = jnp.dot(ending, full_dec, preferred_element_type=jnp.float32) + full_dec_bias.astype(
        jnp.float32
    )
    decoded = decoded.astype(jnp.bfloat16).reshape(chips, seen, dec_width)
    chip_ids = jnp.arange(chips, dtype=jnp.int32)[:, None]
    canvas = jnp.broadcast_to(full_mask, (chips, PATCH, dec_width))
    canvas = canvas.at[chip_ids, visible].set(decoded)
    ordered = jnp.take(canvas, block_order, axis=1)
    decoder_in = lax.all_to_all(ordered, AXES, split_axis=1, concat_axis=0, tiled=True)
    returned = lax.all_to_all(cotangent, AXES, split_axis=0, concat_axis=1, tiled=True)
    (
        full_pre_gain,
        full_pre_shift,
        full_qkv,
        full_out,
        full_mid_gain,
        full_mid_shift,
        full_up,
        full_up_bias,
        full_down,
        full_down_bias,
        full_dec,
        full_dec_bias,
        full_mask,
    ) = (
        lax.all_gather(pre_gain, AXES, axis=0, tiled=True),
        lax.all_gather(pre_shift, AXES, axis=0, tiled=True),
        lax.all_gather(qkv_weight, AXES, axis=0, tiled=True),
        lax.all_gather(out_weight, AXES, axis=0, tiled=True),
        lax.all_gather(mid_gain, AXES, axis=0, tiled=True),
        lax.all_gather(mid_shift, AXES, axis=0, tiled=True),
        lax.all_gather(up_weight, AXES, axis=0, tiled=True),
        lax.all_gather(up_bias, AXES, axis=0, tiled=True),
        lax.all_gather(down_weight, AXES, axis=0, tiled=True),
        lax.all_gather(down_bias, AXES, axis=0, tiled=True),
        lax.all_gather(dec_weight, AXES, axis=0, tiled=True),
        lax.all_gather(dec_bias, AXES, axis=0, tiled=True),
        lax.all_gather(mask_token, AXES, axis=0, tiled=True),
    )
    restored = jnp.zeros_like(returned).at[:, block_order].set(returned)
    seen_grad = jnp.take_along_axis(restored, visible[:, :, None], axis=1)
    grad_mask = jnp.sum(restored.astype(jnp.float32), axis=(0, 1)) - jnp.sum(
        seen_grad.astype(jnp.float32), axis=(0, 1)
    )
    grad_rows = seen_grad.reshape(rows, dec_width)
    grad_dec_weight = tdot(ending, grad_rows)
    grad_dec_bias = jnp.sum(grad_rows.astype(jnp.float32), axis=0)
    grad_ending = ndot(grad_rows, full_dec)
    grad_branch = grad_ending.astype(jnp.bfloat16)
    grad_down_bias = jnp.sum(grad_branch.astype(jnp.float32), axis=0)
    grad_down_weight = tdot(activ, grad_branch)
    grad_activ = ndot(grad_branch, full_down)
    gelu_out, gelu_back = jax.vjp(exact_gelu, upper)
    grad_upper = gelu_back(grad_activ)[0].astype(jnp.bfloat16)
    grad_up_bias = jnp.sum(grad_upper.astype(jnp.float32), axis=0)
    grad_up_weight = tdot(normed2, grad_upper)
    grad_normed2 = ndot(grad_upper, full_up)
    norm_out, norm_back = jax.vjp(norm_rows, middle, mid_gain32, mid_shift32)
    through_mid, grad_mid_gain, grad_mid_shift = norm_back(grad_normed2)
    grad_middle = grad_ending + through_mid
    grad_attended = grad_middle.astype(jnp.bfloat16)
    grad_out_weight = tdot(context, grad_attended)
    grad_context = (
        ndot(grad_attended, full_out).astype(jnp.bfloat16).reshape(chips, seen, HEADS, head_dim)
    )
    again_scores = (
        jnp.einsum("cqhe,ckhe->chqk", queries, keys, preferred_element_type=jnp.float32) * scale
    )
    probs_full = jnp.exp(again_scores - log_total)
    probs_low = probs_full.astype(jnp.bfloat16)
    grad_values = jnp.einsum(
        "chqk,cqhe->ckhe", probs_low, grad_context, preferred_element_type=jnp.float32
    ).astype(jnp.bfloat16)
    grad_probs = jnp.einsum(
        "cqhe,ckhe->chqk", grad_context, values, preferred_element_type=jnp.float32
    )
    row_dot = jnp.sum(probs_full * grad_probs, axis=-1, keepdims=True)
    grad_scores = (probs_full * (grad_probs - row_dot)).astype(jnp.bfloat16)
    grad_queries = (
        jnp.einsum("chqk,ckhe->cqhe", grad_scores, keys, preferred_element_type=jnp.float32) * scale
    ).astype(jnp.bfloat16)
    grad_keys = (
        jnp.einsum("chqk,cqhe->ckhe", grad_scores, queries, preferred_element_type=jnp.float32)
        * scale
    ).astype(jnp.bfloat16)
    grad_joint = jnp.stack([grad_queries, grad_keys, grad_values], axis=2).reshape(rows, 3 * width)
    grad_qkv_weight = tdot(normed, grad_joint)
    grad_normed = ndot(grad_joint, full_qkv)
    first_out, first_back = jax.vjp(norm_rows, start, pre_gain32, pre_shift32)
    through_pre, grad_pre_gain, grad_pre_shift = first_back(grad_normed)
    grad_start = grad_middle + through_pre
    grad_conv_part = jnp.sum(grad_start, axis=0)
    grad_embedded = grad_start.astype(jnp.bfloat16).reshape(chips, seen, width)
    grad_band = jnp.einsum(
        "cvbp,cvd->cbpd", masked, grad_embedded, preferred_element_type=jnp.float32
    )
    grad_band = grad_band.reshape(chips, bands, pix * width)
    grad_pixels = jnp.einsum(
        "cvd,cbpd->cvbp", grad_embedded, band_kernels, preferred_element_type=jnp.float32
    )
    grad_pixels = grad_pixels * valid[:, None, :, None]
    grad_kernels_part = jnp.einsum("cbw,cbk->wk", onehot, grad_band, precision=HIGH)
    kernel_sum, grad_conv = lax.psum((grad_kernels_part, grad_conv_part), AXES)
    kernel_low = kernel_sum.astype(jnp.bfloat16)
    own_low = own_part(kernel_low, 1)
    grad_kernel_weight = tdot(feature_low, own_low)
    grad_kernel_bias = jnp.sum(own_low.astype(jnp.float32), axis=0)
    grad_feature = ndot(kernel_low, full_kernel)
    grad_bias_weight = own_part(source_low.astype(jnp.float32)[:, None] * grad_conv[None, :], 0)
    grad_source = jnp.dot(full_bias_weight.astype(jnp.float32), grad_conv, precision=HIGH)
    core_grads = core_back((grad_feature, grad_source))
    summed = (
        lax.psum_scatter(grad_pre_gain, AXES, scatter_dimension=0, tiled=True),
        lax.psum_scatter(grad_pre_shift, AXES, scatter_dimension=0, tiled=True),
        lax.psum_scatter(grad_qkv_weight, AXES, scatter_dimension=0, tiled=True),
        lax.psum_scatter(grad_out_weight, AXES, scatter_dimension=0, tiled=True),
        lax.psum_scatter(grad_mid_gain, AXES, scatter_dimension=0, tiled=True),
        lax.psum_scatter(grad_mid_shift, AXES, scatter_dimension=0, tiled=True),
        lax.psum_scatter(grad_up_weight, AXES, scatter_dimension=0, tiled=True),
        lax.psum_scatter(grad_up_bias, AXES, scatter_dimension=0, tiled=True),
        lax.psum_scatter(grad_down_weight, AXES, scatter_dimension=0, tiled=True),
        lax.psum_scatter(grad_down_bias, AXES, scatter_dimension=0, tiled=True),
        lax.psum_scatter(grad_dec_weight, AXES, scatter_dimension=0, tiled=True),
        lax.psum_scatter(grad_dec_bias, AXES, scatter_dimension=0, tiled=True),
        lax.psum_scatter(grad_mask, AXES, scatter_dimension=0, tiled=True),
    )
    return (
        decoder_in,
        grad_pixels,
        summed[0],
        summed[1],
        summed[2],
        summed[3],
        summed[4],
        summed[5],
        summed[6],
        summed[7],
        summed[8],
        summed[9],
        summed[10],
        summed[11],
        summed[12],
        own_part(core_grads[0], 1),
        own_part(core_grads[1], 0),
        own_part(core_grads[2], 0),
        own_part(core_grads[3], 0),
        own_part(core_grads[4], 0),
        own_part(core_grads[5], 0),
        own_part(core_grads[6], 0),
        own_part(core_grads[7], 0),
        own_part(core_grads[8], 0),
        own_part(core_grads[9], 0),
        own_part(core_grads[10], 0),
        own_part(core_grads[11], 0),
        grad_kernel_weight,
        grad_kernel_bias,
        grad_bias_weight,
    )


def on_device(
    pixels,
    sensor,
    band_wave,
    visible,
    block_order,
    pre_gain,
    pre_shift,
    qkv_weight,
    out_weight,
    mid_gain,
    mid_shift,
    up_weight,
    up_bias,
    down_weight,
    down_bias,
    dec_weight,
    dec_bias,
    mask_token,
    gen_tokens,
    gen_qkv,
    gen_out,
    gen_out_bias,
    gen_gain1,
    gen_shift1,
    gen_up,
    gen_up_bias,
    gen_down,
    gen_down_bias,
    gen_gain2,
    gen_shift2,
    kernel_weight,
    kernel_bias,
    bias_weight,
    cotangent,
):
    arguments = (
        pixels,
        sensor,
        band_wave,
        visible,
        block_order,
        pre_gain,
        pre_shift,
        qkv_weight,
        out_weight,
        mid_gain,
        mid_shift,
        up_weight,
        up_bias,
        down_weight,
        down_bias,
        dec_weight,
        dec_bias,
        mask_token,
        gen_tokens,
        gen_qkv,
        gen_out,
        gen_out_bias,
        gen_gain1,
        gen_shift1,
        gen_up,
        gen_up_bias,
        gen_down,
        gen_down_bias,
        gen_gain2,
        gen_shift2,
        kernel_weight,
        kernel_bias,
        bias_weight,
        cotangent,
    )
    planes = lax.axis_size("dp") // 2
    devices = planes * 8
    if lax.axis_size("fsdp") != 4 or planes & (planes - 1) or pre_gain.shape[0] % 8:
        return on_device_plain(*arguments)
    low = jnp.bfloat16
    chips, seen, bands, pix = pixels.shape
    width = qkv_weight.shape[0] * devices
    hidden_width = up_weight.shape[1]
    head_dim = width // HEADS
    scale = 1.0 / math.sqrt(head_dim)
    dec_width = dec_weight.shape[1]
    rows = chips * seen
    gen_width = gen_qkv.shape[0] * devices
    up_size = gen_up.shape[1]
    thin = (
        pre_gain, pre_shift, mid_gain, mid_shift, down_bias, up_bias, dec_bias, mask_token,
        gen_out_bias, gen_gain1, gen_shift1, gen_down_bias, gen_gain2, gen_shift2, gen_up_bias,
    )
    thin = tuple(item.reshape(1, -1) for item in thin)
    wave_code = jnp.asarray(code_table(NWAVE, gen_width // 2).astype(low).astype(np.float32))
    valid = band_valid(sensor, bands)
    sizes = (rows, width, hidden_width, dec_width, chips, PATCH)
    share = PATCH // devices
    order = block_order.reshape(PATCH // 128, 128)
    (
        full_wide, full_down, kernels, slots, returned, normed, joint, probs, context, middle,
        normed2, activ, slope, ending, start, ordered, gen_rows, gen_down_full, gen_vec, vecs,
        feature_low, source_low,
    ) = prepare(
        planes,
        (rows, width, hidden_width, dec_width, chips, up_size, PATCH),
        qkv_weight,
        up_weight,
        out_weight,
        dec_weight,
        down_weight,
        kernel_weight,
        kernel_bias.reshape(1, -1),
        pixels.transpose(0, 2, 3, 1).reshape(chips, bands * pix, seen),
        sensor.reshape(1, chips),
        band_wave,
        visible,
        jnp.asarray(code_table(GRID, width // 4)),
        wave_code,
        gen_up,
        gen_qkv,
        gen_out,
        bias_weight,
        gen_tokens.T,
        gen_down,
        cotangent.reshape(devices, chips, share, dec_width),
        order,
        *thin,
    )
    onehot = (band_wave[:, :, None] == jnp.arange(NWAVE, dtype=jnp.int32)[None, None, :]).astype(
        low
    )
    band_kernels = jnp.einsum(
        "cbw,pwd->cbpd",
        onehot,
        kernels.reshape(pix, NWAVE, width),
        preferred_element_type=jnp.float32,
    ).astype(low)
    (
        sum_dec, sum_up, sum_oq, sum_down, grad_kernel_weight, grad_kernel_bias, sum_all,
        gen_wide, gen_tall, gen_seq, gen_lines, grad_bias_weight, grad_embedded, decoder_in,
    ) = backward(
        planes,
        sizes,
        ordered,
        returned.reshape(chips * PATCH, dec_width),
        visible,
        order,
        ending,
        full_wide,
        full_down,
        activ,
        slope,
        normed2,
        middle,
        context,
        joint,
        probs,
        normed,
        start,
        slots,
        vecs,
        kernel_weight,
        feature_low,
        source_low,
        gen_rows,
        gen_down_full,
        gen_vec,
        wave_code,
    )
    handed = hand_out(
        planes,
        (width, hidden_width, dec_width, gen_qkv.shape[0]),
        sum_dec, sum_up, sum_oq, sum_down, grad_kernel_weight, grad_kernel_bias, sum_all,
        gen_wide, gen_tall, gen_seq, gen_lines, grad_bias_weight,
    )
    flat = (0, 1, 4, 5, 7, 9, 11, 12, 16, 17, 18, 20, 22, 23, 24, 26)
    handed = [item.reshape(-1) if i in flat else item for i, item in enumerate(handed)]
    grad_embedded = grad_embedded.reshape(chips, seen, width)
    grad_pixels = jnp.einsum(
        "cvd,cbpd->cvbp", grad_embedded, band_kernels, preferred_element_type=jnp.float32
    )
    grad_pixels = grad_pixels * valid[:, None, :, None]
    decoder_in = decoder_in.reshape(devices * chips, share, dec_width)
    return (decoder_in, grad_pixels) + tuple(handed)


def solution(mesh):
    in_specs = (
        P(AXES, None, None, None),
        P(AXES),
        P(AXES, None),
        P(AXES, None),
        P(),
        P(AXES),
        P(AXES),
        P(AXES, None),
        P(AXES, None),
        P(AXES),
        P(AXES),
        P(AXES, None),
        P(AXES),
        P(AXES, None),
        P(AXES),
        P(AXES, None),
        P(AXES),
        P(AXES),
        P(None, AXES),
        P(AXES, None),
        P(AXES, None),
        P(AXES),
        P(AXES),
        P(AXES),
        P(AXES, None),
        P(AXES),
        P(AXES, None),
        P(AXES),
        P(AXES),
        P(AXES),
        P(None, AXES),
        P(AXES),
        P(AXES, None),
        P(None, AXES, None),
    )
    out_specs = (
        P(None, AXES, None),
        P(AXES, None, None, None),
        P(AXES),
        P(AXES),
        P(AXES, None),
        P(AXES, None),
        P(AXES),
        P(AXES),
        P(AXES, None),
        P(AXES),
        P(AXES, None),
        P(AXES),
        P(AXES, None),
        P(AXES),
        P(AXES),
        P(None, AXES),
        P(AXES, None),
        P(AXES, None),
        P(AXES),
        P(AXES),
        P(AXES),
        P(AXES, None),
        P(AXES),
        P(AXES, None),
        P(AXES),
        P(AXES),
        P(AXES),
        P(None, AXES),
        P(AXES),
        P(AXES, None),
    )
    return jax.shard_map(
        on_device, mesh=mesh, in_specs=in_specs, out_specs=out_specs, check_vma=False
    )
```

```python
from functools import partial
import math

import jax
import jax.numpy as jnp
import numpy as np
from jax import lax
from jax.experimental import pallas as pl
from jax.experimental.pallas import tpu as pltpu
from jax.sharding import PartitionSpec as P

HEADS = 12
WD = 128
GHEADS = 4
LAT = 128
NWAVE = 32
GRID = 32
PATCH = 1024


EPS = 1e-05
AXES = ("dp", "fsdp")
BAND_DROP = (0, 6, 9, 7)
HIGH = lax.Precision.HIGHEST


def sincos(values, count):
    freq = jnp.exp(jnp.arange(count, dtype=jnp.float32) * (-math.log(10000.0) / count))
    angle = values[..., None] * freq
    return jnp.concatenate([jnp.sin(angle), jnp.cos(angle)], axis=-1)


def code_table(count, size):
    freq = np.exp(np.arange(size, dtype=np.float32) * np.float32(-math.log(10000.0) / size))
    angle = np.arange(count, dtype=np.float32)[:, None] * freq.astype(np.float32)
    return np.concatenate([np.sin(angle), np.cos(angle)], axis=-1).astype(np.float32)


def norm_rows(rows, gain, shift):
    mean = jnp.mean(rows, axis=-1, keepdims=True)
    centred = rows - mean
    spread = jnp.mean(centred * centred, axis=-1, keepdims=True)
    return centred * lax.rsqrt(spread + EPS) * gain + shift


def exact_gelu(values):
    return jax.nn.gelu(values, approximate=False)


def band_valid(sensor, bands):
    drops = jnp.array(BAND_DROP, jnp.int32)
    picked = jnp.where(
        sensor[:, None] == jnp.arange(4, dtype=jnp.int32)[None, :], drops[None, :], 0
    )
    count = bands - jnp.sum(picked, axis=1)
    return (jnp.arange(bands, dtype=jnp.int32)[None, :] < count[:, None]).astype(jnp.float32)


def place_code(visible, width):
    row = (visible // GRID).astype(jnp.float32)
    col = (visible % GRID).astype(jnp.float32)
    return jnp.concatenate([sincos(row, width // 4), sincos(col, width // 4)], axis=-1)


def gen_core(
    wave_code,
    tokens,
    gen_qkv,
    gen_out,
    gen_out_bias,
    gen_gain1,
    gen_shift1,
    gen_up,
    gen_up_bias,
    gen_down,
    gen_down_bias,
    gen_gain2,
    gen_shift2,
):
    sequence = jnp.concatenate([tokens[:LAT], wave_code, tokens[LAT:]], axis=0)
    length = sequence.shape[0]
    width = sequence.shape[1]
    head_dim = width // GHEADS
    joint = jnp.dot(sequence, gen_qkv, precision=HIGH).reshape(length, 3, GHEADS, head_dim)
    scores = jnp.einsum("qhe,khe->hqk", joint[:, 0], joint[:, 1], precision=HIGH) / math.sqrt(
        head_dim
    )
    probs = jax.nn.softmax(scores, axis=-1)
    context = jnp.einsum("hqk,khe->qhe", probs, joint[:, 2], precision=HIGH).reshape(length, width)
    mixed = norm_rows(
        sequence + jnp.dot(context, gen_out, precision=HIGH) + gen_out_bias, gen_gain1, gen_shift1
    )
    hidden = jax.nn.gelu(jnp.dot(mixed, gen_up, precision=HIGH) + gen_up_bias, approximate=False)
    final = norm_rows(
        mixed + jnp.dot(hidden, gen_down, precision=HIGH) + gen_down_bias, gen_gain2, gen_shift2
    )
    feature = final[LAT : LAT + NWAVE] + sequence[LAT : LAT + NWAVE]
    return (feature, final[length - 1])


def own_part(full, dim):
    count = lax.axis_size("dp") * lax.axis_size("fsdp")
    index = lax.axis_index("dp") * lax.axis_size("fsdp") + lax.axis_index("fsdp")
    piece = full.shape[dim] // count
    return lax.dynamic_slice_in_dim(full, index * piece, piece, dim)


def tdot(left, right):
    return lax.dot_general(
        left, right, (((0,), (0,)), ((), ())), preferred_element_type=jnp.float32
    )


def ndot(left, right):
    return lax.dot_general(
        left, right, (((1,), (1,)), ((), ())), preferred_element_type=jnp.float32
    )


MESH_ID = pl.DeviceIdType.MESH
ANY = pl.BlockSpec(memory_space=pl.ANY)
VMEM = pl.BlockSpec(memory_space=pltpu.VMEM)


class Net:
    def __init__(self, planes):
        dp, fs = lax.axis_index("dp"), lax.axis_index("fsdp")
        self.planes = planes
        self.z, self.x = lax.div(dp, 2), lax.rem(dp, 2)
        self.y, self.c = lax.div(fs, 2), lax.rem(fs, 2)
        self.sib = self.at(self.z, self.x, self.y, 1 - self.c)
        self.nx = self.at(self.z, 1 - self.x, self.y, self.c)
        self.ny = self.at(self.z, self.x, 1 - self.y, self.c)

    def at(self, z, x, y, c):
        return (z * 2 + x, y * 2 + c)

    def plane(self, k):
        return lax.rem(self.z + k, self.planes)

    def zpeer(self, k):
        return self.at(self.plane(k), self.x, self.y, self.c)

    def chip(self, k, dx=0, dy=0):
        x = 1 - self.x if dx else self.x
        y = 1 - self.y if dy else self.y
        return self.plane(k) * 4 + x * 2 + y

    def greet(self):
        barrier = pltpu.get_barrier_semaphore()
        partners = [self.sib, self.nx, self.ny]
        partners += [self.zpeer(k) for k in range(1, self.planes)]
        for partner in partners:
            pl.semaphore_signal(barrier, inc=1, device_id=partner, device_id_type=MESH_ID)
        pl.semaphore_wait(barrier, len(partners))


class Wires:
    def __init__(self, send, recv):
        self.send, self.recv, self.used, self.started = send, recv, 0, []

    def push(self, src, dst, device):
        index = self.used
        self.used += 1
        copy = pltpu.make_async_remote_copy(
            src_ref=src,
            dst_ref=dst,
            send_sem=self.send.at[index],
            recv_sem=self.recv.at[index],
            device_id=device,
            device_id_type=MESH_ID,
        )
        copy.start()
        self.started.append(copy)
        return copy

    def drain(self):
        for copy in self.started:
            copy.wait_send()


class Gather:
    def __init__(self, net, wires, own, piece):
        self.net, self.wires, self.own, self.piece = net, wires, own, piece
        self.z_in, self.first, self.second, self.twins = {}, {}, {}, []

    def near(self, h):
        return self.net.ny if h else self.net.nx

    def far(self, h):
        return self.net.nx if h else self.net.ny

    def share(self, chip, h, src=None):
        spot = self.piece(chip, h)
        self.twins.append(self.wires.push(spot if src is None else src, spot, self.net.sib))

    def begin_z(self):
        for k in range(1, self.net.planes):
            for h in range(2):
                spot = self.piece(self.net.chip(0), h)
                self.z_in[k, h] = self.wires.push(self.own(h), spot, self.net.zpeer(k))

    def spread(self, k):
        back = (self.net.planes - k) % self.net.planes
        for h in range(2):
            if k:
                self.z_in[k, h].wait_recv()
            spot = self.piece(self.net.chip(back), h)
            src = self.own(h) if k == 0 else spot
            self.first[k, h] = self.wires.push(src, spot, self.near(h))
            self.second[k, h, 0] = self.wires.push(src, spot, self.far(h))
            self.share(self.net.chip(back), h, src)

    def relay(self, k):
        back = (self.net.planes - k) % self.net.planes
        for h in range(2):
            self.first[k, h].wait_recv()
            chip = self.net.chip(back, dx=h == 0, dy=h == 1)
            spot = self.piece(chip, h)
            self.second[k, h, 1] = self.wires.push(spot, spot, self.far(h))
            self.share(chip, h)

    def close(self, k):
        back = (self.net.planes - k) % self.net.planes
        for h in range(2):
            for hop in range(2):
                self.second[k, h, hop].wait_recv()
                chip = self.net.chip(back, dx=hop == 1 or h == 1, dy=hop == 1 or h == 0)
                self.share(chip, h)

    def finish(self):
        for copy in self.twins:
            copy.wait_recv()


def gather_copies(planes):
    return 2 * (planes - 1) + 4 * planes + 2 * planes + 8 * planes


class Reduce:
    def __init__(self, net, wires, part, held, near_in, far_in, z_in):
        self.net, self.wires, self.part, self.held = net, wires, part, held
        self.near_in, self.far_in, self.z_in = near_in, far_in, z_in
        self.pairs, self.near, self.far, self.along = {}, {}, {}, {}

    def add(self, spot, other):
        size = 16 if spot.shape[0] % 16 == 0 else 8

        def some(i, _):
            at = pl.ds(pl.multiple_of(i * size, size), size)
            total = spot[at].astype(jnp.float32) + other[at].astype(jnp.float32)
            spot[at] = total.astype(spot.dtype)
            return 0

        lax.fori_loop(0, spot.shape[0] // size, some, 0)

    def begin(self, k):
        for dx in range(2):
            for dy in range(2):
                for h in range(2):
                    chip = self.net.chip(k, dx, dy)
                    self.pairs[k, dx, dy, h] = self.wires.push(
                        self.part(chip, 1 - self.net.c, h), self.held.at[chip, h], self.net.sib
                    )

    def stage0(self, k):
        for dx, dy in ((1, 1), (0, 1), (1, 0), (0, 0)):
            for h in range(2):
                self.pairs[k, dx, dy, h].wait_recv()
                chip = self.net.chip(k, dx, dy)
                self.add(self.held.at[chip, h], self.part(chip, self.net.c, h))
                if (dy if h == 0 else dx) == 1:
                    other = dx if h == 0 else dy
                    self.near[k, h, other] = self.wires.push(
                        self.held.at[chip, h],
                        self.near_in.at[k, h, other],
                        self.net.ny if h == 0 else self.net.nx,
                    )

    def stage1(self, k):
        for h in range(2):
            for other in (1, 0):
                self.near[k, h, other].wait_recv()
                chip = self.net.chip(k, other, 0) if h == 0 else self.net.chip(k, 0, other)
                self.add(self.held.at[chip, h], self.near_in.at[k, h, other])
                if other:
                    self.far[k, h] = self.wires.push(
                        self.held.at[chip, h],
                        self.far_in.at[k, h],
                        self.net.nx if h == 0 else self.net.ny,
                    )

    def stage2(self, k):
        for h in range(2):
            self.far[k, h].wait_recv()
            spot = self.held.at[self.net.chip(k), h]
            self.add(spot, self.far_in.at[k, h])
            if k:
                self.along[k, h] = self.wires.push(spot, self.z_in.at[k - 1, h], self.net.zpeer(k))

    def total(self, h):
        value = self.held[self.net.chip(0), h].astype(jnp.float32)
        for k in range(1, self.net.planes):
            self.along[k, h].wait_recv()
            value = value + self.z_in[k - 1, h].astype(jnp.float32)
        return value


def reduce_copies(planes):
    return 8 * planes + 4 * planes + 2 * planes + 2 * (planes - 1)


def reduce_scratch(planes, rows, cols, dtype):
    return [
        pltpu.VMEM((planes * 4, 2, rows, cols), dtype),
        pltpu.VMEM((planes, 2, 2, rows, cols), dtype),
        pltpu.VMEM((planes, 2, rows, cols), dtype),
        pltpu.VMEM((planes - 1, 2, rows, cols), dtype),
    ]


def dot_nn(left, right):
    return jnp.dot(left, right, preferred_element_type=jnp.float32)


class Trade:
    def __init__(self, src, dst, send, recv, local):
        self.src, self.dst, self.send, self.recv = src, dst, send, recv
        self.count = src.shape[0]
        self.me = lax.axis_index("dp") * 4 + lax.axis_index("fsdp")
        self.own = pltpu.make_async_copy(src.at[self.me], dst.at[self.me], local)

    def place(self, i):
        to = lax.rem(self.me + i, self.count)
        return to, (lax.div(to, 4), lax.rem(to, 4))

    def greet(self):
        barrier = pltpu.get_barrier_semaphore()

        def call(i, _):
            pl.semaphore_signal(
                barrier, inc=1, device_id=self.place(i)[1], device_id_type=MESH_ID
            )
            return 0

        lax.fori_loop(1, self.count, call, 0)
        pl.semaphore_wait(barrier, self.count - 1)

    def copy(self, i):
        to, device = self.place(i)
        return pltpu.make_async_remote_copy(
            src_ref=self.src.at[to],
            dst_ref=self.dst.at[self.me],
            send_sem=self.send.at[i],
            recv_sem=self.recv.at[i],
            device_id=device,
            device_id_type=MESH_ID,
        )

    def begin(self, part=0, parts=1):
        def go(i, _):
            self.copy(i).start()
            return 0

        cuts = [1 + (self.count - 1) * p // parts for p in (part, part + 1)]
        lax.fori_loop(*cuts, go, 0)
        if part == 0:
            self.own.start()

    def finish(self):
        def end(i, _):
            self.copy(i).wait()
            return 0

        lax.fori_loop(1, self.count, end, 0)
        self.own.wait()


class Pump:
    def __init__(self):
        self.units, self.at, self.last = [], 0, False

    def put(self, item, order):
        for k in order:
            item.begin(k)
        self.units += [(item, k) for k in order]

    def step(self, count=1):
        for _ in range(count):
            if self.at >= len(self.units) and not self.last:
                return
            for stage, lag in enumerate(LAGS):
                at = self.at - lag
                if 0 <= at < len(self.units) and self.units[at]:
                    item, k = self.units[at]
                    (item.stage0, item.stage1, item.stage2)[stage](k)
            self.at += 1

    def until(self, item):
        self.last = True
        last = max(i for i, unit in enumerate(self.units) if unit and unit[0] is item)
        while self.at <= last + LAGS[2]:
            self.step()


def order_column(order):
    turned = order[...].astype(jnp.float32).T
    column = [turned[:, i : i + 1] for i in range(turned.shape[1])]
    return jnp.concatenate(column, axis=0).astype(jnp.int32)


def tile_rows(i, size):
    return pl.ds(pl.multiple_of(i * size, size), size)


def norm_back(grad, rows, gain):
    mean = jnp.mean(rows, axis=-1, keepdims=True)
    centred = rows - mean
    spread = jnp.mean(centred * centred, axis=-1, keepdims=True)
    inverse = lax.rsqrt(spread + EPS)
    unit = centred * inverse
    scaled = grad * gain
    inner = scaled - jnp.mean(scaled, axis=-1, keepdims=True)
    inner = inner - unit * jnp.mean(scaled * unit, axis=-1, keepdims=True)
    return inverse * inner, grad * unit


def lay_lines(box, at, value):
    for i in range(value.shape[1] // 128):
        box[0, pl.ds(at + i, 1), :] = value[:, i * 128 : (i + 1) * 128]
    return at + value.shape[1] // 128


def box_lines(waves, width, hidden, dec_width):
    used = waves + (6 * width + hidden + 2 * dec_width) // 128
    return used + (-used) % 8


FT = 256
TRADES = 1
LAGS = (0, 3, 6)
BUBBLES = 3
HOP_STEPS = 1
NORM_STEPS = 2
HEAD_STEPS = 1
FEED_STEPS = 1
BLOCK = 128


def backward_kernel(planes, steps, sizes, *refs):
    (rows, width, hidden, dec_width, chips, patches) = sizes
    devices = planes * 8
    seen = rows // chips
    (
        blocks, returned, visible, order, ending, wide, down, activ, slope, normed2, middle, context,
        joint, probs, normed, start, slots, gains, weight, feature, source, gen_rows, gen_down,
        gen_vec, wave_code,
    ) = refs[:25]
    (
        dec_out, up_out, oq_out, down_out, kw_out, kb_out, all_out, gen_wide, gen_tall, gen_seq,
        gen_lines, bias_out, embed_out, decoder_out,
    ) = refs[25:39]
    scratch = refs[39:61]
    (
        big, left, w_down, w_up, t_activ, t_slope, resid, w_sq, t_joint, t_probs,
        g_dec, g_up, g_down, g_oq, g_table, run, back, g_low, g_joint, v_sums,
        f_dec, f_up, f_oq, hand_dec, hand_up, hand_oq, box, send, recv, trade_send, trade_recv, tile_sem, load_sem,
    ) = refs[61:]
    loads = {}

    def load(name, src, dst):
        copy = pltpu.make_async_copy(src, dst, load_sem.at[len(loads)])
        copy.start()
        loads[name] = copy

    up_at, out_at, dec_at = 3 * width, 3 * width + hidden, 4 * width + hidden
    load("returned", returned, big)
    w_dec = w_sq.at[0, :, pl.ds(0, dec_width)]
    load("dec", wide.at[:, pl.ds(dec_at, dec_width)], w_dec)
    load("ending", ending, left.at[0])

    def tile_copies(t):
        slot = lax.rem(t, 2)
        at = tile_rows(t, FT)
        return (
            pltpu.make_async_copy(down.at[at], w_down.at[slot], tile_sem.at[slot, 0]),
            pltpu.make_async_copy(
                wide.at[:, pl.ds(pl.multiple_of(up_at + t * FT, 128), FT)],
                w_up.at[slot],
                tile_sem.at[slot, 1],
            ),
            pltpu.make_async_copy(activ.at[:, at], t_activ.at[slot], tile_sem.at[slot, 2]),
            pltpu.make_async_copy(slope.at[:, at], t_slope.at[slot], tile_sem.at[slot, 3]),
        )

    for copy in tile_copies(0):
        copy.start()
    load("normed2", normed2, left.at[1])
    load("middle", middle, resid)
    load("query", wide.at[:, pl.ds(0, width)], w_sq.at[1])

    net = Net(planes)
    trade = Trade(blocks, decoder_out, trade_send, trade_recv, load_sem.at[15])
    trade.greet()
    trade.begin(0, TRADES)
    wires = Wires(send, recv)
    pump = Pump()
    shard = width // (devices // 2)
    w_rows = lambda chip: pl.ds(pl.multiple_of(chip * shard, 16), shard)

    def quarter(ref, size):
        return lambda chip, c, h: ref.at[
            w_rows(chip), pl.ds(pl.multiple_of((c * 2 + h) * size, 128), size)
        ]

    def stripe(ref, size):
        return lambda chip, c, h: ref.at[
            pl.ds(pl.multiple_of(((chip * 2 + c) * 2 + h) * size, 16), size)
        ]

    q_dec, q_up = dec_width // 4, hidden // 8
    d_rows = hidden // devices // 2
    t_rows = g_table.shape[0] // devices // 2
    parts = (
        quarter(g_dec, q_dec),
        quarter(g_up.at[0], q_up),
        quarter(g_up.at[1], q_up),
        stripe(g_down, d_rows),
        stripe(g_table, t_rows),
        lambda chip, c, h: g_oq.at[c * 2 + h, w_rows(chip)],
    )
    lands = [scratch[i * 4 : i * 4 + 4] for i in range(5)]
    lands.append((scratch[20], lands[3][1], lands[3][2], scratch[21]))
    dec, up0, up1, downs, tables, oq = [
        Reduce(net, wires, part, *land) for part, land in zip(parts, lands)
    ]
    away = list(range(1, planes)) + [0]

    loads["returned"].wait()
    grad_mask = jnp.zeros((8, dec_width), jnp.float32)
    column = order_column(order)
    spread = big.reshape(devices, chips, patches // devices, dec_width)
    for chip in range(chips):
        got = spread[:, chip].reshape(patches, dec_width)
        chosen = (column == visible[pl.ds(chip, 1), :]).astype(jnp.float32)
        picked = tdot(chosen.astype(jnp.bfloat16), got)
        g_joint[pl.ds(chip * seen, seen), pl.ds(0, dec_width)] = picked.astype(jnp.bfloat16)
        left_out = 1.0 - jnp.sum(chosen, axis=1, keepdims=True)
        left_out = jnp.broadcast_to(left_out, (patches, 8)).astype(jnp.bfloat16)
        grad_mask = grad_mask + tdot(left_out, got)
    v_sums[pl.ds(7, 1), pl.ds(dec_width, dec_width)] = grad_mask[:1]
    load("slots", slots, big)
    grad_rows = g_joint[:, pl.ds(0, dec_width)]
    v_sums[pl.ds(7, 1), pl.ds(0, dec_width)] = jnp.sum(
        grad_rows.astype(jnp.float32), axis=0, keepdims=True
    )
    loads["ending"].wait()

    def dec_part(i, _):
        at = tile_rows(i, FT)
        g_dec[at, :] = tdot(left[0, :, at], grad_rows).astype(jnp.bfloat16)
        return 0

    lax.fori_loop(0, width // FT, dec_part, 0)
    pump.put(dec, away)
    loads["dec"].wait()

    def end_part(i, _):
        at = tile_rows(i, FT)
        run[at, :] = ndot(g_joint[at, pl.ds(0, dec_width)], w_dec[...])
        g_low[at, :] = run[at, :].astype(jnp.bfloat16)
        return 0

    lax.fori_loop(0, rows // FT, end_part, 0)
    load("out", wide.at[:, pl.ds(out_at, width)], w_sq.at[0])
    load("context", context, left.at[0])
    back[...] = jnp.zeros_like(back)
    v_sums[pl.ds(0, 1), pl.ds(0, width)] = jnp.sum(
        g_low[...].astype(jnp.float32), axis=0, keepdims=True
    )
    loads["normed2"].wait()
    tiles = hidden // FT

    parts_sent = [1]

    def trade_more():
        if parts_sent[0] < TRADES:
            trade.begin(parts_sent[0], TRADES)
            parts_sent[0] += 1

    def feed(t, _):
        slot = lax.rem(t, 2)

        @pl.when(t + 1 < tiles)
        def _():
            for copy in tile_copies(t + 1):
                copy.start()

        for copy in tile_copies(t):
            copy.wait()
        grad = ndot(g_low[...], w_down[slot])
        grad_upper = (grad * t_slope[slot].astype(jnp.float32)).astype(jnp.bfloat16)
        at = tile_rows(t, FT)
        v_sums[pl.ds(1, 1), at] = jnp.sum(
            grad_upper.astype(jnp.float32), axis=0, keepdims=True
        )
        g_down[at, :] = tdot(t_activ[slot], g_low[...]).astype(jnp.bfloat16)
        g_up[lax.div(t, tiles // 2), :, tile_rows(lax.rem(t, tiles // 2), FT)] = tdot(
            left[1], grad_upper
        ).astype(jnp.bfloat16)
        for i in range(rows // FT):
            part = pl.ds(i * FT, FT)
            back[part, :] += ndot(grad_upper[i * FT : (i + 1) * FT], w_up[slot])
        return 0

    for i in range(0, tiles, 2):
        lax.fori_loop(i, i + 2, feed, 0)
        if i + 2 == tiles // 2:
            pump.put(up0, away)
        if i + 2 < tiles:
            trade_more()
            pump.step(FEED_STEPS)
    pump.put(up1, away)
    pump.put(downs, away)
    load("normed", normed, left.at[1])
    loads["middle"].wait()

    def through_norm(gain_row, sums_at):
        gain = gains[pl.ds(gain_row, 1), pl.ds(0, width)]

        def block(i, sums):
            at = tile_rows(i, BLOCK)
            grad = back[at, :]
            inner, terms = norm_back(grad, resid[at, :], gain)
            run[at, :] += inner
            return (
                sums[0] + jnp.sum(terms, axis=0, keepdims=True),
                sums[1] + jnp.sum(grad, axis=0, keepdims=True),
            )

        zero = jnp.zeros((1, width), jnp.float32)
        sums = lax.fori_loop(0, rows // BLOCK, block, (zero, zero))
        v_sums[pl.ds(sums_at, 1), pl.ds(0, width)] = sums[0]
        v_sums[pl.ds(sums_at + 1, 1), pl.ds(0, width)] = sums[1]

    through_norm(2, 2)
    pump.step(NORM_STEPS)
    load("start", start, resid)
    g_low[...] = run[...].astype(jnp.bfloat16)
    loads["context"].wait()
    loads["out"].wait()

    def out_part(i, _):
        at = tile_rows(i, FT)
        g_oq[0, at, :] = tdot(left[0, :, at], g_low[...]).astype(jnp.bfloat16)
        return 0

    lax.fori_loop(0, width // FT, out_part, 0)

    def context_part(i, _):
        at = tile_rows(i, FT)
        g_low[at, :] = ndot(g_low[at, :], w_sq[0]).astype(jnp.bfloat16)
        return 0

    lax.fori_loop(0, rows // FT, context_part, 0)
    load("key", wide.at[:, pl.ds(width, width)], w_sq.at[0])
    pump.step(2)

    pairs = width // 128
    head = width // HEADS
    scale = 1.0 / math.sqrt(head)
    odd = lax.broadcasted_iota(jnp.int32, (1, 128), 1) >= head

    def pair_copies(n):
        slot = lax.rem(n, 2)
        at = tile_rows(lax.div(n, pairs), seen)
        copies = [
            pltpu.make_async_copy(probs.at[pl.ds(2 * n, 2)], t_probs.at[slot], tile_sem.at[slot, 0])
        ]
        for i in range(3):
            lane = pl.ds(pl.multiple_of(lax.rem(n, pairs) * 128 + i * width, 128), 128)
            copies.append(
                pltpu.make_async_copy(
                    joint.at[at, lane], t_joint.at[slot, i], tile_sem.at[slot, i + 1]
                )
            )
        return copies

    for copy in pair_copies(0):
        copy.start()

    def attend(n, _):
        slot = lax.rem(n, 2)

        @pl.when(n + 1 < chips * pairs)
        def _():
            for copy in pair_copies(n + 1):
                copy.start()

        for copy in pair_copies(n):
            copy.wait()
        chip = lax.div(n, pairs)
        pair = lax.rem(n, pairs)
        at = tile_rows(chip, seen)
        lanes = [
            pl.ds(pl.multiple_of(pair * 128 + i * width, 128), 128) for i in range(3)
        ]
        query, key, value = [t_joint[slot, i] for i in range(3)]
        grad = g_low[at, lanes[0]]
        zero = jnp.zeros_like(grad)
        totals = [None, None, None]
        for h in range(2):
            mine = odd if h else jnp.logical_not(odd)
            grad_h = jnp.where(mine, grad, zero)
            query_h = jnp.where(mine, query, zero)
            key_h = jnp.where(mine, key, zero)
            prob = t_probs[slot, h]
            prob32 = prob.astype(jnp.float32)
            grad_prob = ndot(grad_h, value)
            row_dot = jnp.sum(prob32 * grad_prob, axis=-1, keepdims=True)
            grad_score = (prob32 * (grad_prob - row_dot)).astype(jnp.bfloat16)
            terms = (dot_nn(grad_score, key_h), tdot(grad_score, query_h), tdot(prob, grad_h))
            totals = [new if old is None else old + new for old, new in zip(totals, terms)]
        g_joint[at, lanes[0]] = (totals[0] * scale).astype(jnp.bfloat16)
        g_joint[at, lanes[1]] = (totals[1] * scale).astype(jnp.bfloat16)
        g_joint[at, lanes[2]] = totals[2].astype(jnp.bfloat16)
        return 0

    for i in range(0, chips * pairs, 2):
        lax.fori_loop(i, i + 2, attend, 0)
        trade_more()
        pump.step(HEAD_STEPS)

    loads["normed"].wait()
    def joint_part(i, _):
        which, at = lax.div(i, width // FT), tile_rows(lax.rem(i, width // FT), FT)
        lane = pl.ds(pl.multiple_of(which * width, 128), width)
        g_oq[which + 1, at, :] = tdot(left[1, :, at], g_joint[:, lane]).astype(jnp.bfloat16)
        return 0

    lax.fori_loop(0, 3 * width // FT, joint_part, 0)
    value = pltpu.make_async_copy(
        wide.at[:, pl.ds(2 * width, width)], w_sq.at[1], load_sem.at[len(loads)]
    )
    back[...] = jnp.zeros_like(back)

    def joint_back(i, _):
        for j, copy in enumerate((loads["query"], loads["key"], value)):

            @pl.when(i == j)
            def _():
                copy.wait()

        lane = pl.ds(pl.multiple_of(i * width, 128), width)

        def some(j, _):
            at = tile_rows(j, FT)
            back[at, :] += ndot(g_joint[at, lane], w_sq[lax.rem(i + 1, 2)])
            return 0

        lax.fori_loop(0, rows // FT, some, 0)

        @pl.when(i == 0)
        def _():
            value.start()

        return 0

    lax.fori_loop(0, 3, joint_back, 0)
    pump.step(1)
    loads["start"].wait()
    through_norm(0, 4)
    g_low[...] = run[...].astype(jnp.bfloat16)
    conv = jnp.sum(run[...], axis=0, keepdims=True)
    embed = pltpu.make_async_copy(g_low, embed_out, tile_sem.at[0, 1])
    embed.start()
    loads["slots"].wait()
    span = 512

    def table_block(i, _):
        at = tile_rows(i, span)
        g_table[at, :] = dot_nn(big[at, :], g_low[...]).astype(jnp.bfloat16)
        return 0

    lax.fori_loop(0, g_table.shape[0] // span, table_block, 0)
    pump.put(tables, away)
    pump.units += [None] * BUBBLES
    pump.put(oq, away)

    waves = t_rows
    lines = width // 128
    box[0, pl.ds(waves, box.shape[1] - waves), :] = jnp.zeros(
        (box.shape[1] - waves, 128), jnp.float32
    )
    at = lay_lines(box, waves, conv)
    for line in (4, 5, 2, 3, 0):
        at = lay_lines(box, at, v_sums[pl.ds(line, 1), pl.ds(0, width)])
    at = lay_lines(box, at, v_sums[pl.ds(1, 1), :])
    lay_lines(box, at, v_sums[pl.ds(7, 1), pl.ds(0, 2 * dec_width)])

    while parts_sent[0] < TRADES:
        trade_more()
    pump.until(tables)
    held = tables.held
    partial_sum = jnp.zeros((waves, 128), jnp.float32)
    for h in range(2):
        own = tables.total(h).astype(jnp.bfloat16)
        cols = pl.ds(h * width, width)
        kw_out[:, cols] = tdot(feature[...], own)
        kb_out[:, cols] = jnp.sum(own.astype(jnp.float32), axis=0, keepdims=True)
        partial_sum = partial_sum + ndot(own, weight[:, cols])
    box[0, pl.ds(0, waves), :] = partial_sum
    peers = [net.sib, net.nx, net.ny]
    for bit in range(steps):
        step = 1 << bit
        up = lax.rem(lax.div(net.z, step), 2) == 0
        peers.append(net.at(jnp.where(up, net.z + step, net.z - step), net.x, net.y, net.c))
    for i, peer in enumerate(peers):
        hop = wires.push(box.at[2 * i], box.at[2 * i + 1], peer)
        pump.step(HOP_STEPS)
        hop.wait_recv()
        box[2 * i + 2] = box[2 * i] + box[2 * i + 1]
    end = box.at[2 * len(peers)]
    all_out[...] = end[...]
    me = net.chip(0) * 2 + net.c
    conv = jnp.concatenate(
        [end[pl.ds(waves + i, 1), :] for i in range(lines)], axis=1
    )
    gen_width = gen_rows.shape[0]
    up_size = gen_down.shape[0]
    bias_at = gen_rows.shape[1] - gen_width - width
    grad_source = lax.dot_general(
        jnp.broadcast_to(conv, (8, width)),
        gen_rows[:, pl.ds(bias_at, width)].astype(jnp.float32),
        (((1,), (1,)), ((), ())),
        precision=HIGH,
        preferred_element_type=jnp.float32,
    )
    top = lax.broadcasted_iota(jnp.int32, (8, gen_width), 0)
    grad_source = jnp.where(top == 0, grad_source, 0.0)
    pump.step(1)
    small = gen_width // devices
    lane = lax.broadcasted_iota(jnp.int32, (8, gen_width), 1)
    pick = ((lane == me * small + top) & (top < small)).astype(jnp.float32)
    exact = partial(
        lax.dot_general, precision=HIGH, preferred_element_type=jnp.float32
    )
    rows_of = lambda value: exact(pick, value, (((1,), (0,)), ((), ())))
    lanes_of = lambda value: exact(value, pick, (((1,), (1,)), ((), ())))
    chunk = up_size // 4

    def put_up(i, value):
        gen_wide[:, pl.ds(pl.multiple_of(i * chunk, chunk), chunk)] = rows_of(value)

    def put_down(i, value):
        back[:, pl.ds(pl.multiple_of(i * gen_width, gen_width), gen_width)] = value

    g_seq, g_qkv, g_out, thin = gen_back(
        gen_rows, gen_down, gen_vec, wave_code[...], LAT + NWAVE + 1, end[pl.ds(0, waves), :],
        grad_source, v_sums, put_up, put_down,
    )
    pump.step(2)
    gen_wide[:, pl.ds(up_size, 3 * gen_width)] = rows_of(g_qkv)
    gen_wide[:, pl.ds(up_size + 3 * gen_width, gen_width)] = rows_of(g_out)
    tall = up_size // devices
    per = devices // 4
    gen_tall[...] = back[
        tile_rows(lax.rem(me, per), tall),
        pl.ds(pl.multiple_of(lax.div(me, per) * gen_width, 128), gen_width),
    ]
    gen_seq[...] = lanes_of(g_seq)
    for i, value in enumerate(thin):
        gen_lines[pl.ds(i, 1), pl.ds(0, gen_width)] = value
    gen_lines[pl.ds(6, 1), :] = v_sums[pl.ds(6, 1), pl.ds(0, up_size)]
    own_source = jnp.sum(
        pick * source[pl.ds(0, 1), :].astype(jnp.float32), axis=1, keepdims=True
    )
    bias_out[...] = own_source * conv
    pump.until(oq)
    half = shard // 2
    own_rows = pl.ds(pl.multiple_of(net.c * half, 8), half)
    their_rows = pl.ds(pl.multiple_of((1 - net.c) * half, 8), half)
    jobs = (
        (dec, f_dec, hand_dec, dec_out, 0, q_dec),
        (up0, f_up.at[0], hand_up.at[0], up_out, 0, q_up),
        (up1, f_up.at[1], hand_up.at[1], up_out, hidden // 2, q_up),
        (oq, f_oq, hand_oq, oq_out, 0, width),
    )
    swaps = []
    for item, final, hand, out, base, size in jobs:
        for h in range(2):
            final[h] = item.total(h)
            swaps.append(wires.push(final.at[h, their_rows], hand.at[h], net.sib))
    for h in range(2):
        down_out[pl.ds(h * d_rows, d_rows)] = downs.total(h)
    for item, final, hand, out, base, size in jobs:
        for h in range(2):
            own = pl.ds(pl.multiple_of(base + (net.c * 2 + h) * size, 128), size)
            other = pl.ds(pl.multiple_of(base + ((1 - net.c) * 2 + h) * size, 128), size)
            out[:, own] = final[h, own_rows]
            swaps.pop(0).wait_recv()
            out[:, other] = hand[h]
    embed.wait()
    trade.finish()
    wires.drain()


def backward(planes, sizes, *args):
    (rows, width, hidden, dec_width, chips, patches) = sizes
    devices = planes * 8
    steps = (planes - 1).bit_length()
    low, full = jnp.bfloat16, jnp.float32
    shard = width // (devices // 2)
    q_dec, q_up = dec_width // 4, hidden // 8
    d_rows = hidden // devices // 2
    slots = args[16].shape[0]
    t_rows = slots // devices // 2
    box_rows = box_lines(t_rows, width, hidden, dec_width)
    up_size, gen_width = args[22].shape
    copies = 6 * reduce_copies(planes) + 3 + steps + 8
    scratch = []
    for shape in (
        (shard, q_dec), (shard, q_up), (shard, q_up), (d_rows, width), (t_rows, width),
    ):
        scratch += reduce_scratch(planes, *shape, low)
    assert d_rows == shard
    last = reduce_scratch(planes, shard, width, low)
    scratch += [last[0], last[3]]
    scratch += [
        pltpu.VMEM((chips * patches, dec_width), low),
        pltpu.VMEM((2, rows, width), low),
        pltpu.VMEM((2, FT, width), low),
        pltpu.VMEM((2, width, FT), low),
        pltpu.VMEM((2, rows, FT), low),
        pltpu.VMEM((2, rows, FT), low),
        pltpu.VMEM((rows, width), full),
        pltpu.VMEM((2, width, width), low),
        pltpu.VMEM((2, 3, rows // chips, 128), low),
        pltpu.VMEM((2, 2, rows // chips, rows // chips), low),
        pltpu.VMEM((width, dec_width), low),
        pltpu.VMEM((2, width, hidden // 2), low),
        pltpu.VMEM((hidden, width), low),
        pltpu.VMEM((4, width, width), low),
        pltpu.VMEM((slots, width), low),
        pltpu.VMEM((rows, width), full),
        pltpu.VMEM((rows, width), full),
        pltpu.VMEM((rows, width), low),
        pltpu.VMEM((rows, 3 * width), low),
        pltpu.VMEM((8, hidden), full),
        pltpu.VMEM((2, shard, q_dec), full),
        pltpu.VMEM((2, 2, shard, q_up), full),
        pltpu.VMEM((2, shard, width), full),
        pltpu.VMEM((2, shard // 2, q_dec), full),
        pltpu.VMEM((2, 2, shard // 2, q_up), full),
        pltpu.VMEM((2, shard // 2, width), full),
        pltpu.VMEM((2 * (3 + steps) + 1, box_rows, 128), full),
        pltpu.SemaphoreType.DMA((copies,)),
        pltpu.SemaphoreType.DMA((copies,)),
        pltpu.SemaphoreType.DMA((devices,)),
        pltpu.SemaphoreType.DMA((devices,)),
        pltpu.SemaphoreType.DMA((2, 4)),
        pltpu.SemaphoreType.DMA((16,)),
    ]
    shapes = (
        ((width // devices, dec_width), full),
        ((width // devices, hidden), full),
        ((width // devices, 4 * width), full),
        ((hidden // devices, width), full),
        ((args[19].shape[1], 2 * width), full),
        ((1, 2 * width), full),
        ((box_rows, 128), full),
        ((8, up_size + 4 * gen_width), full),
        ((up_size // devices, gen_width), full),
        ((args[24].shape[0] + gen_width + 8, 8), full),
        ((8, up_size), full),
        ((8, width), full),
        ((rows, width), low),
        (args[0].shape, low),
    )
    spots = [ANY, ANY, VMEM, VMEM] + [ANY] * 13 + [VMEM] * 8
    return pl.pallas_call(
        partial(backward_kernel, planes, steps, sizes),
        out_shape=tuple(jax.ShapeDtypeStruct(shape, dtype) for shape, dtype in shapes),
        in_specs=spots,
        out_specs=[VMEM] * 12 + [ANY] * 2,
        scratch_shapes=scratch,
        compiler_params=pltpu.CompilerParams(
            collective_id=2, has_side_effects=True, vmem_limit_bytes=125 * 2**19
        ),
    )(*args)


CHUNK = 896
TRADE_PARTS = 1


def gen_layer(
    seq, qkv, out, out_bias, gain1, shift1, up, up_bias, down, down_bias, gain2, shift2, length
):
    width = seq.shape[1]
    size = width // GHEADS

    def times(left, right):
        return jnp.dot(left, right, precision=HIGH, preferred_element_type=jnp.float32)

    joint = times(seq, qkv)
    query, key, value = [joint[:, i * width : (i + 1) * width] for i in range(3)]
    lane = lax.broadcasted_iota(jnp.int32, (1, width), 1)
    spot = lax.broadcasted_iota(jnp.int32, (1, seq.shape[0]), 1)
    context = jnp.zeros_like(seq)
    for h in range(GHEADS):
        mine = (lax.div(lane, size) == h).astype(jnp.float32)
        scores = lax.dot_general(
            query * mine,
            key,
            (((1,), (1,)), ((), ())),
            precision=HIGH,
            preferred_element_type=jnp.float32,
        ) * (1.0 / math.sqrt(size))
        scores = jnp.where(spot < length, scores, -1e30)
        peak = lax.stop_gradient(jnp.max(scores, axis=-1, keepdims=True))
        raised = jnp.exp(scores - peak)
        probs = raised / jnp.sum(raised, axis=-1, keepdims=True)
        context = context + times(probs, value * mine)
    mixed = norm_rows(seq + times(context, out) + out_bias, gain1, shift1)
    inner = times(mixed, up) + up_bias
    hidden = 0.5 * inner * (1.0 + lax.erf(inner * math.sqrt(0.5)))
    return norm_rows(mixed + times(hidden, down) + down_bias, gain2, shift2)


def gen_seq_of(gen_rows, wave_code, up_size):
    width = gen_rows.shape[0]
    full = jnp.float32
    tokens = gen_rows[:, pl.ds(up_size + 4 * width, width)].astype(full).T
    last = gen_rows[:, pl.ds(gen_rows.shape[1] - width, width)].astype(full).T
    return jnp.concatenate([tokens, wave_code, last[:8]], axis=0)


def gen_parts(gen_rows, gen_down, gen_vec, wave_code, up_size):
    width = gen_rows.shape[0]
    full = jnp.float32
    at = up_size
    up = gen_rows[:, pl.ds(0, up_size)].astype(full)
    qkv = gen_rows[:, pl.ds(at, 3 * width)].astype(full)
    out = gen_rows[:, pl.ds(at + 3 * width, width)].astype(full)
    seq = gen_seq_of(gen_rows, wave_code, up_size)
    vec = [gen_vec[pl.ds(i, 1), pl.ds(0, width)] for i in range(6)]
    up_bias = gen_vec[pl.ds(6, 1), :]
    down = gen_down[...].astype(full)
    return (seq, qkv, out, vec[0], vec[1], vec[2], up, up_bias, down, vec[3], vec[4], vec[5])


def join_lanes(parts, size):
    owners = parts.shape[0]
    shape = (128, owners * size)
    lane = lax.broadcasted_iota(jnp.int32, shape, 0)
    column = lax.broadcasted_iota(jnp.int32, shape, 1)
    spread = dot_nn(parts, (lax.rem(column, size) == lane).astype(parts.dtype))
    shape = (owners, owners * size)
    row = lax.broadcasted_iota(jnp.int32, shape, 0)
    column = lax.broadcasted_iota(jnp.int32, shape, 1)
    return jnp.sum(
        jnp.where(lax.div(column, size) == row, spread, 0.0), axis=0, keepdims=True
    )


def prepare_kernel(planes, sizes, *refs):
    (rows, width, hidden, dec_width, chips, up_size, patches) = sizes
    devices = planes * 8
    (
        qkv, up, out, dec, down, weight, weight_bias, pixels, sensor, waves, visible, places,
        wave_code, gen_up, gen_qkv, gen_out, bias_weight, gen_tokens, gen_low, cotangent, order,
    ) = refs[:21]
    thin = refs[21:36]
    (
        wide_out, down_out, table_out, slots_out, returned, normed_out, joint_out, probs_out,
        context_out, middle_out, normed2_out, activ_out, slope_out, ending_out, start_out, ordered,
        gen_rows, gen_down, gen_vec, vecs, feature_out, source_out,
    ) = refs[36:58]
    (
        g_rows, g_tail, table, slots, wide, fresh, joined, rows32, tail32, s_rows, s_tail, w_qkv,
        w_out, w_up, w_down, w_dec, normed, joint, probs, context, middle, normed2, activ, slope,
        ending, start, total, send, recv, trade_send, trade_recv, local, load_sem, keep_sem,
    ) = refs[58:]
    net = Net(planes)
    trade = Trade(cotangent, returned, trade_send, trade_recv, load_sem.at[5])
    trade.greet()
    sent = [0]

    def trade_more(count=1):
        for _ in range(count):
            if sent[0] < TRADE_PARTS:
                trade.begin(sent[0], TRADE_PARTS)
                sent[0] += 1

    seen = rows // chips
    loads, stashed = [], []
    spans = ((0, 3 * width), (3 * width + hidden, width), (3 * width, hidden))
    spans += ((4 * width + hidden, dec_width),)
    for (at, size), dst in zip(spans, (w_qkv, w_out, w_up, w_dec)):
        loads.append((wide_out.at[:, pl.ds(at, size)], dst))
    loads.append((down_out, w_down))
    loads = [
        pltpu.make_async_copy(src, dst, load_sem.at[i]) for i, (src, dst) in enumerate(loads)
    ]

    def stash(src, dst):
        copy = pltpu.make_async_copy(src, dst, keep_sem.at[len(stashed)])
        copy.start()
        stashed.append(copy)

    wires = Wires(send, recv)
    me = net.chip(0) * 2 + net.c
    low = jnp.bfloat16
    copies = []

    def keep(src, dst):
        copy = pltpu.make_async_copy(src, dst, local.at[len(copies)])
        copy.start()
        copies.append(copy)

    small = gen_up.shape[0]
    gen_width = gen_out.shape[1]
    turned = gen_tokens[...].astype(jnp.float32)
    turned = jnp.concatenate(
        [turned, jnp.zeros((small, 2 * gen_width - turned.shape[1]), jnp.float32)], axis=1
    )
    line = jnp.concatenate(
        [item[...].astype(jnp.float32) for item in (gen_up, gen_qkv, gen_out)]
        + [turned[:, :gen_width], bias_weight[...].astype(jnp.float32), turned[:, gen_width:]],
        axis=1,
    )
    for q in range(16 // small):
        rows32[pl.ds(q * small, small), :] = line[:, q * CHUNK : (q + 1) * CHUNK]
    s_rows[...] = rows32[...].astype(low)
    tail32[...] = jnp.zeros_like(tail32)
    for i, item in enumerate(thin):
        tail32[pl.ds(i, 1), pl.ds(0, item.shape[1])] = item[...].astype(jnp.float32)
    s_tail[pl.ds(0, gen_low.shape[0]), :] = gen_low[...]
    s_tail[pl.ds(gen_low.shape[0], 16), :] = tail32[...].astype(low)
    r_size, r_cols = s_rows.shape
    r_cut = (r_cols // 256) * 128 + 128
    r_span = lambda h: pl.ds(r_cut * h, r_cols - r_cut if h else r_cut)
    t_size = s_tail.shape[0]
    t_cut = (t_size // 32) * 16 + 16
    t_span = lambda h: pl.ds(t_cut * h, t_size - t_cut if h else t_cut)
    smalls = [
        Gather(
            net,
            wires,
            lambda h: s_rows.at[:, r_span(h)],
            lambda chip, h: g_rows.at[tile_rows(chip * 2 + net.c, r_size), r_span(h)],
        ),
        Gather(
            net,
            wires,
            lambda h: s_tail.at[t_span(h)],
            lambda chip, h: g_tail.at[chip * 2 + net.c, t_span(h)],
        ),
    ]
    for item in smalls:
        item.begin_z()
        item.spread(0)
    keep(s_rows, g_rows.at[tile_rows(me, r_size)])
    keep(s_tail, g_tail.at[me])

    at = 0
    for item in (qkv, up, out, dec):
        wide[:, pl.ds(at, item.shape[1])] = item[...]
        at += item.shape[1]
    w_cols = at // 2
    quarter = w_cols // 2
    shard = wide.shape[0]
    mine = pl.ds(pl.multiple_of(net.c * w_cols, 128), w_cols)
    theirs = pl.ds(pl.multiple_of((1 - net.c) * w_cols, 128), w_cols)
    pair = wires.push(wide.at[:, theirs], fresh, net.sib)
    d_rows = down.shape[0]
    d_half = d_rows // 2
    d_own = lambda h: down.at[pl.ds(h * d_half, d_half)]
    d_piece = lambda chip, h: down_out.at[
        pl.ds(pl.multiple_of((chip * 2 + net.c) * d_rows + h * d_half, 16), d_half)
    ]
    w_own = lambda h: joined.at[:, pl.ds(h * quarter, quarter)]
    w_piece = lambda chip, h: wide_out.at[
        pl.ds(pl.multiple_of(chip * 2 * shard, 16), 2 * shard),
        pl.ds(pl.multiple_of((net.c * 2 + h) * quarter, 128), quarter),
    ]
    t_lines = table.shape[0] // devices // 2
    t_piece = lambda chip, h: table.at[tile_rows((chip * 2 + net.c) * 2 + h, t_lines)]
    t_own = lambda h: table.at[tile_rows(me * 2 + h, t_lines)]
    d_gather = Gather(net, wires, d_own, d_piece)
    w_gather = Gather(net, wires, w_own, w_piece)
    t_gather = Gather(net, wires, t_own, t_piece)
    d_gather.begin_z()
    for item in smalls:
        item.relay(0)
    pair.wait_recv()
    own32 = wide[:, mine].astype(jnp.float32)
    sib32 = fresh[...].astype(jnp.float32)
    first = net.c == 0
    joined[...] = jnp.concatenate(
        [jnp.where(first, own32, sib32), jnp.where(first, sib32, own32)], axis=0
    ).astype(low)
    for k in range(1, planes):
        for item in smalls:
            item.spread(k)
        for item in smalls:
            item.relay(k)
    w_gather.begin_z()
    for h in range(2):
        keep(w_own(h), w_piece(net.chip(0), h))
        keep(d_own(h), d_piece(net.chip(0), h))
    for k in range(planes):
        for item in smalls:
            item.close(k)
    w_gather.spread(0)
    d_gather.spread(0)
    steps = [partial(w_gather.relay, 0)]
    for k in range(1, planes):
        steps += [partial(w_gather.spread, k), partial(w_gather.relay, k)]
    steps.append(partial(d_gather.relay, 0))
    for k in range(1, planes):
        steps += [partial(d_gather.spread, k), partial(d_gather.relay, k)]
        steps.append(partial(w_gather.close, k - 1))
    steps.append(partial(w_gather.close, planes - 1))
    steps += [partial(d_gather.close, k) for k in range(planes)]

    def pump(count):
        for _ in range(min(count, len(steps))):
            steps.pop(0)()

    for item in smalls:
        item.finish()
    for copy in copies[:2]:
        copy.wait()

    lines = width // devices
    groups = r_size // small
    shape = (gen_rows.shape[0], devices * r_size)
    row = lax.broadcasted_iota(jnp.int32, shape, 0)
    column = lax.broadcasted_iota(jnp.int32, shape, 1)
    for q in range(groups):
        source = lax.div(row, small) * r_size + q * small + lax.rem(row, small)
        gen_rows[:, pl.ds(q * r_cols, r_cols)] = dot_nn(
            (column == source).astype(low), g_rows[...]
        ).astype(low)
    gen_down[...] = g_tail[:, pl.ds(0, t_size - 16), :].reshape(gen_down.shape)
    tail = g_tail[:, pl.ds(t_size - 16, 16), :].reshape(devices * 16, 128)
    shape = (devices * 16, devices * 16)
    row = lax.broadcasted_iota(jnp.int32, shape, 0)
    column = lax.broadcasted_iota(jnp.int32, shape, 1)
    source = lax.rem(row, devices) * 16 + lax.div(row, devices)
    tail = dot_nn((column == source).astype(low), tail).astype(low)
    part = lambda i: tail[i * devices : (i + 1) * devices]
    vecs[...] = jnp.zeros_like(vecs)
    for i in range(5):
        vecs[pl.ds(i, 1), pl.ds(0, width)] = join_lanes(part(i), lines)
    vecs[pl.ds(5, 1), :] = join_lanes(part(5), hidden // devices)
    for i in (6, 7):
        vecs[pl.ds(i, 1), pl.ds(0, dec_width)] = join_lanes(part(i), dec_width // devices)
    gen_vec[...] = jnp.zeros_like(gen_vec)
    for i in range(6):
        gen_vec[pl.ds(i, 1), pl.ds(0, gen_rows.shape[0])] = join_lanes(part(8 + i), small)
    gen_vec[pl.ds(6, 1), :] = join_lanes(part(14), up_size // devices)

    pump(2)
    operands = gen_parts(gen_rows, gen_down, gen_vec, wave_code[...], up_size)
    seq = operands[0]
    final = gen_layer(*operands, LAT + NWAVE + 1)
    feature = (final[LAT : LAT + NWAVE] + seq[LAT : LAT + NWAVE]).astype(low)
    feature_out[...] = feature
    source = final[LAT + NWAVE : LAT + NWAVE + 8].astype(low)
    source_out[...] = source
    own = (dot_nn(feature, weight[...]) + weight_bias[...].astype(jnp.float32).reshape(1, -1)).astype(low)
    for h in range(2):
        table[tile_rows(me * 2 + h, t_lines), :] = own[:, h * width : (h + 1) * width]
    t_gather.begin_z()
    t_gather.spread(0)
    pump(2)

    bias_at = gen_rows.shape[1] - gen_rows.shape[0] - width
    conv = dot_nn(source, gen_rows[:, pl.ds(bias_at, width)])[:1]
    t_gather.relay(0)
    grid_line = lax.broadcasted_iota(jnp.int32, (GRID, seen), 0)
    for chip in range(chips):
        patch = visible[pl.ds(chip, 1), :]
        for i, spot in enumerate((lax.div(patch, GRID), lax.rem(patch, GRID))):
            half = pl.ds(i * (width // 2), width // 2)
            picked = lax.dot_general(
                (spot == grid_line).astype(jnp.float32),
                places[...],
                (((0,), (0,)), ((), ())),
                precision=HIGH,
                preferred_element_type=jnp.float32,
            )
            start[pl.ds(chip * seen, seen), half] = (
                picked + conv[:, i * (width // 2) : (i + 1) * (width // 2)]
            )
    t_gather.spread(1)
    t_gather.relay(1)
    pump(2)
    span = 256
    bands_pix = pixels.shape[1]
    bands = waves.shape[1]
    band_of = lax.div(lax.broadcasted_iota(jnp.int32, (1, bands_pix), 1), bands_pix // bands)
    wave_lines = []
    for chip in range(chips):
        drop = jnp.zeros((1, 1), jnp.int32)
        for i, less in enumerate(BAND_DROP):
            drop = jnp.where(sensor[:, pl.ds(chip, 1)] == i, less, drop)
        wave = jnp.full((1, bands_pix), -1, jnp.int32)
        for i in range(bands):
            wave = jnp.where(band_of == i, waves[pl.ds(chip, 1), pl.ds(i, 1)], wave)
        wave_lines.append(jnp.where(band_of < bands - drop, wave, -1))

    def slot_block(i, _):
        shape = (span, bands_pix)
        line = lax.broadcasted_iota(jnp.int32, shape, 0) + i * span
        column = lax.broadcasted_iota(jnp.int32, shape, 1)
        count = slots.shape[0] // NWAVE
        same = lax.div(line, NWAVE) == lax.rem(column, count)
        for chip in range(chips):
            chosen = same & (lax.rem(line, NWAVE) == wave_lines[chip])
            slots[tile_rows(i, span), pl.ds(chip * seen, seen)] = dot_nn(
                chosen.astype(jnp.float32).astype(low), pixels[chip]
            ).astype(low)
        return 0

    blocks = slots.shape[0] // span
    lax.fori_loop(0, blocks // 2, slot_block, 0)
    for k in range(2, planes):
        t_gather.spread(k)
        t_gather.relay(k)
    pump(2)
    lax.fori_loop(blocks // 2, blocks, slot_block, 0)
    keep(slots, slots_out)
    pump(4)
    for k in range(planes):
        t_gather.close(k)
    pump(2)
    t_gather.finish()
    keep(table, table_out)
    wide_span = 512

    def embed(i, _):
        at = tile_rows(i, wide_span)
        start[...] += tdot(slots[at, :], table[at, :])
        return 0

    lax.fori_loop(0, slots.shape[0] // wide_span, embed, 0)
    stash(start, start_out)
    while len(steps) > planes:
        pump(1)

    def norm_into(src, dst, row):
        gain = vecs[pl.ds(row, 1), pl.ds(0, width)]
        shift = vecs[pl.ds(row + 1, 1), pl.ds(0, width)]

        def block(i, _):
            at = tile_rows(i, BLOCK)
            dst[at, :] = norm_rows(src[at, :], gain, shift).astype(low)
            return 0

        lax.fori_loop(0, rows // BLOCK, block, 0)

    norm_into(start, normed, 0)
    for copy in copies[2:6]:
        copy.wait()
    w_gather.finish()
    trade_more(TRADE_PARTS)
    for copy in loads[:4]:
        copy.start()
    stash(normed, normed_out)
    loads[0].wait()

    def project(i, _):
        lane = pl.ds(pl.multiple_of(i * width, 128), width)
        joint[:, lane] = dot_nn(normed[...], w_qkv[:, lane]).astype(low)
        return 0

    lax.fori_loop(0, 3, project, 0)
    pump(2)
    stash(joint, joint_out)
    pairs = width // 128
    head = width // HEADS
    scale = 1.0 / math.sqrt(head)
    odd = lax.broadcasted_iota(jnp.int32, (1, 128), 1) >= head

    def attend(n, _):
        at = tile_rows(lax.div(n, pairs), seen)
        pair = lax.rem(n, pairs)
        query, key, value = [
            joint[at, pl.ds(pl.multiple_of(pair * 128 + i * width, 128), 128)] for i in range(3)
        ]
        zero = jnp.zeros_like(query)
        parts = []
        for h in range(2):
            mine = odd if h else jnp.logical_not(odd)
            scores = ndot(jnp.where(mine, query, zero), key) * scale
            raised = jnp.exp(scores - jnp.max(scores, axis=-1, keepdims=True))
            prob = (raised / jnp.sum(raised, axis=-1, keepdims=True)).astype(low)
            probs[2 * n + h] = prob
            parts.append(dot_nn(prob, value))
        lane = pl.ds(pl.multiple_of(pair * 128, 128), 128)
        context[at, lane] = jnp.where(odd, parts[1], parts[0]).astype(low)
        return 0

    for i in range(0, chips * pairs, 3):
        lax.fori_loop(i, i + 3, attend, 0)
        pump(1)
    stash(probs, probs_out)
    stash(context, context_out)
    loads[1].wait()
    middle[...] = start[...] + dot_nn(context[...], w_out[...])
    stash(middle, middle_out)
    norm_into(middle, normed2, 2)
    stash(normed2, normed2_out)
    total[...] = middle[...] + vecs[pl.ds(4, 1), pl.ds(0, width)]
    pump(len(steps))
    d_gather.finish()
    loads[4].start()
    loads[2].wait()
    loads[4].wait()

    def feed(t, _):
        at = tile_rows(t, FT)
        upper = dot_nn(normed2[...], w_up[:, at]) + vecs[pl.ds(5, 1), at]
        bell = 0.5 * (1.0 + lax.erf(upper * math.sqrt(0.5)))
        active = (upper * bell).astype(low)
        activ[:, at] = active
        tilt = upper * jnp.exp(-0.5 * upper * upper) * (1.0 / math.sqrt(2.0 * math.pi))
        slope[:, at] = (bell + tilt).astype(low)
        total[...] += dot_nn(active, w_down[at, :])
        return 0

    lax.fori_loop(0, hidden // FT, feed, 0)
    stash(activ, activ_out)
    stash(slope, slope_out)
    ending[...] = total[...].astype(low)
    stash(ending, ending_out)
    loads[3].wait()
    decoded = dot_nn(ending[...], w_dec[...]) + vecs[pl.ds(6, 1), pl.ds(0, dec_width)]
    total[:, pl.ds(0, dec_width)] = decoded
    mask = vecs[pl.ds(7, 1), pl.ds(0, dec_width)]
    blocks, _, lines, _ = ordered.shape
    column = order_column(order)
    for chip in range(chips):
        at = pl.ds(chip * seen, seen)
        chosen = (column == visible[pl.ds(chip, 1), :]).astype(jnp.float32)
        found = jnp.sum(chosen, axis=1, keepdims=True) > 0.0
        placed = dot_nn(chosen.astype(low), total[at, pl.ds(0, dec_width)].astype(low))
        placed = jnp.where(found, placed, mask).astype(low)
        ordered[:, chip] = placed.reshape(blocks, lines, dec_width)
    for copy in copies[6:] + stashed:
        copy.wait()
    trade_more(TRADE_PARTS)
    trade.finish()
    wires.drain()


def prepare(planes, sizes, *args):
    (rows, width, hidden, dec_width, chips, up_size, patches) = sizes
    seen = rows // chips
    heads = chips * HEADS
    devices = planes * 8
    low, full = jnp.bfloat16, jnp.float32
    qkv, up, out, dec, down = args[:5]
    gen_width = args[12].shape[1]
    tail = args[18].shape[0] + 16
    cols = qkv.shape[1] + up.shape[1] + out.shape[1] + dec.shape[1]
    shard = qkv.shape[0]
    slots = args[5].shape[1] // width * devices * NWAVE
    copies = 5 * gather_copies(planes) + 1
    shapes = (
        ((width, cols), low),
        ((hidden, width), low),
        ((slots, width), low),
        ((slots, rows), low),
        (args[19].shape, low),
        ((rows, width), low),
        ((rows, 3 * width), low),
        ((heads, seen, seen), low),
        ((rows, width), low),
        ((rows, width), full),
        ((rows, width), low),
        ((rows, hidden), low),
        ((rows, hidden), low),
        ((rows, width), low),
        ((rows, width), full),
        ((devices, chips, patches // devices, dec_width), low),
        ((gen_width, CHUNK * 16 * devices // gen_width), low),
        ((up_size, gen_width), low),
        ((8, up_size), full),
        ((8, hidden), full),
        ((NWAVE, gen_width), low),
        ((8, gen_width), low),
    )
    return pl.pallas_call(
        partial(prepare_kernel, planes, sizes),
        out_shape=tuple(jax.ShapeDtypeStruct(shape, dtype) for shape, dtype in shapes),
        in_specs=[VMEM] * 19 + [ANY] + [VMEM] * (len(args) - 20),
        out_specs=[ANY] * 15 + [VMEM] * 7,
        scratch_shapes=[
            pltpu.VMEM((devices * 16, CHUNK), low),
            pltpu.VMEM((devices, tail, 128), low),
            pltpu.VMEM((slots, width), low),
            pltpu.VMEM((slots, rows), low),
            pltpu.VMEM((shard, cols), low),
            pltpu.VMEM((shard, cols // 2), low),
            pltpu.VMEM((2 * shard, cols // 2), low),
            pltpu.VMEM((16, CHUNK), full),
            pltpu.VMEM((16, 128), full),
            pltpu.VMEM((16, CHUNK), low),
            pltpu.VMEM((tail, 128), low),
            pltpu.VMEM((width, 3 * width), low),
            pltpu.VMEM((width, width), low),
            pltpu.VMEM((width, hidden), low),
            pltpu.VMEM((hidden, width), low),
            pltpu.VMEM((width, dec_width), low),
        ]
        + [pltpu.VMEM(shape, dtype) for shape, dtype in shapes[5:15]]
        + [
            pltpu.VMEM((rows, width), full),
            pltpu.SemaphoreType.DMA((copies,)),
            pltpu.SemaphoreType.DMA((copies,)),
            pltpu.SemaphoreType.DMA((devices,)),
            pltpu.SemaphoreType.DMA((devices,)),
            pltpu.SemaphoreType.DMA((8,)),
            pltpu.SemaphoreType.DMA((6,)),
            pltpu.SemaphoreType.DMA((10,)),
        ],
        compiler_params=pltpu.CompilerParams(
            collective_id=0, has_side_effects=True, vmem_limit_bytes=60 * 2**20
        ),
    )(*args)


def gen_back(
    gen_rows, gen_down, gen_vec, wave_code, length, grad_feature, grad_source, sums, put_up, put_down
):
    up_size, width = gen_down.shape
    size = width // GHEADS
    scale = 1.0 / math.sqrt(size)
    total = lambda value: jnp.sum(value, axis=0, keepdims=True)
    chunk = up_size // 4

    def dot(left, right, dims):
        return lax.dot_general(
            left.astype(jnp.bfloat16),
            right.astype(jnp.bfloat16),
            (dims, ((), ())),
            preferred_element_type=jnp.float32,
        )

    nn = lambda left, right: dot(left, right, ((1,), (0,)))
    nt = lambda left, right: dot(left, right, ((1,), (1,)))
    tn = lambda left, right: dot(left, right, ((0,), (0,)))
    seq = gen_seq_of(gen_rows, wave_code, up_size)
    full = jnp.float32
    qkv = gen_rows[:, pl.ds(up_size, 3 * width)].astype(full)
    out = gen_rows[:, pl.ds(up_size + 3 * width, width)].astype(full)
    out_bias, gain1, shift1, down_bias, gain2, _ = [
        gen_vec[pl.ds(i, 1), pl.ds(0, width)] for i in range(6)
    ]
    joint = nn(seq, qkv)
    query, key, value = [joint[:, i * width : (i + 1) * width] for i in range(3)]
    lane = lax.broadcasted_iota(jnp.int32, (1, width), 1)
    spot = lax.broadcasted_iota(jnp.int32, (1, seq.shape[0]), 1)
    masks = [(lax.div(lane, size) == h).astype(full) for h in range(GHEADS)]
    probs = []
    context = jnp.zeros_like(seq)
    for mine in masks:
        scores = jnp.where(spot < length, nt(query * mine, key) * scale, -1e30)
        raised = jnp.exp(scores - jnp.max(scores, axis=-1, keepdims=True))
        probs.append(raised / jnp.sum(raised, axis=-1, keepdims=True))
        context = context + nn(probs[-1], value * mine)
    first = seq + nn(context, out) + out_bias
    mixed = norm_rows(first, gain1, shift1)

    def piece(i):
        at = pl.ds(pl.multiple_of(i * chunk, chunk), chunk)
        up = gen_rows[:, at].astype(full)
        down = gen_down[at, :].astype(full)
        inner = nn(mixed, up) + gen_vec[pl.ds(6, 1), at]
        return up, down, inner, 0.5 * (1.0 + lax.erf(inner * math.sqrt(0.5)))

    def ahead(i, so_far):
        _, down, inner, bell = piece(i)
        return so_far + nn(inner * bell, down)

    second = lax.fori_loop(0, 4, ahead, mixed + down_bias)
    rest = seq.shape[0] - LAT - NWAVE
    zeros = jnp.zeros((LAT, width), full)
    grad = jnp.concatenate([zeros, grad_feature, grad_source], axis=0)
    through, terms = norm_back(grad, second, gain2)
    g_gain2, g_shift2, g_down_bias = total(terms), total(grad), total(through)

    def behind(i, so_far):
        up, down, inner, bell = piece(i)
        put_down(i, tn(inner * bell, through))
        slope = bell + inner * jnp.exp(-0.5 * inner * inner) * (1.0 / math.sqrt(2.0 * math.pi))
        g_inner = nt(through, down) * slope
        put_up(i, tn(mixed, g_inner))
        sums[pl.ds(6, 1), pl.ds(pl.multiple_of(i * chunk, chunk), chunk)] = total(g_inner)
        return so_far + nt(g_inner, up)

    g_mixed = lax.fori_loop(0, 4, behind, through)
    through, terms = norm_back(g_mixed, first, gain1)
    g_gain1, g_shift1, g_out_bias = total(terms), total(g_mixed), total(through)
    g_out = tn(context, through)
    g_context = nt(through, out)
    g_query = g_key = g_value = jnp.zeros_like(seq)
    for mine, prob in zip(masks, probs):
        g_head = g_context * mine
        g_prob = nt(g_head, value)
        g_value = g_value + tn(prob, g_head)
        g_score = prob * (g_prob - jnp.sum(prob * g_prob, axis=-1, keepdims=True)) * scale
        g_query = g_query + nn(g_score, key * mine)
        g_key = g_key + tn(g_score, query * mine)
    g_joint = jnp.concatenate([g_query, g_key, g_value], axis=1)
    direct = jnp.concatenate([zeros, grad_feature, jnp.zeros((rest, width), full)], axis=0)
    g_seq = through + nt(g_joint, qkv) + direct
    thin = (g_out_bias, g_gain1, g_shift1, g_down_bias, g_gain2, g_shift2)
    return g_seq, tn(seq, g_joint), g_out, thin


def hand_out_kernel(planes, sizes, *refs):
    (width, hidden, dec_width, small) = sizes
    devices = planes * 8
    (
        s_dec, s_up, s_oq, s_down, kernels, kernel_sums, lines, g_wide, g_tall, g_seq, g_lines,
        g_bias,
    ) = refs[40:52]
    copies = [
        pltpu.make_async_copy(refs[i], refs[40 + i], refs[52].at[i]) for i in range(12)
    ]
    for copy in copies:
        copy.start()
    for copy in copies:
        copy.wait()
    outs = refs[12:40]
    (
        pre_gain, pre_shift, qkv, out, mid_gain, mid_shift, up, up_bias, down, down_bias, dec,
        dec_bias, mask, tokens, gen_qkv, gen_out, gen_out_bias, gain1, shift1, gen_up,
        gen_up_bias, gen_down, gen_down_bias, gain2, shift2, kernel_weight, kernel_bias, bias,
    ) = outs
    me = lax.axis_index("dp") * 4 + lax.axis_index("fsdp")
    qkv[...] = s_oq[:, pl.ds(width, 3 * width)]
    out[...] = s_oq[:, pl.ds(0, width)]
    up[...] = s_up[...]
    down[...] = s_down[...]
    dec[...] = s_dec[...]
    kernel_weight[...] = kernels[...]
    for i in range(kernel_bias.shape[0]):
        kernel_bias[pl.ds(i, 1), :] = kernel_sums[:, i * 128 : (i + 1) * 128]
    gen_down[...] = g_tall[...]
    up_size = gen_up.shape[1]
    gen_width = gen_out.shape[1]
    gen_up[...] = g_wide[pl.ds(0, small), pl.ds(0, up_size)]
    gen_qkv[...] = g_wide[pl.ds(0, small), pl.ds(up_size, 3 * gen_width)]
    gen_out[...] = g_wide[pl.ds(0, small), pl.ds(up_size + 3 * gen_width, gen_width)]
    tokens[pl.ds(0, LAT), :] = g_seq[pl.ds(0, LAT), pl.ds(0, small)]
    tokens[pl.ds(LAT, 1), :] = g_seq[pl.ds(LAT + NWAVE, 1), pl.ds(0, small)]
    bias[...] = g_bias[pl.ds(0, small), :]

    def own(values, part):
        shape = (values.shape[1], 128)
        row = lax.broadcasted_iota(jnp.int32, shape, 0)
        lane = lax.broadcasted_iota(jnp.int32, shape, 1)
        pick = ((row == me * part + lane) & (lane < part)).astype(jnp.float32)
        return jnp.dot(values, pick, precision=HIGH, preferred_element_type=jnp.float32)

    at = NWAVE + width // 128

    def row_of(size):
        nonlocal at
        count = size // 128
        row = jnp.concatenate([lines[pl.ds(at + i, 1), :] for i in range(count)], axis=1)
        at += count
        return row

    def rows_of(sizes_):
        rows = [row_of(size) for size in sizes_]
        rows.append(jnp.zeros((8 - len(rows), rows[0].shape[1]), jnp.float32))
        return jnp.concatenate(rows, axis=0)

    def split(values, part, refs_):
        mine = own(values, part)
        for i, ref in enumerate(refs_):
            ref[...] = mine[i : i + 1, :part]

    split(rows_of((width,) * 5), width // devices, (pre_gain, pre_shift, mid_gain, mid_shift, down_bias))
    part = hidden // devices
    first = lax.div(me * part, 128)
    pair = jnp.concatenate([lines[pl.ds(at + first + i, 1), :] for i in range(2)], axis=1)
    row = lax.broadcasted_iota(jnp.int32, (256, 128), 0)
    lane = lax.broadcasted_iota(jnp.int32, (256, 128), 1)
    pick = ((row == me * part - first * 128 + lane) & (lane < part)).astype(jnp.float32)
    pair = jnp.broadcast_to(pair, (8, 256))
    up_bias[...] = jnp.dot(pair, pick, precision=HIGH, preferred_element_type=jnp.float32)[
        :1, :part
    ]
    at += hidden // 128
    split(rows_of((dec_width,) * 2), dec_width // devices, (dec_bias, mask))
    split(
        g_lines[:, pl.ds(0, gen_width)],
        small,
        (gen_out_bias, gain1, shift1, gen_down_bias, gain2, shift2),
    )
    split(
        jnp.concatenate(
            [g_lines[pl.ds(6, 1), :], jnp.zeros((7, up_size), jnp.float32)], axis=0
        ),
        up_size // devices,
        (gen_up_bias,),
    )


def hand_out(planes, sizes, *args):
    (width, hidden, dec_width, small) = sizes
    devices = planes * 8
    up_size = args[10].shape[1]
    gen_width = args[8].shape[1]
    wide, thin = width // devices, (1, width // devices)
    row = lambda size: (1, size // devices)
    shapes = (
        thin, thin, (wide, 3 * width), (wide, width), thin, thin, (wide, hidden), row(hidden),
        (hidden // devices, width), thin, (wide, dec_width), row(dec_width), row(dec_width),
        (LAT + 1, small), (small, 3 * gen_width), (small, gen_width), (1, small), (1, small),
        (1, small), (small, up_size), row(up_size), (up_size // devices, gen_width), (1, small),
        (1, small), (1, small), args[4].shape, (args[5].shape[1] // 128, 128), (small, width),
    )
    return pl.pallas_call(
        partial(hand_out_kernel, planes, sizes),
        out_shape=tuple(jax.ShapeDtypeStruct(shape, jnp.float32) for shape in shapes),
        in_specs=[ANY] * 12,
        out_specs=[VMEM] * 28,
        scratch_shapes=[pltpu.VMEM(item.shape, item.dtype) for item in args]
        + [pltpu.SemaphoreType.DMA((12,))],
        compiler_params=pltpu.CompilerParams(vmem_limit_bytes=60 * 2**20),
    )(*args)


def on_device_plain(
    pixels,
    sensor,
    band_wave,
    visible,
    block_order,
    pre_gain,
    pre_shift,
    qkv_weight,
    out_weight,
    mid_gain,
    mid_shift,
    up_weight,
    up_bias,
    down_weight,
    down_bias,
    dec_weight,
    dec_bias,
    mask_token,
    gen_tokens,
    gen_qkv,
    gen_out,
    gen_out_bias,
    gen_gain1,
    gen_shift1,
    gen_up,
    gen_up_bias,
    gen_down,
    gen_down_bias,
    gen_gain2,
    gen_shift2,
    kernel_weight,
    kernel_bias,
    bias_weight,
    cotangent,
):
    fetched = (
        lax.all_gather(pre_gain, AXES, axis=0, tiled=True),
        lax.all_gather(pre_shift, AXES, axis=0, tiled=True),
        lax.all_gather(qkv_weight, AXES, axis=0, tiled=True),
        lax.all_gather(out_weight, AXES, axis=0, tiled=True),
        lax.all_gather(mid_gain, AXES, axis=0, tiled=True),
        lax.all_gather(mid_shift, AXES, axis=0, tiled=True),
        lax.all_gather(up_weight, AXES, axis=0, tiled=True),
        lax.all_gather(up_bias, AXES, axis=0, tiled=True),
        lax.all_gather(down_weight, AXES, axis=0, tiled=True),
        lax.all_gather(down_bias, AXES, axis=0, tiled=True),
        lax.all_gather(dec_weight, AXES, axis=0, tiled=True),
        lax.all_gather(dec_bias, AXES, axis=0, tiled=True),
        lax.all_gather(mask_token, AXES, axis=0, tiled=True),
        lax.all_gather(gen_tokens, AXES, axis=1, tiled=True),
        lax.all_gather(gen_qkv, AXES, axis=0, tiled=True),
        lax.all_gather(gen_out, AXES, axis=0, tiled=True),
        lax.all_gather(gen_out_bias, AXES, axis=0, tiled=True),
        lax.all_gather(gen_gain1, AXES, axis=0, tiled=True),
        lax.all_gather(gen_shift1, AXES, axis=0, tiled=True),
        lax.all_gather(gen_up, AXES, axis=0, tiled=True),
        lax.all_gather(gen_up_bias, AXES, axis=0, tiled=True),
        lax.all_gather(gen_down, AXES, axis=0, tiled=True),
        lax.all_gather(gen_down_bias, AXES, axis=0, tiled=True),
        lax.all_gather(gen_gain2, AXES, axis=0, tiled=True),
        lax.all_gather(gen_shift2, AXES, axis=0, tiled=True),
        lax.all_gather(kernel_weight, AXES, axis=1, tiled=True),
        lax.all_gather(kernel_bias, AXES, axis=0, tiled=True),
        lax.all_gather(bias_weight, AXES, axis=0, tiled=True),
    )
    full_kernel = fetched[25]
    full_kernel_bias = fetched[26]
    full_bias_weight = fetched[27]
    (
        full_pre_gain,
        full_pre_shift,
        full_qkv,
        full_out,
        full_mid_gain,
        full_mid_shift,
        full_up,
        full_up_bias,
        full_down,
        full_down_bias,
        full_dec,
        full_dec_bias,
        full_mask,
    ) = fetched[:13]
    core32 = tuple((item.astype(jnp.float32) for item in fetched[13:25]))
    chips, seen, bands, pix = pixels.shape
    width = full_qkv.shape[0]
    head_dim = width // HEADS
    scale = 1.0 / math.sqrt(head_dim)
    dec_width = full_dec.shape[1]
    rows = chips * seen
    wave_code = lax.optimization_barrier(
        sincos(jnp.arange(NWAVE, dtype=jnp.float32), WD // 2).astype(jnp.bfloat16)
    ).astype(jnp.float32)
    (feature, source), core_back = jax.vjp(partial(gen_core, wave_code), *core32)
    feature_low = feature.astype(jnp.bfloat16)
    source_low = source.astype(jnp.bfloat16)
    conv_bias = jnp.dot(source_low[None, :], full_bias_weight, preferred_element_type=jnp.float32)[
        0
    ]
    kernels = (
        jnp.dot(feature_low, full_kernel, preferred_element_type=jnp.float32)
        + full_kernel_bias.astype(jnp.float32)[None, :]
    ).astype(jnp.bfloat16)
    valid = band_valid(sensor, bands)
    onehot = (band_wave[:, :, None] == jnp.arange(NWAVE, dtype=jnp.int32)[None, None, :]).astype(
        jnp.float32
    )
    place = place_code(visible, width)
    band_kernels = jnp.einsum(
        "cbw,wk->cbk", onehot.astype(jnp.bfloat16), kernels, preferred_element_type=jnp.float32
    ).astype(jnp.bfloat16)
    band_kernels = band_kernels.reshape(chips, bands, pix, width)
    masked = pixels * valid.astype(jnp.bfloat16)[:, None, :, None]
    embedded = jnp.einsum(
        "cvbp,cbpd->cvd", masked, band_kernels, preferred_element_type=jnp.float32
    )
    start = (embedded + conv_bias + place).reshape(rows, width)
    pre_gain32 = full_pre_gain.astype(jnp.float32)
    pre_shift32 = full_pre_shift.astype(jnp.float32)
    normed = norm_rows(start, pre_gain32, pre_shift32).astype(jnp.bfloat16)
    joint = jnp.dot(normed, full_qkv, preferred_element_type=jnp.float32).astype(jnp.bfloat16)
    joint = joint.reshape(chips, seen, 3, HEADS, head_dim)
    queries = joint[:, :, 0]
    keys = joint[:, :, 1]
    values = joint[:, :, 2]
    scores = (
        jnp.einsum("cqhe,ckhe->chqk", queries, keys, preferred_element_type=jnp.float32) * scale
    )
    peak = jnp.max(scores, axis=-1, keepdims=True)
    expd = jnp.exp(scores - peak)
    total = jnp.sum(expd, axis=-1, keepdims=True)
    probs = (expd / total).astype(jnp.bfloat16)
    log_total = peak + jnp.log(total)
    context = jnp.einsum("chqk,ckhe->cqhe", probs, values, preferred_element_type=jnp.float32)
    context = context.astype(jnp.bfloat16).reshape(rows, width)
    attended = jnp.dot(context, full_out, preferred_element_type=jnp.float32)
    middle = start + attended
    mid_gain32 = full_mid_gain.astype(jnp.float32)
    mid_shift32 = full_mid_shift.astype(jnp.float32)
    normed2 = norm_rows(middle, mid_gain32, mid_shift32).astype(jnp.bfloat16)
    upper = jnp.dot(normed2, full_up, preferred_element_type=jnp.float32) + full_up_bias.astype(
        jnp.float32
    )
    activ = exact_gelu(upper).astype(jnp.bfloat16)
    branch = jnp.dot(activ, full_down, preferred_element_type=jnp.float32) + full_down_bias.astype(
        jnp.float32
    )
    ending = (middle + branch).astype(jnp.bfloat16)
    decoded = jnp.dot(ending, full_dec, preferred_element_type=jnp.float32) + full_dec_bias.astype(
        jnp.float32
    )
    decoded = decoded.astype(jnp.bfloat16).reshape(chips, seen, dec_width)
    chip_ids = jnp.arange(chips, dtype=jnp.int32)[:, None]
    canvas = jnp.broadcast_to(full_mask, (chips, PATCH, dec_width))
    canvas = canvas.at[chip_ids, visible].set(decoded)
    ordered = jnp.take(canvas, block_order, axis=1)
    decoder_in = lax.all_to_all(ordered, AXES, split_axis=1, concat_axis=0, tiled=True)
    returned = lax.all_to_all(cotangent, AXES, split_axis=0, concat_axis=1, tiled=True)
    (
        full_pre_gain,
        full_pre_shift,
        full_qkv,
        full_out,
        full_mid_gain,
        full_mid_shift,
        full_up,
        full_up_bias,
        full_down,
        full_down_bias,
        full_dec,
        full_dec_bias,
        full_mask,
    ) = (
        lax.all_gather(pre_gain, AXES, axis=0, tiled=True),
        lax.all_gather(pre_shift, AXES, axis=0, tiled=True),
        lax.all_gather(qkv_weight, AXES, axis=0, tiled=True),
        lax.all_gather(out_weight, AXES, axis=0, tiled=True),
        lax.all_gather(mid_gain, AXES, axis=0, tiled=True),
        lax.all_gather(mid_shift, AXES, axis=0, tiled=True),
        lax.all_gather(up_weight, AXES, axis=0, tiled=True),
        lax.all_gather(up_bias, AXES, axis=0, tiled=True),
        lax.all_gather(down_weight, AXES, axis=0, tiled=True),
        lax.all_gather(down_bias, AXES, axis=0, tiled=True),
        lax.all_gather(dec_weight, AXES, axis=0, tiled=True),
        lax.all_gather(dec_bias, AXES, axis=0, tiled=True),
        lax.all_gather(mask_token, AXES, axis=0, tiled=True),
    )
    restored = jnp.zeros_like(returned).at[:, block_order].set(returned)
    seen_grad = jnp.take_along_axis(restored, visible[:, :, None], axis=1)
    grad_mask = jnp.sum(restored.astype(jnp.float32), axis=(0, 1)) - jnp.sum(
        seen_grad.astype(jnp.float32), axis=(0, 1)
    )
    grad_rows = seen_grad.reshape(rows, dec_width)
    grad_dec_weight = tdot(ending, grad_rows)
    grad_dec_bias = jnp.sum(grad_rows.astype(jnp.float32), axis=0)
    grad_ending = ndot(grad_rows, full_dec)
    grad_branch = grad_ending.astype(jnp.bfloat16)
    grad_down_bias = jnp.sum(grad_branch.astype(jnp.float32), axis=0)
    grad_down_weight = tdot(activ, grad_branch)
    grad_activ = ndot(grad_branch, full_down)
    gelu_out, gelu_back = jax.vjp(exact_gelu, upper)
    grad_upper = gelu_back(grad_activ)[0].astype(jnp.bfloat16)
    grad_up_bias = jnp.sum(grad_upper.astype(jnp.float32), axis=0)
    grad_up_weight = tdot(normed2, grad_upper)
    grad_normed2 = ndot(grad_upper, full_up)
    norm_out, norm_back = jax.vjp(norm_rows, middle, mid_gain32, mid_shift32)
    through_mid, grad_mid_gain, grad_mid_shift = norm_back(grad_normed2)
    grad_middle = grad_ending + through_mid
    grad_attended = grad_middle.astype(jnp.bfloat16)
    grad_out_weight = tdot(context, grad_attended)
    grad_context = (
        ndot(grad_attended, full_out).astype(jnp.bfloat16).reshape(chips, seen, HEADS, head_dim)
    )
    again_scores = (
        jnp.einsum("cqhe,ckhe->chqk", queries, keys, preferred_element_type=jnp.float32) * scale
    )
    probs_full = jnp.exp(again_scores - log_total)
    probs_low = probs_full.astype(jnp.bfloat16)
    grad_values = jnp.einsum(
        "chqk,cqhe->ckhe", probs_low, grad_context, preferred_element_type=jnp.float32
    ).astype(jnp.bfloat16)
    grad_probs = jnp.einsum(
        "cqhe,ckhe->chqk", grad_context, values, preferred_element_type=jnp.float32
    )
    row_dot = jnp.sum(probs_full * grad_probs, axis=-1, keepdims=True)
    grad_scores = (probs_full * (grad_probs - row_dot)).astype(jnp.bfloat16)
    grad_queries = (
        jnp.einsum("chqk,ckhe->cqhe", grad_scores, keys, preferred_element_type=jnp.float32) * scale
    ).astype(jnp.bfloat16)
    grad_keys = (
        jnp.einsum("chqk,cqhe->ckhe", grad_scores, queries, preferred_element_type=jnp.float32)
        * scale
    ).astype(jnp.bfloat16)
    grad_joint = jnp.stack([grad_queries, grad_keys, grad_values], axis=2).reshape(rows, 3 * width)
    grad_qkv_weight = tdot(normed, grad_joint)
    grad_normed = ndot(grad_joint, full_qkv)
    first_out, first_back = jax.vjp(norm_rows, start, pre_gain32, pre_shift32)
    through_pre, grad_pre_gain, grad_pre_shift = first_back(grad_normed)
    grad_start = grad_middle + through_pre
    grad_conv_part = jnp.sum(grad_start, axis=0)
    grad_embedded = grad_start.astype(jnp.bfloat16).reshape(chips, seen, width)
    grad_band = jnp.einsum(
        "cvbp,cvd->cbpd", masked, grad_embedded, preferred_element_type=jnp.float32
    )
    grad_band = grad_band.reshape(chips, bands, pix * width)
    grad_pixels = jnp.einsum(
        "cvd,cbpd->cvbp", grad_embedded, band_kernels, preferred_element_type=jnp.float32
    )
    grad_pixels = grad_pixels * valid[:, None, :, None]
    grad_kernels_part = jnp.einsum("cbw,cbk->wk", onehot, grad_band, precision=HIGH)
    kernel_sum, grad_conv = lax.psum((grad_kernels_part, grad_conv_part), AXES)
    kernel_low = kernel_sum.astype(jnp.bfloat16)
    own_low = own_part(kernel_low, 1)
    grad_kernel_weight = tdot(feature_low, own_low)
    grad_kernel_bias = jnp.sum(own_low.astype(jnp.float32), axis=0)
    grad_feature = ndot(kernel_low, full_kernel)
    grad_bias_weight = own_part(source_low.astype(jnp.float32)[:, None] * grad_conv[None, :], 0)
    grad_source = jnp.dot(full_bias_weight.astype(jnp.float32), grad_conv, precision=HIGH)
    core_grads = core_back((grad_feature, grad_source))
    summed = (
        lax.psum_scatter(grad_pre_gain, AXES, scatter_dimension=0, tiled=True),
        lax.psum_scatter(grad_pre_shift, AXES, scatter_dimension=0, tiled=True),
        lax.psum_scatter(grad_qkv_weight, AXES, scatter_dimension=0, tiled=True),
        lax.psum_scatter(grad_out_weight, AXES, scatter_dimension=0, tiled=True),
        lax.psum_scatter(grad_mid_gain, AXES, scatter_dimension=0, tiled=True),
        lax.psum_scatter(grad_mid_shift, AXES, scatter_dimension=0, tiled=True),
        lax.psum_scatter(grad_up_weight, AXES, scatter_dimension=0, tiled=True),
        lax.psum_scatter(grad_up_bias, AXES, scatter_dimension=0, tiled=True),
        lax.psum_scatter(grad_down_weight, AXES, scatter_dimension=0, tiled=True),
        lax.psum_scatter(grad_down_bias, AXES, scatter_dimension=0, tiled=True),
        lax.psum_scatter(grad_dec_weight, AXES, scatter_dimension=0, tiled=True),
        lax.psum_scatter(grad_dec_bias, AXES, scatter_dimension=0, tiled=True),
        lax.psum_scatter(grad_mask, AXES, scatter_dimension=0, tiled=True),
    )
    return (
        decoder_in,
        grad_pixels,
        summed[0],
        summed[1],
        summed[2],
        summed[3],
        summed[4],
        summed[5],
        summed[6],
        summed[7],
        summed[8],
        summed[9],
        summed[10],
        summed[11],
        summed[12],
        own_part(core_grads[0], 1),
        own_part(core_grads[1], 0),
        own_part(core_grads[2], 0),
        own_part(core_grads[3], 0),
        own_part(core_grads[4], 0),
        own_part(core_grads[5], 0),
        own_part(core_grads[6], 0),
        own_part(core_grads[7], 0),
        own_part(core_grads[8], 0),
        own_part(core_grads[9], 0),
        own_part(core_grads[10], 0),
        own_part(core_grads[11], 0),
        grad_kernel_weight,
        grad_kernel_bias,
        grad_bias_weight,
    )


def on_device(
    pixels,
    sensor,
    band_wave,
    visible,
    block_order,
    pre_gain,
    pre_shift,
    qkv_weight,
    out_weight,
    mid_gain,
    mid_shift,
    up_weight,
    up_bias,
    down_weight,
    down_bias,
    dec_weight,
    dec_bias,
    mask_token,
    gen_tokens,
    gen_qkv,
    gen_out,
    gen_out_bias,
    gen_gain1,
    gen_shift1,
    gen_up,
    gen_up_bias,
    gen_down,
    gen_down_bias,
    gen_gain2,
    gen_shift2,
    kernel_weight,
    kernel_bias,
    bias_weight,
    cotangent,
):
    arguments = (
        pixels,
        sensor,
        band_wave,
        visible,
        block_order,
        pre_gain,
        pre_shift,
        qkv_weight,
        out_weight,
        mid_gain,
        mid_shift,
        up_weight,
        up_bias,
        down_weight,
        down_bias,
        dec_weight,
        dec_bias,
        mask_token,
        gen_tokens,
        gen_qkv,
        gen_out,
        gen_out_bias,
        gen_gain1,
        gen_shift1,
        gen_up,
        gen_up_bias,
        gen_down,
        gen_down_bias,
        gen_gain2,
        gen_shift2,
        kernel_weight,
        kernel_bias,
        bias_weight,
        cotangent,
    )
    planes = lax.axis_size("dp") // 2
    devices = planes * 8
    if lax.axis_size("fsdp") != 4 or planes & (planes - 1) or pre_gain.shape[0] % 8:
        return on_device_plain(*arguments)
    low = jnp.bfloat16
    chips, seen, bands, pix = pixels.shape
    width = qkv_weight.shape[0] * devices
    hidden_width = up_weight.shape[1]
    head_dim = width // HEADS
    scale = 1.0 / math.sqrt(head_dim)
    dec_width = dec_weight.shape[1]
    rows = chips * seen
    gen_width = gen_qkv.shape[0] * devices
    up_size = gen_up.shape[1]
    thin = (
        pre_gain, pre_shift, mid_gain, mid_shift, down_bias, up_bias, dec_bias, mask_token,
        gen_out_bias, gen_gain1, gen_shift1, gen_down_bias, gen_gain2, gen_shift2, gen_up_bias,
    )
    thin = tuple(item.reshape(1, -1) for item in thin)
    wave_code = jnp.asarray(code_table(NWAVE, gen_width // 2).astype(low).astype(np.float32))
    valid = band_valid(sensor, bands)
    sizes = (rows, width, hidden_width, dec_width, chips, PATCH)
    share = PATCH // devices
    order = block_order.reshape(PATCH // 128, 128)
    (
        full_wide, full_down, kernels, slots, returned, normed, joint, probs, context, middle,
        normed2, activ, slope, ending, start, ordered, gen_rows, gen_down_full, gen_vec, vecs,
        feature_low, source_low,
    ) = prepare(
        planes,
        (rows, width, hidden_width, dec_width, chips, up_size, PATCH),
        qkv_weight,
        up_weight,
        out_weight,
        dec_weight,
        down_weight,
        kernel_weight,
        kernel_bias,
        pixels.transpose(0, 2, 3, 1).reshape(chips, bands * pix, seen),
        sensor.reshape(1, chips),
        band_wave,
        visible,
        jnp.asarray(code_table(GRID, width // 4)),
        wave_code,
        gen_up,
        gen_qkv,
        gen_out,
        bias_weight,
        gen_tokens.T,
        gen_down,
        cotangent.reshape(devices, chips, share, dec_width),
        order,
        *thin,
    )
    onehot = (band_wave[:, :, None] == jnp.arange(NWAVE, dtype=jnp.int32)[None, None, :]).astype(
        low
    )
    band_kernels = jnp.einsum(
        "cbw,pwd->cbpd",
        onehot,
        kernels.reshape(pix, NWAVE, width),
        preferred_element_type=jnp.float32,
    ).astype(low)
    (
        sum_dec, sum_up, sum_oq, sum_down, grad_kernel_weight, grad_kernel_bias, sum_all,
        gen_wide, gen_tall, gen_seq, gen_lines, grad_bias_weight, grad_embedded, decoder_in,
    ) = backward(
        planes,
        sizes,
        ordered,
        returned.reshape(chips * PATCH, dec_width),
        visible,
        order,
        ending,
        full_wide,
        full_down,
        activ,
        slope,
        normed2,
        middle,
        context,
        joint,
        probs,
        normed,
        start,
        slots,
        vecs,
        kernel_weight,
        feature_low,
        source_low,
        gen_rows,
        gen_down_full,
        gen_vec,
        wave_code,
    )
    handed = hand_out(
        planes,
        (width, hidden_width, dec_width, gen_qkv.shape[0]),
        sum_dec, sum_up, sum_oq, sum_down, grad_kernel_weight, grad_kernel_bias, sum_all,
        gen_wide, gen_tall, gen_seq, gen_lines, grad_bias_weight,
    )
    flat = (0, 1, 4, 5, 7, 9, 11, 12, 16, 17, 18, 20, 22, 23, 24, 26)
    handed = [item.reshape(-1) if i in flat else item for i, item in enumerate(handed)]
    grad_embedded = grad_embedded.reshape(chips, seen, width)
    grad_pixels = jnp.einsum(
        "cvd,cbpd->cvbp", grad_embedded, band_kernels, preferred_element_type=jnp.float32
    )
    grad_pixels = grad_pixels * valid[:, None, :, None]
    decoder_in = decoder_in.reshape(devices * chips, share, dec_width)
    return (decoder_in, grad_pixels) + tuple(handed)


def solution(mesh):
    in_specs = (
        P(AXES, None, None, None),
        P(AXES),
        P(AXES, None),
        P(AXES, None),
        P(),
        P(AXES),
        P(AXES),
        P(AXES, None),
        P(AXES, None),
        P(AXES),
        P(AXES),
        P(AXES, None),
        P(AXES),
        P(AXES, None),
        P(AXES),
        P(AXES, None),
        P(AXES),
        P(AXES),
        P(None, AXES),
        P(AXES, None),
        P(AXES, None),
        P(AXES),
        P(AXES),
        P(AXES),
        P(AXES, None),
        P(AXES),
        P(AXES, None),
        P(AXES),
        P(AXES),
        P(AXES),
        P(None, AXES),
        P(AXES),
        P(AXES, None),
        P(None, AXES, None),
    )
    out_specs = (
        P(None, AXES, None),
        P(AXES, None, None, None),
        P(AXES),
        P(AXES),
        P(AXES, None),
        P(AXES, None),
        P(AXES),
        P(AXES),
        P(AXES, None),
        P(AXES),
        P(AXES, None),
        P(AXES),
        P(AXES, None),
        P(AXES),
        P(AXES),
        P(None, AXES),
        P(AXES, None),
        P(AXES, None),
        P(AXES),
        P(AXES),
        P(AXES),
        P(AXES, None),
        P(AXES),
        P(AXES, None),
        P(AXES),
        P(AXES),
        P(AXES),
        P(None, AXES),
        P(AXES),
        P(AXES, None),
    )
    return jax.shard_map(
        on_device, mesh=mesh, in_specs=in_specs, out_specs=out_specs, check_vma=False
    )
```
